32 devices in a mesh: dp: 8 (over z, x), tensor: 4 (over y, core).
Axes of the slice: x: 2, y: 2, z: 4, core: 2. Of those that a mesh axis runs over, the one named last changes fastest.
Arguments:
- tokens: bfloat16 [5120, 2048], P('dp'), may hold values from -6 to 6
- cotangent: bfloat16 [5120, 2048], P('dp'), may hold values from -6 to 6
- gain_attn: bfloat16 [2048], replicated, may hold values from 0.099609375 to 1.8984375
- gain_mlp: bfloat16 [2048], replicated, may hold values from 0.099609375 to 1.8984375
- w_query: bfloat16 [2048, 2048], P(None, 'tensor'), may hold values from -0.125 to 0.125
- w_kv: bfloat16 [2048, 2, 512], P(None, None, 'tensor'), may hold values from -0.125 to 0.125
- w_out: bfloat16 [2048, 2048], P('tensor'), may hold values from -1 to 1
- w_gate_up: bfloat16 [2048, 2, 8192], P(None, None, 'tensor'), may hold values from -0.125 to 0.125
- w_down: bfloat16 [8192, 2048], P('tensor'), may hold values from -0.0625 to 0.0625
- a_attn: bfloat16 [2048, 3, 4, 16], replicated, may hold values from -0.125 to 0.125
- b_query: bfloat16 [4, 16, 2048], P(None, None, 'tensor'), may hold values from -0.75 to 0.75
- b_kv: bfloat16 [4, 16, 2, 512], P(None, None, None, 'tensor'), may hold values from -0.75 to 0.75
- a_out: bfloat16 [2048, 4, 16], P('tensor'), may hold values from -1 to 1
- b_out: bfloat16 [4, 16, 2048], replicated, may hold values from -0.75 to 0.75
- a_mlp: bfloat16 [2048, 2, 4, 16], replicated, may hold values from -0.125 to 0.125
- b_mlp: bfloat16 [4, 16, 2, 8192], P(None, None, None, 'tensor'), may hold values from -0.75 to 0.75
- a_down: bfloat16 [8192, 4, 16], P('tensor'), may hold values from -0.125 to 0.125
- b_down: bfloat16 [4, 16, 2048], replicated, may hold values from -0.75 to 0.75
- prompt_adapter: int32 [8], P('dp'), may hold values from 0 to 3
- cont_adapter: int32 [16], P('dp'), may hold values from 0 to 3
- group_map: int32 [16], replicated, may hold values from 0 to 7, as said below
Outputs:
- output: bfloat16 [5120, 2048], P('dp')
- tokens_grad: bfloat16 [5120, 2048], P('dp')
- grad_a_attn: float32 [2048, 3, 4, 16], replicated
- grad_b_query: float32 [4, 16, 2048], P(None, None, 'tensor')
- grad_b_kv: float32 [4, 16, 2, 512], P(None, None, None, 'tensor')
- grad_a_out: float32 [2048, 4, 16], P('tensor')
- grad_b_out: float32 [4, 16, 2048], replicated
- grad_a_mlp: float32 [2048, 2, 4, 16], replicated
- grad_b_mlp: float32 [4, 16, 2, 8192], P(None, None, None, 'tensor')
- grad_a_down: float32 [8192, 4, 16], P('tensor')
- grad_b_down: float32 [4, 16, 2048], replicated
The draws below stay inside these ranges and needn't reach their ends.
Inputs may be any that keep to these rules, and one draw needn't show every extreme that they name: `group_map`: every prompt is named by exactly 2 continuations.
All inputs are finite; a program needn't handle non-finite values.
Results may differ from the reference program's by a relative error of at most 0.02.
Values may be sent and summed in bfloat16 or wider, within the bound.
A program may use at most 256 MiB of HBM per device.

```python
import math
import jax
import jax.numpy as jnp
from jax import lax

D = 2048
H = 32
KV = 8
HD = 64
FF = 8192
R = 16
NA = 4
PLEN = 384
CLEN = 128
CONT_DEV = 2
PROMPTS = 8
CONTS = 16
TOK_DEV = 640
TOKENS = 5120


def one_order(subkey):
    return jax.random.permutation(subkey, PROMPTS)


def draw_group_map(key, part):
    key = jax.random.fold_in(key, 11)
    orders = jax.vmap(one_order)(jax.random.split(key, CONT_DEV))
    return jnp.transpose(orders).reshape(PROMPTS * CONT_DEV).astype(jnp.int32)


def plant(array, own_key, least, top_value):
    spot = [jax.random.randint(jax.random.fold_in(own_key, axis), (), 0, length) for axis, length in enumerate(array.shape)]
    longest = array.shape.index(max(array.shape))
    next_to = spot[:longest] + [(spot[longest] + 1) % array.shape[longest]] + spot[longest + 1:]
    return array.at[tuple(spot)].set(least).at[tuple(next_to)].set(top_value)


def block_scale(key, extent, shards, least, largest):
    level = 1.0
    for dim, blocks in shards:
        steps = jax.random.uniform(jax.random.fold_in(jax.random.fold_in(key, 6), dim), (blocks,), jnp.float32, least / len(shards), largest / len(shards))
        level = level * jnp.repeat(jnp.exp(steps), extent[dim] // blocks).reshape((-1,) + (1,) * (len(extent) - 1 - dim))
    return level


def normal_values(key, shape, spread, limit, shards=(), kind=jnp.bfloat16):
    entries = jax.random.normal(key, shape, jnp.float32) * spread
    if len(shards) > 0:
        entries = block_scale(key, shape, shards, -0.22, 0.18) * entries
    return jnp.clip(entries, min=-limit, max=limit).astype(kind)


def setup_inputs(seed: int = 0) -> dict:
    splits = jax.random.split(jax.random.key(seed), 22)
    return {
        "tokens": normal_values(splits[0], (TOKENS, D), 1.0, 6.0, ((0, 8),)),
        "cotangent": normal_values(splits[1], (TOKENS, D), 1.0, 6.0, ((0, 8),)),
        "gain_attn": jnp.clip(1.0 + 0.18 * jax.random.normal(splits[2], (D,), jnp.float32), 0.099609375, 1.8984375).astype(jnp.bfloat16),
        "gain_mlp": jnp.clip(1.0 + 0.18 * jax.random.normal(splits[3], (D,), jnp.float32), 0.099609375, 1.8984375).astype(jnp.bfloat16),
        "w_query": normal_values(splits[4], (D, H * HD), D ** -0.5, 0.125, ((1, 4),)),
        "w_kv": normal_values(splits[5], (D, 2, KV * HD), D ** -0.5, 0.125, ((2, 4),)),
        "w_out": normal_values(splits[6], (H * HD, D), (max(H * HD // 64, 1)) ** -0.5, 1.0, ((0, 4),)),
        "w_gate_up": normal_values(splits[7], (D, 2, FF), D ** -0.5, 0.125, ((2, 4),)),
        "w_down": normal_values(splits[8], (FF, D), FF ** -0.5, 0.0625, ((0, 4),)),
        "a_attn": normal_values(splits[9], (D, 3, NA, R), D ** -0.5, 0.125),
        "b_query": normal_values(splits[10], (NA, R, H * HD), (4 * R) ** -0.5, 0.75, ((2, 4),)),
        "b_kv": normal_values(splits[11], (NA, R, 2, KV * HD), (4 * R) ** -0.5, 0.75, ((3, 4),)),
        "a_out": normal_values(splits[12], (H * HD, NA, R), (max(H * HD // 64, 1)) ** -0.5, 1.0, ((0, 4),)),
        "b_out": normal_values(splits[13], (NA, R, D), (4 * R) ** -0.5, 0.75),
        "a_mlp": normal_values(splits[14], (D, 2, NA, R), D ** -0.5, 0.125),
        "b_mlp": normal_values(splits[15], (NA, R, 2, FF), (4 * R) ** -0.5, 0.75, ((3, 4),)),
        "a_down": normal_values(splits[16], (FF, NA, R), (FF // 4) ** -0.5, 0.125, ((0, 4),)),
        "b_down": normal_values(splits[17], (NA, R, D), (4 * R) ** -0.5, 0.75),
        "prompt_adapter": plant(jax.random.randint(splits[18], (PROMPTS,), 0, NA), jax.random.fold_in(splits[18], 1), 0, NA - 1).astype(jnp.int32),
        "cont_adapter": plant(jax.random.randint(splits[19], (CONTS,), 0, NA), jax.random.fold_in(splits[19], 1), 0, NA - 1).astype(jnp.int32),
        "group_map": draw_group_map(jax.random.fold_in(splits[21], 71), 0),
    }


PRECISE = lax.Precision.HIGHEST
EPSILON = 1e-05
ROPE_BASE = 500000.0
MASKED_SCORE = -1e+30

@jax.custom_vjp
def low(v):
    return lax.optimization_barrier(v.astype(jnp.bfloat16)).astype(jnp.float32)

@jax.custom_vjp
def low_back(v):
    return v

def low_keep(v):
    return (low(v), None)

def low_pass(kept, grad):
    return (grad,)

def back_keep(v):
    return (v, None)

def back_low(kept, grad):
    return (low(grad),)
low.defvjp(low_keep, low_pass)
low_back.defvjp(back_keep, back_low)

def rounded_both(value):
    return low(low_back(value))

def exact_dot(left, right):
    return jnp.dot(left, right, precision=PRECISE, preferred_element_type=jnp.float32)

def rms_norm(value, gain):
    return value * lax.rsqrt(lax.optimization_barrier(jnp.mean(value * value, axis=-1, keepdims=True)) + EPSILON) * gain

def rotate(value, cosine, sine):
    half = value.shape[-1] // 2
    first = value[..., :half]
    second = value[..., half:]
    return jnp.concatenate([first * cosine - second * sine, second * cosine + first * sine], axis=-1)

def layout_rows():
    segment = jnp.concatenate([jnp.zeros((PLEN,), jnp.int32), 1 + jnp.arange(CONT_DEV * CLEN, dtype=jnp.int32) // CLEN])
    position = jnp.concatenate([jnp.arange(PLEN, dtype=jnp.int32), PLEN + jnp.arange(CONT_DEV * CLEN, dtype=jnp.int32) % CLEN])
    return (segment, position)

def rope_tables(position):
    exponent = jnp.arange(HD // 2, dtype=jnp.float32) * (2.0 / HD)
    frequency = jnp.exp(-math.log(ROPE_BASE) * exponent)
    angle = position.astype(jnp.float32)[:, None] * frequency[None, :]
    return (jnp.cos(angle)[:, None, :], jnp.sin(angle)[:, None, :])

def allowed_keys(segment):
    row_index = jnp.arange(segment.shape[0], dtype=jnp.int32)
    inside = (segment[:, None] == segment[None, :]) & (row_index[None, :] <= row_index[:, None])
    remote = segment[:, None] == (1 + jnp.arange(CONT_DEV, dtype=jnp.int32))[None, :]
    return jnp.concatenate([inside, jnp.repeat(remote, PLEN, axis=1)], axis=1)

def selection(prompt_ids, cont_ids, segment):
    table = jnp.concatenate([prompt_ids, cont_ids])
    member = (segment[:, None] == jnp.arange(1 + CONT_DEV, dtype=jnp.int32)[None, :]).astype(jnp.int32)
    adapter_ids = lax.optimization_barrier(jnp.sum(member * table[None, :], axis=1))
    onehot = (adapter_ids[:, None] == jnp.arange(NA, dtype=jnp.int32)[None, :]).astype(jnp.float32)
    return jnp.repeat(onehot, R, axis=1)

def reference(tokens, cotangent, gain_attn, gain_mlp, w_query, w_kv, w_out, w_gate_up, w_down, a_attn, b_query, b_kv, a_out, b_out, a_mlp, b_mlp, a_down, b_down, prompt_adapter, cont_adapter, group_map):
    ranked = NA * R
    kv_width = KV * HD
    group = H // KV
    scale = 1.0 / math.sqrt(HD)
    segment, position = layout_rows()
    cosine, sine = rope_tables(position)
    cosine = jnp.tile(cosine, (PROMPTS, 1, 1))
    sine = jnp.tile(sine, (PROMPTS, 1, 1))
    allowed = allowed_keys(segment)
    select = jax.vmap(selection, in_axes=(0, 0, None))(prompt_adapter[:, None], cont_adapter.reshape(PROMPTS, CONT_DEV), segment).reshape(TOKENS, ranked)
    partners = group_map.reshape(PROMPTS, CONT_DEV)
    gain_one = gain_attn.astype(jnp.float32)
    gain_two = gain_mlp.astype(jnp.float32)
    query_weight = w_query.astype(jnp.float32)
    kv_weight = w_kv.astype(jnp.float32)
    out_weight = w_out.astype(jnp.float32)
    gate_up_weight = w_gate_up.astype(jnp.float32)
    down_weight = w_down.astype(jnp.float32)

    def attend(pieces):
        queries, keys, values = pieces
        grouped = queries.reshape(TOK_DEV, KV, group, HD)
        scores = low_back(jnp.einsum('tkgd,skd->kgts', grouped, keys, precision=PRECISE) * scale)
        scores = jnp.where(allowed[None, None], scores, MASKED_SCORE)
        top = lax.optimization_barrier(jnp.max(scores, axis=-1, keepdims=True))
        weight = jnp.exp(scores - top)
        probs = low(weight / lax.optimization_barrier(jnp.sum(weight, axis=-1, keepdims=True)))
        return jnp.einsum('kgts,skd->tkgd', probs, values, precision=PRECISE).reshape(TOK_DEV, H * HD)

    def forward(inputs, fa_attn, fb_query, fb_kv, fa_out, fb_out, fa_mlp, fb_mlp, fa_down, fb_down):
        normed_one = low(rms_norm(inputs, gain_one))
        adapter_qkv = low(exact_dot(normed_one, fa_attn.reshape(D, 3 * ranked)) * jnp.tile(select, (1, 3)))
        query_pre = low_back(exact_dot(normed_one, query_weight[:, :]) + exact_dot(adapter_qkv[:, :ranked], fb_query.reshape(ranked, H * HD)))
        key_pre = low_back(exact_dot(normed_one, kv_weight[:, 0]) + exact_dot(adapter_qkv[:, ranked:2 * ranked], fb_kv[:, :, 0].reshape(ranked, kv_width)))
        values = rounded_both(exact_dot(normed_one, kv_weight[:, 1]) + exact_dot(adapter_qkv[:, 2 * ranked:], fb_kv[:, :, 1].reshape(ranked, kv_width)))
        queries = rounded_both(rotate(query_pre.reshape(TOKENS, H, HD), cosine, sine))
        keys = rounded_both(rotate(key_pre.reshape(TOKENS, KV, HD), cosine, sine))
        values = values.reshape(TOKENS, KV, HD)
        key_blocks = keys.reshape(PROMPTS, TOK_DEV, KV, HD)
        value_blocks = values.reshape(PROMPTS, TOK_DEV, KV, HD)
        far_keys = key_blocks[:, :PLEN][partners].reshape(PROMPTS, CONT_DEV * PLEN, KV, HD)
        far_values = value_blocks[:, :PLEN][partners].reshape(PROMPTS, CONT_DEV * PLEN, KV, HD)
        all_keys = jnp.concatenate([key_blocks, far_keys], axis=1)
        all_values = jnp.concatenate([value_blocks, far_values], axis=1)
        query_blocks = queries.reshape(PROMPTS, TOK_DEV, H, HD)
        attended = rounded_both(lax.map(jax.checkpoint(attend), (query_blocks, all_keys, all_values)).reshape(TOKENS, H * HD))
        adapter_out = low_back(exact_dot(attended, fa_out.reshape(H * HD, ranked)) * select)
        attn = low_back(exact_dot(attended, out_weight) + exact_dot(adapter_out, fb_out.reshape(ranked, D)))
        resid = inputs + attn
        normed_two = low(rms_norm(resid, gain_two))
        adapter_mlp = low(exact_dot(normed_two, fa_mlp.reshape(D, 2 * ranked)) * jnp.tile(select, (1, 2)))
        gate = low_back(exact_dot(normed_two, gate_up_weight[:, 0]) + exact_dot(adapter_mlp[:, :ranked], fb_mlp[:, :, 0].reshape(ranked, FF)))
        upper = low_back(exact_dot(normed_two, gate_up_weight[:, 1]) + exact_dot(adapter_mlp[:, ranked:], fb_mlp[:, :, 1].reshape(ranked, FF)))
        activ = low(jax.nn.silu(gate) * upper)
        adapter_down = low_back(exact_dot(activ, fa_down.reshape(FF, ranked)) * select)
        return resid + exact_dot(activ, down_weight) + exact_dot(adapter_down, fb_down.reshape(ranked, D))

    def widen(value):
        return value.astype(jnp.float32)
    result, pullback = jax.vjp(forward, widen(tokens), widen(a_attn), widen(b_query), widen(b_kv), widen(a_out), widen(b_out), widen(a_mlp), widen(b_mlp), widen(a_down), widen(b_down))
    grads = pullback(widen(cotangent))
    return (result.astype(jnp.bfloat16), grads[0].astype(jnp.bfloat16), grads[1], grads[2], grads[3], grads[4], grads[5], grads[6], grads[7], grads[8], grads[9])
```

```python
import functools
import math

import jax
import jax.numpy as jnp
import numpy as np
from jax import lax
from jax.experimental import pallas as pl
from jax.experimental.pallas import tpu as pltpu
from jax.sharding import PartitionSpec as P

HD = 64
R = 16
NA = 4
RK = NA * R
PLEN = 384
CLEN = 128
CONT_DEV = 2
ROWS = PLEN + CONT_DEV * CLEN
EPSILON = 1e-05
ROPE_BASE = 500000.0
MASKED_SCORE = -1e30

BF = jnp.bfloat16
F32 = jnp.float32
VM = pltpu.VMEM
LANE = 128


def dn(a, b):
    return jnp.dot(a, b, preferred_element_type=F32)


def dt(a, b):
    return lax.dot_general(a, b, (((1,), (1,)), ((), ())), preferred_element_type=F32)


def dr(a, b):
    return lax.dot_general(a, b, (((0,), (0,)), ((), ())), preferred_element_type=F32)


def sel_row(adapter):
    lane = lax.broadcasted_iota(jnp.int32, (1, RK), 1)
    return (lax.shift_right_logical(lane, 4) == adapter).astype(F32)


def swap_halves(v):
    lane = lax.broadcasted_iota(jnp.int32, v.shape, 1)
    return jnp.where((lane & 63) < 32, pltpu.roll(v, LANE - 32, 1), pltpu.roll(v, 32, 1))


def rot(v, cos, sin):
    return v * cos + swap_halves(v) * sin


def call(kernel, name, ins, outs, scratch=(), grid=None, in_specs=None, out_specs=None, flops=0, limit=56 << 20):
    nbytes = sum(int(np.prod(a.shape)) * a.dtype.itemsize for a in ins) + sum(
        int(np.prod(s)) * jnp.dtype(d).itemsize for s, d in outs
    )
    whole = pl.BlockSpec(memory_space=VM)
    smem = pl.BlockSpec(memory_space=pltpu.SMEM)
    if in_specs is None:
        in_specs = [smem] + [whole] * (len(ins) - 1)
    if out_specs is None:
        out_specs = [whole] * len(outs)
    kw = {} if grid is None else {"grid": grid}
    return pl.pallas_call(
        kernel,
        out_shape=[jax.ShapeDtypeStruct(s, d) for s, d in outs],
        in_specs=in_specs,
        out_specs=out_specs,
        scratch_shapes=list(scratch),
        compiler_params=pltpu.CompilerParams(vmem_limit_bytes=limit),
        cost_estimate=pl.CostEstimate(flops=int(flops), bytes_accessed=int(nbytes), transcendentals=0),
        name=name,
        **kw,
    )(*ins)


def qkv_kernel(sc, x_ref, gain, aT, wq, wkv, bq, bkv, cos_ref, sin_ref, n1_ref, q_ref, k_ref, v_ref, u_ref):
    rows = x_ref.shape[0]
    x = x_ref[...].astype(F32)
    inv = lax.rsqrt(jnp.mean(x * x, axis=-1, keepdims=True) + EPSILON)
    n1_ref[...] = (x * inv * gain[...].astype(F32)).astype(BF)
    n1 = n1_ref[...]
    row = pl.program_id(0) * rows + lax.broadcasted_iota(jnp.int32, (rows, RK), 0)
    adapter = jnp.where(row < PLEN, sc[0], jnp.where(row < PLEN + CLEN, sc[1], sc[2]))
    lane = lax.broadcasted_iota(jnp.int32, (rows, RK), 1)
    sel = (lax.shift_right_logical(lane, 4) == adapter).astype(F32)
    u = dt(n1, aT[...])
    for part in range(3):
        u_ref[:, part * RK : (part + 1) * RK] = (u[:, part * RK : (part + 1) * RK] * sel).astype(BF)
    cos = cos_ref[...]
    sin = sin_ref[...]
    q = dn(n1, wq[...]) + dn(u_ref[:, :RK], bq[...])
    for c in range(q.shape[1] // LANE):
        q_ref[:, c * LANE : (c + 1) * LANE] = (
            rot(q[:, c * LANE : (c + 1) * LANE], cos, sin).astype(BF) * BF(0.125)
        )
    kv = dn(n1, wkv[...])
    width = k_ref.shape[1]
    kp = kv[:, :width] + dn(u_ref[:, RK : 2 * RK], bkv[:, :width])
    k_ref[...] = rot(kp, cos, sin).astype(BF)
    v_ref[...] = (kv[:, width:] + dn(u_ref[:, 2 * RK :], bkv[:, width:])).astype(BF)


def stack_heads(ref, r0, g):
    return jnp.concatenate(
        [ref[r0 : r0 + CLEN, (4 * g + h) * HD : (4 * g + h + 1) * HD] for h in range(4)], axis=0
    )


def softmax_low(s):
    top = jnp.max(s, axis=-1, keepdims=True)
    e = jnp.exp(s - top)
    return (e * (1.0 / jnp.sum(e, axis=-1, keepdims=True))).astype(BF)


def causal_tile():
    r = lax.broadcasted_iota(jnp.int32, (4 * CLEN, CLEN), 0) & (CLEN - 1)
    c = lax.broadcasted_iota(jnp.int32, (4 * CLEN, CLEN), 1)
    return c <= r


def project_out(sc, o_ref, wo, aoT, mine, other, scr):
    half = mine.shape[0]
    o = o_ref[...]
    width = wo.shape[1]
    for n in range(0, width, 512):
        part = dn(o, wo[:, n : n + 512]).astype(BF)
        scr[0, :, n : n + 512] = part[:half]
        scr[1, :, n : n + 512] = part[half:]
    u = dt(o, aoT[...]).astype(BF)
    pad = jnp.zeros((half, LANE - RK), BF)
    scr[0, :, width:] = jnp.concatenate([u[:half], pad], axis=1)
    scr[1, :, width:] = jnp.concatenate([u[half:], pad], axis=1)
    lo = sc[3]
    mine[...] = scr[lo]
    other[...] = scr[1 - lo]


P_OFF = (0, 128, 384)


def attn_p_kernel(sc, q_ref, k_ref, v_ref, wo, aoT, p_ref, o_ref, mine, other, scr):
    mask = causal_tile()
    for g in range(2):
        kg = k_ref[:, g * HD : (g + 1) * HD]
        vg = v_ref[:, g * HD : (g + 1) * HD]
        for i in range(PLEN // CLEN):
            size = (i + 1) * CLEN
            s = dt(stack_heads(q_ref, i * CLEN, g), kg[:size])
            tail = jnp.where(mask, s[:, size - CLEN :], MASKED_SCORE)
            s = tail if i == 0 else jnp.concatenate([s[:, : size - CLEN], tail], axis=1)
            p = softmax_low(s)
            p_ref[g, :, P_OFF[i] : P_OFF[i] + size] = p
            o = dn(p, vg[:size]).astype(BF)
            for h in range(4):
                o_ref[i * CLEN : (i + 1) * CLEN, (4 * g + h) * HD : (4 * g + h + 1) * HD] = o[
                    h * CLEN : (h + 1) * CLEN
                ]
    project_out(sc, o_ref, wo, aoT, mine, other, scr)


def attn_c_kernel(sc, q_ref, k_ref, v_ref, far, wo, aoT, p_ref, o_ref, mine, other, scr):
    mask = causal_tile()
    width = k_ref.shape[1]
    for j in range(CONT_DEV):
        r0 = j * CLEN
        for g in range(2):
            lanes = slice(g * HD, (g + 1) * HD)
            vlanes = slice(width + g * HD, width + (g + 1) * HD)
            qs = stack_heads(q_ref, r0, g)
            sf = dt(qs, far[j, :, lanes])
            so = jnp.where(mask, dt(qs, k_ref[r0 : r0 + CLEN, lanes]), MASKED_SCORE)
            p = softmax_low(jnp.concatenate([sf, so], axis=1))
            p_ref[j, g] = p
            o = (dn(p[:, :PLEN], far[j, :, vlanes]) + dn(p[:, PLEN:], v_ref[r0 : r0 + CLEN, lanes])).astype(BF)
            for h in range(4):
                o_ref[r0 : r0 + CLEN, (4 * g + h) * HD : (4 * g + h + 1) * HD] = o[h * CLEN : (h + 1) * CLEN]
    project_out(sc, o_ref, wo, aoT, mine, other, scr)


def norm2_kernel(which, sc, s_ref, t_ref, x_ref, gain, bo, h_ref, n2u_ref):
    width = x_ref.shape[1]
    sel = sel_row(sc[which] if which == 0 else sc[1 + sc[3]])
    u = ((s_ref[:, width : width + RK].astype(F32) + t_ref[:, width : width + RK].astype(F32)) * sel).astype(BF)
    attn = s_ref[:, :width].astype(F32) + t_ref[:, :width].astype(F32) + dn(u, bo[...])
    h = x_ref[...].astype(F32) + attn
    h_ref[...] = h
    inv = lax.rsqrt(jnp.mean(h * h, axis=-1, keepdims=True) + EPSILON)
    n2u_ref[:, :width] = (h * inv * gain[...].astype(F32)).astype(BF)
    n2u_ref[:, width:] = jnp.concatenate([u, jnp.zeros((u.shape[0], LANE - RK), BF)], axis=1)


def row_sel(which, sc, rows):
    if which == 0:
        return sel_row(sc[0])
    return jnp.concatenate(
        [jnp.broadcast_to(sel_row(sc[1]), (rows // 2, RK)), jnp.broadcast_to(sel_row(sc[2]), (rows // 2, RK))], axis=0
    )


def dact_kernel(sc, dy_ref, wd, bd, adT, dact_ref, dud_ref):
    @pl.when(pl.program_id(0) == 0)
    def _():
        sel = jnp.concatenate(
            [
                jnp.broadcast_to(sel_row(sc[0]), (PLEN, RK)),
                jnp.broadcast_to(sel_row(sc[1]), (CLEN, RK)),
                jnp.broadcast_to(sel_row(sc[2]), (CLEN, RK)),
            ],
            axis=0,
        )
        dud_ref[...] = (dt(dy_ref[...], bd[...]) * sel).astype(BF)

    dact_ref[...] = dt(dy_ref[...], wd[...]) + dn(dud_ref[...], adT[...])


def mlp_kernel(
    which, sc, mine, other, dact, dud, wg, wu, wd, bg, bu, adT, amT,
    mlp_mine, mlp_other, dn2_mine, dn2_other, gbg, gbu, gadT,
    n2s, um, mlp_acc, dn2_acc, ud_acc, dum_acc,
):
    half, width = mine.shape[0], mlp_acc.shape[1]
    rows = 2 * half
    lo = sc[3]
    step = pl.program_id(0)

    @pl.when(step == 0)
    def _():
        n2s[lo] = mine[:, :width]
        n2s[1 - lo] = other[:, :width]
        sel = row_sel(which, sc, rows)
        u = dt(n2s[...].reshape(rows, width), amT[...])
        um[:, :RK] = (u[:, :RK] * sel).astype(BF)
        um[:, RK:] = (u[:, RK:] * sel).astype(BF)

    n2 = n2s[...].reshape(rows, width)
    ug = um[:, :RK]
    uu = um[:, RK:]
    gate = dn(n2, wg[...]) + dn(ug, bg[...])
    upper = dn(n2, wu[...]) + dn(uu, bu[...])
    sigma = 1.0 / (1.0 + jnp.exp(-gate))
    silu = gate * sigma
    act = (silu * upper).astype(BF)
    da = dact[...].astype(F32)
    dg = (da * upper * (sigma * (1.0 + gate * (1.0 - sigma)))).astype(BF)
    du = (da * silu).astype(BF)
    gbg[...] = dr(ug, dg)
    gbu[...] = dr(uu, du)
    gadT[...] = dr(dud[...], act)
    mlp_part = dn(act, wd[...])
    dn2_part = dt(dg, wg[...]) + dt(du, wu[...])
    ud_part = dt(act, adT[...])
    dum_part = jnp.concatenate([dt(dg, bg[...]), dt(du, bu[...])], axis=1)

    @pl.when(step == 0)
    def _():
        mlp_acc[...] = mlp_part
        dn2_acc[...] = dn2_part
        ud_acc[...] = ud_part
        dum_acc[...] = dum_part

    @pl.when(step > 0)
    def _():
        mlp_acc[...] += mlp_part
        dn2_acc[...] += dn2_part
        ud_acc[...] += ud_part
        dum_acc[...] += dum_part

    @pl.when(step == pl.num_programs(0) - 1)
    def _():
        pad = jnp.zeros((half, LANE - RK), BF)
        for ref, who in ((mlp_mine, lo), (mlp_other, 1 - lo)):
            start = pl.multiple_of(who * half, half)
            ref[:, :width] = mlp_acc[pl.ds(start, half)].astype(BF)
            ref[:, width:] = jnp.concatenate([ud_acc[pl.ds(start, half)].astype(BF), pad], axis=1)
        for ref, who in ((dn2_mine, lo), (dn2_other, 1 - lo)):
            start = pl.multiple_of(who * half, half)
            ref[:, :width] = dn2_acc[pl.ds(start, half)].astype(BF)
            ref[:, width:] = dum_acc[pl.ds(start, half)].astype(BF)


def norm_back(v, gain, upstream):
    inv = lax.rsqrt(jnp.mean(v * v, axis=-1, keepdims=True) + EPSILON)
    scaled = v * inv
    weighted = upstream * gain
    return inv * (weighted - scaled * jnp.mean(weighted * scaled, axis=-1, keepdims=True))


def nbwd_kernel(which, sc, s_ref, t_ref, h_ref, dy_ref, gain, amT, dh_ref, dau_ref):
    width = h_ref.shape[1]
    sel = sel_row(sc[which] if which == 0 else sc[1 + sc[3]])
    du = s_ref[:, width:].astype(F32) + t_ref[:, width:].astype(F32)
    dum = (du * jnp.concatenate([sel, sel], axis=1)).astype(BF)
    dn2 = s_ref[:, :width].astype(F32) + t_ref[:, :width].astype(F32) + dn(dum, amT[...])
    dh = dy_ref[...].astype(F32) + norm_back(h_ref[...], gain[...].astype(F32), dn2)
    dh_ref[...] = dh
    dau_ref[:, :width] = dh.astype(BF)
    dau_ref[:, width:] = dum


def out_kernel(which, sc, s_ref, t_ref, h_ref, bd, out_ref):
    width = h_ref.shape[1]
    sel = sel_row(sc[which] if which == 0 else sc[1 + sc[3]])
    u = ((s_ref[:, width : width + RK].astype(F32) + t_ref[:, width : width + RK].astype(F32)) * sel).astype(BF)
    mlp = s_ref[:, :width].astype(F32) + t_ref[:, :width].astype(F32) + dn(u, bd[...])
    out_ref[:, :width] = (h_ref[...] + mlp).astype(BF)
    out_ref[:, width:] = jnp.concatenate([u, jnp.zeros((u.shape[0], LANE - RK), BF)], axis=1)


def out_grads(which, sc, mine, other, n2_mine, n2_other, o_ref, wo, aoT, bo, do_ref, gaoT, gbo, gamT, das):
    half = mine.shape[0]
    width = das.shape[2]
    rows = 2 * half
    lo = sc[3]
    das[lo] = mine[:, :width]
    das[1 - lo] = other[:, :width]
    da = das[...].reshape(rows, width)
    duo = (dt(da, bo[...]) * row_sel(which, sc, rows)).astype(BF)
    do_ref[...] = (dt(da, wo[...]) + dn(duo, aoT[...])).astype(BF)
    gaoT[...] = dr(duo, o_ref[...])
    quarter = gbo.shape[1]
    col = pl.ds(pl.multiple_of(sc[4] * quarter, quarter), quarter)
    gbo[...] = dr(n2_mine[:, width : width + RK], mine[:, col]) + dr(n2_other[:, width : width + RK], other[:, col])
    gamT[...] = dr(mine[:, width:], n2_mine[:, col]) + dr(other[:, width:], n2_other[:, col])


def put_dq(dq, dq_ref, r0, g):
    for h in range(4):
        dq_ref[r0 : r0 + CLEN, (4 * g + h) * HD : (4 * g + h + 1) * HD] = dq[h * CLEN : (h + 1) * CLEN]


def back_scores(p, dp):
    pf = p.astype(F32)
    return (pf * (dp - jnp.sum(pf * dp, axis=-1, keepdims=True))).astype(BF)


def unrotate_q(dq_scr, cos_ref, sin_ref, dqp_ref):
    cos = cos_ref[...]
    sin = sin_ref[...]
    for c in range(dqp_ref.shape[1] // LANE):
        lanes = slice(c * LANE, (c + 1) * LANE)
        dqp_ref[:, lanes] = rot(dq_scr[:, lanes].astype(F32), cos, -sin).astype(BF)


def abwd_p_kernel(
    sc, mine, other, n2_mine, n2_other, o_ref, wo, aoT, bo, p_ref, q_ref, k_ref, v_ref, cos_ref, sin_ref,
    dqp_ref, dkv_ref, gaoT, gbo, gamT,
    das, do_ref, dq_scr,
):
    out_grads(0, sc, mine, other, n2_mine, n2_other, o_ref, wo, aoT, bo, do_ref, gaoT, gbo, gamT, das)
    width = k_ref.shape[1]
    for g in range(2):
        lanes = slice(g * HD, (g + 1) * HD)
        vlanes = slice(width + g * HD, width + (g + 1) * HD)
        kg = k_ref[:, lanes]
        vg = v_ref[:, lanes]
        for i in reversed(range(PLEN // CLEN)):
            size = (i + 1) * CLEN
            qi = stack_heads(q_ref, i * CLEN, g)
            doi = stack_heads(do_ref, i * CLEN, g)
            p = p_ref[g, :, P_OFF[i] : P_OFF[i] + size]
            ds = back_scores(p, dt(doi, vg[:size]))
            put_dq((dn(ds, kg[:size]) * 0.125).astype(BF), dq_scr, i * CLEN, g)
            dk = dr(ds, qi)
            dv = dr(p, doi)
            if size == PLEN:
                dkv_ref[:, lanes] = dk
                dkv_ref[:, vlanes] = dv
            else:
                dkv_ref[:size, lanes] += dk
                dkv_ref[:size, vlanes] += dv
    unrotate_q(dq_scr, cos_ref, sin_ref, dqp_ref)


def abwd_c_kernel(
    sc, mine, other, n2_mine, n2_other, o_ref, wo, aoT, bo, p_ref, q_ref, k_ref, v_ref, far, cos_ref, sin_ref,
    dqp_ref, dkvp_ref, dfar_ref, gaoT, gbo, gamT,
    das, do_ref, dq_scr, dkv_scr,
):
    out_grads(1, sc, mine, other, n2_mine, n2_other, o_ref, wo, aoT, bo, do_ref, gaoT, gbo, gamT, das)
    width = k_ref.shape[1]
    for j in range(CONT_DEV):
        r0 = j * CLEN
        for g in range(2):
            lanes = slice(g * HD, (g + 1) * HD)
            vlanes = slice(width + g * HD, width + (g + 1) * HD)
            qi = stack_heads(q_ref, r0, g)
            doi = stack_heads(do_ref, r0, g)
            p = p_ref[j, g]
            dp = jnp.concatenate([dt(doi, far[j, :, vlanes]), dt(doi, v_ref[r0 : r0 + CLEN, lanes])], axis=1)
            ds = back_scores(p, dp)
            dq = dn(ds[:, :PLEN], far[j, :, lanes]) + dn(ds[:, PLEN:], k_ref[r0 : r0 + CLEN, lanes])
            put_dq((dq * 0.125).astype(BF), dq_scr, r0, g)
            dk = dr(ds, qi)
            dv = dr(p, doi)
            dfar_ref[j, :, lanes] = dk[:PLEN]
            dfar_ref[j, :, vlanes] = dv[:PLEN]
            dkv_scr[r0 : r0 + CLEN, lanes] = dk[PLEN:]
            dkv_scr[r0 : r0 + CLEN, vlanes] = dv[PLEN:]
    unrotate_q(dq_scr, cos_ref, sin_ref, dqp_ref)
    dkvp_ref[:, :width] = rot(dkv_scr[:, :width].astype(BF).astype(F32), cos_ref[...], -sin_ref[...]).astype(BF)
    dkvp_ref[:, width:] = dkv_scr[:, width:].astype(BF)


def dn1_tail(sc, which, dqp, dkvp, u_ref, wq, wkv, bq, bkv, mine, other, gbq, gbkv, scr):
    half = mine.shape[0]
    width = wq.shape[0]
    kvw = dkvp.shape[1] // 2
    for n in range(0, width, 512):
        part = (dt(dqp, wq[n : n + 512]) + dt(dkvp, wkv[n : n + 512])).astype(BF)
        scr[0, :, n : n + 512] = part[:half]
        scr[1, :, n : n + 512] = part[half:]
    du = jnp.concatenate(
        [
            dt(dqp, bq[...]),
            dt(dkvp[:, :kvw], bkv[:, :kvw]),
            dt(dkvp[:, kvw:], bkv[:, kvw:]),
            jnp.zeros((2 * half, RK), F32),
        ],
        axis=1,
    ).astype(BF)
    scr[0, :, width:] = du[:half]
    scr[1, :, width:] = du[half:]
    gbq[...] = dr(u_ref[:, :RK], dqp)
    gbkv[:, :kvw] = dr(u_ref[:, RK : 2 * RK], dkvp[:, :kvw])
    gbkv[:, kvw:] = dr(u_ref[:, 2 * RK :], dkvp[:, kvw:])
    lo = sc[3]
    mine[...] = scr[lo]
    other[...] = scr[1 - lo]


def dn1_c_kernel(sc, dqp, dkvp, u_ref, wq, wkv, bq, bkv, mine, other, gbq, gbkv, scr):
    dn1_tail(sc, 1, dqp[...], dkvp[...], u_ref, wq, wkv, bq, bkv, mine, other, gbq, gbkv, scr)


def dn1_p_kernel(
    sc, dqp, dkv, own, u_ref, wq, wkv, bq, bkv, cos_ref, sin_ref, mine, other, gbq, gbkv, scr, dkvp_scr
):
    kvw = dkv.shape[1] // 2
    tot = dkv[...] + own[...].astype(F32)
    dkvp_scr[:, :kvw] = rot(tot[:, :kvw].astype(BF).astype(F32), cos_ref[...], -sin_ref[...]).astype(BF)
    dkvp_scr[:, kvw:] = tot[:, kvw:].astype(BF)
    dn1_tail(sc, 0, dqp[...], dkvp_scr[...], u_ref, wq, wkv, bq, bkv, mine, other, gbq, gbkv, scr)


def fin_kernel(which, sc, s_ref, t_ref, x_ref, dh_ref, gain, aT, out_ref):
    width = x_ref.shape[1]
    sel = sel_row(sc[which] if which == 0 else sc[1 + sc[3]])
    du = s_ref[:, width : width + 3 * RK].astype(F32) + t_ref[:, width : width + 3 * RK].astype(F32)
    duq = (du * jnp.concatenate([sel, sel, sel], axis=1)).astype(BF)
    dn1 = s_ref[:, :width].astype(F32) + t_ref[:, :width].astype(F32) + dn(duq, aT[...])
    grad = dh_ref[...] + norm_back(x_ref[...].astype(F32), gain[...].astype(F32), dn1)
    out_ref[:, :width] = grad.astype(BF)
    out_ref[:, width:] = jnp.concatenate([duq, jnp.zeros((duq.shape[0], RK), BF)], axis=1)


MESH = pl.DeviceIdType.MESH


def rows_loop(total, step, body):
    def one(i, carry):
        body(pl.multiple_of(i * step, step))
        return carry

    lax.fori_loop(0, total // step, one, 0)


def place():
    d = lax.axis_index("dp")
    t = lax.axis_index("tensor")
    return d, t


def remote(src, dst, send, recv, device):
    return pltpu.make_async_remote_copy(
        src_ref=src, dst_ref=dst, send_sem=send, recv_sem=recv, device_id=device, device_id_type=MESH
    )


def greet(d, t, n_dp):
    barrier = pltpu.get_barrier_semaphore()
    for device in ((d, t ^ 1), (d, t ^ 2), (d ^ 1, t), ((d + 2) % n_dp, t), ((d + n_dp - 2) % n_dp, t)):
        pl.semaphore_signal(barrier, inc=1, device_id=device, device_id_type=MESH)


def greeted():
    pl.semaphore_wait(pltpu.get_barrier_semaphore(), 5)


class Spread:
    def __init__(self, every, sems, d, t, hi):
        self.every, self.sems, self.d, self.t, self.hi = every, sems, d, t, hi
        self.z, self.x = d // 2, d % 2

    def across(self, z):
        block = z * 2 + self.x
        up_s, up_r, down_s, down_r, x_s, x_r = self.sems
        return remote(self.every.at[block], self.every.at[block], x_s.at[z], x_r.at[z], (self.d ^ 1, self.t))

    def along(self, z, s, up):
        block = z * 2 + self.x
        up_s, up_r, down_s, down_r, x_s, x_r = self.sems
        send, recv, step = (up_s, up_r, 2) if up else (down_s, down_r, -2)
        return remote(self.every.at[block], self.every.at[block], send.at[s], recv.at[s], (self.d + step, self.t))

    def start(self):
        self.across(self.z).start()

        @pl.when(self.z < self.hi - 1)
        def _():
            self.along(self.z, 1, True).start()

        @pl.when(self.z > 0)
        def _():
            self.along(self.z, 1, False).start()

    def hop(self, s):
        if s > self.hi - 1:
            return
        for up in (True, False):
            origin = self.z - s if up else self.z + s
            held = origin >= 0 if up else origin < self.hi
            further = self.z < self.hi - 1 if up else self.z > 0

            @pl.when(held)
            def _(origin=origin, up=up, further=further):
                self.along(origin, s, up).wait_recv()
                self.across(origin).start()
                if s + 1 <= self.hi - 1:

                    @pl.when(further)
                    def _():
                        self.along(origin, s + 1, up).start()

    def finish(self):
        for z in range(self.hi):
            across = self.across(z)
            across.wait_send()
            block = z * 2 + 1 - self.x
            up_s, up_r, down_s, down_r, x_s, x_r = self.sems
            remote(self.every.at[block], self.every.at[block], x_s.at[z], x_r.at[z], (self.d ^ 1, self.t)).wait_recv()
        for s in range(1, self.hi):
            for up in (True, False):
                origin = self.z - s + 1 if up else self.z + s - 1
                held = origin >= 0 if up else origin < self.hi
                further = self.z < self.hi - 1 if up else self.z > 0

                @pl.when(held & further)
                def _(origin=origin, up=up, s=s):
                    self.along(origin, s, up).wait_send()


class TensorSum:
    def __init__(self, snd, got, mine, theirs, sems, d, t):
        self.snd, self.got, self.mine, self.theirs, self.sems, self.t = snd, got, mine, theirs, sems, t
        self.lo = t % 2
        self.core = remote(snd.at[1 - self.lo], got, sems.at[0], sems.at[1], (d, t ^ 1))
        self.chip = remote(mine, theirs, sems.at[2], sems.at[3], (d, t ^ 2))

    def begin(self):
        self.core.start()

    def middle(self):
        self.core.wait_recv()

        def add(r):
            rows = pl.ds(r, 16)
            self.mine[rows] = (self.snd[self.lo, rows].astype(F32) + self.got[rows].astype(F32)).astype(BF)

        rows_loop(self.mine.shape[0], 16, add)
        self.chip.start()

    def end(self):
        self.chip.wait_recv()

    def drain(self):
        self.core.wait_send()
        self.chip.wait_send()


def all_sel(sc):
    return jnp.concatenate(
        [
            jnp.broadcast_to(sel_row(sc[0]), (PLEN, RK)),
            jnp.broadcast_to(sel_row(sc[1]), (CLEN, RK)),
            jnp.broadcast_to(sel_row(sc[2]), (CLEN, RK)),
        ],
        axis=0,
    )


def front_kernel(
    n_dp, sc, gain1, gain2, aT, bq, bkvd, aoT, bo, bd, cos, sin, tok_h, wq_h, wkv_h, wo_h, dy_h, wd_h, adp_h,
    n1q_h, q_h, kv_h, u_h, pp_h, pc_h, o_h, far_h, hp_h, hc_h, n2p_h, n2c_h, dact_h, dud_h,
    tok, n1, wq, wkv, wo, dyu, wdc, dact, every, kv, q, u, far, pp, pc, o,
    snd_p, got_p, s_p, t_p, snd_c, got_c, s_c, t_c, n2p, n2c, hp, hc, tmp,
    lsem, osem, wsem, dsem, psem, csem, nsem, up_s, up_r, down_s, down_r, x_s, x_r,
):
    d, t = place()
    lo = t % 2
    hi = n_dp // 2
    rows, width = tok.shape
    qw = wq.shape[1]
    kvw = wkv.shape[1] // 2
    hidden = wd_h.shape[0]
    ht = wdc.shape[1]
    steps = hidden // ht
    hpn, hcn = PLEN // 2, CLEN
    quarter = n1q_h.shape[1]
    greet(d, t, n_dp)
    loads = [
        pltpu.make_async_copy(src, dst, lsem.at[i])
        for i, (src, dst) in enumerate(
            [(tok_h, tok), (wkv_h, wkv), (wq_h, wq), (wo_h, wo), (dy_h, dyu.at[:, :width])]
        )
    ]
    for c in loads:
        c.start()

    def wd_copies(i, slot):
        return (
            pltpu.make_async_copy(wd_h.at[pl.ds(i * ht, ht)], wdc.at[slot, :, :width], wsem.at[slot, 0]),
            pltpu.make_async_copy(adp_h.at[pl.ds(i * ht, ht)], wdc.at[slot, :, width:], wsem.at[slot, 1]),
        )

    for i in range(2):
        for c in wd_copies(i, i):
            c.start()
    stores = []

    def store(src, dst):
        c = pltpu.make_async_copy(src, dst, osem.at[len(stores)])
        c.start()
        stores.append(c)

    loads[0].wait()

    def norm1(r):
        x = tok[pl.ds(r, 16)].astype(F32)
        inv = lax.rsqrt(jnp.mean(x * x, axis=-1, keepdims=True) + EPSILON)
        n1[pl.ds(r, 16)] = (x * inv * gain1[...].astype(F32)).astype(BF)

    rows_loop(rows, 16, norm1)
    sel = all_sel(sc)
    uf = dt(n1[...], aT[...])
    for part in range(3):
        u[:, part * RK : (part + 1) * RK] = (uf[:, part * RK : (part + 1) * RK] * sel).astype(BF)
    loads[1].wait()
    kvf = dn(n1[...], wkv[...]) + dn(u[:, RK : 3 * RK], bkvd[...])
    kv[:, :kvw] = rot(kvf[:, :kvw], cos[...], sin[...]).astype(BF)
    kv[:, kvw:] = kvf[:, kvw:].astype(BF)
    every[d] = kv[:PLEN]
    greeted()
    spread = Spread(every, (up_s, up_r, down_s, down_r, x_s, x_r), d, t, hi)
    spread.start()

    loads[2].wait()
    qf = dn(n1[...], wq[...]) + dn(u[:, :RK], bq[...])
    for c in range(qw // LANE):
        lanes = slice(c * LANE, (c + 1) * LANE)
        q[:, lanes] = rot(qf[:, lanes], cos[...], sin[...]).astype(BF) * BF(0.125)
    store(n1.at[:, pl.ds(pl.multiple_of(t * quarter, quarter), quarter)], n1q_h)
    store(q, q_h)
    store(kv, kv_h)
    store(u, u_h)

    def keep_o(of, r0, g):
        for h in range(4):
            o[r0 : r0 + CLEN, (4 * g + h) * HD : (4 * g + h + 1) * HD] = of[h * CLEN : (h + 1) * CLEN]

    mask = causal_tile()
    spread.hop(1)
    for g in range(2):
        kg = kv[:PLEN, g * HD : (g + 1) * HD]
        vg = kv[:PLEN, kvw + g * HD : kvw + (g + 1) * HD]
        for i in range(PLEN // CLEN):
            size = (i + 1) * CLEN
            s = dt(stack_heads(q, i * CLEN, g), kg[:size])
            tail = jnp.where(mask, s[:, size - CLEN :], MASKED_SCORE)
            s = tail if i == 0 else jnp.concatenate([s[:, : size - CLEN], tail], axis=1)
            p = softmax_low(s)
            pp[g, :, P_OFF[i] : P_OFF[i] + size] = p
            keep_o(dn(p, vg[:size]).astype(BF), i * CLEN, g)
    store(pp, pp_h)
    spread.hop(2)

    def project(r0, half, snd):
        ov = o[r0 : r0 + 2 * half]
        for n in range(0, width, 512):
            part = dn(ov, wo[:, n : n + 512]).astype(BF)
            snd[0, :, n : n + 512] = part[:half]
            snd[1, :, n : n + 512] = part[half:]
        uo = dt(ov, aoT[...]).astype(BF)
        pad = jnp.zeros((half, LANE - RK), BF)
        snd[0, :, width:] = jnp.concatenate([uo[:half], pad], axis=1)
        snd[1, :, width:] = jnp.concatenate([uo[half:], pad], axis=1)

    loads[3].wait()
    project(0, hpn, snd_p)
    sum_p = TensorSum(snd_p, got_p, s_p, t_p, psem, d, t)
    sum_p.begin()
    spread.hop(3)

    loads[4].wait()
    dud = (dt(dyu[:, :width], bd[...]) * sel).astype(BF)
    dyu[:, width:] = jnp.concatenate([dud, jnp.zeros((rows, LANE - RK), BF)], axis=1)
    store(dyu.at[:, width:], dud_h)
    outs = []

    def act_grad(i):
        slot = i % 2
        for c in wd_copies(i, slot):
            c.wait()
        if i >= 2:
            outs[i - 2].wait()
        dact[slot] = dt(dyu[...], wdc[slot]).astype(BF)
        c = pltpu.make_async_copy(dact.at[slot], dact_h.at[:, pl.ds(i * ht, ht)], dsem.at[slot])
        c.start()
        outs.append(c)
        if i + 2 < steps:
            for c in wd_copies(i + 2, slot):
                c.start()

    act_grad(0)
    sum_p.middle()
    for i in range(1, steps):
        act_grad(i)
        spread.hop(i + 3)
    for s in range(steps + 3, hi):
        spread.hop(s)
    spread.finish()

    far[0] = every[sc[3]]
    far[1] = every[sc[4]]
    store(far, far_h)
    for j in range(CONT_DEV):
        r0 = PLEN + j * CLEN
        for g in range(2):
            lanes = slice(g * HD, (g + 1) * HD)
            vlanes = slice(kvw + g * HD, kvw + (g + 1) * HD)
            qs = stack_heads(q, r0, g)
            sf = dt(qs, far[j, :, lanes])
            so = jnp.where(mask, dt(qs, kv[r0 : r0 + CLEN, lanes]), MASKED_SCORE)
            p = softmax_low(jnp.concatenate([sf, so], axis=1))
            pc[2 * j + g] = p
            keep_o((dn(p[:, :PLEN], far[j, :, vlanes]) + dn(p[:, PLEN:], kv[r0 : r0 + CLEN, vlanes])).astype(BF), r0, g)
    store(pc, pc_h)
    store(o, o_h)
    project(PLEN, hcn, snd_c)
    sum_c = TensorSum(snd_c, got_c, s_c, t_c, csem, d, t)
    sum_c.begin()
    sum_c.middle()

    def norm2(which, total, r0, h, n2, adapter):
        half = h.shape[0]
        total.end()
        sr = sel_row(adapter)
        uo = ((total.mine[:, width : width + RK].astype(F32) + total.theirs[:, width : width + RK].astype(F32)) * sr).astype(BF)
        tmp[:half] = dn(uo, bo[...])
        start = r0 + lo * half

        def one(r):
            here = pl.ds(r, 16)
            hv = (
                tok[pl.ds(pl.multiple_of(start + r, 16), 16)].astype(F32)
                + total.mine[here, :width].astype(F32)
                + total.theirs[here, :width].astype(F32)
                + tmp[here]
            )
            h[here] = hv
            inv = lax.rsqrt(jnp.mean(hv * hv, axis=-1, keepdims=True) + EPSILON)
            n2[lo, here, :width] = (hv * inv * gain2[...].astype(F32)).astype(BF)

        rows_loop(half, 16, one)
        n2[lo, :, width:] = jnp.concatenate([uo, jnp.zeros((half, LANE - RK), BF)], axis=1)
        c = remote(n2.at[lo], n2.at[lo], nsem.at[which, 0], nsem.at[which, 1], (d, t ^ 1))
        c.start()
        return c

    n2_copy_p = norm2(0, sum_p, 0, hp, n2p, sc[0])
    store(hp, hp_h)
    n2_copy_c = norm2(1, sum_c, PLEN, hc, n2c, jnp.where(lo == 0, sc[1], sc[2]))
    store(hc, hc_h)

    def arrived(which, n2):
        remote(n2.at[1 - lo], n2.at[1 - lo], nsem.at[which, 0], nsem.at[which, 1], (d, t ^ 1)).wait_recv()

    arrived(0, n2p)
    store(n2p, n2p_h)
    arrived(1, n2c)
    store(n2c, n2c_h)
    n2_copy_p.wait_send()
    n2_copy_c.wait_send()
    sum_p.drain()
    sum_c.drain()
    for c in outs[-2:]:
        c.wait()
    for c in stores:
        c.wait()


def front(n_dp, sc, small, large):
    rows, width = large[0].shape
    qw = large[1].shape[1]
    kvw2 = large[2].shape[1]
    hidden = large[5].shape[0]
    quarter = width // 4
    wide = width + LANE
    ht = 512
    hpn, hcn = PLEN // 2, CLEN
    outs = [
        ((rows, quarter), BF), ((rows, qw), BF), ((rows, kvw2), BF), ((rows, 3 * RK), BF), ((2, 4 * CLEN, 768), BF),
        ((4, 4 * CLEN, 4 * CLEN), BF), ((rows, qw), BF), ((CONT_DEV, PLEN, kvw2), BF), ((hpn, width), F32),
        ((hcn, width), F32), ((2, hpn, wide), BF), ((2, hcn, wide), BF), ((rows, hidden), BF), ((rows, LANE), BF),
    ]
    dma = pltpu.SemaphoreType.DMA
    scratch = [
        VM((rows, width), BF), VM((rows, width), BF), VM((width, qw), BF), VM((width, kvw2), BF), VM((qw, width), BF),
        VM((rows, wide), BF), VM((2, ht, wide), BF), VM((2, rows, ht), BF), VM((n_dp, PLEN, kvw2), BF), VM((rows, kvw2), BF),
        VM((rows, qw), BF), VM((rows, 3 * RK), BF), VM((CONT_DEV, PLEN, kvw2), BF), VM((2, 4 * CLEN, 768), BF),
        VM((4, 4 * CLEN, 4 * CLEN), BF), VM((rows, qw), BF),
        VM((2, hpn, wide), BF), VM((hpn, wide), BF), VM((hpn, wide), BF), VM((hpn, wide), BF),
        VM((2, hcn, wide), BF), VM((hcn, wide), BF), VM((hcn, wide), BF), VM((hcn, wide), BF),
        VM((2, hpn, wide), BF), VM((2, hcn, wide), BF), VM((hpn, width), F32), VM((hcn, width), F32), VM((hpn, width), F32),
        dma((5,)), dma((13,)), dma((2, 2)), dma((2,)), dma((4,)), dma((4,)), dma((2, 2)),
    ] + [dma((n_dp // 2 + 1,))] * 6
    vm = pl.BlockSpec(memory_space=VM)
    anyspace = pl.BlockSpec(memory_space=pl.ANY)
    return pl.pallas_call(
        functools.partial(front_kernel, n_dp),
        out_shape=[jax.ShapeDtypeStruct(s, dtype) for s, dtype in outs],
        in_specs=[pl.BlockSpec(memory_space=pltpu.SMEM)] + [vm] * len(small) + [anyspace] * len(large),
        out_specs=[anyspace] * len(outs),
        scratch_shapes=scratch,
        compiler_params=pltpu.CompilerParams(vmem_limit_bytes=60 << 20, collective_id=1, has_side_effects=True),
        cost_estimate=pl.CostEstimate(flops=2 * rows * width * 4096, bytes_accessed=40 << 20, transcendentals=0),
        name="front",
    )(sc, *small, *large)


def rope_tables():
    position = np.concatenate([np.arange(PLEN)] + [PLEN + np.arange(CLEN)] * CONT_DEV).astype(np.float32)
    exponent = np.arange(HD // 2, dtype=np.float32) * np.float32(2.0 / HD)
    frequency = np.exp(np.float32(-math.log(ROPE_BASE)) * exponent).astype(np.float32)
    angle = position[:, None] * frequency[None, :]
    cos, sin = np.cos(angle).astype(np.float32), np.sin(angle).astype(np.float32)
    return np.tile(cos, (1, 4)), np.concatenate([-sin, sin, -sin, sin], axis=1)


def shards(
    tokens, cotangent, gain_attn, gain_mlp, w_query, w_kv, w_out, w_gate_up, w_down, a_attn, b_query, b_kv,
    a_out, b_out, a_mlp, b_mlp, a_down, b_down, prompt_adapter, cont_adapter, group_map,
):
    rows, width = tokens.shape
    qw = w_query.shape[1]
    kvw = w_kv.shape[2]
    hidden = w_down.shape[0]
    n_dp = lax.axis_size("dp")
    n_t = lax.axis_size("tensor")
    quarter = width // n_t
    t = lax.axis_index("tensor")
    lo = t & 1
    sc = jnp.concatenate(
        [prompt_adapter, cont_adapter, jnp.stack([lo, t]).astype(jnp.int32), jnp.zeros((3,), jnp.int32)]
    )
    partners = lax.dynamic_slice_in_dim(group_map, lax.axis_index("dp") * CONT_DEV, CONT_DEV)
    cos_np, sin_np = rope_tables()
    cos, sin = jnp.asarray(cos_np), jnp.asarray(sin_np)
    gain1 = gain_attn.reshape(1, width)
    gain2 = gain_mlp.reshape(1, width)
    aT = a_attn.transpose(1, 2, 3, 0).reshape(3 * RK, width)
    aoT = a_out.transpose(1, 2, 0).reshape(RK, qw)
    amT = a_mlp.transpose(1, 2, 3, 0).reshape(2 * RK, width)
    adT = a_down.transpose(1, 2, 0).reshape(RK, hidden)
    bq = b_query.reshape(RK, qw)
    bkv = b_kv.reshape(RK, 2 * kvw)
    bo = b_out.reshape(RK, width)
    bm = b_mlp.reshape(RK, 2 * hidden)
    bd = b_down.reshape(RK, width)
    wkv = w_kv.reshape(width, 2 * kvw)
    wgu = w_gate_up.reshape(width, 2 * hidden)

    core_pairs = [(i, i ^ 1) for i in range(n_t)]
    chip_pairs = [(i, i ^ 2) for i in range(n_t)]

    def to_core(v):
        return lax.ppermute(v, "tensor", core_pairs)

    def to_chip(v):
        return lax.ppermute(v, "tensor", chip_pairs)

    def tensor_sum(mine, other):
        s = (mine.astype(F32) + to_core(other).astype(F32)).astype(BF)
        return s, to_chip(s)

    def join(mine, other):
        return jnp.where(lo == 0, jnp.concatenate([mine, other], 0), jnp.concatenate([other, mine], 0))

    def mine_rows(v):
        hp = PLEN // 2
        hc = CLEN
        return (
            lax.dynamic_slice_in_dim(v, lo * hp, hp, 0),
            lax.dynamic_slice_in_dim(v, PLEN + lo * hc, hc, 0),
        )

    x_p, x_c = mine_rows(tokens)
    dy_p, dy_c = mine_rows(cotangent)

    hp, hc = PLEN // 2, CLEN
    wide = width + LANE
    zero_kv = jnp.zeros((RK, kvw), BF)
    bkvd = jnp.concatenate(
        [jnp.concatenate([bkv[:, :kvw], zero_kv], 1), jnp.concatenate([zero_kv, bkv[:, kvw:]], 1)], 0
    )
    adp = jnp.concatenate([adT.T, jnp.zeros((hidden, LANE - RK), BF)], axis=1)
    fsc = jnp.concatenate([prompt_adapter, cont_adapter, partners, jnp.zeros((3,), jnp.int32)])
    (n1q, q, kv, u, p_p, p_c, o, far, h_p, h_c, n2pa, n2ca, dact, dud) = front(
        n_dp, fsc,
        [gain1, gain2, aT, bq, bkvd, aoT, bo, bd, cos, sin],
        [tokens, w_query, wkv, w_out, cotangent, w_down, adp],
    )
    k, v = kv[:, :kvw], kv[:, kvw:]
    p_c = p_c.reshape(2, 2, 4 * CLEN, 4 * CLEN)
    o_p, o_c = o[:PLEN], o[PLEN:]
    dud = dud[:, :RK]
    n2_p, n2_po = n2pa[lo], n2pa[1 - lo]
    n2_c, n2_co = n2ca[lo], n2ca[1 - lo]
    ht = 256
    steps = hidden // ht
    smem = pl.BlockSpec(memory_space=pltpu.SMEM)
    fixed = lambda a: pl.BlockSpec(a.shape, lambda i: (0, 0))
    down_rows = pl.BlockSpec((ht, width), lambda i: (i, 0))
    hid_cols = lambda r: pl.BlockSpec((r, ht), lambda i: (0, i))
    hid_cols2 = lambda r: pl.BlockSpec((r, ht), lambda i: (0, i + steps))

    def mlp(which, n2u, n2u_other, r0):
        half = n2u.shape[0]
        r = 2 * half
        blk = pl.BlockSpec((r, ht), lambda i: (0, i))
        hold = pl.BlockSpec((half, wide), lambda i: (0, 0))
        return call(
            functools.partial(mlp_kernel, which), "mlp_pc"[: 5 + which],
            [sc, n2u, n2u_other, dact[r0 : r0 + r], dud[r0 : r0 + r], wgu, wgu, w_down, bm, bm, adT, amT],
            [((half, wide), BF)] * 4 + [((RK, hidden), F32)] * 3,
            grid=(steps,),
            in_specs=[smem, hold, hold, blk, pl.BlockSpec((r, RK), lambda i: (0, 0)), hid_cols(width), hid_cols2(width),
                      down_rows, hid_cols(RK), hid_cols2(RK), hid_cols(RK), fixed(amT)],
            out_specs=[hold] * 4 + [hid_cols(RK)] * 3,
            scratch=[VM((2, half, width), BF), VM((r, 2 * RK), BF), VM((r, width), F32), VM((r, width), F32),
                     VM((r, RK), F32), VM((r, 2 * RK), F32)],
            flops=2 * r * width * hidden * 5,
        )

    mlp_pm, mlp_po, dn2_pm, dn2_po, gbg_p, gbu_p, gad_p = mlp(0, n2_p, n2_po, 0)
    sd_p, td_p = tensor_sum(dn2_pm, dn2_po)
    mlp_cm, mlp_co, dn2_cm, dn2_co, gbg_c, gbu_c, gad_c = mlp(1, n2_c, n2_co, PLEN)
    sd_c, td_c = tensor_sum(dn2_cm, dn2_co)
    sm_p, tm_p = tensor_sum(mlp_pm, mlp_po)
    sm_c, tm_c = tensor_sum(mlp_cm, mlp_co)

    def back(which, s, tt, h, dy):
        half = s.shape[0]
        dh, dau = call(
            functools.partial(nbwd_kernel, which), "nbwd_pc"[: 6 + which],
            [sc, s, tt, h, dy, gain2, amT], [((half, width), F32), ((half, wide), BF)], flops=2 * half * 256 * width,
        )
        return dh, dau, to_core(dau)

    grad_outs = [((RK, qw), F32), ((RK, quarter), F32), ((2 * RK, quarter), F32)]
    dh_c, da_c, da_co = back(1, sd_c, td_c, h_c, dy_c)
    rc = 2 * CLEN
    dqp_c, dkvp_c, dfar, gao_c, gbo_c, gam_c = call(
        abwd_c_kernel, "abwd_c",
        [sc, da_c, da_co, n2_c, n2_co, o_c, w_out, aoT, bo, p_c, q[PLEN:], k[PLEN:], v[PLEN:], far, cos[PLEN:], sin[PLEN:]],
        [((rc, qw), BF), ((rc, 2 * kvw), BF), ((CONT_DEV, PLEN, 2 * kvw), F32)] + grad_outs,
        scratch=[VM((2, hc, width), BF), VM((rc, qw), BF), VM((rc, qw), BF), VM((rc, 2 * kvw), F32)],
        flops=2 * rc * width * qw * 3,
    )
    slot = jnp.arange(n_dp, dtype=jnp.int32)[:, None, None]
    scatter = sum(jnp.where(slot == partners[j], dfar[j][None], 0.0) for j in range(CONT_DEV)).astype(BF)
    own = lax.psum_scatter(scatter.reshape(n_dp * PLEN, 2 * kvw), "dp", scatter_dimension=0, tiled=True)

    dh_p, da_p, da_po = back(0, sd_p, td_p, h_p, dy_p)
    dqp_p, dkv_p, gao_p, gbo_p, gam_p = call(
        abwd_p_kernel, "abwd_p",
        [sc, da_p, da_po, n2_p, n2_po, o_p, w_out, aoT, bo, p_p, q[:PLEN], k[:PLEN], v[:PLEN], cos[:PLEN], sin[:PLEN]],
        [((PLEN, qw), BF), ((PLEN, 2 * kvw), F32)] + grad_outs,
        scratch=[VM((2, hp, width), BF), VM((PLEN, qw), BF), VM((PLEN, qw), BF)],
        flops=2 * PLEN * width * qw * 3,
    )

    far_wide = width + 2 * LANE
    gq = [((RK, qw), F32), ((RK, 2 * kvw), F32)]
    mine, other, gbq_c, gbkv_c = call(
        dn1_c_kernel, "dn1_c",
        [sc, dqp_c, dkvp_c, u[PLEN:], w_query, wkv, bq, bkv],
        [((hc, far_wide), BF)] * 2 + gq, scratch=[VM((2, hc, far_wide), BF)], flops=2 * rc * width * (qw + 2 * kvw),
    )
    s1_c, t1_c = tensor_sum(mine, other)
    mine, other, gbq_p, gbkv_p = call(
        dn1_p_kernel, "dn1_p",
        [sc, dqp_p, dkv_p, own, u[:PLEN], w_query, wkv, bq, bkv, cos[:PLEN], sin[:PLEN]],
        [((hp, far_wide), BF)] * 2 + gq, scratch=[VM((2, hp, far_wide), BF), VM((PLEN, 2 * kvw), BF)],
        flops=2 * PLEN * width * (qw + 2 * kvw),
    )
    s1_p, t1_p = tensor_sum(mine, other)

    def last(which, s, tt, x, dh):
        half = s.shape[0]
        (out,) = call(
            functools.partial(fin_kernel, which), "fin_pc"[: 5 + which],
            [sc, s, tt, x, dh, gain1, aT], [((half, far_wide), BF)], flops=2 * half * 256 * width,
        )
        return out, to_core(out)

    tg_p = join(*last(0, s1_p, t1_p, x_p, dh_p))
    tg_c = join(*last(1, s1_c, t1_c, x_c, dh_c))
    tokens_grad = jnp.concatenate([tg_p[:, :width], tg_c[:, :width]], 0)
    duq = jnp.concatenate([tg_p[:, width : width + 3 * RK], tg_c[:, width : width + 3 * RK]], 0)

    def finish(which, s, tt, h):
        half = s.shape[0]
        (out,) = call(
            functools.partial(out_kernel, which), "out_pc"[: 5 + which],
            [sc, s, tt, h, bd], [((half, wide), BF)], flops=2 * half * 256 * width,
        )
        return out, to_core(out)

    out_p = join(*finish(0, sm_p, tm_p, h_p))
    out_c = join(*finish(1, sm_c, tm_c, h_c))
    output = jnp.concatenate([out_p[:, :width], out_c[:, :width]], 0)
    ud = jnp.concatenate([out_p[:, width : width + RK], out_c[:, width : width + RK]], 0)

    dyq = lax.dynamic_slice_in_dim(cotangent, t * quarter, quarter, 1)
    gbd = dr(ud, dyq)
    gaT = dr(duq, n1q)
    gam = gam_p + gam_c
    early = jnp.concatenate(
        [gbg_p + gbg_c, gbu_p + gbu_c, gad_p + gad_c, gao_p + gao_c, gbo_p + gbo_c, gbd, gam[:RK], gam[RK:]], axis=1
    ).astype(BF)
    late = jnp.concatenate([gbq_p + gbq_c, gbkv_p + gbkv_c, gaT[:RK], gaT[RK : 2 * RK], gaT[2 * RK :]], axis=1).astype(BF)
    early = lax.psum(early, "dp")
    late = lax.psum(late, "dp")
    cuts = np.cumsum([hidden, hidden, hidden, qw])
    grad_b_mlp = early[:, : 2 * hidden].astype(F32)
    grad_a_down = early[:, cuts[1] : cuts[2]].astype(F32)
    grad_a_out = early[:, cuts[2] : cuts[3]].astype(F32)
    grad_b_query = late[:, :qw].astype(F32)
    grad_b_kv = late[:, qw : qw + 2 * kvw].astype(F32)

    def gather_quarters(v):
        return lax.all_gather(v, "tensor", axis=0, tiled=False)

    eq = gather_quarters(early[:, cuts[3] :])
    lq = gather_quarters(late[:, qw + 2 * kvw :])

    def columns(g, i):
        return jnp.transpose(g[:, :, i * quarter : (i + 1) * quarter], (1, 0, 2)).reshape(RK, width).astype(F32)

    grad_b_out = columns(eq, 0)
    grad_b_down = columns(eq, 1)
    grad_amT = jnp.concatenate([columns(eq, 2), columns(eq, 3)], axis=0)
    grad_aT = jnp.concatenate([columns(lq, 0), columns(lq, 1), columns(lq, 2)], axis=0)
    return (
        output,
        tokens_grad,
        grad_aT.reshape(3, NA, R, width).transpose(3, 0, 1, 2),
        grad_b_query.reshape(b_query.shape),
        grad_b_kv.reshape(b_kv.shape),
        grad_a_out.reshape(NA, R, qw).transpose(2, 0, 1),
        grad_b_out.reshape(b_out.shape),
        grad_amT.reshape(2, NA, R, width).transpose(3, 0, 1, 2),
        grad_b_mlp.reshape(b_mlp.shape),
        grad_a_down.reshape(NA, R, hidden).transpose(2, 0, 1),
        grad_b_down.reshape(b_down.shape),
    )


def solution(mesh):
    in_specs = (
        P("dp", None), P("dp", None), P(), P(), P(None, "tensor"), P(None, None, "tensor"), P("tensor", None),
        P(None, None, "tensor"), P("tensor", None), P(), P(None, None, "tensor"), P(None, None, None, "tensor"),
        P("tensor", None, None), P(), P(), P(None, None, None, "tensor"), P("tensor", None, None), P(),
        P("dp"), P("dp"), P(),
    )
    out_specs = (
        P("dp", None), P("dp", None), P(), P(None, None, "tensor"), P(None, None, None, "tensor"),
        P("tensor", None, None), P(), P(), P(None, None, None, "tensor"), P("tensor", None, None), P(),
    )
    return jax.shard_map(shards, mesh=mesh, in_specs=in_specs, out_specs=out_specs, check_vma=False)
```

```python
import functools
import math

import jax
import jax.numpy as jnp
import numpy as np
from jax import lax
from jax.experimental import pallas as pl
from jax.experimental.pallas import tpu as pltpu
from jax.sharding import PartitionSpec as P

HD = 64
R = 16
NA = 4
RK = NA * R
PLEN = 384
CLEN = 128
CONT_DEV = 2
ROWS = PLEN + CONT_DEV * CLEN
EPSILON = 1e-05
ROPE_BASE = 500000.0
MASKED_SCORE = -1e30

BF = jnp.bfloat16
F32 = jnp.float32
VM = pltpu.VMEM
LANE = 128


def dn(a, b):
    return jnp.dot(a, b, preferred_element_type=F32)


def dt(a, b):
    return lax.dot_general(a, b, (((1,), (1,)), ((), ())), preferred_element_type=F32)


def dr(a, b):
    return lax.dot_general(a, b, (((0,), (0,)), ((), ())), preferred_element_type=F32)


def sel_row(adapter):
    lane = lax.broadcasted_iota(jnp.int32, (1, RK), 1)
    return (lax.shift_right_logical(lane, 4) == adapter).astype(F32)


def swap_halves(v):
    lane = lax.broadcasted_iota(jnp.int32, v.shape, 1)
    return jnp.where((lane & 63) < 32, pltpu.roll(v, LANE - 32, 1), pltpu.roll(v, 32, 1))


def rot(v, cos, sin):
    return v * cos + swap_halves(v) * sin


def stack_heads(ref, r0, g):
    return jnp.concatenate(
        [ref[r0 : r0 + CLEN, (4 * g + h) * HD : (4 * g + h + 1) * HD] for h in range(4)], axis=0
    )


def softmax_low(s):
    top = jnp.max(s, axis=-1, keepdims=True)
    e = jnp.exp(s - top)
    return (e * (1.0 / jnp.sum(e, axis=-1, keepdims=True))).astype(BF)


def causal_tile():
    r = lax.broadcasted_iota(jnp.int32, (4 * CLEN, CLEN), 0) & (CLEN - 1)
    c = lax.broadcasted_iota(jnp.int32, (4 * CLEN, CLEN), 1)
    return c <= r


P_OFF = (0, 128, 384)


def norm_back(v, gain, upstream):
    inv = lax.rsqrt(jnp.mean(v * v, axis=-1, keepdims=True) + EPSILON)
    scaled = v * inv
    weighted = upstream * gain
    return inv * (weighted - scaled * jnp.mean(weighted * scaled, axis=-1, keepdims=True))


def put_dq(dq, dq_ref, r0, g):
    for h in range(4):
        dq_ref[r0 : r0 + CLEN, (4 * g + h) * HD : (4 * g + h + 1) * HD] = dq[h * CLEN : (h + 1) * CLEN]


def back_scores(p, dp):
    pf = p.astype(F32)
    return (pf * (dp - jnp.sum(pf * dp, axis=-1, keepdims=True))).astype(BF)


MESH = pl.DeviceIdType.MESH


def rows_loop(total, step, body):
    def one(i, carry):
        body(pl.multiple_of(i * step, step))
        return carry

    lax.fori_loop(0, total // step, one, 0)


def place():
    d = lax.axis_index("dp")
    t = lax.axis_index("tensor")
    return d, t


def remote(src, dst, send, recv, device):
    return pltpu.make_async_remote_copy(
        src_ref=src, dst_ref=dst, send_sem=send, recv_sem=recv, device_id=device, device_id_type=MESH
    )


def greet(d, t, n_dp):
    barrier = pltpu.get_barrier_semaphore()
    for device in [(d, t ^ 1), (d, t ^ 2)] + [((d + k) % n_dp, t) for k in range(1, n_dp)]:
        pl.semaphore_signal(barrier, inc=1, device_id=device, device_id_type=MESH)


def greeted(n_dp):
    pl.semaphore_wait(pltpu.get_barrier_semaphore(), n_dp + 1)


class Spread:
    def __init__(self, every, sems, d, t, hi):
        self.every, self.sems, self.d, self.t, self.hi = every, sems, d, t, hi
        self.z, self.x = d // 2, d % 2

    def across(self, z):
        block = z * 2 + self.x
        up_s, up_r, down_s, down_r, x_s, x_r = self.sems
        return remote(self.every.at[block], self.every.at[block], x_s.at[z], x_r.at[z], (self.d ^ 1, self.t))

    def along(self, z, s, up):
        block = z * 2 + self.x
        up_s, up_r, down_s, down_r, x_s, x_r = self.sems
        send, recv, step = (up_s, up_r, 2) if up else (down_s, down_r, -2)
        return remote(self.every.at[block], self.every.at[block], send.at[s], recv.at[s], (self.d + step, self.t))

    def start(self):
        self.across(self.z).start()

        @pl.when(self.z < self.hi - 1)
        def _():
            self.along(self.z, 1, True).start()

        @pl.when(self.z > 0)
        def _():
            self.along(self.z, 1, False).start()

    def hop(self, s):
        if s > self.hi - 1:
            return
        for up in (True, False):
            origin = self.z - s if up else self.z + s
            held = origin >= 0 if up else origin < self.hi
            further = self.z < self.hi - 1 if up else self.z > 0

            @pl.when(held)
            def _(origin=origin, up=up, further=further):
                self.along(origin, s, up).wait_recv()
                self.across(origin).start()
                if s + 1 <= self.hi - 1:

                    @pl.when(further)
                    def _():
                        self.along(origin, s + 1, up).start()

    def finish(self):
        for z in range(self.hi):
            across = self.across(z)
            across.wait_send()
            block = z * 2 + 1 - self.x
            up_s, up_r, down_s, down_r, x_s, x_r = self.sems
            remote(self.every.at[block], self.every.at[block], x_s.at[z], x_r.at[z], (self.d ^ 1, self.t)).wait_recv()
        for s in range(1, self.hi):
            for up in (True, False):
                origin = self.z - s + 1 if up else self.z + s - 1
                held = origin >= 0 if up else origin < self.hi
                further = self.z < self.hi - 1 if up else self.z > 0

                @pl.when(held & further)
                def _(origin=origin, up=up, s=s):
                    self.along(origin, s, up).wait_send()


class TensorSum:
    def __init__(self, snd, got, mine, theirs, sems, d, t):
        self.snd, self.got, self.mine, self.theirs, self.sems, self.t = snd, got, mine, theirs, sems, t
        self.lo = t % 2
        self.core = remote(snd.at[1 - self.lo], got, sems.at[0], sems.at[1], (d, t ^ 1))
        self.chip = remote(mine, theirs, sems.at[2], sems.at[3], (d, t ^ 2))

    def begin(self):
        self.core.start()

    def middle(self):
        self.core.wait_recv()

        def add(r):
            rows = pl.ds(r, 64)
            self.mine[rows] = (self.snd[self.lo, rows].astype(F32) + self.got[rows].astype(F32)).astype(BF)

        rows_loop(self.mine.shape[0], 64, add)
        self.chip.start()

    def end(self):
        self.chip.wait_recv()

    def drain(self):
        self.core.wait_send()
        self.chip.wait_send()


UNIT = (16, LANE)


def put_units(blocks, first, value):
    for b in range(value.shape[1] // LANE):
        for r in range(RK // 16):
            blocks[first + b * (RK // 16) + r] = value[r * 16 : (r + 1) * 16, b * LANE : (b + 1) * LANE]


class DirectReduce:
    def __init__(self, src, got, out, sems, d, t, n_dp):
        self.src, self.got, self.out, self.sems, self.d, self.t, self.n = src, got, out, sems, d, t, n_dp
        self.share = out.shape[0] // n_dp

    def part(self, d):
        return pl.ds(d * self.share, self.share)

    def to(self, k):
        peer = (self.d + k) % self.n
        return remote(self.src.at[self.part(peer)], self.got.at[k], self.sems[0].at[k], self.sems[1].at[k], (peer, self.t))

    def back(self, k):
        peer = (self.d + k) % self.n
        here = self.part(self.d)
        return remote(self.out.at[here], self.out.at[here], self.sems[2].at[k], self.sems[3].at[k], (peer, self.t))

    def from_back(self, k):
        peer = (self.d + self.n - k) % self.n
        there = self.part(peer)
        return remote(self.out.at[there], self.out.at[there], self.sems[2].at[k], self.sems[3].at[k], (peer, self.t))

    def start(self):
        for k in range(1, self.n):
            self.to(k).start()

    def add(self):
        for k in range(1, self.n):
            self.to(k).wait_recv()
        here = self.part(self.d)
        total = self.src[here].astype(F32)
        for k in range(1, self.n):
            total = total + self.got[k].astype(F32)
        self.out[here] = total.astype(BF)

    def sent(self):
        for k in range(1, self.n):
            self.to(k).wait_send()

    def spread(self):
        for k in range(1, self.n):
            self.back(k).start()

    def finish(self):
        for k in range(1, self.n):
            self.from_back(k).wait_recv()

    def spread_sent(self):
        for k in range(1, self.n):
            self.back(k).wait_send()


class QuarterGather:
    def __init__(self, buf, sems, d, t):
        self.buf, self.sems, self.d, self.t = buf, sems, d, t

    def copy(self, slot, n, peer):
        return remote(self.buf.at[slot], self.buf.at[slot], self.sems.at[n, 0], self.sems.at[n, 1], (self.d, peer))

    def start(self):
        self.copy(self.t, 0, self.t ^ 2).start()
        self.copy(self.t, 1, self.t ^ 1).start()

    def relay(self):
        self.copy(self.t ^ 2, 0, self.t ^ 2).wait_recv()
        self.copy(self.t ^ 2, 2, self.t ^ 1).start()

    def finish(self):
        self.copy(self.t ^ 1, 1, self.t ^ 1).wait_recv()
        self.copy(self.t ^ 3, 2, self.t ^ 1).wait_recv()
        self.copy(self.t, 0, self.t ^ 2).wait_send()
        self.copy(self.t, 1, self.t ^ 1).wait_send()
        self.copy(self.t ^ 2, 2, self.t ^ 1).wait_send()


def evens_first(n):
    r = lax.broadcasted_iota(jnp.int32, (n, n), 0)
    c = lax.broadcasted_iota(jnp.int32, (n, n), 1)
    return (c == jnp.where(r < n // 2, 2 * r, 2 * (r - n // 2) + 1)).astype(BF)


def all_sel(sc):
    return jnp.concatenate(
        [
            jnp.broadcast_to(sel_row(sc[0]), (PLEN, RK)),
            jnp.broadcast_to(sel_row(sc[1]), (CLEN, RK)),
            jnp.broadcast_to(sel_row(sc[2]), (CLEN, RK)),
        ],
        axis=0,
    )


def front_kernel(
    n_dp, ids_p, ids_c, group_map, gain1, gain2, bkv_ref, bm_ref,
    tok_h, aT_h, wkv_h, cos_h, sin_h, wq_h, bq_h, aoT_h, wo_h, dy_h, bd_h, adT_h, bo_h, wd_h, raw_h,
    n1q_h, q_h, kv_h, u_h, pp_h, pc_h, o_h, far_h, hp_h, hc_h, n2p_h, n2c_h, dact_h, dud_h, wgu_h,
    tok, n1, aT, wkv, cos, sin, wq, bq, aoT, wo, dyu, bd, adT, bo, wdc, raw, flat, bflat, dact, every, kv, q, u, far, pp, pc, o,
    snd_p, got_p, s_p, t_p, snd_c, got_c, s_c, t_c, n2p, n2c, hp, hc, tmp,
    lsem, osem, wsem, dsem, rsem, fsem, psem, csem, nsem, up_s, up_r, down_s, down_r, x_s, x_r,
):
    d, t = place()
    sc = [ids_p[0], ids_c[0], ids_c[1], group_map[d * CONT_DEV], group_map[d * CONT_DEV + 1]]
    lo = t % 2
    hi = n_dp // 2
    rows, width = tok.shape
    qw = wq.shape[1]
    kvw = wkv.shape[1] // 2
    hidden = wd_h.shape[0]
    ht = wdc.shape[1]
    steps = hidden // ht
    hpn, hcn = PLEN // 2, CLEN
    quarter = n1q_h.shape[1]
    greet(d, t, n_dp)
    loads = {}
    for i, (src, dst) in enumerate(
        [(tok_h, tok), (aT_h, aT), (wkv_h, wkv), (cos_h, cos), (sin_h, sin), (wq_h, wq), (bq_h, bq), (aoT_h, aoT), (wo_h, wo),
         (dy_h, dyu.at[:, :width]), (bd_h, bd), (adT_h, adT), (bo_h, bo)]
    ):
        loads[i] = pltpu.make_async_copy(src, dst, lsem.at[i])
        loads[i].start()

    def need(*which):
        for i in which:
            loads.pop(i).wait()

    def wd_copies(i, slot):
        return (
            pltpu.make_async_copy(wd_h.at[pl.ds(i * ht, ht)], wdc.at[slot, :, :width], wsem.at[slot]),
        )

    kt = raw.shape[1]
    raw_steps = width // kt

    def raw_copy(i, slot):
        return pltpu.make_async_copy(raw_h.at[pl.ds(i * kt, kt)], raw.at[slot], rsem.at[slot])

    def flat_copies(i, slot):
        here = pl.ds(i * kt, kt)
        return (
            pltpu.make_async_copy(flat.at[slot, 0], wgu_h.at[here, :hidden], fsem.at[slot, 0]),
            pltpu.make_async_copy(flat.at[slot, 1], wgu_h.at[here, hidden:], fsem.at[slot, 1]),
        )

    for i in range(2):
        for c in wd_copies(i, i):
            c.start()
        raw_copy(i, i).start()
    stores = []

    def store(src, dst):
        c = pltpu.make_async_copy(src, dst, osem.at[len(stores)])
        c.start()
        stores.append(c)

    b2 = 2 * RK
    bkv = dn(evens_first(b2), bkv_ref[...].reshape(b2, kvw)).astype(BF)
    gain_row = gain1[...].astype(F32)
    need(0)

    def norm1(r):
        x = tok[pl.ds(r, 128)].astype(F32)
        inv = lax.rsqrt(jnp.mean(x * x, axis=-1, keepdims=True) + EPSILON)
        n1[pl.ds(r, 128)] = (x * inv * gain_row).astype(BF)

    rows_loop(rows, 128, norm1)
    need(1)
    sel = all_sel(sc)
    uf = dt(n1[...], aT[...])
    for part in range(3):
        u[:, part * RK : (part + 1) * RK] = (uf[:, part * RK : (part + 1) * RK] * sel).astype(BF)
    need(2, 3, 4)
    kvf = dn(n1[...], wkv[...])
    kv[:, :kvw] = rot(kvf[:, :kvw] + dn(u[:, RK : 2 * RK], bkv[:RK]), cos[...], sin[...]).astype(BF)
    kv[:, kvw:] = (kvf[:, kvw:] + dn(u[:, 2 * RK :], bkv[RK:])).astype(BF)
    every[d] = kv[:PLEN]
    greeted(n_dp)
    spread = Spread(every, (up_s, up_r, down_s, down_r, x_s, x_r), d, t, hi)
    spread.start()

    need(5, 6)
    qf = dn(n1[...], wq[...]) + dn(u[:, :RK], bq[...])
    for c in range(qw // LANE):
        lanes = slice(c * LANE, (c + 1) * LANE)
        q[:, lanes] = rot(qf[:, lanes], cos[...], sin[...]).astype(BF) * BF(0.125)
    store(n1.at[:, pl.ds(pl.multiple_of(t * quarter, quarter), quarter)], n1q_h)
    store(q, q_h)
    store(kv, kv_h)
    store(u, u_h)

    def keep_o(of, r0, g):
        for h in range(4):
            o[r0 : r0 + CLEN, (4 * g + h) * HD : (4 * g + h + 1) * HD] = of[h * CLEN : (h + 1) * CLEN]

    mask = causal_tile()
    spread.hop(1)
    for g in range(2):
        kg = kv[:PLEN, g * HD : (g + 1) * HD]
        vg = kv[:PLEN, kvw + g * HD : kvw + (g + 1) * HD]
        for i in range(PLEN // CLEN):
            size = (i + 1) * CLEN
            s = dt(stack_heads(q, i * CLEN, g), kg[:size])
            tail = jnp.where(mask, s[:, size - CLEN :], MASKED_SCORE)
            s = tail if i == 0 else jnp.concatenate([s[:, : size - CLEN], tail], axis=1)
            p = softmax_low(s)
            pp[g, :, P_OFF[i] : P_OFF[i] + size] = p
            keep_o(dn(p, vg[:size]).astype(BF), i * CLEN, g)
    store(pp, pp_h)
    spread.hop(2)

    def project(r0, half, snd):
        ov = o[r0 : r0 + 2 * half]
        for n in range(0, width, 512):
            part = dn(ov, wo[:, n : n + 512]).astype(BF)
            snd[0, :, n : n + 512] = part[:half]
            snd[1, :, n : n + 512] = part[half:]
        uo = dt(ov, aoT[...]).astype(BF)
        pad = jnp.zeros((half, LANE - RK), BF)
        snd[0, :, width:] = jnp.concatenate([uo[:half], pad], axis=1)
        snd[1, :, width:] = jnp.concatenate([uo[half:], pad], axis=1)

    need(7, 8)
    project(0, hpn, snd_p)
    sum_p = TensorSum(snd_p, got_p, s_p, t_p, psem, d, t)
    sum_p.begin()
    spread.hop(3)

    need(9, 10, 11)
    dud = (dt(dyu[:, :width], bd[...]) * sel).astype(BF)
    dyu[:, width:] = jnp.concatenate([dud, jnp.zeros((rows, LANE - RK), BF)], axis=1)
    store(dyu.at[:, width:], dud_h)
    outs = []
    flats = []
    eye = (lax.broadcasted_iota(jnp.int32, (RK, RK), 0) == lax.broadcasted_iota(jnp.int32, (RK, RK), 1)).astype(BF)
    split = evens_first(256)

    def part_weights(i):
        slot = i % 2
        raw_copy(i, slot).wait()
        if i >= 2:
            for c in flats[i - 2]:
                c.wait()
        pairs = raw[slot].reshape(2 * kt, hidden)
        for n in range(2 * kt // 256):
            apart = dn(split, pairs[n * 256 : (n + 1) * 256]).astype(BF)
            flat[slot, 0, n * 128 : (n + 1) * 128] = apart[:128]
            flat[slot, 1, n * 128 : (n + 1) * 128] = apart[128:]
        flats.append(flat_copies(i, slot))
        for c in flats[i]:
            c.start()
        if i + 2 < raw_steps:
            raw_copy(i + 2, slot).start()

    def act_grad(i):
        slot = i % 2
        for c in wd_copies(i, slot):
            c.wait()
        if i >= 2:
            outs[i - 2].wait()
        ad = dr(adT[:, i * ht : (i + 1) * ht], eye).astype(BF)
        wdc[slot, :, width:] = jnp.concatenate([ad, jnp.zeros((ht, LANE - RK), BF)], axis=1)
        dact[slot] = dt(dyu[...], wdc[slot]).astype(BF)
        c = pltpu.make_async_copy(dact.at[slot], dact_h.at[:, pl.ds(i * ht, ht)], dsem.at[slot])
        c.start()
        outs.append(c)
        if i + 2 < steps:
            for c in wd_copies(i + 2, slot):
                c.start()

    act_grad(0)
    sum_p.middle()
    bsplit = dn(evens_first(b2), bm_ref[...].reshape(b2, hidden)).astype(BF)
    zero = jnp.zeros((RK, hidden), BF)
    bflat[:RK, :hidden] = bsplit[:RK]
    bflat[:RK, hidden:] = zero
    bflat[RK:, :hidden] = zero
    bflat[RK:, hidden:] = bsplit[RK:]
    store(bflat, wgu_h.at[pl.ds(width, b2)])
    for i in range(1, steps):
        act_grad(i)
        spread.hop(i + 3)
    for s in range(steps + 3, hi):
        spread.hop(s)
    for i in range(raw_steps):
        part_weights(i)
    spread.finish()

    far[0] = every[sc[3]]
    far[1] = every[sc[4]]
    store(far, far_h)
    for j in range(CONT_DEV):
        r0 = PLEN + j * CLEN
        for g in range(2):
            lanes = slice(g * HD, (g + 1) * HD)
            vlanes = slice(kvw + g * HD, kvw + (g + 1) * HD)
            qs = stack_heads(q, r0, g)
            sf = dt(qs, far[j, :, lanes])
            so = jnp.where(mask, dt(qs, kv[r0 : r0 + CLEN, lanes]), MASKED_SCORE)
            p = softmax_low(jnp.concatenate([sf, so], axis=1))
            pc[2 * j + g] = p
            keep_o((dn(p[:, :PLEN], far[j, :, vlanes]) + dn(p[:, PLEN:], kv[r0 : r0 + CLEN, vlanes])).astype(BF), r0, g)
    store(pc, pc_h)
    store(o, o_h)
    project(PLEN, hcn, snd_c)
    sum_c = TensorSum(snd_c, got_c, s_c, t_c, csem, d, t)
    sum_c.begin()
    sum_c.middle()

    def norm2(which, total, r0, h, n2, adapter):
        half = h.shape[0]
        total.end()
        sr = sel_row(adapter)
        uo = ((total.mine[:, width : width + RK].astype(F32) + total.theirs[:, width : width + RK].astype(F32)) * sr).astype(BF)
        tmp[:half] = dn(uo, bo[...])
        start = r0 + lo * half
        gain_two = gain2[...].astype(F32)

        def one(r):
            here = pl.ds(r, 64)
            hv = (
                tok[pl.ds(pl.multiple_of(start + r, 64), 64)].astype(F32)
                + (total.mine[here, :width].astype(F32) + total.theirs[here, :width].astype(F32))
                + tmp[here]
            )
            h[here] = hv
            inv = lax.rsqrt(jnp.mean(hv * hv, axis=-1, keepdims=True) + EPSILON)
            n2[lo, here, :width] = (hv * inv * gain_two).astype(BF)

        rows_loop(half, 64, one)
        n2[lo, :, width:] = jnp.concatenate([uo, jnp.zeros((half, LANE - RK), BF)], axis=1)
        c = remote(n2.at[lo], n2.at[lo], nsem.at[which, 0], nsem.at[which, 1], (d, t ^ 1))
        c.start()
        return c

    need(12)
    n2_copy_p = norm2(0, sum_p, 0, hp, n2p, sc[0])
    store(hp, hp_h)
    n2_copy_c = norm2(1, sum_c, PLEN, hc, n2c, jnp.where(lo == 0, sc[1], sc[2]))
    store(hc, hc_h)

    def arrived(which, n2):
        remote(n2.at[1 - lo], n2.at[1 - lo], nsem.at[which, 0], nsem.at[which, 1], (d, t ^ 1)).wait_recv()

    arrived(0, n2p)
    store(n2p, n2p_h)
    arrived(1, n2c)
    store(n2c, n2c_h)
    n2_copy_p.wait_send()
    n2_copy_c.wait_send()
    sum_p.drain()
    sum_c.drain()
    for c in outs[-2:]:
        c.wait()
    for pair in flats[-2:]:
        for c in pair:
            c.wait()
    for c in stores:
        c.wait()


def front(n_dp, scalars, small, large):
    tok, aT, wkv, cos, sin, wq, bq, aoT, wo, dy, bd, adT, bo, wd, raw = large
    rows, width = tok.shape
    qw = wq.shape[1]
    kvw2 = wkv.shape[1]
    hidden = wd.shape[0]
    quarter = width // 4
    wide = width + LANE
    ht, kt = 512, 256
    hpn, hcn = PLEN // 2, CLEN
    outs = [
        ((rows, quarter), BF), ((rows, qw), BF), ((rows, kvw2), BF), ((rows, 3 * RK), BF), ((2, 4 * CLEN, 768), BF),
        ((4, 4 * CLEN, 4 * CLEN), BF), ((rows, qw), BF), ((CONT_DEV, PLEN, kvw2), BF), ((hpn, width), F32),
        ((hcn, width), F32), ((2, hpn, wide), BF), ((2, hcn, wide), BF), ((rows, hidden), BF), ((rows, LANE), BF),
        ((width + 2 * RK, 2 * hidden), BF),
    ]
    dma = pltpu.SemaphoreType.DMA
    same = lambda a: VM(a.shape, a.dtype)
    scratch = [
        same(tok), same(tok), same(aT), same(wkv), same(cos), same(sin), same(wq), same(bq), same(aoT), same(wo),
        VM((rows, wide), BF), same(bd), same(adT), same(bo), VM((2, ht, wide), BF), VM((2, kt, 2, hidden), BF),
        VM((2, 2, kt, hidden), BF), VM((2 * RK, 2 * hidden), BF),
        VM((2, rows, ht), BF), VM((n_dp, PLEN, kvw2), BF), VM((rows, kvw2), BF),
        VM((rows, qw), BF), VM((rows, 3 * RK), BF), VM((CONT_DEV, PLEN, kvw2), BF), VM((2, 4 * CLEN, 768), BF),
        VM((4, 4 * CLEN, 4 * CLEN), BF), VM((rows, qw), BF),
        VM((2, hpn, wide), BF), VM((hpn, wide), BF), VM((hpn, wide), BF), VM((hpn, wide), BF),
        VM((2, hcn, wide), BF), VM((hcn, wide), BF), VM((hcn, wide), BF), VM((hcn, wide), BF),
        VM((2, hpn, wide), BF), VM((2, hcn, wide), BF), VM((hpn, width), F32), VM((hcn, width), F32), VM((hpn, width), F32),
        dma((13,)), dma((14,)), dma((2,)), dma((2,)), dma((2,)), dma((2, 2)), dma((4,)), dma((4,)), dma((2, 2)),
    ] + [dma((n_dp // 2 + 1,))] * 6
    vm = pl.BlockSpec(memory_space=VM)
    anyspace = pl.BlockSpec(memory_space=pl.ANY)
    return pl.pallas_call(
        functools.partial(front_kernel, n_dp),
        out_shape=[jax.ShapeDtypeStruct(s, dtype) for s, dtype in outs],
        in_specs=[pl.BlockSpec(memory_space=pltpu.SMEM)] * 3 + [vm] * len(small) + [anyspace] * len(large),
        out_specs=[anyspace] * len(outs),
        scratch_shapes=scratch,
        compiler_params=pltpu.CompilerParams(vmem_limit_bytes=61 << 20, collective_id=1, has_side_effects=True),
        cost_estimate=pl.CostEstimate(flops=2 * rows * width * 4096, bytes_accessed=80 << 20, transcendentals=0),
        name="front",
    )(*scalars, *small, *large)


def middle_kernel(
    n_dp, ids_p, ids_c, gain2, amT, adT, n2p_h, n2c_h, dact_h, dud_h, wgu_h, wd_h, hp_h, hc_h, dy_h,
    dhp_h, dhc_h, dap_h, dac_h, smp_h, smc_h, ge_h,
    wcat, wdn, n2p, n2c, dact, dud, acc, gu, dga, act, gg, ge, gots, gsum,
    snd_p, got_p, s_p, t_p, snd_c, got_c, s_c, t_c, msnd_p, mgot_p, msnd_c, mgot_c, hp, hc, dyp, dyc, dap, dac, tmp,
    lsem, osem, wsem, vsem, psem, csem, msem, nsem, g0, g1,
):
    d, t = place()
    sc = [ids_p[0], ids_c[0], ids_c[1]]
    lo = t % 2
    width = hp.shape[1]
    wide = n2p.shape[2]
    hidden = wd_h.shape[0]
    ht = wcat.shape[2] // 2
    nt = wdn.shape[2]
    steps = hidden // ht
    hpn, hcn = PLEN // 2, CLEN
    greet(d, t, n_dp)

    def weights(k, slot):
        i = k % steps
        here = pl.ds(pl.multiple_of(i * ht, ht), ht)
        there = pl.ds(pl.multiple_of(hidden + i * ht, ht), ht)
        return [
            pltpu.make_async_copy(src, dst, wsem.at[slot, n])
            for n, (src, dst) in enumerate(
                [(wgu_h.at[:, here], wcat.at[slot, :, :ht]), (wgu_h.at[:, there], wcat.at[slot, :, ht:])]
            )
        ]

    def down(n, slot):
        return pltpu.make_async_copy(wd_h.at[:, pl.ds(n * nt, nt)], wdn.at[slot], vsem.at[slot])

    def load(n, src, dst):
        c = pltpu.make_async_copy(src, dst, lsem.at[n])
        c.start()
        return c

    load_p = load(0, n2p_h, n2p)
    for c in weights(0, 0):
        c.start()
    load_da = load(1, dact_h, dact)
    load_du = load(2, dud_h, dud)
    load_c = load(3, n2c_h, n2c)
    load_hp = load(4, hp_h, hp)
    load_hc = load(5, hc_h, hc)
    load_dyp = load(6, dy_h.at[pl.ds(pl.multiple_of(lo * hpn, hpn), hpn)], dyp)
    load_dyc = load(7, dy_h.at[pl.ds(pl.multiple_of(PLEN + lo * hcn, hcn), hcn)], dyc)
    for n in range(2):
        down(n, n).start()
    stores = []

    def store(src, dst):
        c = pltpu.make_async_copy(src, dst, osem.at[len(stores)])
        c.start()
        stores.append(c)

    def begin(n2, sel):
        half = n2.shape[1]
        r = 2 * half
        u = dt(n2[:, :, :width].reshape(r, width), amT[...])
        um = jnp.concatenate([(u[:, :RK] * sel).astype(BF), (u[:, RK:] * sel).astype(BF)], axis=1)
        n2[:, :, width:] = um.reshape(2, half, 2 * RK)

        acc[:r] = jnp.zeros((r, wide), F32)

    def tile(k, n2, base, add):
        r = 2 * n2.shape[1]
        slot = k % 2
        i = k % steps
        for c in weights(k, slot):
            c.wait()

        @pl.when(k + 1 < 2 * steps)
        def _():
            for c in weights(k + 1, 1 - slot):
                c.start()

        gu[:r] = dn(n2[...].reshape(r, wide), wcat[slot])
        lanes = pl.ds(pl.multiple_of(i * ht, ht), ht)

        def swiglu(r0):
            here = pl.ds(r0, 64)
            gate = gu[here, :ht]
            upper = gu[here, ht:]
            sigma = 1.0 / (1.0 + jnp.exp(-gate))
            silu = gate * sigma
            there = pl.ds(pl.multiple_of(base + r0, 64), 64)
            da = dact[there, lanes].astype(F32)
            dga[here, :ht] = (da * upper * (sigma * (1.0 + gate * (1.0 - sigma)))).astype(BF)
            dga[here, ht : 2 * ht] = (da * silu).astype(BF)
            av = (silu * upper).astype(BF)
            dga[here, 2 * ht :] = av
            act[there, lanes] = av

        rows_loop(r, 64, swiglu)
        acc[:r] += dt(dga[:r, : 2 * ht], wcat[slot])
        small = jnp.concatenate([n2[:, :, width:].reshape(r, 2 * RK), dud[base : base + r, :RK]], axis=1)
        g = dr(small, dga[:r])
        for n in range(3):
            part = g[n * RK : (n + 1) * RK, n * ht : (n + 1) * ht]
            if add:
                total = (gg[n, :, lanes] + part).astype(BF)
                units = ht // LANE * (RK // 16)
                put_units(ge, n * (hidden // LANE * (RK // 16)) + i * units, total)
            else:
                gg[n, :, lanes] = part

    def halves(a, snd):
        half = snd.shape[1]

        def one(r0):
            for n in range(2):
                snd[n, pl.ds(r0, 64)] = a[pl.ds(pl.multiple_of(n * half + r0, 64), 64)].astype(BF)

        rows_loop(half, 64, one)

    load_p.wait()
    begin(n2p, sel_row(sc[0]))
    load_da.wait()
    load_du.wait()

    def loop_p(k, carry):
        tile(k, n2p, 0, False)
        return carry

    lax.fori_loop(0, steps, loop_p, 0)
    halves(acc, snd_p)
    greeted(n_dp)
    sum_p = TensorSum(snd_p, got_p, s_p, t_p, psem, d, t)
    sum_p.begin()

    load_c.wait()
    begin(n2c, jnp.concatenate([jnp.broadcast_to(sel_row(sc[1]), (hcn, RK)), jnp.broadcast_to(sel_row(sc[2]), (hcn, RK))], axis=0))
    tile(steps, n2c, PLEN, True)
    sum_p.middle()

    def loop_c(k, carry):
        tile(k, n2c, PLEN, True)
        return carry

    lax.fori_loop(steps + 1, 2 * steps, loop_c, 0)
    halves(acc, snd_c)
    sum_c = TensorSum(snd_c, got_c, s_c, t_c, csem, d, t)
    sum_c.begin()
    reduce = DirectReduce(ge, gots, gsum, (g0, g1, None, None), d, t, n_dp)
    reduce.start()

    ud = dt(act[...], adT[...]).astype(BF)
    pad = jnp.zeros((hpn, LANE - RK), BF)
    for n in range(2):
        msnd_p[n, :, width:] = jnp.concatenate([ud[n * hpn : (n + 1) * hpn], pad], axis=1)
        msnd_c[n, :, width:] = jnp.concatenate([ud[PLEN + n * hcn : PLEN + (n + 1) * hcn], pad[:hcn]], axis=1)
    sum_c.middle()
    for n in range(width // nt):
        slot = n % 2
        down(n, slot).wait()
        part = dn(act[...], wdn[slot]).astype(BF)
        lanes = slice(n * nt, (n + 1) * nt)
        for i in range(2):
            msnd_p[i, :, lanes] = part[i * hpn : (i + 1) * hpn]
            msnd_c[i, :, lanes] = part[PLEN + i * hcn : PLEN + (i + 1) * hcn]
        if n + 2 < width // nt:
            down(n + 2, slot).start()
    mcore_p = remote(msnd_p.at[1 - lo], mgot_p, msem.at[0], msem.at[1], (d, t ^ 1))
    mcore_p.start()
    mcore_c = remote(msnd_c.at[1 - lo], mgot_c, msem.at[2], msem.at[3], (d, t ^ 1))
    mcore_c.start()

    def mlp_sum(core, snd, got, out):
        core.wait_recv()

        def add(r0):
            rows = pl.ds(r0, 64)
            got[rows] = (snd[lo, rows].astype(F32) + got[rows].astype(F32)).astype(BF)

        rows_loop(got.shape[0], 64, add)
        store(got, out)

    def back(which, total, h, dy, da, adapter):
        half = h.shape[0]
        total.end()
        sr = sel_row(adapter)
        du = total.mine[:, width:].astype(F32) + total.theirs[:, width:].astype(F32)
        dum = (du * jnp.concatenate([sr, sr], axis=1)).astype(BF)
        tmp[:half] = dn(dum, amT[...])
        gain = gain2[...].astype(F32)

        def one(r0):
            here = pl.ds(r0, 64)
            dn2 = total.mine[here, :width].astype(F32) + total.theirs[here, :width].astype(F32) + tmp[here]
            dh = dy[here].astype(F32) + norm_back(h[here], gain, dn2)
            h[here] = dh
            da[lo, here, :width] = dh.astype(BF)

        rows_loop(half, 64, one)
        da[lo, :, width:] = dum
        c = remote(da.at[lo], da.at[lo], nsem.at[which, 0], nsem.at[which, 1], (d, t ^ 1))
        c.start()
        return c

    load_hp.wait()
    load_dyp.wait()
    copy_p = back(0, sum_p, hp, dyp, dap, sc[0])
    store(hp, dhp_h)
    mlp_sum(mcore_p, msnd_p, mgot_p, smp_h)
    mlp_sum(mcore_c, msnd_c, mgot_c, smc_h)
    reduce.add()
    store(gsum.at[reduce.part(d)], ge_h)
    load_hc.wait()
    load_dyc.wait()
    copy_c = back(1, sum_c, hc, dyc, dac, jnp.where(lo == 0, sc[1], sc[2]))
    store(hc, dhc_h)

    def arrived(which, da):
        remote(da.at[1 - lo], da.at[1 - lo], nsem.at[which, 0], nsem.at[which, 1], (d, t ^ 1)).wait_recv()

    arrived(0, dap)
    store(dap, dap_h)
    arrived(1, dac)
    store(dac, dac_h)
    copy_p.wait_send()
    copy_c.wait_send()
    sum_p.drain()
    sum_c.drain()
    mcore_p.wait_send()
    mcore_c.wait_send()
    reduce.sent()
    for c in stores:
        c.wait()


def middle(n_dp, scalars, small, large):
    n2p, n2c, dact, dud, wgu, wd, hp, hc, dy = large
    rows, width = dy.shape
    hidden = wd.shape[0]
    wide = n2p.shape[2]
    ht, nt = 512, 512
    hpn, hcn = PLEN // 2, CLEN
    units = 3 * hidden // LANE * (RK // 16)
    share = units // n_dp
    outs = [
        ((hpn, width), F32), ((hcn, width), F32), ((2, hpn, wide), BF), ((2, hcn, wide), BF), ((hpn, wide), BF),
        ((hcn, wide), BF), ((share, *UNIT), BF),
    ]
    dma = pltpu.SemaphoreType.DMA
    scratch = [
        VM((2, wide, 2 * ht), BF), VM((2, hidden, nt), BF), VM((2, hpn, wide), BF), VM((2, hcn, wide), BF),
        VM((rows, hidden), BF), VM((rows, LANE), BF), VM((PLEN, wide), F32),
        VM((PLEN, 2 * ht), F32), VM((PLEN, 3 * ht), BF), VM((rows, hidden), BF), VM((3, RK, hidden), F32),
        VM((units, *UNIT), BF), VM((n_dp, share, *UNIT), BF), VM((units, *UNIT), BF),
        VM((2, hpn, wide), BF), VM((hpn, wide), BF), VM((hpn, wide), BF), VM((hpn, wide), BF),
        VM((2, hcn, wide), BF), VM((hcn, wide), BF), VM((hcn, wide), BF), VM((hcn, wide), BF),
        VM((2, hpn, wide), BF), VM((hpn, wide), BF), VM((2, hcn, wide), BF), VM((hcn, wide), BF),
        VM((hpn, width), F32), VM((hcn, width), F32), VM((hpn, width), BF), VM((hcn, width), BF),
        VM((2, hpn, wide), BF), VM((2, hcn, wide), BF), VM((hpn, width), F32),
        dma((8,)), dma((7,)), dma((2, 2)), dma((2,)), dma((4,)), dma((4,)), dma((4,)), dma((2, 2)), dma((n_dp,)), dma((n_dp,)),
    ]
    vm = pl.BlockSpec(memory_space=VM)
    anyspace = pl.BlockSpec(memory_space=pl.ANY)
    return pl.pallas_call(
        functools.partial(middle_kernel, n_dp),
        out_shape=[jax.ShapeDtypeStruct(s, dtype) for s, dtype in outs],
        in_specs=[pl.BlockSpec(memory_space=pltpu.SMEM)] * 2 + [vm] * len(small) + [anyspace] * len(large),
        out_specs=[anyspace] * len(outs),
        scratch_shapes=scratch,
        compiler_params=pltpu.CompilerParams(vmem_limit_bytes=61 << 20, collective_id=2, has_side_effects=True),
        cost_estimate=pl.CostEstimate(flops=10 * rows * width * hidden, bytes_accessed=60 << 20, transcendentals=0),
        name="middle",
    )(*scalars, *small, *large)


class Fold:
    def __init__(self, dfar, xs, xr, ur, dr_, sems, sc, d, t, hi):
        self.dfar, self.xs, self.xr, self.ur, self.dr, self.sems, self.sc = dfar, xs, xr, ur, dr_, sems, sc
        self.d, self.t, self.hi = d, t, hi
        self.z, self.x = d // 2, d % 2
        self.order = []
        low, high = 0, hi - 1
        while low <= high:
            self.order.append(high)
            if low != high:
                self.order.append(low)
            low, high = low + 1, high - 1

    def piece(self, dest, rows):
        first = (self.sc[3] == dest).astype(F32)
        second = (self.sc[4] == dest).astype(F32)
        return self.dfar[0, rows] * first + self.dfar[1, rows] * second

    def across(self, z):
        return remote(self.xs.at[z], self.xr.at[z], self.sems[0].at[z], self.sems[1].at[z], (self.d ^ 1, self.t))

    def up(self, z):
        return remote(self.xr.at[z], self.ur.at[z], self.sems[2].at[z], self.sems[3].at[z], (self.d + 2, self.t))

    def down(self, z):
        return remote(self.xr.at[z], self.dr.at[z], self.sems[4].at[z], self.sems[5].at[z], (self.d - 2, self.t))

    def start(self):
        for z in self.order:

            def put(r, z=z):
                rows = pl.ds(r, 64)
                self.xs[z, rows] = self.piece(z * 2 + 1 - self.x, rows).astype(BF)

            rows_loop(PLEN, 64, put)
            self.across(z).start()

    def fold(self, n):
        z = self.order[n]
        self.across(z).wait_recv()

        def add(r):
            rows = pl.ds(r, 64)
            self.xr[z, rows] = (self.xr[z, rows].astype(F32) + self.piece(z * 2 + self.x, rows)).astype(BF)

        rows_loop(PLEN, 64, add)
        if z > 0:

            @pl.when(self.z == 0)
            def _():
                self.up(z).start()

        if z < self.hi - 1:

            @pl.when(self.z == self.hi - 1)
            def _():
                self.down(z).start()

    def forward(self, k):
        up, down = self.hi - 1 - k, k

        def add(z, got):
            def one(r):
                rows = pl.ds(r, 64)
                self.xr[z, rows] = (self.xr[z, rows].astype(F32) + got[z, rows].astype(F32)).astype(BF)

            rows_loop(PLEN, 64, one)

        @pl.when((self.z > 0) & (self.z < up))
        def _():
            self.up(up).wait_recv()
            add(up, self.ur)
            self.up(up).start()

        @pl.when((self.z > down) & (self.z < self.hi - 1))
        def _():
            self.down(down).wait_recv()
            add(down, self.dr)
            self.down(down).start()

    def finish(self, total):
        total[...] += self.xr[self.z].astype(F32)

        @pl.when(self.z > 0)
        def _():
            self.up(self.z).wait_recv()
            total[...] += self.ur[self.z].astype(F32)

        @pl.when(self.z < self.hi - 1)
        def _():
            self.down(self.z).wait_recv()
            total[...] += self.dr[self.z].astype(F32)

    def drain(self):
        for z in range(self.hi):
            self.across(z).wait_send()
            if z > 0:

                @pl.when(z > self.z)
                def _(z=z):
                    self.up(z).wait_send()

            if z < self.hi - 1:

                @pl.when(z < self.z)
                def _(z=z):
                    self.down(z).wait_send()


def back_kernel(
    n_dp, ids_p, ids_c, group_map, gain1, bkv_ref,
    dac_h, wo_h, o_h, aoT_h, bo_h, n2c_h, q_h, kv_h, far_h, pc_h, cos_h, sin_h, dap_h, pp_h, n2p_h, u_h, wq_h, wkv_h, bq_h,
    smp_h, hp_h, bd_h, smc_h, hc_h, dy_h, n1q_h, dhc_h, aT_h, dhp_h, tok_h, ge_h,
    out_h, tg_h, gef_h, l1_h, l2_h, t1_h, t2_h,
    dac, wo, o, aoT, bo, n2c, uoc, q, kv, far, pc, cos, sin, dap, pp, n2p, uop, u, wq, wkv, bq,
    smp, hp, bd, smc, hc, dyq, n1q, aT, xc, xp, gef, tmp_p, tmp_c,
    do, dq, dqp, dkv, dkvp, dfar, gacc, snd_p, got_p, s_p, t_p, snd_c, got_c, s_c, t_c,
    dsnd_p, dgot_p, ds_p, dt_p, dsnd_c, dgot_c, ds_c, dt_c, dup, duc, outp, outc, tgp, tgc, tmp,
    l1s, l1g, l1, l2s, l2g, l2, t1, t2, xs, xr, ur, dr_,
    lsem, osem, ysem, psem, csem, dpsem, dcsem, nsem, q1, q2, f0, f1, f2, f3, f4, f5, *rsems,
):
    d, t = place()
    sc = [ids_p[0], ids_c[0], ids_c[1], group_map[d * CONT_DEV], group_map[d * CONT_DEV + 1]]
    lo = t % 2
    hi = n_dp // 2
    width = wq.shape[0]
    qw = wq.shape[1]
    kvw = wkv.shape[1] // 2
    quarter = n1q.shape[1]
    hpn, hcn = PLEN // 2, CLEN
    greet(d, t, n_dp)
    qlanes = pl.ds(pl.multiple_of(t * quarter, quarter), quarter)
    every = DirectReduce(None, None, gef, (None, None, rsems[0], rsems[1]), d, t, n_dp)
    pairs = [
        (ge_h, gef.at[every.part(d)]), (dac_h, dac), (wo_h, wo), (o_h, o), (aoT_h, aoT), (bo_h, bo), (n2c_h.at[:, :, qlanes], n2c),
        (n2c_h.at[:, :, width:], uoc), (q_h, q), (kv_h, kv), (far_h, far), (pc_h, pc), (cos_h, cos), (sin_h, sin), (dap_h, dap),
        (pp_h, pp), (n2p_h.at[:, :, qlanes], n2p), (n2p_h.at[:, :, width:], uop), (u_h, u), (wq_h, wq), (wkv_h, wkv), (bq_h, bq),
        (smp_h, smp), (hp_h, hp), (bd_h, bd), (smc_h, smc), (hc_h, hc), (dy_h.at[:, qlanes], dyq), (n1q_h, n1q),
        (aT_h, aT), (tok_h.at[pl.ds(pl.multiple_of(PLEN + lo * hcn, hcn), hcn)], xc),
        (tok_h.at[pl.ds(pl.multiple_of(lo * hpn, hpn), hpn)], xp),
    ]
    loads = {}
    for n, (src, dst) in enumerate(pairs):
        c = pltpu.make_async_copy(src, dst, lsem.at[n])
        c.start()
        loads[id(dst) if n else 0] = c

    def need(*refs):
        for ref in refs:
            loads.pop(id(ref)).wait()

    stores = []

    def store(src, dst):
        c = pltpu.make_async_copy(src, dst, osem.at[len(stores)])
        c.start()
        stores.append(c)

    greeted(n_dp)
    loads.pop(0).wait()
    every.spread()
    mlp_p = remote(smp_h, tmp_p, ysem.at[0], ysem.at[1], (d, t ^ 2))
    mlp_p.start()
    mlp_c = remote(smc_h, tmp_c, ysem.at[2], ysem.at[3], (d, t ^ 2))
    mlp_c.start()

    at = np.cumsum([0, qw, quarter, quarter, quarter, qw, 2 * kvw]).tolist()
    bkv = dn(evens_first(2 * RK), bkv_ref[...].reshape(2 * RK, kvw)).astype(BF)

    def out_grads(da, n2, uo, sel, r0, first):
        half = da.shape[1]
        r = 2 * half
        dav = da[:, :, :width].reshape(r, width)
        duo = (dt(dav, bo[...]) * sel).astype(BF)
        do[r0 : r0 + r] = (dt(dav, wo[...]) + dn(duo, aoT[...])).astype(BF)
        gao = dr(duo, o[r0 : r0 + r])
        dum = da[:, :, width:].reshape(r, 2 * RK)
        gam = dr(dum, n2[...].reshape(r, quarter))
        gbo = dr(uo[:, :, :RK].reshape(r, RK), da[:, :, qlanes].reshape(r, quarter))
        parts = (gao, gbo, gam[:RK], gam[RK:])
        for n, part in enumerate(parts):
            lanes = slice(at[n], at[n + 1])
            gacc[:, lanes] = part if first else gacc[:, lanes] + part

    def unrotate(r0, r):
        here = slice(r0, r0 + r)
        for c in range(qw // LANE):
            lanes = slice(c * LANE, (c + 1) * LANE)
            dqp[here, lanes] = rot(dq[here, lanes].astype(F32), cos[here], -sin[here]).astype(BF)
        dkvp[here, :kvw] = rot(dkv[here, :kvw].astype(BF).astype(F32), cos[here], -sin[here]).astype(BF)
        dkvp[here, kvw:] = dkv[here, kvw:].astype(BF)

    need(dac, wo, o, aoT, bo, n2c, uoc)
    sel_c = jnp.concatenate([jnp.broadcast_to(sel_row(sc[1]), (hcn, RK)), jnp.broadcast_to(sel_row(sc[2]), (hcn, RK))], axis=0)
    out_grads(dac, n2c, uoc, sel_c, PLEN, True)
    need(q, kv, far, pc)
    for j in range(CONT_DEV):
        r0 = PLEN + j * CLEN
        for g in range(2):
            lanes = slice(g * HD, (g + 1) * HD)
            vlanes = slice(kvw + g * HD, kvw + (g + 1) * HD)
            qi = stack_heads(q, r0, g)
            doi = stack_heads(do, r0, g)
            p = pc[2 * j + g]
            dp = jnp.concatenate([dt(doi, far[j, :, vlanes]), dt(doi, kv[r0 : r0 + CLEN, vlanes])], axis=1)
            ds = back_scores(p, dp)
            dqv = dn(ds[:, :PLEN], far[j, :, lanes]) + dn(ds[:, PLEN:], kv[r0 : r0 + CLEN, lanes])
            put_dq((dqv * 0.125).astype(BF), dq, r0, g)
            dk = dr(ds, qi)
            dv = dr(p, doi)
            dfar[j, :, lanes] = dk[:PLEN]
            dfar[j, :, vlanes] = dv[:PLEN]
            dkv[r0 : r0 + CLEN, lanes] = dk[PLEN:]
            dkv[r0 : r0 + CLEN, vlanes] = dv[PLEN:]
    fold = Fold(dfar, xs, xr, ur, dr_, (f0, f1, f2, f3, f4, f5), sc, d, t, hi)
    fold.start()
    need(cos, sin)
    unrotate(PLEN, 2 * hcn)

    def dn1(r0, snd, dsnd, dsum, first):
        half = snd.shape[1]
        r = 2 * half
        here = slice(r0, r0 + r)
        a, b = dqp[here], dkvp[here]
        du = jnp.concatenate(
            [dt(a, bq[...]), dt(b[:, :kvw], bkv[:RK]), dt(b[:, kvw:], bkv[RK:]), jnp.zeros((r, RK), F32)], axis=1
        ).astype(BF)
        dsnd[0] = du[:half]
        dsnd[1] = du[half:]
        dsum.begin()
        for n in range(0, width, 512):
            part = (dt(a, wq[n : n + 512]) + dt(b, wkv[n : n + 512])).astype(BF)
            snd[0, :, n : n + 512] = part[:half]
            snd[1, :, n : n + 512] = part[half:]
        gbq = dr(u[here, :RK], a)
        gkv = dr(u[here, RK:], b)
        parts = (gbq, gkv[:RK, :kvw], gkv[RK:, kvw:])
        for part, start in zip(parts, (at[4], at[5], at[5] + kvw)):
            lanes = slice(start, start + part.shape[1])
            gacc[:, lanes] = part if first else gacc[:, lanes] + part

    need(wq, wkv, u, bq)
    dsum_c = TensorSum(dsnd_c, dgot_c, ds_c, dt_c, dcsem, d, t)
    dn1(PLEN, snd_c, dsnd_c, dsum_c, True)
    sum_c = TensorSum(snd_c, got_c, s_c, t_c, csem, d, t)
    sum_c.begin()
    fold.fold(0)
    if hi > 1:
        fold.fold(1)

    need(dap, n2p, uop)
    out_grads(dap, n2p, uop, jnp.broadcast_to(sel_row(sc[0]), (PLEN, RK)), 0, False)
    dsum_c.middle()
    sum_c.middle()
    need(pp)
    for g in range(2):
        lanes = slice(g * HD, (g + 1) * HD)
        vlanes = slice(kvw + g * HD, kvw + (g + 1) * HD)
        kg = kv[:PLEN, lanes]
        vg = kv[:PLEN, vlanes]
        for i in reversed(range(PLEN // CLEN)):
            size = (i + 1) * CLEN
            qi = stack_heads(q, i * CLEN, g)
            doi = stack_heads(do, i * CLEN, g)
            p = pp[g, :, P_OFF[i] : P_OFF[i] + size]
            ds = back_scores(p, dt(doi, vg[:size]))
            put_dq((dn(ds, kg[:size]) * 0.125).astype(BF), dq, i * CLEN, g)
            dk = dr(ds, qi)
            dv = dr(p, doi)
            if size == PLEN:
                dkv[:size, lanes] = dk
                dkv[:size, vlanes] = dv
            else:
                dkv[:size, lanes] += dk
                dkv[:size, vlanes] += dv
        if g == 0:
            for n in range(2, hi):
                fold.fold(n)
            fold.forward(0)
    for k in range(1, hi - 1):
        fold.forward(k)

    def finish_out(which, sm, theirs, copy, h, out, r0, adapter):
        half = h.shape[0]
        copy.wait_recv()
        sr = sel_row(adapter)
        ud = ((sm[:, width : width + RK].astype(F32) + theirs[:, width : width + RK].astype(F32)) * sr).astype(BF)
        tmp[:half] = dn(ud, bd[...])

        def one(r):
            here = pl.ds(r, 64)
            out[lo, here, :width] = (
                h[here] + (sm[here, :width].astype(F32) + theirs[here, :width].astype(F32)) + tmp[here]
            ).astype(BF)

        rows_loop(half, 64, one)
        out[lo, :, width:] = jnp.concatenate([ud, jnp.zeros((half, LANE - RK), BF)], axis=1)
        c = remote(out.at[lo], out.at[lo], nsem.at[which, 0], nsem.at[which, 1], (d, t ^ 1))
        c.start()
        return c

    def arrived(which, out):
        remote(out.at[1 - lo], out.at[1 - lo], nsem.at[which, 0], nsem.at[which, 1], (d, t ^ 1)).wait_recv()

    need(smp, hp, bd)
    out_copy_p = finish_out(0, smp, tmp_p, mlp_p, hp, outp, 0, sc[0])
    load_dhp = pltpu.make_async_copy(dhp_h, hp, lsem.at[32])
    load_dhp.start()

    put_units(l1s, 0, gacc[:, : at[4]].astype(BF))
    red1 = DirectReduce(l1s, l1g, l1, rsems[2:6], d, t, n_dp)
    red1.start()

    fold.finish(dkv.at[:PLEN])
    unrotate(0, PLEN)
    dsum_p = TensorSum(dsnd_p, dgot_p, ds_p, dt_p, dpsem, d, t)
    dn1(0, snd_p, dsnd_p, dsum_p, False)
    sum_p = TensorSum(snd_p, got_p, s_p, t_p, psem, d, t)
    sum_p.begin()
    dsum_p.middle()
    need(smc, hc)
    adapter_c = jnp.where(lo == 0, sc[1], sc[2])
    sum_p.middle()
    out_copy_c = finish_out(1, smc, tmp_c, mlp_c, hc, outc, PLEN, adapter_c)
    load_dhc = pltpu.make_async_copy(dhc_h, hc, lsem.at[33])
    load_dhc.start()
    put_units(l2s, 0, gacc[:, at[4] :].astype(BF))

    def share_du(which, total, du, adapter):
        total.end()
        sr = sel_row(adapter)
        raw = total.mine[:, : 3 * RK].astype(F32) + total.theirs[:, : 3 * RK].astype(F32)
        duq = (raw * jnp.concatenate([sr, sr, sr], axis=1)).astype(BF)
        du[lo] = jnp.concatenate([duq, jnp.zeros((duq.shape[0], RK), BF)], axis=1)
        c = remote(du.at[lo], du.at[lo], nsem.at[which, 0], nsem.at[which, 1], (d, t ^ 1))
        c.start()
        return c

    du_copy_c = share_du(4, dsum_c, duc, adapter_c)
    arrived(0, outp)
    arrived(1, outc)
    for n in range(2):
        store(outp.at[n, :, :width], out_h.at[pl.ds(n * hpn, hpn)])
        store(outc.at[n, :, :width], out_h.at[pl.ds(PLEN + n * hcn, hcn)])
    need(dyq, n1q)
    gbd = dr(outp[:, :, width : width + RK].reshape(PLEN, RK), dyq[:PLEN])
    gbd = gbd + dr(outc[:, :, width : width + RK].reshape(2 * hcn, RK), dyq[PLEN:])
    part1 = (at[6] - at[4]) // LANE * (RK // 16)
    put_units(l2s, part1, gbd.astype(BF))
    arrived(4, duc)
    ga = dr(duc[:, :, : 3 * RK].reshape(2 * hcn, 3 * RK), n1q[PLEN:])
    du_copy_p = share_du(5, dsum_p, dup, sc[0])
    arrived(5, dup)
    ga = (ga + dr(dup[:, :, : 3 * RK].reshape(PLEN, 3 * RK), n1q[:PLEN])).astype(BF)
    per = quarter // LANE * (RK // 16)
    for n in range(3):
        put_units(l2s, part1 + (1 + n) * per, ga[n * RK : (n + 1) * RK])
    if l2s.shape[0] > part1 + 4 * per:
        l2s[part1 + 4 * per :] = jnp.zeros((l2s.shape[0] - part1 - 4 * per, *UNIT), BF)
    red2 = DirectReduce(l2s, l2g, l2, rsems[6:10], d, t, n_dp)
    red2.start()

    def last(which, total, du, x, dh, tg):
        half = x.shape[0]
        tmp[:half] = dn(du[lo, :, : 3 * RK], aT[...])
        gain = gain1[...].astype(F32)
        total.end()

        def one(r):
            here = pl.ds(r, 64)
            dn1v = total.mine[here].astype(F32) + total.theirs[here].astype(F32) + tmp[here]
            grad = dh[here] + norm_back(x[here].astype(F32), gain, dn1v)
            tg[lo, here] = grad.astype(BF)

        rows_loop(half, 64, one)
        c = remote(tg.at[lo], tg.at[lo], nsem.at[which, 0], nsem.at[which, 1], (d, t ^ 1))
        c.start()
        return c

    need(xc, aT)
    load_dhc.wait()
    tg_copy_c = last(2, sum_c, duc, xc, hc, tgc)
    red1.add()
    red1.spread()
    arrived(2, tgc)
    for n in range(2):
        store(tgc.at[n], tg_h.at[pl.ds(PLEN + n * hcn, hcn)])
    every.finish()
    store(gef, gef_h)
    red2.add()
    red2.spread()
    need(xp)
    load_dhp.wait()
    tg_copy_p = last(3, sum_p, dup, xp, hp, tgp)
    red1.finish()
    store(l1, l1_h)
    t1[t] = l1[per : 4 * per]
    gather1 = QuarterGather(t1, q1, d, t)
    gather1.start()
    red2.finish()
    store(l2, l2_h)
    t2[t] = l2[part1 : part1 + 4 * per]
    gather2 = QuarterGather(t2, q2, d, t)
    gather2.start()
    arrived(3, tgp)
    for n in range(2):
        store(tgp.at[n], tg_h.at[pl.ds(n * hpn, hpn)])
    gather1.relay()
    gather2.relay()
    gather1.finish()
    store(t1, t1_h)
    gather2.finish()
    store(t2, t2_h)
    for c in (out_copy_p, out_copy_c, tg_copy_c, tg_copy_p, du_copy_c, du_copy_p, mlp_p, mlp_c):
        c.wait_send()
    for total in (sum_p, sum_c, dsum_p, dsum_c):
        total.drain()
    fold.drain()
    every.spread_sent()
    for red in (red1, red2):
        red.sent()
        red.spread_sent()
    for c in stores:
        c.wait()


def backward(n_dp, scalars, small, large):
    (dac, wo, o, aoT, bo, n2c, q, kv, far, pc, cos, sin, dap, pp, n2p, u, wq, wkv, bq, smp, hp, bd, smc, hc, dy, n1q, dhc, aT, dhp,
     tok, ge) = large
    rows, width = tok.shape
    qw = wq.shape[1]
    kvw2 = wkv.shape[1]
    quarter = n1q.shape[1]
    wide = dap.shape[2]
    hpn, hcn = PLEN // 2, CLEN
    per = quarter // LANE * (RK // 16)
    up = lambda a: -(-a // n_dp) * n_dp
    ue = ge.shape[0] * n_dp
    u1 = up((qw + 3 * quarter) // LANE * (RK // 16))
    u2 = up((qw + kvw2 + 4 * quarter) // LANE * (RK // 16))
    outs = [
        ((rows, width), BF), ((rows, width), BF), ((ue, *UNIT), BF), ((u1, *UNIT), BF), ((u2, *UNIT), BF),
        ((4, 3 * per, *UNIT), BF), ((4, 4 * per, *UNIT), BF),
    ]
    dma = pltpu.SemaphoreType.DMA
    hi = n_dp // 2
    same = lambda a: VM(a.shape, a.dtype)

    def sums(half, n):
        return [VM((2, half, n), BF), VM((half, n), BF), VM((half, n), BF), VM((half, n), BF)]

    scratch = [
        same(dac), same(wo), same(o), same(aoT), same(bo), VM((2, hcn, quarter), BF), VM((2, hcn, LANE), BF), same(q), same(kv),
        same(far), same(pc), same(cos), same(sin), same(dap), same(pp), VM((2, hpn, quarter), BF), VM((2, hpn, LANE), BF),
        same(u), same(wq), same(wkv), same(bq), same(smp), same(hp), same(bd), same(smc), same(hc), VM((rows, quarter), BF),
        same(n1q), same(aT), VM((hcn, width), BF), VM((hpn, width), BF), VM((ue, *UNIT), BF),
        same(smp), same(smc),
        VM((rows, qw), BF), VM((rows, qw), BF), VM((rows, qw), BF), VM((rows, kvw2), F32), VM((rows, kvw2), BF),
        VM((CONT_DEV, PLEN, kvw2), F32), VM((RK, 2 * qw + 3 * quarter + kvw2), F32),
        *sums(hpn, width), *sums(hcn, width), *sums(hpn, 2 * LANE), *sums(hcn, 2 * LANE),
        VM((2, hpn, 2 * LANE), BF), VM((2, hcn, 2 * LANE), BF),
        VM((2, hpn, wide), BF), VM((2, hcn, wide), BF), VM((2, hpn, width), BF), VM((2, hcn, width), BF), VM((hpn, width), F32),
        VM((u1, *UNIT), BF), VM((n_dp, u1 // n_dp, *UNIT), BF), VM((u1, *UNIT), BF),
        VM((u2, *UNIT), BF), VM((n_dp, u2 // n_dp, *UNIT), BF), VM((u2, *UNIT), BF),
        VM((4, 3 * per, *UNIT), BF), VM((4, 4 * per, *UNIT), BF),
        VM((hi, PLEN, kvw2), BF), VM((hi, PLEN, kvw2), BF), VM((hi, PLEN, kvw2), BF), VM((hi, PLEN, kvw2), BF),
        dma((34,)), dma((13,)), dma((4,)), dma((4,)), dma((4,)), dma((4,)), dma((4,)), dma((6, 2)), dma((3, 2)), dma((3, 2)),
    ] + [dma((hi,))] * 6 + [dma((n_dp,))] * 10
    vm = pl.BlockSpec(memory_space=VM)
    anyspace = pl.BlockSpec(memory_space=pl.ANY)
    return pl.pallas_call(
        functools.partial(back_kernel, n_dp),
        out_shape=[jax.ShapeDtypeStruct(s, dtype) for s, dtype in outs],
        in_specs=[pl.BlockSpec(memory_space=pltpu.SMEM)] * 3 + [vm] * len(small) + [anyspace] * len(large),
        out_specs=[anyspace] * len(outs),
        scratch_shapes=scratch,
        compiler_params=pltpu.CompilerParams(vmem_limit_bytes=63 << 20, collective_id=3, has_side_effects=True),
        cost_estimate=pl.CostEstimate(flops=6 * rows * width * (2 * qw + kvw2), bytes_accessed=40 << 20, transcendentals=0),
        name="back",
    )(*scalars, *small, *large)


def emit_kernel(
    qw, kvw, quarter, hidden, ge, l1, l2, t1, t2, out_h, tg_h,
    gbm, gad, gao, gbq, gbkv, gbo, gam, gbd, ga, out_o, tg_o, sem,
):
    copies = [pltpu.make_async_copy(out_h, out_o, sem.at[0]), pltpu.make_async_copy(tg_h, tg_o, sem.at[1])]
    for c in copies:
        c.start()
    high = RK // 16

    def take(blocks, first, count, put):
        for b in range(count // LANE):
            for r in range(high):
                put(slice(r * 16, (r + 1) * 16), slice(b * LANE, (b + 1) * LANE), blocks[first + b * high + r].astype(F32))

    def plain(dst, row=0, lane=0):
        def put(rows, lanes, value):
            dst[rows.start + row : rows.stop + row, lanes.start + lane : lanes.stop + lane] = value

        return put

    def paired(dst, n):
        def put(rows, lanes, value):
            dst[rows, n, lanes] = value

        return put

    seg = hidden // LANE * high
    take(ge, 0, hidden, paired(gbm, 0))
    take(ge, seg, hidden, paired(gbm, 1))
    take(ge, 2 * seg, hidden, plain(gad))
    take(l1, 0, qw, plain(gao))
    take(l2, 0, qw, plain(gbq))
    first = qw // LANE * high
    half = kvw // LANE * high
    take(l2, first, kvw, paired(gbkv, 0))
    take(l2, first + half, kvw, paired(gbkv, 1))
    per = quarter // LANE * high
    for t in range(t1.shape[0]):
        take(t1.at[t], 0, quarter, plain(gbo, 0, t * quarter))
        take(t1.at[t], per, quarter, plain(gam, 0, t * quarter))
        take(t1.at[t], 2 * per, quarter, plain(gam, RK, t * quarter))
        take(t2.at[t], 0, quarter, plain(gbd, 0, t * quarter))
        for n in range(3):
            take(t2.at[t], (1 + n) * per, quarter, plain(ga, n * RK, t * quarter))
    for c in copies:
        c.wait()


def emit(qw, kvw, quarter, hidden, grads, results):
    width = 4 * quarter
    outs = [
        ((RK, 2, hidden), F32), ((RK, hidden), F32), ((RK, qw), F32), ((RK, qw), F32), ((RK, 2, kvw), F32), ((RK, width), F32),
        ((2 * RK, width), F32), ((RK, width), F32), ((3 * RK, width), F32),
    ] + [(a.shape, a.dtype) for a in results]
    vm = pl.BlockSpec(memory_space=VM)
    anyspace = pl.BlockSpec(memory_space=pl.ANY)
    return pl.pallas_call(
        functools.partial(emit_kernel, qw, kvw, quarter, hidden),
        out_shape=[jax.ShapeDtypeStruct(s, dtype) for s, dtype in outs],
        in_specs=[vm] * len(grads) + [anyspace] * len(results),
        out_specs=[vm] * 9 + [anyspace] * 2,
        scratch_shapes=[pltpu.SemaphoreType.DMA((2,))],
        compiler_params=pltpu.CompilerParams(vmem_limit_bytes=61 << 20),
        cost_estimate=pl.CostEstimate(flops=0, bytes_accessed=20 << 20, transcendentals=0),
        name="emit",
    )(*grads, *results)


def rope_tables():
    position = np.concatenate([np.arange(PLEN)] + [PLEN + np.arange(CLEN)] * CONT_DEV).astype(np.float32)
    exponent = np.arange(HD // 2, dtype=np.float32) * np.float32(2.0 / HD)
    frequency = np.exp(np.float32(-math.log(ROPE_BASE)) * exponent).astype(np.float32)
    angle = position[:, None] * frequency[None, :]
    cos, sin = np.cos(angle).astype(np.float32), np.sin(angle).astype(np.float32)
    return np.tile(cos, (1, 4)), np.concatenate([-sin, sin, -sin, sin], axis=1)


def shards(
    tokens, cotangent, gain_attn, gain_mlp, w_query, w_kv, w_out, w_gate_up, w_down, a_attn, b_query, b_kv,
    a_out, b_out, a_mlp, b_mlp, a_down, b_down, prompt_adapter, cont_adapter, group_map,
):
    rows, width = tokens.shape
    qw = w_query.shape[1]
    kvw = w_kv.shape[2]
    hidden = w_down.shape[0]
    n_dp = lax.axis_size("dp")
    quarter = width // lax.axis_size("tensor")
    cos_np, sin_np = rope_tables()
    cos, sin = jnp.asarray(cos_np), jnp.asarray(sin_np)
    gain1 = gain_attn.reshape(1, width)
    gain2 = gain_mlp.reshape(1, width)
    aT = a_attn.transpose(1, 2, 3, 0).reshape(3 * RK, width)
    aoT = a_out.transpose(1, 2, 0).reshape(RK, qw)
    amT = a_mlp.transpose(1, 2, 3, 0).reshape(2 * RK, width)
    adT = a_down.transpose(1, 2, 0).reshape(RK, hidden)
    bq = b_query.reshape(RK, qw)
    bkv = b_kv.reshape(RK, 2, kvw)
    bo = b_out.reshape(RK, width)
    bm = b_mlp.reshape(RK, 2, hidden)
    bd = b_down.reshape(RK, width)
    wkv = w_kv.reshape(width, 2 * kvw)
    n1q, q, kv, u, pp, pc, o, far, h_p, h_c, n2p, n2c, dact, dud, wgu = front(
        n_dp, [prompt_adapter, cont_adapter, group_map], [gain1, gain2, bkv, bm],
        [tokens, aT, wkv, cos, sin, w_query, bq, aoT, w_out, cotangent, bd, adT, bo, w_down, w_gate_up],
    )
    dh_p, dh_c, dap, dac, sm_p, sm_c, ge = middle(
        n_dp, [prompt_adapter, cont_adapter], [gain2, amT, adT], [n2p, n2c, dact, dud, wgu, w_down, h_p, h_c, cotangent]
    )
    results = backward(
        n_dp, [prompt_adapter, cont_adapter, group_map], [gain1, bkv],
        [dac, w_out, o, aoT, bo, n2c, q, kv, far, pc, cos, sin, dap, pp, n2p, u, w_query, wkv, bq, sm_p, h_p, bd, sm_c, h_c,
         cotangent, n1q, dh_c, aT, dh_p, tokens, ge],
    )
    gbm, gad, gao, gbq, gbkv, gbo, gam, gbd, ga, output, tokens_grad = emit(qw, kvw, quarter, hidden, results[2:], results[:2])
    return (
        output,
        tokens_grad,
        ga.reshape(3, NA, R, width).transpose(3, 0, 1, 2),
        gbq.reshape(b_query.shape),
        gbkv.reshape(b_kv.shape),
        gao.reshape(NA, R, qw).transpose(2, 0, 1),
        gbo.reshape(b_out.shape),
        gam.reshape(2, NA, R, width).transpose(3, 0, 1, 2),
        gbm.reshape(b_mlp.shape),
        gad.reshape(NA, R, hidden).transpose(2, 0, 1),
        gbd.reshape(b_down.shape),
    )


def solution(mesh):
    in_specs = (
        P("dp", None), P("dp", None), P(), P(), P(None, "tensor"), P(None, None, "tensor"), P("tensor", None),
        P(None, None, "tensor"), P("tensor", None), P(), P(None, None, "tensor"), P(None, None, None, "tensor"),
        P("tensor", None, None), P(), P(), P(None, None, None, "tensor"), P("tensor", None, None), P(),
        P("dp"), P("dp"), P(),
    )
    out_specs = (
        P("dp", None), P("dp", None), P(), P(None, None, "tensor"), P(None, None, None, "tensor"),
        P("tensor", None, None), P(), P(), P(None, None, None, "tensor"), P("tensor", None, None), P(),
    )
    return jax.shard_map(shards, mesh=mesh, in_specs=in_specs, out_specs=out_specs, check_vma=False)
```

```python
import functools
import math

import jax
import jax.numpy as jnp
import numpy as np
from jax import lax
from jax.experimental import pallas as pl
from jax.experimental.pallas import tpu as pltpu
from jax.sharding import PartitionSpec as P

HD = 64
R = 16
NA = 4
RK = NA * R
PLEN = 384
CLEN = 128
CONT_DEV = 2
ROWS = PLEN + CONT_DEV * CLEN
EPSILON = 1e-05
ROPE_BASE = 500000.0
MASKED_SCORE = -1e30

BF = jnp.bfloat16
F32 = jnp.float32
VM = pltpu.VMEM
LANE = 128


def dn(a, b):
    return jnp.dot(a, b, preferred_element_type=F32)


def dt(a, b):
    return lax.dot_general(a, b, (((1,), (1,)), ((), ())), preferred_element_type=F32)


def dr(a, b):
    return lax.dot_general(a, b, (((0,), (0,)), ((), ())), preferred_element_type=F32)


def sel_row(adapter):
    lane = lax.broadcasted_iota(jnp.int32, (1, RK), 1)
    return (lax.shift_right_logical(lane, 4) == adapter).astype(F32)


def swap_halves(v):
    lane = lax.broadcasted_iota(jnp.int32, v.shape, 1)
    return jnp.where((lane & 63) < 32, pltpu.roll(v, LANE - 32, 1), pltpu.roll(v, 32, 1))


def rot(v, cos, sin):
    return v * cos + swap_halves(v) * sin


def stack_heads(ref, r0, g):
    return jnp.concatenate(
        [ref[pl.ds(r0, CLEN), (4 * g + h) * HD : (4 * g + h + 1) * HD] for h in range(4)], axis=0
    )


def softmax_low(s):
    top = jnp.max(s, axis=-1, keepdims=True)
    e = jnp.exp(s - top)
    return (e * (1.0 / jnp.sum(e, axis=-1, keepdims=True))).astype(BF)


def causal_tile():
    r = lax.broadcasted_iota(jnp.int32, (4 * CLEN, CLEN), 0) & (CLEN - 1)
    c = lax.broadcasted_iota(jnp.int32, (4 * CLEN, CLEN), 1)
    return c <= r


P_OFF = (0, 128, 384)


def norm_back(v, gain, upstream):
    inv = lax.rsqrt(jnp.mean(v * v, axis=-1, keepdims=True) + EPSILON)
    scaled = v * inv
    weighted = upstream * gain
    return inv * (weighted - scaled * jnp.mean(weighted * scaled, axis=-1, keepdims=True))


def put_dq(dq, dq_ref, r0, g):
    for h in range(4):
        dq_ref[pl.ds(r0, CLEN), (4 * g + h) * HD : (4 * g + h + 1) * HD] = dq[h * CLEN : (h + 1) * CLEN]


def back_scores(p, dp):
    pf = p.astype(F32)
    return (pf * (dp - jnp.sum(pf * dp, axis=-1, keepdims=True))).astype(BF)


MESH = pl.DeviceIdType.MESH


def rows_loop(total, step, body):
    def one(i, carry):
        body(pl.multiple_of(i * step, step))
        return carry

    lax.fori_loop(0, total // step, one, 0)


def loop(first, last, body):
    def one(i, carry):
        body(i)
        return carry

    lax.fori_loop(first, last, one, 0)


def place():
    d = lax.axis_index("dp")
    t = lax.axis_index("tensor")
    return d, t


def remote(src, dst, send, recv, device):
    return pltpu.make_async_remote_copy(
        src_ref=src, dst_ref=dst, send_sem=send, recv_sem=recv, device_id=device, device_id_type=MESH
    )


def greet(d, t, n_dp):
    barrier = pltpu.get_barrier_semaphore()
    for device in [(d, t ^ 1), (d, t ^ 2)] + [((d + k) % n_dp, t) for k in range(1, n_dp)]:
        pl.semaphore_signal(barrier, inc=1, device_id=device, device_id_type=MESH)


def greeted(n_dp):
    pl.semaphore_wait(pltpu.get_barrier_semaphore(), n_dp + 1)


class Spread:
    def __init__(self, every, sems, d, t, hi):
        self.every, self.sems, self.d, self.t, self.hi = every, sems, d, t, hi
        self.z, self.x = d // 2, d % 2

    def across(self, z):
        block = z * 2 + self.x
        up_s, up_r, down_s, down_r, x_s, x_r = self.sems
        return remote(self.every.at[block], self.every.at[block], x_s.at[z], x_r.at[z], (self.d ^ 1, self.t))

    def along(self, z, s, up):
        block = z * 2 + self.x
        up_s, up_r, down_s, down_r, x_s, x_r = self.sems
        send, recv, step = (up_s, up_r, 2) if up else (down_s, down_r, -2)
        return remote(self.every.at[block], self.every.at[block], send.at[s], recv.at[s], (self.d + step, self.t))

    def start(self):
        self.across(self.z).start()

        @pl.when(self.z < self.hi - 1)
        def _():
            self.along(self.z, 1, True).start()

        @pl.when(self.z > 0)
        def _():
            self.along(self.z, 1, False).start()

    def hop(self, s):
        if s > self.hi - 1:
            return
        for up in (True, False):
            origin = self.z - s if up else self.z + s
            held = origin >= 0 if up else origin < self.hi
            further = self.z < self.hi - 1 if up else self.z > 0

            @pl.when(held)
            def _(origin=origin, up=up, further=further):
                self.along(origin, s, up).wait_recv()
                self.across(origin).start()
                if s + 1 <= self.hi - 1:

                    @pl.when(further)
                    def _():
                        self.along(origin, s + 1, up).start()

    def finish(self):
        for z in range(self.hi):
            across = self.across(z)
            across.wait_send()
            block = z * 2 + 1 - self.x
            up_s, up_r, down_s, down_r, x_s, x_r = self.sems
            remote(self.every.at[block], self.every.at[block], x_s.at[z], x_r.at[z], (self.d ^ 1, self.t)).wait_recv()
        for s in range(1, self.hi):
            for up in (True, False):
                origin = self.z - s + 1 if up else self.z + s - 1
                held = origin >= 0 if up else origin < self.hi
                further = self.z < self.hi - 1 if up else self.z > 0

                @pl.when(held & further)
                def _(origin=origin, up=up, s=s):
                    self.along(origin, s, up).wait_send()


class TensorSum:
    def __init__(self, snd, got, mine, theirs, sems, d, t):
        self.snd, self.got, self.mine, self.theirs, self.sems, self.t = snd, got, mine, theirs, sems, t
        self.lo = t % 2
        self.core = remote(snd.at[1 - self.lo], got, sems.at[0], sems.at[1], (d, t ^ 1))
        self.chip = remote(mine, theirs, sems.at[2], sems.at[3], (d, t ^ 2))

    def begin(self):
        self.core.start()

    def middle(self):
        self.core.wait_recv()

        def add(r):
            rows = pl.ds(r, 64)
            self.mine[rows] = (self.snd[self.lo, rows].astype(F32) + self.got[rows].astype(F32)).astype(BF)

        rows_loop(self.mine.shape[0], 64, add)
        self.chip.start()

    def end(self):
        self.chip.wait_recv()

    def drain(self):
        self.core.wait_send()
        self.chip.wait_send()


UNIT = (16, LANE)


def put_units(blocks, first, value):
    for b in range(value.shape[1] // LANE):
        for r in range(RK // 16):
            blocks[first + b * (RK // 16) + r] = value[r * 16 : (r + 1) * 16, b * LANE : (b + 1) * LANE]


class DirectReduce:
    def __init__(self, src, got, out, sems, d, t, n_dp):
        self.src, self.got, self.out, self.sems, self.d, self.t, self.n = src, got, out, sems, d, t, n_dp
        self.share = src.shape[0] // n_dp if src is not None else out.shape[0] // n_dp

    def part(self, d):
        return pl.ds(((d % 2) * (self.n // 2) + d // 2) * self.share, self.share)

    def to(self, k):
        peer = (self.d + k) % self.n
        return remote(self.src.at[self.part(peer)], self.got.at[k], self.sems[0].at[k], self.sems[1].at[k], (peer, self.t))

    def back(self, k):
        peer = (self.d + k) % self.n
        here = self.part(self.d)
        return remote(self.out.at[here], self.out.at[here], self.sems[2].at[k], self.sems[3].at[k], (peer, self.t))

    def from_back(self, k):
        peer = (self.d + self.n - k) % self.n
        there = self.part(peer)
        return remote(self.out.at[there], self.out.at[there], self.sems[2].at[k], self.sems[3].at[k], (peer, self.t))

    def start(self):
        for k in range(1, self.n):
            self.to(k).start()

    def add(self):
        for k in range(1, self.n):
            self.to(k).wait_recv()
        here = self.part(self.d)
        total = self.src[here].astype(F32)
        for k in range(1, self.n):
            total = total + self.got[k].astype(F32)
        self.out[here] = total.astype(BF)

    def sent(self):
        for k in range(1, self.n):
            self.to(k).wait_send()

    def spread(self):
        for k in range(1, self.n):
            self.back(k).start()

    def finish(self):
        for k in range(1, self.n):
            self.from_back(k).wait_recv()

    def spread_sent(self):
        for k in range(1, self.n):
            self.back(k).wait_send()


class PairReduce:
    def __init__(self, src, gx, gz, out, sems, d, t, n_dp):
        self.src, self.gx, self.gz, self.out, self.sems, self.t = src, gx, gz, out, sems, t
        self.hi, self.z, self.x = n_dp // 2, d // 2, d % 2
        self.share = out.shape[0] // n_dp
        self.mate = (d ^ 1, t)

    def part(self, z):
        return pl.ds((self.x * self.hi + z) * self.share, self.share)

    def half(self, x):
        return pl.ds(x * self.hi * self.share, self.hi * self.share)

    def on_line(self, k):
        z = (self.z + k) % self.hi
        return z, (z * 2 + self.x, self.t)

    def over(self):
        return remote(self.src.at[self.half(1 - self.x)], self.gx, self.sems[0].at[0], self.sems[1].at[0], self.mate)

    def to(self, k):
        z, device = self.on_line(k)
        return remote(self.src.at[self.part(z)], self.gz.at[k], self.sems[2].at[k], self.sems[3].at[k], device)

    def back(self, k, come=False):
        z, device = self.on_line(self.hi - k if come else k)
        here = self.part(z if come else self.z)
        return remote(self.out.at[here], self.out.at[here], self.sems[4].at[k], self.sems[5].at[k], device)

    def over_back(self, x):
        here = self.half(x)
        return remote(self.out.at[here], self.out.at[here], self.sems[6].at[0], self.sems[7].at[0], self.mate)

    def start(self):
        self.over().start()

    def middle(self):
        self.over().wait_recv()
        here = self.half(self.x)
        self.src[here] = (self.src[here].astype(F32) + self.gx[...].astype(F32)).astype(BF)
        for k in range(1, self.hi):
            self.to(k).start()

    def add(self):
        here = self.part(self.z)
        total = self.src[here].astype(F32)
        for k in range(1, self.hi):
            self.to(k).wait_recv()
            total = total + self.gz[k].astype(F32)
        self.out[here] = total.astype(BF)
        self.spread()

    def spread(self):
        for k in range(1, self.hi):
            self.back(k).start()

    def cross(self):
        for k in range(1, self.hi):
            self.back(k, True).wait_recv()
        self.over_back(self.x).start()

    def finish(self):
        self.over_back(1 - self.x).wait_recv()

    def spread_sent(self):
        for k in range(1, self.hi):
            self.back(k).wait_send()
        self.over_back(self.x).wait_send()

    def sent(self):
        self.over().wait_send()
        for k in range(1, self.hi):
            self.to(k).wait_send()


class Trade:
    def __init__(self, halves, sems, d, t):
        self.halves, self.sems, self.d, self.t = halves, sems, d, t

    def slot(self, n):
        return remote(self.halves.at[n], self.halves.at[n], self.sems.at[0], self.sems.at[1], (self.d, self.t ^ 1))

    def start(self):
        self.slot(self.t % 2).start()

    def finish(self):
        self.slot(1 - self.t % 2).wait_recv()

    def sent(self):
        self.slot(self.t % 2).wait_send()


def evens_first(n):
    r = lax.broadcasted_iota(jnp.int32, (n, n), 0)
    c = lax.broadcasted_iota(jnp.int32, (n, n), 1)
    return (c == jnp.where(r < n // 2, 2 * r, 2 * (r - n // 2) + 1)).astype(BF)


def all_sel(sc):
    return jnp.concatenate(
        [
            jnp.broadcast_to(sel_row(sc[0]), (PLEN, RK)),
            jnp.broadcast_to(sel_row(sc[1]), (CLEN, RK)),
            jnp.broadcast_to(sel_row(sc[2]), (CLEN, RK)),
        ],
        axis=0,
    )


def first_kernel(
    n_dp, ids_p, ids_c, group_map, gain1, gain2, bkv_ref, bm_h, amT_h, adT_h, bo_h,
    tok_h, aT_h, wkv_h, cos_h, sin_h, wq_h, bq_h, aoT_h, wo_h, dy_h, bd_h, wd_h, raw_h,
    n1q_h, q_h, kv_h, u_h, pp_h, pc_h, o_h, far_h, hp_h, hc_h, n2p_h, n2c_h, uop_h, uoc_h, wgu_h,
    dhp_h, dhc_h, dap_h, dac_h, smp_h, smc_h, ge_h,
    every, snd_p, s_p, snd_c, s_c, got0_p, t0_p, got0_c, t0_c, got1_p, t1_p, got1_c, t1_c,
    n2p, n2c, uop, uoc, hp, hc, xp, xc, dyp, dyc, dact, dud, tmp, ge, gots, gsum, bm, amT, adT, bo,
    lsem, osem, wsem, rsem, fsem, vsem, psem, csem, psem2, csem2, msem, nsem, up_s, up_r, down_s, down_r, x_s, x_r, g0, g1,
):
    d, t = place()
    sc = [ids_p[0], ids_c[0], ids_c[1], group_map[d * CONT_DEV], group_map[d * CONT_DEV + 1]]
    lo = t % 2
    hi = n_dp // 2
    rows, width = tok_h.shape
    wide = n2p.shape[2]
    qw = wq_h.shape[1]
    kvw = wkv_h.shape[1] // 2
    hidden = wd_h.shape[0]
    ht = 512
    steps = hidden // ht
    hpn, hcn = PLEN // 2, CLEN
    part = n1q_h.shape[1]
    qlanes = pl.ds(pl.multiple_of(lo * part, part), part)
    adapter_c = jnp.where(lo == 0, sc[1], sc[2])
    greet(d, t, n_dp)
    counts = [0, 0]

    def load(src, dst):
        c = pltpu.make_async_copy(src, dst, lsem.at[counts[0]])
        counts[0] += 1
        c.start()
        return c

    def store(src, dst):
        c = pltpu.make_async_copy(src, dst, osem.at[counts[1]])
        counts[1] += 1
        c.start()
        return c

    spread = Spread(every, (up_s, up_r, down_s, down_r, x_s, x_r), d, t, hi)
    sum_p = TensorSum(snd_p, got0_p, s_p, t0_p, psem, d, t)
    sum_c = TensorSum(snd_c, got0_c, s_c, t0_c, csem, d, t)
    sel = all_sel(sc)
    b2 = 2 * RK

    def attention(tok, n1, aT, wkv, cos, sin, wq, bq, aoT, wo, bd, wdc, raw, flat, bflat, kv, q, u, far, pp, pc, o):
        kt = raw.shape[1]
        raw_steps = width // kt

        def raw_copy(i, slot):
            return pltpu.make_async_copy(raw_h.at[pl.ds(i * kt, kt)], raw.at[slot], rsem.at[slot])

        def flat_copies(i, slot):
            here = pl.ds(i * kt, kt)
            return (
                pltpu.make_async_copy(flat.at[slot, 0], wgu_h.at[here, :hidden], fsem.at[slot, 0]),
                pltpu.make_async_copy(flat.at[slot, 1], wgu_h.at[here, hidden:], fsem.at[slot, 1]),
            )

        def wd_copy(i, slot):
            return pltpu.make_async_copy(wd_h.at[pl.ds(i * ht, ht)], wdc.at[slot, :, :width], wsem.at[slot, 0])

        load_tok = load(tok_h, tok.at[:, :width])
        load_kv = [load(a, b) for a, b in ((aT_h, aT), (wkv_h, wkv), (cos_h, cos), (sin_h, sin))]
        load_q = [load(a, b) for a, b in ((wq_h, wq), (bq_h, bq))]
        stores = []

        bkv = dn(evens_first(b2), bkv_ref[...].reshape(b2, kvw)).astype(BF)
        gain_row = gain1[...].astype(F32).reshape(1, width)
        load_tok.wait()

        def norm1(r):
            x = tok[pl.ds(r, 128), :width].astype(F32)
            inv = lax.rsqrt(jnp.mean(x * x, axis=-1, keepdims=True) + EPSILON)
            n1[pl.ds(r, 128)] = (x * inv * gain_row).astype(BF)

        rows_loop(rows, 128, norm1)
        load_o = [load(a, b) for a, b in ((aoT_h, aoT), (wo_h, wo))]
        load_dy = [load(a, b) for a, b in ((dy_h, tok.at[:, :width]), (bd_h, bd), (adT_h, adT))]
        for i in range(2):
            wd_copy(i, i).start()
        for i in range(raw.shape[0]):
            raw_copy(i, i).start()
        load_bm = load(bm_h, bm)
        load_x = [
            load(tok_h.at[pl.ds(pl.multiple_of(lo * hpn, hpn), hpn)], xp),
            load(tok_h.at[pl.ds(pl.multiple_of(PLEN + lo * hcn, hcn), hcn)], xc),
            load(amT_h, amT),
            load(bo_h, bo),
        ]
        for c in load_kv:
            c.wait()
        uf = dt(n1[...], aT[...])
        for part in range(3):
            u[:, part * RK : (part + 1) * RK] = (uf[:, part * RK : (part + 1) * RK] * sel).astype(BF)
        kvf = dn(n1[...], wkv[...])
        kv[:, :kvw] = rot(kvf[:, :kvw] + dn(u[:, RK : 2 * RK], bkv[:RK]), cos[...], sin[...]).astype(BF)
        kv[:, kvw:] = (kvf[:, kvw:] + dn(u[:, 2 * RK :], bkv[RK:])).astype(BF)
        every[d] = kv[:PLEN]
        greeted(n_dp)
        spread.start()

        for c in load_q:
            c.wait()
        qf = dn(n1[...], wq[...]) + dn(u[:, :RK], bq[...])
        for c in range(qw // LANE):
            lanes = slice(c * LANE, (c + 1) * LANE)
            q[:, lanes] = rot(qf[:, lanes], cos[...], sin[...]).astype(BF) * BF(0.125)
        stores.append(store(n1.at[:, qlanes], n1q_h))
        stores.append(store(q, q_h))
        stores.append(store(kv, kv_h))
        stores.append(store(u, u_h))

        def keep_o(of, r0, g):
            for h in range(4):
                o[pl.ds(r0, CLEN), (4 * g + h) * HD : (4 * g + h + 1) * HD] = of[h * CLEN : (h + 1) * CLEN]

        mask = causal_tile()
        for g in range(2):
            kg = kv[:PLEN, g * HD : (g + 1) * HD]
            vg = kv[:PLEN, kvw + g * HD : kvw + (g + 1) * HD]
            for i in range(PLEN // CLEN):
                size = (i + 1) * CLEN
                s = dt(stack_heads(q, i * CLEN, g), kg[:size])
                tail = jnp.where(mask, s[:, size - CLEN :], MASKED_SCORE)
                s = tail if i == 0 else jnp.concatenate([s[:, : size - CLEN], tail], axis=1)
                p = softmax_low(s)
                pp[g, :, P_OFF[i] : P_OFF[i] + size] = p
                keep_o(dn(p, vg[:size]).astype(BF), i * CLEN, g)
        stores.append(store(pp, pp_h))
        spread.hop(1)

        def project(r0, half, snd):
            ov = o[r0 : r0 + 2 * half]

            def columns(n):
                lanes = pl.ds(pl.multiple_of(n * 512, 512), 512)
                part = dn(ov, wo[:, lanes]).astype(BF)
                snd[0, :, lanes] = part[:half]
                snd[1, :, lanes] = part[half:]

            loop(0, width // 512, columns)
            uo = dt(ov, aoT[...]).astype(BF)
            pad = jnp.zeros((half, LANE - RK), BF)
            snd[0, :, width:] = jnp.concatenate([uo[:half], pad], axis=1)
            snd[1, :, width:] = jnp.concatenate([uo[half:], pad], axis=1)

        for c in load_o:
            c.wait()
        project(0, hpn, snd_p)
        sum_p.begin()

        for c in load_dy:
            c.wait()
        dudv = (dt(tok[:, :width], bd[...]) * sel).astype(BF)
        dud[...] = jnp.concatenate([dudv, jnp.zeros((rows, LANE - RK), BF)], axis=1)
        tok[:, width:] = dud[...]
        eye = (lax.broadcasted_iota(jnp.int32, (RK, RK), 0) == lax.broadcasted_iota(jnp.int32, (RK, RK), 1)).astype(BF)
        split = evens_first(256)

        slots, flats = raw.shape[0], flat.shape[0]

        def part_weights(i):
            slot = i % slots
            raw_copy(i, slot).wait()

            put = i % flats

            @pl.when(i >= flats)
            def _():
                for c in flat_copies(i - flats, put):
                    c.wait()

            apart = dn(split, raw[slot].reshape(2 * kt, hidden)).astype(BF)
            flat[put, 0] = apart[:kt]
            flat[put, 1] = apart[kt:]
            for c in flat_copies(i, put):
                c.start()

            @pl.when(i + slots < raw_steps)
            def _():
                raw_copy(i + slots, slot).start()

        def act_grad(i):
            slot = i % 2
            wd_copy(i, slot).wait()
            lanes = pl.ds(pl.multiple_of(i * ht, ht), ht)
            ad = dr(adT[:, lanes], eye).astype(BF)
            wdc[slot, :, width:] = jnp.concatenate([ad, jnp.zeros((ht, LANE - RK), BF)], axis=1)
            dact[:, lanes] = dt(tok[...], wdc[slot]).astype(BF)

            @pl.when(i + 2 < steps)
            def _():
                wd_copy(i + 2, slot).start()

        def both(i):
            act_grad(i)

            @pl.when(i == 0)
            def _():
                spread.hop(2)

            @pl.when(i == 1)
            def _():
                spread.hop(3)

            per = raw_steps // steps
            loop(i * per, (i + 1) * per, part_weights)

        sum_p.middle()
        loop(0, steps, both)
        load_bm.wait()
        bsplit = dn(evens_first(b2), bm[...].reshape(b2, hidden)).astype(BF)
        zero = jnp.zeros((RK, hidden), BF)
        bflat[:RK, :hidden] = bsplit[:RK]
        bflat[:RK, hidden:] = zero
        bflat[RK:, :hidden] = zero
        bflat[RK:, hidden:] = bsplit[RK:]
        stores.append(store(bflat, wgu_h.at[pl.ds(width, b2)]))
        for s in range(4, hi):
            spread.hop(s)
        spread.finish()

        far[0] = every[sc[3]]
        far[1] = every[sc[4]]
        stores.append(store(far, far_h))

        def attend(j):
            r0 = pl.multiple_of(PLEN + j * CLEN, CLEN)
            own = pl.ds(r0, CLEN)
            for g in range(2):
                lanes = slice(g * HD, (g + 1) * HD)
                vlanes = slice(kvw + g * HD, kvw + (g + 1) * HD)
                qs = stack_heads(q, r0, g)
                sf = dt(qs, far[j, :, lanes])
                so = jnp.where(mask, dt(qs, kv[own, lanes]), MASKED_SCORE)
                p = softmax_low(jnp.concatenate([sf, so], axis=1))
                pc[2 * j + g] = p
                keep_o((dn(p[:, :PLEN], far[j, :, vlanes]) + dn(p[:, PLEN:], kv[own, vlanes])).astype(BF), r0, g)

        loop(0, CONT_DEV, attend)
        stores.append(store(pc, pc_h))
        stores.append(store(o, o_h))
        project(PLEN, hcn, snd_c)
        sum_c.begin()
        for c in load_x:
            c.wait()
        for i in range(raw_steps - flats, raw_steps):
            for c in flat_copies(i, i % flats):
                c.wait()
        for c in stores:
            c.wait()

    pl.run_scoped(
        attention,
        VM((rows, wide), BF), VM((rows, width), BF), VM(aT_h.shape, BF), VM(wkv_h.shape, BF), VM(cos_h.shape, F32),
        VM(sin_h.shape, F32), VM(wq_h.shape, BF), VM(bq_h.shape, BF), VM(aoT_h.shape, BF), VM(wo_h.shape, BF), VM(bd_h.shape, BF),
        VM((2, ht, wide), BF), VM((3, 128, 2, hidden), BF), VM((3, 2, 128, hidden), BF), VM((b2, 2 * hidden), BF),
        VM((rows, 2 * kvw), BF), VM((rows, qw), BF), VM((rows, 3 * RK), BF), VM((CONT_DEV, PLEN, 2 * kvw), BF),
        VM((2, 4 * CLEN, 768), BF), VM((4, 4 * CLEN, 4 * CLEN), BF), VM((rows, qw), BF),
    )

    def feed_forward(wcat, wdn, acc, gu, dga, act, gg):
        nt = wdn.shape[2]

        def weights(k, slot):
            i = k % steps
            here = pl.ds(pl.multiple_of(i * ht, ht), ht)
            there = pl.ds(pl.multiple_of(hidden + i * ht, ht), ht)
            return [
                pltpu.make_async_copy(src, dst, wsem.at[slot, n])
                for n, (src, dst) in enumerate(
                    [(wgu_h.at[:, here], wcat.at[slot, :, :ht]), (wgu_h.at[:, there], wcat.at[slot, :, ht:])]
                )
            ]

        def down(n, slot):
            return pltpu.make_async_copy(wd_h.at[:, pl.ds(n * nt, nt)], wdn.at[slot], vsem.at[slot])

        for c in weights(0, 0):
            c.start()
        load_dy = [
            load(dy_h.at[pl.ds(pl.multiple_of(lo * hpn, hpn), hpn)], dyp),
            load(dy_h.at[pl.ds(pl.multiple_of(PLEN + lo * hcn, hcn), hcn)], dyc),
        ]
        for n in range(2):
            down(n, n).start()
        sum_c.middle()

        def norm2(which, total, x, h, n2, adapter):
            half = h.shape[0]
            total.end()
            sr = sel_row(adapter)
            uo = (total.mine[:, width : width + RK].astype(F32) + total.theirs[:, width : width + RK].astype(F32)) * sr
            uo = uo.astype(BF)
            tmp[:half] = dn(uo, bo[...])
            gain_two = gain2[...].astype(F32).reshape(1, width)

            def one(r):
                here = pl.ds(r, 64)
                hv = (
                    x[here].astype(F32)
                    + (total.mine[here, :width].astype(F32) + total.theirs[here, :width].astype(F32))
                    + tmp[here]
                )
                h[here] = hv
                inv = lax.rsqrt(jnp.mean(hv * hv, axis=-1, keepdims=True) + EPSILON)
                n2[lo, here, :width] = (hv * inv * gain_two).astype(BF)

            rows_loop(half, 64, one)
            n2[lo, :, width:] = jnp.concatenate([uo, jnp.zeros((half, LANE - RK), BF)], axis=1)
            c = remote(n2.at[lo], n2.at[lo], nsem.at[which, 0], nsem.at[which, 1], (d, t ^ 1))
            c.start()
            return c

        def arrived(which, n2):
            remote(n2.at[1 - lo], n2.at[1 - lo], nsem.at[which, 0], nsem.at[which, 1], (d, t ^ 1)).wait_recv()

        def begin(n2, uo, chosen):
            half = n2.shape[1]
            r = 2 * half
            um = dt(n2[:, :, :width].reshape(r, width), amT[...])
            um = jnp.concatenate([(um[:, :RK] * chosen).astype(BF), (um[:, RK:] * chosen).astype(BF)], axis=1)
            uo[...] = n2[:, :, width:]
            n2[:, :, width:] = um.reshape(2, half, 2 * RK)
            acc[:r] = jnp.zeros((r, wide), F32)

        def tile(k, n2, base, add):
            r = 2 * n2.shape[1]
            slot = k % 2
            i = k % steps
            for c in weights(k, slot):
                c.wait()

            @pl.when(k + 1 < 2 * steps)
            def _():
                for c in weights(k + 1, 1 - slot):
                    c.start()

            gu[:r] = dn(n2[...].reshape(r, wide), wcat[slot])
            lanes = pl.ds(pl.multiple_of(i * ht, ht), ht)

            def swiglu(r0):
                here = pl.ds(r0, 64)
                gate = gu[here, :ht]
                upper = gu[here, ht:]
                sigma = 1.0 / (1.0 + jnp.exp(-gate))
                silu = gate * sigma
                there = pl.ds(base + r0, 64)
                da = dact[there, lanes].astype(F32)
                dga[here, :ht] = (da * upper * (sigma * (1.0 + gate * (1.0 - sigma)))).astype(BF)
                dga[here, ht : 2 * ht] = (da * silu).astype(BF)
                av = (silu * upper).astype(BF)
                dga[here, 2 * ht :] = av
                act[there, lanes] = av

            for r0 in range(0, r, 64):
                swiglu(r0)
            acc[:r] += dt(dga[:r, : 2 * ht], wcat[slot])
            small = jnp.concatenate([n2[:, :, width:].reshape(r, 2 * RK), dud[base : base + r, :RK]], axis=1)
            g = dr(small, dga[:r])
            for n in range(3):
                part = g[n * RK : (n + 1) * RK, n * ht : (n + 1) * ht]
                if add:
                    total = (gg[n, :, lanes] + part).astype(BF)
                    units = ht // LANE * (RK // 16)
                    put_units(ge, n * (hidden // LANE * (RK // 16)) + i * units, total)
                else:
                    gg[n, :, lanes] = part

        def halves(a, snd):
            half = snd.shape[1]

            def one(r0):
                for n in range(2):
                    snd[n, pl.ds(r0, 64)] = a[pl.ds(pl.multiple_of(n * half + r0, 64), 64)].astype(BF)

            rows_loop(half, 64, one)

        n2_copy_p = norm2(0, sum_p, xp, hp, n2p, sc[0])
        store_hp = store(hp, hp_h)
        arrived(0, n2p)
        n2_copy_p.wait_send()
        store_n2p = store(n2p.at[:, :, qlanes], n2p_h)
        begin(n2p, uop, sel_row(sc[0]))
        tail_stores = [store(uop, uop_h)]

        def tile_p(k):
            tile(k, n2p, 0, False)

            @pl.when(k == steps // 2 - 1)
            def _():
                norm2(1, sum_c, xc, hc, n2c, adapter_c)

        loop(0, steps, tile_p)
        store_hc = store(hc, hc_h)
        n2_copy_c = remote(n2c.at[lo], n2c.at[lo], nsem.at[1, 0], nsem.at[1, 1], (d, t ^ 1))
        sum_p.drain()
        halves(acc, snd_p)
        store_n2p.wait()
        sum2_p = TensorSum(snd_p, got1_p, s_p, t1_p, psem2, d, t)
        sum2_p.begin()

        arrived(1, n2c)
        n2_copy_c.wait_send()
        store_n2c = store(n2c.at[:, :, qlanes], n2c_h)
        begin(
            n2c, uoc,
            jnp.concatenate([jnp.broadcast_to(sel_row(sc[1]), (hcn, RK)), jnp.broadcast_to(sel_row(sc[2]), (hcn, RK))], axis=0),
        )
        tail_stores.append(store(uoc, uoc_h))
        sum2_p.middle()

        loop(steps, 2 * steps, lambda k: tile(k, n2c, PLEN, True))
        sum_c.drain()
        halves(acc, snd_c)
        store_n2c.wait()
        sum2_c = TensorSum(snd_c, got1_c, s_c, t1_c, csem2, d, t)
        sum2_c.begin()
        reduce = DirectReduce(ge, gots, gsum, (g0, g1, None, None), d, t, n_dp)
        reduce.start()

        ud = dt(act[...], adT[...]).astype(BF)
        sum2_c.middle()
        sum2_p.core.wait_send()
        sum2_c.core.wait_send()
        pad = jnp.zeros((hpn, LANE - RK), BF)
        for n in range(2):
            snd_p[n, :, width:] = jnp.concatenate([ud[n * hpn : (n + 1) * hpn], pad], axis=1)
            snd_c[n, :, width:] = jnp.concatenate([ud[PLEN + n * hcn : PLEN + (n + 1) * hcn], pad[:hcn]], axis=1)

        def project_down(n):
            slot = n % 2
            down(n, slot).wait()
            part = dn(act[...], wdn[slot]).astype(BF)
            lanes = pl.ds(pl.multiple_of(n * nt, nt), nt)
            for i in range(2):
                snd_p[i, :, lanes] = part[i * hpn : (i + 1) * hpn]
                snd_c[i, :, lanes] = part[PLEN + i * hcn : PLEN + (i + 1) * hcn]

            @pl.when(n + 2 < width // nt)
            def _():
                down(n + 2, slot).start()

        loop(0, width // nt, project_down)
        mcore_p = remote(snd_p.at[1 - lo], got0_p, msem.at[0], msem.at[1], (d, t ^ 1))
        mcore_p.start()
        mcore_c = remote(snd_c.at[1 - lo], got0_c, msem.at[2], msem.at[3], (d, t ^ 1))
        mcore_c.start()

        def mlp_sum(core, snd, got, out):
            core.wait_recv()

            def add(r0):
                here = pl.ds(r0, 64)
                got[here] = (snd[lo, here].astype(F32) + got[here].astype(F32)).astype(BF)

            rows_loop(got.shape[0], 64, add)
            tail_stores.append(store(got, out))

        def back(which, total, h, dy, da, adapter):
            half = h.shape[0]
            total.end()
            sr = sel_row(adapter)
            du = total.mine[:, width:].astype(F32) + total.theirs[:, width:].astype(F32)
            dum = (du * jnp.concatenate([sr, sr], axis=1)).astype(BF)
            tmp[:half] = dn(dum, amT[...])
            gain = gain2[...].astype(F32).reshape(1, width)

            def one(r0):
                here = pl.ds(r0, 64)
                dn2 = total.mine[here, :width].astype(F32) + total.theirs[here, :width].astype(F32) + tmp[here]
                dh = dy[here].astype(F32) + norm_back(h[here], gain, dn2)
                h[here] = dh
                da[lo, here, :width] = dh.astype(BF)

            rows_loop(half, 64, one)
            da[lo, :, width:] = dum
            c = remote(da.at[lo], da.at[lo], nsem.at[which, 0], nsem.at[which, 1], (d, t ^ 1))
            c.start()
            return c

        for c in load_dy:
            c.wait()
        store_hp.wait()
        store_hc.wait()
        copy_p = back(2, sum2_p, hp, dyp, n2p, sc[0])
        tail_stores.append(store(hp, dhp_h))
        mlp_sum(mcore_p, snd_p, got0_p, smp_h)
        mlp_sum(mcore_c, snd_c, got0_c, smc_h)
        arrived(2, n2p)
        tail_stores.append(store(n2p, dap_h))
        reduce.add()
        tail_stores.append(store(gsum.at[reduce.part(d)], ge_h))
        copy_c = back(3, sum2_c, hc, dyc, n2c, adapter_c)
        tail_stores.append(store(hc, dhc_h))
        arrived(3, n2c)
        tail_stores.append(store(n2c, dac_h))
        copy_p.wait_send()
        copy_c.wait_send()
        sum2_p.chip.wait_send()
        sum2_c.chip.wait_send()
        mcore_p.wait_send()
        mcore_c.wait_send()
        reduce.sent()
        for c in tail_stores:
            c.wait()

    pl.run_scoped(
        feed_forward,
        VM((2, wide, 2 * ht), BF), VM((2, hidden, 512), BF), VM((PLEN, wide), F32), VM((PLEN, 2 * ht), F32), VM((PLEN, 3 * ht), BF),
        VM((rows, hidden), BF), VM((3, RK, hidden), F32),
    )


def first(n_dp, scalars, small, large):
    tok, aT, wkv, cos, sin, wq, bq, aoT, wo, dy, bd, wd, raw = large
    rows, width = tok.shape
    qw = wq.shape[1]
    kvw2 = wkv.shape[1]
    hidden = wd.shape[0]
    quarter = width // 2
    wide = width + LANE
    hpn, hcn = PLEN // 2, CLEN
    units = 3 * hidden // LANE * (RK // 16)
    share = units // n_dp
    outs = [
        ((rows, quarter), BF), ((rows, qw), BF), ((rows, kvw2), BF), ((rows, 3 * RK), BF), ((2, 4 * CLEN, 768), BF),
        ((4, 4 * CLEN, 4 * CLEN), BF), ((rows, qw), BF), ((CONT_DEV, PLEN, kvw2), BF), ((hpn, width), F32),
        ((hcn, width), F32), ((2, hpn, quarter), BF), ((2, hcn, quarter), BF), ((2, hpn, LANE), BF), ((2, hcn, LANE), BF),
        ((width + 2 * RK, 2 * hidden), BF),
        ((hpn, width), F32), ((hcn, width), F32), ((2, hpn, wide), BF), ((2, hcn, wide), BF), ((hpn, wide), BF),
        ((hcn, wide), BF), ((share, *UNIT), BF),
    ]
    dma = pltpu.SemaphoreType.DMA
    scratch = [
        VM((n_dp, PLEN, kvw2), BF), VM((2, hpn, wide), BF), VM((hpn, wide), BF), VM((2, hcn, wide), BF), VM((hcn, wide), BF),
    ] + [VM((hpn, wide), BF), VM((hpn, wide), BF), VM((hcn, wide), BF), VM((hcn, wide), BF)] * 2 + [
        VM((2, hpn, wide), BF), VM((2, hcn, wide), BF), VM((2, hpn, LANE), BF), VM((2, hcn, LANE), BF),
        VM((hpn, width), F32), VM((hcn, width), F32), VM((hpn, width), BF), VM((hcn, width), BF), VM((hpn, width), BF),
        VM((hcn, width), BF), VM((rows, hidden), BF), VM((rows, LANE), BF), VM((hpn, width), F32),
        VM((units, *UNIT), BF), VM((n_dp, share, *UNIT), BF), VM((units, *UNIT), BF),
        VM((RK, 2, hidden), BF), VM((2 * RK, width), BF), VM((RK, hidden), BF), VM((RK, width), BF),
        dma((20,)), dma((22,)), dma((2, 2)), dma((4,)), dma((4, 2)), dma((2,)), dma((4,)), dma((4,)), dma((4,)), dma((4,)),
        dma((4,)), dma((4, 2)),
    ] + [dma((n_dp // 2 + 1,))] * 6 + [dma((n_dp,))] * 2
    vm = pl.BlockSpec(memory_space=VM)
    anyspace = pl.BlockSpec(memory_space=pl.ANY)
    return pl.pallas_call(
        functools.partial(first_kernel, n_dp),
        out_shape=[jax.ShapeDtypeStruct(s, dtype) for s, dtype in outs],
        in_specs=[pl.BlockSpec(memory_space=pltpu.SMEM)] * 3 + [vm] * 3 + [anyspace] * (len(small) - 3 + len(large)),
        out_specs=[anyspace] * len(outs),
        scratch_shapes=scratch,
        compiler_params=pltpu.CompilerParams(vmem_limit_bytes=63 << 20, collective_id=1, has_side_effects=True),
        cost_estimate=pl.CostEstimate(flops=12 * rows * width * hidden, bytes_accessed=120 << 20, transcendentals=0),
        name="first",
    )(*scalars, *small, *large)


class Fold:
    def __init__(self, dfar, xr, zs, zr, sems, owners, others, d, t, hi):
        self.dfar, self.xr, self.zs, self.zr, self.sems = dfar, xr, zs, zr, sems
        self.owners, self.others, self.d, self.t, self.hi = owners, others, d, t, hi
        self.z, self.x = d // 2, d % 2

    def across(self, j):
        return remote(self.dfar.at[j], self.xr.at[j], self.sems[0].at[j], self.sems[1].at[j], (self.d ^ 1, self.t))

    def along(self, z, come=False):
        slot = z if come else self.z
        return remote(
            self.zr.at[slot] if come else self.zs.at[z], self.zr.at[slot], self.sems[2].at[z], self.sems[3].at[slot],
            (z * 2 + self.x, self.t),
        )

    def held(self, z, rows):
        dest = z * 2 + self.x
        total = None
        for parts, owners in ((self.dfar, self.owners), (self.xr, self.others)):
            for j in range(CONT_DEV):
                term = parts[j, rows].astype(F32) * (owners[j] == dest).astype(F32)
                total = term if total is None else total + term
        return total

    def fold(self):
        for j in range(CONT_DEV):
            self.across(j).wait_recv()
        order = sorted(range(self.hi), key=lambda z: min(z, self.hi - 1 - z))
        for z in order:

            @pl.when(self.z != z)
            def _(z=z):
                def put(r):
                    rows = pl.ds(r, 64)
                    self.zs[z, rows] = self.held(z, rows).astype(BF)

                rows_loop(PLEN, 64, put)
                self.along(z).start()

    def finish(self, total):
        def own(r):
            rows = pl.ds(r, 64)
            total[rows] += self.held(self.z, rows)

        rows_loop(PLEN, 64, own)
        for z in range(self.hi):

            @pl.when(self.z != z)
            def _(z=z):
                self.along(z, True).wait_recv()
                total[...] += self.zr[z].astype(F32)

    def drain(self):
        for j in range(CONT_DEV):
            self.across(j).wait_send()
        for z in range(self.hi):

            @pl.when(self.z != z)
            def _(z=z):
                self.along(z).wait_send()


def back_kernel(
    n_dp, ids_p, ids_c, group_map, gain1, bkv_ref,
    dac_h, wo_h, o_h, aoT_h, bo_h, n2c_h, uoc_h, q_h, kv_h, far_h, pc_h, cos_h, sin_h, dap_h, pp_h, n2p_h, uop_h, u_h, wq_h, wkv_h, bq_h,
    smp_h, hp_h, bd_h, smc_h, hc_h, dy_h, n1q_h, dhc_h, aT_h, dhp_h, tok_h, ge_h,
    out_h, tg_h, gef_h, l0_h, t1_h, t2_h,
    dac, wo, o, aoT, bo, n2c, uoc, q, kv, far, pc, cos, sin, dap, pp, n2p, uop, u, wq, wkv, bq,
    smp, hp, bd, smc, hc, aT, xc, xp, gef, tmp_p, tmp_c,
    do, dqp, dkv, dkvp, dfar, gacc, snd_p, got_p, s_p, t_p, snd_c, got_c, s_c, t_c,
    dsnd_p, dgot_p, ds_p, dt_p, dsnd_c, dgot_c, ds_c, dt_c, dup, duc, outp, outc, tgp, tgc, tmp,
    l0s, l0x, l0z, l0, l1s, l1x, l1z, l2s, l2x, l2z, t1, t2, xr, zs, zr,
    lsem, osem, dsem, ysem, psem, csem, dpsem, dcsem, nsem, q1, q2, f0, f1, f2, f3, *rsems,
):
    d, t = place()
    sc = [ids_p[0], ids_c[0], ids_c[1], group_map[d * CONT_DEV], group_map[d * CONT_DEV + 1]]
    lo = t % 2
    hi = n_dp // 2
    width = wq.shape[0]
    qw = wq.shape[1]
    kvw = wkv.shape[1] // 2
    quarter = n1q_h.shape[1]
    hpn, hcn = PLEN // 2, CLEN
    greet(d, t, n_dp)
    qlanes = pl.ds(pl.multiple_of(lo * quarter, quarter), quarter)
    every = PairReduce(None, None, None, gef, rsems[0:8], d, t, n_dp)
    pairs = [
        (ge_h, gef.at[every.part(d // 2)]), (dac_h, dac), (wo_h, wo), (o_h, o), (aoT_h, aoT), (bo_h, bo), (n2c_h, n2c),
        (uoc_h, uoc), (q_h, q), (kv_h, kv), (far_h, far), (pc_h, pc), (cos_h, cos), (sin_h, sin), (dap_h, dap),
        (pp_h, pp), (n2p_h, n2p), (uop_h, uop), (u_h, u), (wq_h, wq), (wkv_h, wkv), (bq_h, bq),
        (smp_h, smp), (hp_h, hp), (bd_h, bd), (smc_h, smc), (hc_h, hc),
        (aT_h, aT), (tok_h.at[pl.ds(pl.multiple_of(PLEN + lo * hcn, hcn), hcn)], xc),
        (tok_h.at[pl.ds(pl.multiple_of(lo * hpn, hpn), hpn)], xp),
    ]
    loads = {}

    def fetch(first, last):
        for n in range(first, last):
            src, dst = pairs[n]
            c = pltpu.make_async_copy(src, dst, lsem.at[n])
            c.start()
            loads[id(dst) if n else 0] = c

    fetch(0, 14)

    def need(*refs):
        for ref in refs:
            loads.pop(id(ref)).wait()

    stores = []

    def store(src, dst):
        c = pltpu.make_async_copy(src, dst, osem.at[len(stores)])
        c.start()
        stores.append(c)

    greeted(n_dp)
    loads.pop(0).wait()
    every.spread()
    mlp_p = remote(smp_h, tmp_p, ysem.at[0], ysem.at[1], (d, t ^ 2))
    mlp_p.start()
    mlp_c = remote(smc_h, tmp_c, ysem.at[2], ysem.at[3], (d, t ^ 2))
    mlp_c.start()

    at = np.cumsum([0, quarter, quarter, quarter, qw, qw, 2 * kvw]).tolist()
    bkv = dn(evens_first(2 * RK), bkv_ref[...].reshape(2 * RK, kvw)).astype(BF)

    def out_grads(da, n2, uo, sel, r0, first):
        half = da.shape[1]
        r = 2 * half
        dav = da[:, :, :width].reshape(r, width)
        duo = (dt(dav, bo[...]) * sel).astype(BF)
        do[r0 : r0 + r] = (dt(dav, wo[...]) + dn(duo, aoT[...])).astype(BF)
        gao = dr(duo, o[r0 : r0 + r])
        dum = da[:, :, width:].reshape(r, 2 * RK)
        gam = dr(dum, n2[...].reshape(r, quarter))
        gbo = dr(uo[:, :, :RK].reshape(r, RK), da[:, :, qlanes].reshape(r, quarter))
        parts = (gbo, gam[:RK], gam[RK:], gao)
        for n, part in enumerate(parts):
            lanes = slice(at[n], at[n + 1])
            gacc[:, lanes] = part if first else gacc[:, lanes] + part

    def unrotate(r0, r):
        here = slice(r0, r0 + r)
        for c in range(qw // LANE):
            lanes = slice(c * LANE, (c + 1) * LANE)
            dqp[here, lanes] = rot(dqp[here, lanes].astype(F32), cos[here], -sin[here]).astype(BF)
        dkvp[here, :kvw] = rot(dkv[here, :kvw].astype(BF).astype(F32), cos[here], -sin[here]).astype(BF)
        dkvp[here, kvw:] = dkv[here, kvw:].astype(BF)

    need(dac, wo, o, aoT, bo, n2c, uoc)
    sel_c = jnp.concatenate([jnp.broadcast_to(sel_row(sc[1]), (hcn, RK)), jnp.broadcast_to(sel_row(sc[2]), (hcn, RK))], axis=0)
    out_grads(dac, n2c, uoc, sel_c, PLEN, True)
    fetch(14, 22)
    need(q, kv, far, pc)

    def attend(j):
        r0 = pl.multiple_of(PLEN + j * CLEN, CLEN)
        own = pl.ds(r0, CLEN)
        for g in range(2):
            lanes = slice(g * HD, (g + 1) * HD)
            vlanes = slice(kvw + g * HD, kvw + (g + 1) * HD)
            qi = stack_heads(q, r0, g)
            doi = stack_heads(do, r0, g)
            p = pc[2 * j + g]
            dp = jnp.concatenate([dt(doi, far[j, :, vlanes]), dt(doi, kv[own, vlanes])], axis=1)
            ds = back_scores(p, dp)
            dqv = dn(ds[:, :PLEN], far[j, :, lanes]) + dn(ds[:, PLEN:], kv[own, lanes])
            put_dq((dqv * 0.125).astype(BF), dqp, r0, g)
            dk = dr(ds, qi)
            dv = dr(p, doi)
            dfar[j, :, lanes] = dk[:PLEN].astype(BF)
            dfar[j, :, vlanes] = dv[:PLEN].astype(BF)
            dkv[own, lanes] = dk[PLEN:]
            dkv[own, vlanes] = dv[PLEN:]
        fold.across(j).start()

    mate = (d ^ 1) * CONT_DEV
    others = [group_map[mate + j] for j in range(CONT_DEV)]
    fold = Fold(dfar, xr, zs, zr, (f0, f1, f2, f3), sc[3:], others, d, t, hi)
    loop(0, CONT_DEV, attend)
    fetch(22, len(pairs))
    need(cos, sin)
    unrotate(PLEN, 2 * hcn)

    def dn1(r0, snd, dsnd, dsum, first):
        half = snd.shape[1]
        r = 2 * half
        here = slice(r0, r0 + r)
        a, b = dqp[here], dkvp[here]
        du = jnp.concatenate(
            [dt(a, bq[...]), dt(b[:, :kvw], bkv[:RK]), dt(b[:, kvw:], bkv[RK:]), jnp.zeros((r, RK), F32)], axis=1
        ).astype(BF)
        dsnd[0] = du[:half]
        dsnd[1] = du[half:]
        dsum.begin()

        def columns(n):
            lanes = pl.ds(pl.multiple_of(n * 512, 512), 512)
            part = (dt(a, wq[lanes]) + dt(b, wkv[lanes])).astype(BF)
            snd[0, :, lanes] = part[:half]
            snd[1, :, lanes] = part[half:]

        loop(0, width // 512, columns)
        gbq = dr(u[here, :RK], a)
        gkv = dr(u[here, RK:], b)
        parts = (gbq, gkv[:RK, :kvw], gkv[RK:, kvw:])
        for part, start in zip(parts, (at[4], at[5], at[5] + kvw)):
            lanes = slice(start, start + part.shape[1])
            gacc[:, lanes] = part if first else gacc[:, lanes] + part

    need(wq, wkv, u, bq)
    dsum_c = TensorSum(dsnd_c, dgot_c, ds_c, dt_c, dcsem, d, t)
    dn1(PLEN, snd_c, dsnd_c, dsum_c, True)
    sum_c = TensorSum(snd_c, got_c, s_c, t_c, csem, d, t)
    sum_c.begin()
    fold.fold()

    need(dap, n2p, uop)
    out_grads(dap, n2p, uop, jnp.broadcast_to(sel_row(sc[0]), (PLEN, RK)), 0, False)
    load_dy = []
    for n in range(2):
        for ref, start, half in ((dap, n * hpn, hpn), (dac, PLEN + n * hcn, hcn)):
            here = pl.ds(start, half)
            for src, lanes in ((dy_h.at[here, qlanes], slice(0, quarter)), (n1q_h.at[here], slice(quarter, 2 * quarter))):
                c = pltpu.make_async_copy(src, ref.at[n, :, lanes], dsem.at[len(load_dy)])
                c.start()
                load_dy.append(c)
    dsum_c.middle()
    sum_c.middle()
    need(pp)
    for g in range(2):
        lanes = slice(g * HD, (g + 1) * HD)
        vlanes = slice(kvw + g * HD, kvw + (g + 1) * HD)
        kg = kv[:PLEN, lanes]
        vg = kv[:PLEN, vlanes]
        for i in reversed(range(PLEN // CLEN)):
            size = (i + 1) * CLEN
            qi = stack_heads(q, i * CLEN, g)
            doi = stack_heads(do, i * CLEN, g)
            p = pp[g, :, P_OFF[i] : P_OFF[i] + size]
            ds = back_scores(p, dt(doi, vg[:size]))
            put_dq((dn(ds, kg[:size]) * 0.125).astype(BF), dqp, i * CLEN, g)
            dk = dr(ds, qi)
            dv = dr(p, doi)
            if size == PLEN:
                dkv[:size, lanes] = dk
                dkv[:size, vlanes] = dv
            else:
                dkv[:size, lanes] += dk
                dkv[:size, vlanes] += dv
    every.cross()

    def finish_out(which, sm, theirs, copy, h, out, r0, adapter):
        half = h.shape[0]
        copy.wait_recv()
        sr = sel_row(adapter)
        ud = ((sm[:, width : width + RK].astype(F32) + theirs[:, width : width + RK].astype(F32)) * sr).astype(BF)
        tmp[:half] = dn(ud, bd[...])

        def one(r):
            here = pl.ds(r, 64)
            out[lo, here, :width] = (
                h[here] + (sm[here, :width].astype(F32) + theirs[here, :width].astype(F32)) + tmp[here]
            ).astype(BF)

        rows_loop(half, 64, one)
        out[lo, :, width:] = jnp.concatenate([ud, jnp.zeros((half, LANE - RK), BF)], axis=1)
        c = remote(out.at[lo], out.at[lo], nsem.at[which, 0], nsem.at[which, 1], (d, t ^ 1))
        c.start()
        return c

    def arrived(which, out):
        remote(out.at[1 - lo], out.at[1 - lo], nsem.at[which, 0], nsem.at[which, 1], (d, t ^ 1)).wait_recv()

    need(smp, hp, bd)
    out_copy_p = finish_out(0, smp, tmp_p, mlp_p, hp, outp, 0, sc[0])
    load_dhp = pltpu.make_async_copy(dhp_h, hp, lsem.at[32])
    load_dhp.start()

    adapter_c = jnp.where(lo == 0, sc[1], sc[2])
    per = quarter // LANE * (RK // 16)

    def fill(blocks, used):
        if blocks.shape[0] > used:
            blocks[used:] = jnp.zeros((blocks.shape[0] - used, *UNIT), BF)

    def share_du(which, total, du, adapter):
        total.end()
        sr = sel_row(adapter)
        raw = total.mine[:, : 3 * RK].astype(F32) + total.theirs[:, : 3 * RK].astype(F32)
        duq = (raw * jnp.concatenate([sr, sr, sr], axis=1)).astype(BF)
        du[lo] = jnp.concatenate([duq, jnp.zeros((duq.shape[0], RK), BF)], axis=1)
        c = remote(du.at[lo], du.at[lo], nsem.at[which, 0], nsem.at[which, 1], (d, t ^ 1))
        c.start()
        return c

    need(smc, hc, aT)
    out_copy_c = finish_out(1, smc, tmp_c, mlp_c, hc, outc, PLEN, adapter_c)
    load_dhc = pltpu.make_async_copy(dhc_h, hc, lsem.at[33])
    load_dhc.start()
    du_copy_c = share_du(4, dsum_c, duc, adapter_c)
    for c in load_dy:
        c.wait()
    arrived(0, outp)
    gbd = dr(outp[:, :, width : width + RK].reshape(PLEN, RK), dap[:, :, :quarter].reshape(PLEN, quarter))
    arrived(1, outc)
    gbd = gbd + dr(outc[:, :, width : width + RK].reshape(2 * hcn, RK), dac[:, :, :quarter].reshape(2 * hcn, quarter))

    put_units(l1s, 0, gacc[:, : at[3]].astype(BF))
    put_units(l1s, 3 * per, gbd.astype(BF))
    fill(l1s, 4 * per)
    red1 = PairReduce(l1s, l1x, l1z, t1.at[lo], rsems[8:16], d, t, n_dp)
    red1.start()
    trade1 = Trade(t1, q1, d, t)
    for n in range(2):
        store(outp.at[n, :, :width], out_h.at[pl.ds(n * hpn, hpn)])
        store(outc.at[n, :, :width], out_h.at[pl.ds(PLEN + n * hcn, hcn)])
    arrived(4, duc)
    ga_c = dr(duc[:, :, : 3 * RK].reshape(2 * hcn, 3 * RK), dac[:, :, quarter : 2 * quarter].reshape(2 * hcn, quarter))

    fold.finish(dkv.at[:PLEN])
    unrotate(0, PLEN)
    dsum_p = TensorSum(dsnd_p, dgot_p, ds_p, dt_p, dpsem, d, t)
    dn1(0, snd_p, dsnd_p, dsum_p, False)
    sum_p = TensorSum(snd_p, got_p, s_p, t_p, psem, d, t)
    dsum_p.middle()
    sum_p.begin()
    put_units(l0s, 0, gacc[:, at[3] :].astype(BF))
    fill(l0s, (at[6] - at[3]) // LANE * (RK // 16))
    red0 = PairReduce(l0s, l0x, l0z, l0, rsems[16:24], d, t, n_dp)
    red0.start()
    sum_p.middle()
    red1.middle()
    du_copy_p = share_du(5, dsum_p, dup, sc[0])
    arrived(5, dup)
    ga_p = dr(dup[:, :, : 3 * RK].reshape(PLEN, 3 * RK), dap[:, :, quarter : 2 * quarter].reshape(PLEN, quarter))
    ga = (ga_c + ga_p).astype(BF)
    for n in range(3):
        put_units(l2s, n * per, ga[n * RK : (n + 1) * RK])
    fill(l2s, 3 * per)
    red2 = PairReduce(l2s, l2x, l2z, t2.at[lo], rsems[24:32], d, t, n_dp)
    red2.start()
    trade2 = Trade(t2, q2, d, t)

    def last(which, total, du, x, dh, tg):
        half = x.shape[0]
        tmp[:half] = dn(du[lo, :, : 3 * RK], aT[...])
        gain = gain1[...].astype(F32).reshape(1, width)
        total.end()

        def one(r):
            here = pl.ds(r, 64)
            dn1v = total.mine[here].astype(F32) + total.theirs[here].astype(F32) + tmp[here]
            grad = dh[here] + norm_back(x[here].astype(F32), gain, dn1v)
            tg[lo, here] = grad.astype(BF)

        rows_loop(half, 64, one)
        c = remote(tg.at[lo], tg.at[lo], nsem.at[which, 0], nsem.at[which, 1], (d, t ^ 1))
        c.start()
        return c

    red1.add()
    red0.middle()
    need(xc)
    load_dhc.wait()
    tg_copy_c = last(2, sum_c, duc, xc, hc, tgc)
    red2.middle()
    red1.cross()
    red0.add()
    every.finish()
    store(gef, gef_h)
    red2.add()
    arrived(2, tgc)
    for n in range(2):
        store(tgc.at[n], tg_h.at[pl.ds(PLEN + n * hcn, hcn)])
    red0.cross()
    red1.finish()
    trade1.start()
    red2.cross()
    trade1.finish()
    store(t1, t1_h)
    need(xp)
    load_dhp.wait()
    tg_copy_p = last(3, sum_p, dup, xp, hp, tgp)
    red0.finish()
    store(l0, l0_h)
    red2.finish()
    trade2.start()
    arrived(3, tgp)
    for n in range(2):
        store(tgp.at[n], tg_h.at[pl.ds(n * hpn, hpn)])
    trade2.finish()
    store(t2, t2_h)
    for c in (out_copy_p, out_copy_c, tg_copy_c, tg_copy_p, du_copy_c, du_copy_p, mlp_p, mlp_c):
        c.wait_send()
    for total in (sum_p, sum_c, dsum_p, dsum_c):
        total.drain()
    fold.drain()
    every.spread_sent()
    for red in (red0, red1, red2):
        red.sent()
        red.spread_sent()
    trade1.sent()
    trade2.sent()
    for c in stores:
        c.wait()


def backward(n_dp, scalars, small, large):
    (dac, wo, o, aoT, bo, n2c, uoc, q, kv, far, pc, cos, sin, dap, pp, n2p, uop, u, wq, wkv, bq, smp, hp, bd, smc, hc, dy, n1q,
     dhc, aT, dhp, tok, ge) = large
    rows, width = tok.shape
    qw = wq.shape[1]
    kvw2 = wkv.shape[1]
    quarter = n1q.shape[1]
    wide = dap.shape[2]
    hpn, hcn = PLEN // 2, CLEN
    per = quarter // LANE * (RK // 16)
    up = lambda a: -(-a // n_dp) * n_dp
    ue = ge.shape[0] * n_dp
    u0 = up((2 * qw + kvw2) // LANE * (RK // 16))
    u1 = up(4 * per)
    u2 = up(3 * per)
    outs = [
        ((rows, width), BF), ((rows, width), BF), ((ue, *UNIT), BF), ((u0, *UNIT), BF), ((2, u1, *UNIT), BF),
        ((2, u2, *UNIT), BF),
    ]
    dma = pltpu.SemaphoreType.DMA
    hi = n_dp // 2
    same = lambda a: VM(a.shape, a.dtype)

    def sums(half, n):
        return [VM((2, half, n), BF), VM((half, n), BF), VM((half, n), BF), VM((half, n), BF)]

    scratch = [
        same(dac), same(wo), same(o), same(aoT), same(bo), VM((2, hcn, quarter), BF), VM((2, hcn, LANE), BF), same(q), same(kv),
        same(far), same(pc), same(cos), same(sin), same(dap), same(pp), VM((2, hpn, quarter), BF), VM((2, hpn, LANE), BF),
        same(u), same(wq), same(wkv), same(bq), same(smp), same(hp), same(bd), same(smc), same(hc),
        same(aT), VM((hcn, width), BF), VM((hpn, width), BF), VM((ue, *UNIT), BF),
        same(smp), same(smc),
        VM((rows, qw), BF), VM((rows, qw), BF), VM((rows, kvw2), F32), VM((rows, kvw2), BF),
        VM((CONT_DEV, PLEN, kvw2), BF), VM((RK, 2 * qw + 3 * quarter + kvw2), F32),
        *sums(hpn, width), *sums(hcn, width), *sums(hpn, 2 * LANE), *sums(hcn, 2 * LANE),
        VM((2, hpn, 2 * LANE), BF), VM((2, hcn, 2 * LANE), BF),
        VM((2, hpn, wide), BF), VM((2, hcn, wide), BF), VM((2, hpn, width), BF), VM((2, hcn, width), BF), VM((hpn, width), F32),
        VM((u0, *UNIT), BF), VM((u0 // 2, *UNIT), BF), VM((hi, u0 // n_dp, *UNIT), BF), VM((u0, *UNIT), BF),
        VM((u1, *UNIT), BF), VM((u1 // 2, *UNIT), BF), VM((hi, u1 // n_dp, *UNIT), BF),
        VM((u2, *UNIT), BF), VM((u2 // 2, *UNIT), BF), VM((hi, u2 // n_dp, *UNIT), BF),
        VM((2, u1, *UNIT), BF), VM((2, u2, *UNIT), BF),
        VM((CONT_DEV, PLEN, kvw2), BF), VM((hi, PLEN, kvw2), BF), VM((hi, PLEN, kvw2), BF),
        dma((34,)), dma((13,)), dma((8,)), dma((4,)), dma((4,)), dma((4,)), dma((4,)), dma((4,)), dma((6, 2)), dma((2,)), dma((2,)),
    ] + [dma((CONT_DEV,))] * 2 + [dma((hi,))] * 2 + [dma((n_dp,))] * 32
    vm = pl.BlockSpec(memory_space=VM)
    anyspace = pl.BlockSpec(memory_space=pl.ANY)
    return pl.pallas_call(
        functools.partial(back_kernel, n_dp),
        out_shape=[jax.ShapeDtypeStruct(s, dtype) for s, dtype in outs],
        in_specs=[pl.BlockSpec(memory_space=pltpu.SMEM)] * 3 + [vm] * len(small) + [anyspace] * len(large),
        out_specs=[anyspace] * len(outs),
        scratch_shapes=scratch,
        compiler_params=pltpu.CompilerParams(vmem_limit_bytes=63 << 20, collective_id=3, has_side_effects=True),
        cost_estimate=pl.CostEstimate(flops=6 * rows * width * (2 * qw + kvw2), bytes_accessed=40 << 20, transcendentals=0),
        name="back",
    )(*scalars, *small, *large)


def emit_kernel(
    qw, kvw, quarter, hidden, ge, l0, t1, t2, out_h, tg_h,
    gbm, gad, gao, gbq, gbkv, gbo, gam, gbd, ga, out_o, tg_o, buf, sem,
):
    pairs = ((out_h, out_o), (tg_h, tg_o))
    copies = [pltpu.make_async_copy(src, buf.at[n], sem.at[n]) for n, (src, _) in enumerate(pairs)]
    for c in copies:
        c.start()
    high = RK // 16

    def take(blocks, first, count, put):
        for b in range(count // LANE):
            for r in range(high):
                put(slice(r * 16, (r + 1) * 16), slice(b * LANE, (b + 1) * LANE), blocks[first + b * high + r].astype(F32))

    def plain(dst, row=0, lane=0):
        def put(rows, lanes, value):
            dst[rows.start + row : rows.stop + row, lanes.start + lane : lanes.stop + lane] = value

        return put

    def paired(dst, n):
        def put(rows, lanes, value):
            dst[rows, n, lanes] = value

        return put

    seg = hidden // LANE * high
    take(ge, 0, hidden, paired(gbm, 0))
    take(ge, seg, hidden, paired(gbm, 1))
    take(ge, 2 * seg, hidden, plain(gad))
    take(l0, 0, qw, plain(gao))
    begin = qw // LANE * high
    half = kvw // LANE * high
    take(l0, begin, qw, plain(gbq))
    take(l0, 2 * begin, kvw, paired(gbkv, 0))
    take(l0, 2 * begin + half, kvw, paired(gbkv, 1))
    per = quarter // LANE * high
    for c in copies:
        c.wait()
    copies = [pltpu.make_async_copy(buf.at[n], dst, sem.at[2 + n]) for n, (_, dst) in enumerate(pairs)]
    for c in copies:
        c.start()
    for t in range(t1.shape[0]):
        take(t1.at[t], 0, quarter, plain(gbo, 0, t * quarter))
        take(t1.at[t], per, quarter, plain(gam, 0, t * quarter))
        take(t1.at[t], 2 * per, quarter, plain(gam, RK, t * quarter))
        take(t1.at[t], 3 * per, quarter, plain(gbd, 0, t * quarter))
        for n in range(3):
            take(t2.at[t], n * per, quarter, plain(ga, n * RK, t * quarter))
    for c in copies:
        c.wait()


def emit(qw, kvw, quarter, hidden, grads, results):
    width = 2 * quarter
    outs = [
        ((RK, 2, hidden), F32), ((RK, hidden), F32), ((RK, qw), F32), ((RK, qw), F32), ((RK, 2, kvw), F32), ((RK, width), F32),
        ((2 * RK, width), F32), ((RK, width), F32), ((3 * RK, width), F32),
    ] + [(a.shape, a.dtype) for a in results]
    vm = pl.BlockSpec(memory_space=VM)
    anyspace = pl.BlockSpec(memory_space=pl.ANY)
    return pl.pallas_call(
        functools.partial(emit_kernel, qw, kvw, quarter, hidden),
        out_shape=[jax.ShapeDtypeStruct(s, dtype) for s, dtype in outs],
        in_specs=[vm] * len(grads) + [anyspace] * len(results),
        out_specs=[vm] * 9 + [anyspace] * 2,
        scratch_shapes=[VM((2, *results[0].shape), BF), pltpu.SemaphoreType.DMA((4,))],
        compiler_params=pltpu.CompilerParams(vmem_limit_bytes=61 << 20),
        cost_estimate=pl.CostEstimate(flops=0, bytes_accessed=20 << 20, transcendentals=0),
        name="emit",
    )(*grads, *results)


def rope_tables():
    position = np.concatenate([np.arange(PLEN)] + [PLEN + np.arange(CLEN)] * CONT_DEV).astype(np.float32)
    exponent = np.arange(HD // 2, dtype=np.float32) * np.float32(2.0 / HD)
    frequency = np.exp(np.float32(-math.log(ROPE_BASE)) * exponent).astype(np.float32)
    angle = position[:, None] * frequency[None, :]
    cos, sin = np.cos(angle).astype(np.float32), np.sin(angle).astype(np.float32)
    return np.tile(cos, (1, 4)), np.concatenate([-sin, sin, -sin, sin], axis=1)


def shards(
    tokens, cotangent, gain_attn, gain_mlp, w_query, w_kv, w_out, w_gate_up, w_down, a_attn, b_query, b_kv,
    a_out, b_out, a_mlp, b_mlp, a_down, b_down, prompt_adapter, cont_adapter, group_map,
):
    rows, width = tokens.shape
    qw = w_query.shape[1]
    kvw = w_kv.shape[2]
    hidden = w_down.shape[0]
    n_dp = lax.axis_size("dp")
    quarter = width // 2
    cos_np, sin_np = rope_tables()
    cos, sin = jnp.asarray(cos_np), jnp.asarray(sin_np)
    gain1, gain2 = gain_attn, gain_mlp
    aT = a_attn.transpose(1, 2, 3, 0).reshape(3 * RK, width)
    aoT = a_out.transpose(1, 2, 0).reshape(RK, qw)
    amT = a_mlp.transpose(1, 2, 3, 0).reshape(2 * RK, width)
    adT = a_down.transpose(1, 2, 0).reshape(RK, hidden)
    bq = b_query.reshape(RK, qw)
    bkv = b_kv.reshape(RK, 2, kvw)
    bo = b_out.reshape(RK, width)
    bm = b_mlp.reshape(RK, 2, hidden)
    bd = b_down.reshape(RK, width)
    wkv = w_kv.reshape(width, 2 * kvw)
    (n1q, q, kv, u, pp, pc, o, far, h_p, h_c, n2p, n2c, uop, uoc, _, dh_p, dh_c, dap, dac, sm_p, sm_c, ge) = first(
        n_dp, [prompt_adapter, cont_adapter, group_map], [gain1, gain2, bkv, bm, amT, adT, bo],
        [tokens, aT, wkv, cos, sin, w_query, bq, aoT, w_out, cotangent, bd, w_down, w_gate_up],
    )
    results = backward(
        n_dp, [prompt_adapter, cont_adapter, group_map], [gain1, bkv],
        [dac, w_out, o, aoT, bo, n2c, uoc, q, kv, far, pc, cos, sin, dap, pp, n2p, uop, u, w_query, wkv, bq, sm_p, h_p, bd, sm_c,
         h_c, cotangent, n1q, dh_c, aT, dh_p, tokens, ge],
    )
    gbm, gad, gao, gbq, gbkv, gbo, gam, gbd, ga, output, tokens_grad = emit(qw, kvw, quarter, hidden, results[2:], results[:2])
    return (
        output,
        tokens_grad,
        ga.reshape(3, NA, R, width).transpose(3, 0, 1, 2),
        gbq.reshape(b_query.shape),
        gbkv.reshape(b_kv.shape),
        gao.reshape(NA, R, qw).transpose(2, 0, 1),
        gbo.reshape(b_out.shape),
        gam.reshape(2, NA, R, width).transpose(3, 0, 1, 2),
        gbm.reshape(b_mlp.shape),
        gad.reshape(NA, R, hidden).transpose(2, 0, 1),
        gbd.reshape(b_down.shape),
    )


def solution(mesh):
    in_specs = (
        P("dp", None), P("dp", None), P(), P(), P(None, "tensor"), P(None, None, "tensor"), P("tensor", None),
        P(None, None, "tensor"), P("tensor", None), P(), P(None, None, "tensor"), P(None, None, None, "tensor"),
        P("tensor", None, None), P(), P(), P(None, None, None, "tensor"), P("tensor", None, None), P(),
        P("dp"), P("dp"), P(),
    )
    out_specs = (
        P("dp", None), P("dp", None), P(), P(None, None, "tensor"), P(None, None, None, "tensor"),
        P("tensor", None, None), P(), P(), P(None, None, None, "tensor"), P("tensor", None, None), P(),
    )
    return jax.shard_map(shards, mesh=mesh, in_specs=in_specs, out_specs=out_specs, check_vma=False)
```

```python
import functools
import math

import jax
import jax.numpy as jnp
import numpy as np
from jax import lax
from jax.experimental import pallas as pl
from jax.experimental.pallas import tpu as pltpu
from jax.sharding import PartitionSpec as P

HD = 64
R = 16
NA = 4
RK = NA * R
PLEN = 384
CLEN = 128
CONT_DEV = 2
ROWS = PLEN + CONT_DEV * CLEN
EPSILON = 1e-05
ROPE_BASE = 500000.0
MASKED_SCORE = -1e30

BF = jnp.bfloat16
F32 = jnp.float32
VM = pltpu.VMEM
LANE = 128


def dn(a, b):
    return jnp.dot(a, b, preferred_element_type=F32)


def dt(a, b):
    return lax.dot_general(a, b, (((1,), (1,)), ((), ())), preferred_element_type=F32)


def dr(a, b):
    return lax.dot_general(a, b, (((0,), (0,)), ((), ())), preferred_element_type=F32)


def sel_row(adapter):
    lane = lax.broadcasted_iota(jnp.int32, (1, RK), 1)
    return (lax.shift_right_logical(lane, 4) == adapter).astype(F32)


def swap_halves(v):
    lane = lax.broadcasted_iota(jnp.int32, v.shape, 1)
    return jnp.where((lane & 63) < 32, pltpu.roll(v, LANE - 32, 1), pltpu.roll(v, 32, 1))


def rot(v, cos, sin):
    return v * cos + swap_halves(v) * sin


def stack_heads(ref, r0, g):
    return jnp.concatenate(
        [ref[pl.ds(r0, CLEN), (4 * g + h) * HD : (4 * g + h + 1) * HD] for h in range(4)], axis=0
    )


def softmax_low(s):
    top = jnp.max(s, axis=-1, keepdims=True)
    e = jnp.exp(s - top)
    return (e * (1.0 / jnp.sum(e, axis=-1, keepdims=True))).astype(BF)


def causal_tile():
    r = lax.broadcasted_iota(jnp.int32, (4 * CLEN, CLEN), 0) & (CLEN - 1)
    c = lax.broadcasted_iota(jnp.int32, (4 * CLEN, CLEN), 1)
    return c <= r


P_OFF = (0, 128, 384)


def norm_back(v, gain, upstream):
    inv = lax.rsqrt(jnp.mean(v * v, axis=-1, keepdims=True) + EPSILON)
    scaled = v * inv
    weighted = upstream * gain
    return inv * (weighted - scaled * jnp.mean(weighted * scaled, axis=-1, keepdims=True))


def put_dq(dq, dq_ref, r0, g):
    for h in range(4):
        dq_ref[pl.ds(r0, CLEN), (4 * g + h) * HD : (4 * g + h + 1) * HD] = dq[h * CLEN : (h + 1) * CLEN]


def back_scores(p, dp):
    pf = p.astype(F32)
    return (pf * (dp - jnp.sum(pf * dp, axis=-1, keepdims=True))).astype(BF)


MESH = pl.DeviceIdType.MESH


def rows_loop(total, step, body):
    def one(i, carry):
        body(pl.multiple_of(i * step, step))
        return carry

    lax.fori_loop(0, total // step, one, 0)


def loop(first, last, body):
    def one(i, carry):
        body(i)
        return carry

    lax.fori_loop(first, last, one, 0)


def place():
    d = lax.axis_index("dp")
    t = lax.axis_index("tensor")
    return d, t


def remote(src, dst, send, recv, device):
    return pltpu.make_async_remote_copy(
        src_ref=src, dst_ref=dst, send_sem=send, recv_sem=recv, device_id=device, device_id_type=MESH
    )


def greet(d, t, n_dp):
    barrier = pltpu.get_barrier_semaphore()
    for device in [(d, t ^ 1), (d, t ^ 2)] + [((d + k) % n_dp, t) for k in range(1, n_dp)]:
        pl.semaphore_signal(barrier, inc=1, device_id=device, device_id_type=MESH)


def greeted(n_dp):
    pl.semaphore_wait(pltpu.get_barrier_semaphore(), n_dp + 1)


class Spread:
    def __init__(self, every, sems, d, t, hi):
        self.every, self.sems, self.d, self.t, self.hi = every, sems, d, t, hi
        self.z, self.x = d // 2, d % 2

    def across(self, z):
        block = z * 2 + self.x
        up_s, up_r, down_s, down_r, x_s, x_r = self.sems
        return remote(self.every.at[block], self.every.at[block], x_s.at[z], x_r.at[z], (self.d ^ 1, self.t))

    def along(self, z, s, up):
        block = z * 2 + self.x
        up_s, up_r, down_s, down_r, x_s, x_r = self.sems
        send, recv, step = (up_s, up_r, 2) if up else (down_s, down_r, -2)
        return remote(self.every.at[block], self.every.at[block], send.at[s], recv.at[s], (self.d + step, self.t))

    def start(self):
        self.across(self.z).start()

        @pl.when(self.z < self.hi - 1)
        def _():
            self.along(self.z, 1, True).start()

        @pl.when(self.z > 0)
        def _():
            self.along(self.z, 1, False).start()

    def hop(self, s):
        if s > self.hi - 1:
            return
        for up in (True, False):
            origin = self.z - s if up else self.z + s
            held = origin >= 0 if up else origin < self.hi
            further = self.z < self.hi - 1 if up else self.z > 0

            @pl.when(held)
            def _(origin=origin, up=up, further=further):
                self.along(origin, s, up).wait_recv()
                self.across(origin).start()
                if s + 1 <= self.hi - 1:

                    @pl.when(further)
                    def _():
                        self.along(origin, s + 1, up).start()

    def finish(self):
        for z in range(self.hi):
            across = self.across(z)
            across.wait_send()
            block = z * 2 + 1 - self.x
            up_s, up_r, down_s, down_r, x_s, x_r = self.sems
            remote(self.every.at[block], self.every.at[block], x_s.at[z], x_r.at[z], (self.d ^ 1, self.t)).wait_recv()
        for s in range(1, self.hi):
            for up in (True, False):
                origin = self.z - s + 1 if up else self.z + s - 1
                held = origin >= 0 if up else origin < self.hi
                further = self.z < self.hi - 1 if up else self.z > 0

                @pl.when(held & further)
                def _(origin=origin, up=up, s=s):
                    self.along(origin, s, up).wait_send()


class TensorSum:
    def __init__(self, snd, got, mine, theirs, sems, d, t):
        self.snd, self.got, self.mine, self.theirs, self.sems, self.t = snd, got, mine, theirs, sems, t
        self.lo = t % 2
        self.core = remote(snd.at[1 - self.lo], got, sems.at[0], sems.at[1], (d, t ^ 1))
        self.chip = remote(mine, theirs, sems.at[2], sems.at[3], (d, t ^ 2))

    def begin(self):
        self.core.start()

    def middle(self):
        self.core.wait_recv()

        def add(r):
            rows = pl.ds(r, 64)
            self.mine[rows] = (self.snd[self.lo, rows].astype(F32) + self.got[rows].astype(F32)).astype(BF)

        rows_loop(self.mine.shape[0], 64, add)
        self.chip.start()

    def end(self):
        self.chip.wait_recv()

    def drain(self):
        self.core.wait_send()
        self.chip.wait_send()


UNIT = (16, LANE)


def put_units(blocks, first, value):
    for b in range(value.shape[1] // LANE):
        for r in range(RK // 16):
            blocks[first + b * (RK // 16) + r] = value[r * 16 : (r + 1) * 16, b * LANE : (b + 1) * LANE]


class DirectReduce:
    def __init__(self, src, got, out, sems, d, t, n_dp):
        self.src, self.got, self.out, self.sems, self.d, self.t, self.n = src, got, out, sems, d, t, n_dp
        self.share = src.shape[0] // n_dp if src is not None else out.shape[0] // n_dp

    def part(self, d):
        return pl.ds(((d % 2) * (self.n // 2) + d // 2) * self.share, self.share)

    def to(self, k):
        peer = (self.d + k) % self.n
        return remote(self.src.at[self.part(peer)], self.got.at[k], self.sems[0].at[k], self.sems[1].at[k], (peer, self.t))

    def back(self, k):
        peer = (self.d + k) % self.n
        here = self.part(self.d)
        return remote(self.out.at[here], self.out.at[here], self.sems[2].at[k], self.sems[3].at[k], (peer, self.t))

    def from_back(self, k):
        peer = (self.d + self.n - k) % self.n
        there = self.part(peer)
        return remote(self.out.at[there], self.out.at[there], self.sems[2].at[k], self.sems[3].at[k], (peer, self.t))

    def start(self):
        for k in range(1, self.n):
            self.to(k).start()

    def add(self):
        for k in range(1, self.n):
            self.to(k).wait_recv()
        here = self.part(self.d)
        total = self.src[here].astype(F32)
        for k in range(1, self.n):
            total = total + self.got[k].astype(F32)
        self.out[here] = total.astype(BF)

    def sent(self):
        for k in range(1, self.n):
            self.to(k).wait_send()

    def spread(self):
        for k in range(1, self.n):
            self.back(k).start()

    def finish(self):
        for k in range(1, self.n):
            self.from_back(k).wait_recv()

    def spread_sent(self):
        for k in range(1, self.n):
            self.back(k).wait_send()


class PairReduce:
    def __init__(self, src, gx, gz, out, sems, d, t, n_dp):
        self.src, self.gx, self.gz, self.out, self.sems, self.t = src, gx, gz, out, sems, t
        self.hi, self.z, self.x = n_dp // 2, d // 2, d % 2
        self.share = out.shape[0] // n_dp
        self.mate = (d ^ 1, t)

    def part(self, z):
        return pl.ds((self.x * self.hi + z) * self.share, self.share)

    def half(self, x):
        return pl.ds(x * self.hi * self.share, self.hi * self.share)

    def on_line(self, k):
        z = (self.z + k) % self.hi
        return z, (z * 2 + self.x, self.t)

    def over(self):
        return remote(self.src.at[self.half(1 - self.x)], self.gx, self.sems[0].at[0], self.sems[1].at[0], self.mate)

    def to(self, k):
        z, device = self.on_line(k)
        return remote(self.src.at[self.part(z)], self.gz.at[k], self.sems[2].at[k], self.sems[3].at[k], device)

    def back(self, k, come=False):
        z, device = self.on_line(self.hi - k if come else k)
        here = self.part(z if come else self.z)
        return remote(self.out.at[here], self.out.at[here], self.sems[4].at[k], self.sems[5].at[k], device)

    def over_back(self, x):
        here = self.half(x)
        return remote(self.out.at[here], self.out.at[here], self.sems[6].at[0], self.sems[7].at[0], self.mate)

    def start(self):
        self.over().start()

    def middle(self):
        self.over().wait_recv()
        here = self.half(self.x)
        self.src[here] = (self.src[here].astype(F32) + self.gx[...].astype(F32)).astype(BF)
        for k in range(1, self.hi):
            self.to(k).start()

    def add(self):
        here = self.part(self.z)
        total = self.src[here].astype(F32)
        for k in range(1, self.hi):
            self.to(k).wait_recv()
            total = total + self.gz[k].astype(F32)
        self.out[here] = total.astype(BF)
        self.spread()

    def spread(self):
        for k in range(1, self.hi):
            self.back(k).start()

    def cross(self):
        for k in range(1, self.hi):
            self.back(k, True).wait_recv()
        self.over_back(self.x).start()

    def finish(self):
        self.over_back(1 - self.x).wait_recv()

    def spread_sent(self):
        for k in range(1, self.hi):
            self.back(k).wait_send()
        self.over_back(self.x).wait_send()

    def sent(self):
        self.over().wait_send()
        for k in range(1, self.hi):
            self.to(k).wait_send()


class Trade:
    def __init__(self, halves, sems, d, t):
        self.halves, self.sems, self.d, self.t = halves, sems, d, t

    def slot(self, n):
        return remote(self.halves.at[n], self.halves.at[n], self.sems.at[0], self.sems.at[1], (self.d, self.t ^ 1))

    def start(self):
        self.slot(self.t % 2).start()

    def finish(self):
        self.slot(1 - self.t % 2).wait_recv()

    def sent(self):
        self.slot(self.t % 2).wait_send()


def evens_first(n):
    r = lax.broadcasted_iota(jnp.int32, (n, n), 0)
    c = lax.broadcasted_iota(jnp.int32, (n, n), 1)
    return (c == jnp.where(r < n // 2, 2 * r, 2 * (r - n // 2) + 1)).astype(BF)


def all_sel(sc):
    return jnp.concatenate(
        [
            jnp.broadcast_to(sel_row(sc[0]), (PLEN, RK)),
            jnp.broadcast_to(sel_row(sc[1]), (CLEN, RK)),
            jnp.broadcast_to(sel_row(sc[2]), (CLEN, RK)),
        ],
        axis=0,
    )


def first_kernel(
    n_dp, ids_p, ids_c, group_map, gain1, gain2, bkv_ref, bm_h, amT_h, adT_h, bo_h,
    tok_h, aT_h, wkv_h, cos_h, sin_h, wq_h, bq_h, aoT_h, wo_h, dy_h, bd_h, wd_h, raw_h,
    n1q_h, q_h, kv_h, u_h, pp_h, pc_h, o_h, far_h, hp_h, hc_h, n2p_h, n2c_h, uop_h, uoc_h, wgu_h,
    dhp_h, dhc_h, dap_h, dac_h, smp_h, smc_h, ge_h,
    every, snd_p, s_p, snd_c, s_c, got0_p, t0_p, got0_c, t0_c, got1_p, t1_p, got1_c, t1_c,
    n2p, n2c, uop, uoc, hp, hc, xp, xc, dyp, dyc, dact, dud, tmp, ge, gots, bm, amT, adT, bo,
    lsem, osem, wsem, rsem, fsem, vsem, psem, csem, psem2, csem2, msem, nsem, up_s, up_r, down_s, down_r, x_s, x_r, g0, g1,
):
    d, t = place()
    sc = [ids_p[0], ids_c[0], ids_c[1], group_map[d * CONT_DEV], group_map[d * CONT_DEV + 1]]
    lo = t % 2
    hi = n_dp // 2
    rows, width = tok_h.shape
    wide = n2p.shape[2]
    qw = wq_h.shape[1]
    kvw = wkv_h.shape[1] // 2
    hidden = wd_h.shape[0]
    ht = 512
    steps = hidden // ht
    hpn, hcn = PLEN // 2, CLEN
    part = n1q_h.shape[1]
    qlanes = pl.ds(pl.multiple_of(lo * part, part), part)
    adapter_c = jnp.where(lo == 0, sc[1], sc[2])
    greet(d, t, n_dp)
    counts = [0, 0]

    def load(src, dst):
        c = pltpu.make_async_copy(src, dst, lsem.at[counts[0]])
        counts[0] += 1
        c.start()
        return c

    def store(src, dst):
        c = pltpu.make_async_copy(src, dst, osem.at[counts[1]])
        counts[1] += 1
        c.start()
        return c

    spread = Spread(every, (up_s, up_r, down_s, down_r, x_s, x_r), d, t, hi)
    sum_p = TensorSum(snd_p, got0_p, s_p, t0_p, psem, d, t)
    sum_c = TensorSum(snd_c, got0_c, s_c, t0_c, csem, d, t)
    sel = all_sel(sc)
    b2 = 2 * RK

    def attention(tok, n1, aT, wkv, cos, sin, wq, bq, aoT, wo, bd, wdc, raw, flat, bflat, kv, q, u, far, pp, pc, o):
        kt = raw.shape[1]
        raw_steps = width // kt

        def raw_copy(i, slot):
            return pltpu.make_async_copy(raw_h.at[pl.ds(i * kt, kt)], raw.at[slot], rsem.at[slot])

        def flat_copies(i, slot):
            here = pl.ds(i * kt, kt)
            return (
                pltpu.make_async_copy(flat.at[slot, 0], wgu_h.at[here, :hidden], fsem.at[slot, 0]),
                pltpu.make_async_copy(flat.at[slot, 1], wgu_h.at[here, hidden:], fsem.at[slot, 1]),
            )

        def wd_copy(i, slot):
            return pltpu.make_async_copy(wd_h.at[pl.ds(i * ht, ht)], wdc.at[slot, :, :width], wsem.at[slot, 0])

        load_tok = load(tok_h, tok.at[:, :width])
        load_kv = [load(a, b) for a, b in ((aT_h, aT), (wkv_h, wkv), (cos_h, cos), (sin_h, sin))]
        load_q = [load(a, b) for a, b in ((wq_h, wq), (bq_h, bq))]
        stores = []

        bkv = dn(evens_first(b2), bkv_ref[...].reshape(b2, kvw)).astype(BF)
        gain_row = gain1[...].astype(F32).reshape(1, width)
        load_tok.wait()

        def norm1(r):
            x = tok[pl.ds(r, 128), :width].astype(F32)
            inv = lax.rsqrt(jnp.mean(x * x, axis=-1, keepdims=True) + EPSILON)
            n1[pl.ds(r, 128)] = (x * inv * gain_row).astype(BF)

        rows_loop(rows, 128, norm1)
        load_o = [load(a, b) for a, b in ((aoT_h, aoT), (wo_h, wo))]
        load_dy = [load(a, b) for a, b in ((dy_h, tok.at[:, :width]), (bd_h, bd), (adT_h, adT))]
        for i in range(2):
            wd_copy(i, i).start()
        for i in range(raw.shape[0]):
            raw_copy(i, i).start()
        load_bm = load(bm_h, bm)
        load_x = [
            load(tok_h.at[pl.ds(pl.multiple_of(lo * hpn, hpn), hpn)], xp),
            load(tok_h.at[pl.ds(pl.multiple_of(PLEN + lo * hcn, hcn), hcn)], xc),
            load(amT_h, amT),
            load(bo_h, bo),
        ]
        for c in load_kv:
            c.wait()
        uf = dt(n1[...], aT[...])
        for part in range(3):
            u[:, part * RK : (part + 1) * RK] = (uf[:, part * RK : (part + 1) * RK] * sel).astype(BF)
        kvf = dn(n1[...], wkv[...])
        kv[:, :kvw] = rot(kvf[:, :kvw] + dn(u[:, RK : 2 * RK], bkv[:RK]), cos[...], sin[...]).astype(BF)
        kv[:, kvw:] = (kvf[:, kvw:] + dn(u[:, 2 * RK :], bkv[RK:])).astype(BF)
        every[d] = kv[:PLEN]
        greeted(n_dp)
        spread.start()

        for c in load_q:
            c.wait()
        qf = dn(n1[...], wq[...]) + dn(u[:, :RK], bq[...])
        for c in range(qw // LANE):
            lanes = slice(c * LANE, (c + 1) * LANE)
            q[:, lanes] = rot(qf[:, lanes], cos[...], sin[...]).astype(BF) * BF(0.125)
        stores.append(store(n1.at[:, qlanes], n1q_h))
        stores.append(store(q, q_h))
        stores.append(store(kv, kv_h))
        stores.append(store(u, u_h))

        def keep_o(of, r0, g):
            for h in range(4):
                o[pl.ds(r0, CLEN), (4 * g + h) * HD : (4 * g + h + 1) * HD] = of[h * CLEN : (h + 1) * CLEN]

        mask = causal_tile()
        for g in range(2):
            kg = kv[:PLEN, g * HD : (g + 1) * HD]
            vg = kv[:PLEN, kvw + g * HD : kvw + (g + 1) * HD]
            for i in range(PLEN // CLEN):
                size = (i + 1) * CLEN
                s = dt(stack_heads(q, i * CLEN, g), kg[:size])
                tail = jnp.where(mask, s[:, size - CLEN :], MASKED_SCORE)
                s = tail if i == 0 else jnp.concatenate([s[:, : size - CLEN], tail], axis=1)
                p = softmax_low(s)
                pp[g, :, P_OFF[i] : P_OFF[i] + size] = p
                keep_o(dn(p, vg[:size]).astype(BF), i * CLEN, g)
        stores.append(store(pp, pp_h))
        spread.hop(1)

        def project(r0, half, snd):
            ov = o[r0 : r0 + 2 * half]

            def columns(n):
                lanes = pl.ds(pl.multiple_of(n * 512, 512), 512)
                part = dn(ov, wo[:, lanes]).astype(BF)
                snd[0, :, lanes] = part[:half]
                snd[1, :, lanes] = part[half:]

            loop(0, width // 512, columns)
            uo = dt(ov, aoT[...]).astype(BF)
            pad = jnp.zeros((half, LANE - RK), BF)
            snd[0, :, width:] = jnp.concatenate([uo[:half], pad], axis=1)
            snd[1, :, width:] = jnp.concatenate([uo[half:], pad], axis=1)

        for c in load_o:
            c.wait()
        project(0, hpn, snd_p)
        sum_p.begin()

        for c in load_dy:
            c.wait()
        dudv = (dt(tok[:, :width], bd[...]) * sel).astype(BF)
        dud[...] = jnp.concatenate([dudv, jnp.zeros((rows, LANE - RK), BF)], axis=1)
        tok[:, width:] = dud[...]
        eye = (lax.broadcasted_iota(jnp.int32, (RK, RK), 0) == lax.broadcasted_iota(jnp.int32, (RK, RK), 1)).astype(BF)
        split = evens_first(256)

        slots, flats = raw.shape[0], flat.shape[0]

        def part_weights(i):
            slot = i % slots
            raw_copy(i, slot).wait()

            put = i % flats

            @pl.when(i >= flats)
            def _():
                for c in flat_copies(i - flats, put):
                    c.wait()

            apart = dn(split, raw[slot].reshape(2 * kt, hidden)).astype(BF)
            flat[put, 0] = apart[:kt]
            flat[put, 1] = apart[kt:]
            for c in flat_copies(i, put):
                c.start()

            @pl.when(i + slots < raw_steps)
            def _():
                raw_copy(i + slots, slot).start()

        def act_grad(i):
            slot = i % 2
            wd_copy(i, slot).wait()
            lanes = pl.ds(pl.multiple_of(i * ht, ht), ht)
            ad = dr(adT[:, lanes], eye).astype(BF)
            wdc[slot, :, width:] = jnp.concatenate([ad, jnp.zeros((ht, LANE - RK), BF)], axis=1)
            dact[:, lanes] = dt(tok[...], wdc[slot]).astype(BF)

            @pl.when(i + 2 < steps)
            def _():
                wd_copy(i + 2, slot).start()

        def both(i):
            act_grad(i)

            @pl.when(i == 0)
            def _():
                spread.hop(2)

            @pl.when(i == 1)
            def _():
                spread.hop(3)

            per = raw_steps // steps
            loop(i * per, (i + 1) * per, part_weights)

        def continuations():
            far[0] = every[sc[3]]
            far[1] = every[sc[4]]
            stores.append(store(far, far_h))

            def attend(j):
                r0 = pl.multiple_of(PLEN + j * CLEN, CLEN)
                own = pl.ds(r0, CLEN)
                for g in range(2):
                    lanes = slice(g * HD, (g + 1) * HD)
                    vlanes = slice(kvw + g * HD, kvw + (g + 1) * HD)
                    qs = stack_heads(q, r0, g)
                    sf = dt(qs, far[j, :, lanes])
                    so = jnp.where(mask, dt(qs, kv[own, lanes]), MASKED_SCORE)
                    p = softmax_low(jnp.concatenate([sf, so], axis=1))
                    pc[2 * j + g] = p
                    keep_o((dn(p[:, :PLEN], far[j, :, vlanes]) + dn(p[:, PLEN:], kv[own, vlanes])).astype(BF), r0, g)

            loop(0, CONT_DEV, attend)
            stores.append(store(pc, pc_h))
            stores.append(store(o, o_h))
            project(PLEN, hcn, snd_c)
            sum_c.begin()

        sum_p.middle()
        loop(0, steps - 1, both)
        for s in range(4, hi):
            spread.hop(s)
        spread.finish()
        continuations()
        act_grad(steps - 1)
        sum_c.middle()
        loop((steps - 1) * (raw_steps // steps), raw_steps, part_weights)
        load_bm.wait()
        bsplit = dn(evens_first(b2), bm[...].reshape(b2, hidden)).astype(BF)
        zero = jnp.zeros((RK, hidden), BF)
        bflat[:RK, :hidden] = bsplit[:RK]
        bflat[:RK, hidden:] = zero
        bflat[RK:, :hidden] = zero
        bflat[RK:, hidden:] = bsplit[RK:]
        stores.append(store(bflat, wgu_h.at[pl.ds(width, b2)]))
        for c in load_x:
            c.wait()
        for i in range(raw_steps - flats, raw_steps):
            for c in flat_copies(i, i % flats):
                c.wait()
        for c in stores:
            c.wait()

    pl.run_scoped(
        attention,
        VM((rows, wide), BF), VM((rows, width), BF), VM(aT_h.shape, BF), VM(wkv_h.shape, BF), VM(cos_h.shape, F32),
        VM(sin_h.shape, F32), VM(wq_h.shape, BF), VM(bq_h.shape, BF), VM(aoT_h.shape, BF), VM(wo_h.shape, BF), VM(bd_h.shape, BF),
        VM((2, ht, wide), BF), VM((4, 128, 2, hidden), BF), VM((3, 2, 128, hidden), BF), VM((b2, 2 * hidden), BF),
        VM((rows, 2 * kvw), BF), VM((rows, qw), BF), VM((rows, 3 * RK), BF), VM((CONT_DEV, PLEN, 2 * kvw), BF),
        VM((2, 4 * CLEN, 768), BF), VM((4, 4 * CLEN, 4 * CLEN), BF), VM((rows, qw), BF),
    )

    def feed_forward(wcat, wdn, acc, gu, dga, act, gg):
        nt = wdn.shape[2]

        def weights(k, slot):
            i = k % steps
            here = pl.ds(pl.multiple_of(i * ht, ht), ht)
            there = pl.ds(pl.multiple_of(hidden + i * ht, ht), ht)
            return [
                pltpu.make_async_copy(src, dst, wsem.at[slot, n])
                for n, (src, dst) in enumerate(
                    [(wgu_h.at[:, here], wcat.at[slot, :, :ht]), (wgu_h.at[:, there], wcat.at[slot, :, ht:])]
                )
            ]

        def down(n, slot):
            return pltpu.make_async_copy(wd_h.at[:, pl.ds(n * nt, nt)], wdn.at[slot], vsem.at[slot])

        for c in weights(0, 0):
            c.start()
        load_dy = [
            load(dy_h.at[pl.ds(pl.multiple_of(lo * hpn, hpn), hpn)], dyp),
            load(dy_h.at[pl.ds(pl.multiple_of(PLEN + lo * hcn, hcn), hcn)], dyc),
        ]
        for n in range(2):
            down(n, n).start()

        def norm2(which, total, x, h, n2, adapter):
            half = h.shape[0]
            total.end()
            sr = sel_row(adapter)
            uo = (total.mine[:, width : width + RK].astype(F32) + total.theirs[:, width : width + RK].astype(F32)) * sr
            uo = uo.astype(BF)
            tmp[:half] = dn(uo, bo[...])
            gain_two = gain2[...].astype(F32).reshape(1, width)

            def one(r):
                here = pl.ds(r, 64)
                hv = (
                    x[here].astype(F32)
                    + (total.mine[here, :width].astype(F32) + total.theirs[here, :width].astype(F32))
                    + tmp[here]
                )
                h[here] = hv
                inv = lax.rsqrt(jnp.mean(hv * hv, axis=-1, keepdims=True) + EPSILON)
                n2[lo, here, :width] = (hv * inv * gain_two).astype(BF)

            rows_loop(half, 64, one)
            n2[lo, :, width:] = jnp.concatenate([uo, jnp.zeros((half, LANE - RK), BF)], axis=1)
            c = remote(n2.at[lo], n2.at[lo], nsem.at[which, 0], nsem.at[which, 1], (d, t ^ 1))
            c.start()
            return c

        def arrived(which, n2):
            remote(n2.at[1 - lo], n2.at[1 - lo], nsem.at[which, 0], nsem.at[which, 1], (d, t ^ 1)).wait_recv()

        def begin(n2, uo, chosen):
            half = n2.shape[1]
            r = 2 * half
            um = dt(n2[:, :, :width].reshape(r, width), amT[...])
            um = jnp.concatenate([(um[:, :RK] * chosen).astype(BF), (um[:, RK:] * chosen).astype(BF)], axis=1)
            uo[...] = n2[:, :, width:]
            n2[:, :, width:] = um.reshape(2, half, 2 * RK)
            acc[:r] = jnp.zeros((r, wide), F32)

        def tile(k, n2, base, add):
            r = 2 * n2.shape[1]
            slot = k % 2
            i = k % steps
            for c in weights(k, slot):
                c.wait()

            @pl.when(k + 1 < 2 * steps)
            def _():
                for c in weights(k + 1, 1 - slot):
                    c.start()

            gu[:r] = dn(n2[...].reshape(r, wide), wcat[slot])
            lanes = pl.ds(pl.multiple_of(i * ht, ht), ht)

            def swiglu(r0):
                here = pl.ds(r0, 64)
                gate = gu[here, :ht]
                upper = gu[here, ht:]
                sigma = 1.0 / (1.0 + jnp.exp(-gate))
                silu = gate * sigma
                there = pl.ds(base + r0, 64)
                da = dact[there, lanes].astype(F32)
                dga[here, :ht] = (da * upper * (sigma * (1.0 + gate * (1.0 - sigma)))).astype(BF)
                dga[here, ht : 2 * ht] = (da * silu).astype(BF)
                av = (silu * upper).astype(BF)
                dga[here, 2 * ht :] = av
                act[there, lanes] = av

            for r0 in range(0, r, 64):
                swiglu(r0)
            acc[:r] += dt(dga[:r, : 2 * ht], wcat[slot])
            small = jnp.concatenate([n2[:, :, width:].reshape(r, 2 * RK), dud[base : base + r, :RK]], axis=1)
            g = dr(small, dga[:r])
            for n in range(3):
                part = g[n * RK : (n + 1) * RK, n * ht : (n + 1) * ht]
                if add:
                    total = (gg[n, :, lanes] + part).astype(BF)
                    units = ht // LANE * (RK // 16)
                    put_units(ge, n * (hidden // LANE * (RK // 16)) + i * units, total)
                else:
                    gg[n, :, lanes] = part

        def halves(a, snd):
            half = snd.shape[1]

            def one(r0):
                for n in range(2):
                    snd[n, pl.ds(r0, 64)] = a[pl.ds(pl.multiple_of(n * half + r0, 64), 64)].astype(BF)

            rows_loop(half, 64, one)

        n2_copy_p = norm2(0, sum_p, xp, hp, n2p, sc[0])
        store_hp = store(hp, hp_h)
        arrived(0, n2p)
        n2_copy_p.wait_send()
        store_n2p = store(n2p.at[:, :, qlanes], n2p_h)
        begin(n2p, uop, sel_row(sc[0]))
        tail_stores = [store(uop, uop_h)]

        loop(0, steps, lambda k: tile(k, n2p, 0, False))
        sum_p.drain()
        halves(acc, snd_p)
        store_n2p.wait()
        sum2_p = TensorSum(snd_p, got1_p, s_p, t1_p, psem2, d, t)
        sum2_p.begin()

        n2_copy_c = norm2(1, sum_c, xc, hc, n2c, adapter_c)
        store_hc = store(hc, hc_h)
        sum2_p.middle()
        arrived(1, n2c)
        n2_copy_c.wait_send()
        store_n2c = store(n2c.at[:, :, qlanes], n2c_h)
        begin(
            n2c, uoc,
            jnp.concatenate([jnp.broadcast_to(sel_row(sc[1]), (hcn, RK)), jnp.broadcast_to(sel_row(sc[2]), (hcn, RK))], axis=0),
        )
        tail_stores.append(store(uoc, uoc_h))

        loop(steps, 2 * steps, lambda k: tile(k, n2c, PLEN, True))
        sum_c.drain()
        halves(acc, snd_c)
        store_n2c.wait()
        sum2_c = TensorSum(snd_c, got1_c, s_c, t1_c, csem2, d, t)
        sum2_c.begin()
        reduce = DirectReduce(ge, gots, ge, (g0, g1, None, None), d, t, n_dp)
        reduce.start()

        ud = dt(act[...], adT[...]).astype(BF)
        sum2_c.middle()
        sum2_p.core.wait_send()
        sum2_c.core.wait_send()
        pad = jnp.zeros((hpn, LANE - RK), BF)
        for n in range(2):
            snd_p[n, :, width:] = jnp.concatenate([ud[n * hpn : (n + 1) * hpn], pad], axis=1)
            snd_c[n, :, width:] = jnp.concatenate([ud[PLEN + n * hcn : PLEN + (n + 1) * hcn], pad[:hcn]], axis=1)

        def project_down(n):
            slot = n % 2
            down(n, slot).wait()
            part = dn(act[...], wdn[slot]).astype(BF)
            lanes = pl.ds(pl.multiple_of(n * nt, nt), nt)
            for i in range(2):
                snd_p[i, :, lanes] = part[i * hpn : (i + 1) * hpn]
                snd_c[i, :, lanes] = part[PLEN + i * hcn : PLEN + (i + 1) * hcn]

            @pl.when(n + 2 < width // nt)
            def _():
                down(n + 2, slot).start()

        loop(0, width // nt, project_down)
        mcore_p = remote(snd_p.at[1 - lo], got0_p, msem.at[0], msem.at[1], (d, t ^ 1))
        mcore_p.start()
        mcore_c = remote(snd_c.at[1 - lo], got0_c, msem.at[2], msem.at[3], (d, t ^ 1))
        mcore_c.start()

        def mlp_sum(core, snd, got, out):
            core.wait_recv()

            def add(r0):
                here = pl.ds(r0, 64)
                got[here] = (snd[lo, here].astype(F32) + got[here].astype(F32)).astype(BF)

            rows_loop(got.shape[0], 64, add)
            tail_stores.append(store(got, out))

        def back(which, total, h, dy, da, adapter):
            half = h.shape[0]
            total.end()
            sr = sel_row(adapter)
            du = total.mine[:, width:].astype(F32) + total.theirs[:, width:].astype(F32)
            dum = (du * jnp.concatenate([sr, sr], axis=1)).astype(BF)
            tmp[:half] = dn(dum, amT[...])
            gain = gain2[...].astype(F32).reshape(1, width)

            def one(r0):
                here = pl.ds(r0, 64)
                dn2 = total.mine[here, :width].astype(F32) + total.theirs[here, :width].astype(F32) + tmp[here]
                dh = dy[here].astype(F32) + norm_back(h[here], gain, dn2)
                h[here] = dh
                da[lo, here, :width] = dh.astype(BF)

            rows_loop(half, 64, one)
            da[lo, :, width:] = dum
            c = remote(da.at[lo], da.at[lo], nsem.at[which, 0], nsem.at[which, 1], (d, t ^ 1))
            c.start()
            return c

        for c in load_dy:
            c.wait()
        store_hp.wait()
        store_hc.wait()
        copy_p = back(2, sum2_p, hp, dyp, n2p, sc[0])
        tail_stores.append(store(hp, dhp_h))
        mlp_sum(mcore_p, snd_p, got0_p, smp_h)
        mlp_sum(mcore_c, snd_c, got0_c, smc_h)
        arrived(2, n2p)
        tail_stores.append(store(n2p, dap_h))
        reduce.add()
        tail_stores.append(store(ge.at[reduce.part(d)], ge_h))
        copy_c = back(3, sum2_c, hc, dyc, n2c, adapter_c)
        tail_stores.append(store(hc, dhc_h))
        arrived(3, n2c)
        tail_stores.append(store(n2c, dac_h))
        copy_p.wait_send()
        copy_c.wait_send()
        sum2_p.chip.wait_send()
        sum2_c.chip.wait_send()
        mcore_p.wait_send()
        mcore_c.wait_send()
        reduce.sent()
        for c in tail_stores:
            c.wait()

    pl.run_scoped(
        feed_forward,
        VM((2, wide, 2 * ht), BF), VM((2, hidden, 512), BF), VM((PLEN, wide), F32), VM((PLEN, 2 * ht), F32), VM((PLEN, 3 * ht), BF),
        VM((rows, hidden), BF), VM((3, RK, hidden), F32),
    )


def first(n_dp, scalars, small, large):
    tok, aT, wkv, cos, sin, wq, bq, aoT, wo, dy, bd, wd, raw = large
    rows, width = tok.shape
    qw = wq.shape[1]
    kvw2 = wkv.shape[1]
    hidden = wd.shape[0]
    quarter = width // 2
    wide = width + LANE
    hpn, hcn = PLEN // 2, CLEN
    units = 3 * hidden // LANE * (RK // 16)
    share = units // n_dp
    outs = [
        ((rows, quarter), BF), ((rows, qw), BF), ((rows, kvw2), BF), ((rows, 3 * RK), BF), ((2, 4 * CLEN, 768), BF),
        ((4, 4 * CLEN, 4 * CLEN), BF), ((rows, qw), BF), ((CONT_DEV, PLEN, kvw2), BF), ((hpn, width), F32),
        ((hcn, width), F32), ((2, hpn, quarter), BF), ((2, hcn, quarter), BF), ((2, hpn, LANE), BF), ((2, hcn, LANE), BF),
        ((width + 2 * RK, 2 * hidden), BF),
        ((hpn, width), F32), ((hcn, width), F32), ((2, hpn, wide), BF), ((2, hcn, wide), BF), ((hpn, wide), BF),
        ((hcn, wide), BF), ((share, *UNIT), BF),
    ]
    dma = pltpu.SemaphoreType.DMA
    scratch = [
        VM((n_dp, PLEN, kvw2), BF), VM((2, hpn, wide), BF), VM((hpn, wide), BF), VM((2, hcn, wide), BF), VM((hcn, wide), BF),
    ] + [VM((hpn, wide), BF), VM((hpn, wide), BF), VM((hcn, wide), BF), VM((hcn, wide), BF)] * 2 + [
        VM((2, hpn, wide), BF), VM((2, hcn, wide), BF), VM((2, hpn, LANE), BF), VM((2, hcn, LANE), BF),
        VM((hpn, width), F32), VM((hcn, width), F32), VM((hpn, width), BF), VM((hcn, width), BF), VM((hpn, width), BF),
        VM((hcn, width), BF), VM((rows, hidden), BF), VM((rows, LANE), BF), VM((hpn, width), F32),
        VM((units, *UNIT), BF), VM((n_dp, share, *UNIT), BF),
        VM((RK, 2, hidden), BF), VM((2 * RK, width), BF), VM((RK, hidden), BF), VM((RK, width), BF),
        dma((20,)), dma((22,)), dma((2, 2)), dma((4,)), dma((4, 2)), dma((2,)), dma((4,)), dma((4,)), dma((4,)), dma((4,)),
        dma((4,)), dma((4, 2)),
    ] + [dma((n_dp // 2 + 1,))] * 6 + [dma((n_dp,))] * 2
    vm = pl.BlockSpec(memory_space=VM)
    anyspace = pl.BlockSpec(memory_space=pl.ANY)
    return pl.pallas_call(
        functools.partial(first_kernel, n_dp),
        out_shape=[jax.ShapeDtypeStruct(s, dtype) for s, dtype in outs],
        in_specs=[pl.BlockSpec(memory_space=pltpu.SMEM)] * 3 + [vm] * 3 + [anyspace] * (len(small) - 3 + len(large)),
        out_specs=[anyspace] * len(outs),
        scratch_shapes=scratch,
        compiler_params=pltpu.CompilerParams(vmem_limit_bytes=127 << 19, collective_id=1, has_side_effects=True),
        cost_estimate=pl.CostEstimate(flops=12 * rows * width * hidden, bytes_accessed=120 << 20, transcendentals=0),
        name="first",
    )(*scalars, *small, *large)


class Fold:
    def __init__(self, dfar, xr, zs, zr, sems, owners, others, d, t, hi):
        self.dfar, self.xr, self.zs, self.zr, self.sems = dfar, xr, zs, zr, sems
        self.owners, self.others, self.d, self.t, self.hi = owners, others, d, t, hi
        self.z, self.x = d // 2, d % 2

    def across(self, j):
        return remote(self.dfar.at[j], self.xr.at[j], self.sems[0].at[j], self.sems[1].at[j], (self.d ^ 1, self.t))

    def along(self, z, come=False):
        slot = z if come else self.z
        return remote(
            self.zr.at[slot] if come else self.zs.at[z], self.zr.at[slot], self.sems[2].at[z], self.sems[3].at[slot],
            (z * 2 + self.x, self.t),
        )

    def held(self, z, rows):
        dest = z * 2 + self.x
        total = None
        for parts, owners in ((self.dfar, self.owners), (self.xr, self.others)):
            for j in range(CONT_DEV):
                term = parts[j, rows].astype(F32) * (owners[j] == dest).astype(F32)
                total = term if total is None else total + term
        return total

    def fold(self):
        for j in range(CONT_DEV):
            self.across(j).wait_recv()
        order = sorted(range(self.hi), key=lambda z: min(z, self.hi - 1 - z))
        for z in order:

            @pl.when(self.z != z)
            def _(z=z):
                def put(r):
                    rows = pl.ds(r, 64)
                    self.zs[z, rows] = self.held(z, rows).astype(BF)

                rows_loop(PLEN, 64, put)
                self.along(z).start()

    def finish(self, total):
        def own(r):
            rows = pl.ds(r, 64)
            total[rows] += self.held(self.z, rows)

        rows_loop(PLEN, 64, own)
        for z in range(self.hi):

            @pl.when(self.z != z)
            def _(z=z):
                self.along(z, True).wait_recv()
                total[...] += self.zr[z].astype(F32)

    def drain(self):
        for j in range(CONT_DEV):
            self.across(j).wait_send()
        for z in range(self.hi):

            @pl.when(self.z != z)
            def _(z=z):
                self.along(z).wait_send()


def back_kernel(
    n_dp, ids_p, ids_c, group_map, gain1, bkv_ref,
    dac_h, wo_h, o_h, aoT_h, bo_h, n2c_h, uoc_h, q_h, kv_h, far_h, pc_h, cos_h, sin_h, dap_h, pp_h, n2p_h, uop_h, u_h, wq_h, wkv_h, bq_h,
    smp_h, hp_h, bd_h, smc_h, hc_h, dy_h, n1q_h, dhc_h, aT_h, dhp_h, tok_h, ge_h,
    out_h, tg_h, gef_h, l0_h, t1_h, t2_h,
    dac, wo, o, aoT, bo, n2c, uoc, q, kv, far, pc, cos, sin, dap, pp, n2p, uop, u, wq, wkv, bq,
    smp, hp, bd, smc, hc, aT, xc, xp, gef, tmp_p, tmp_c,
    do, dqp, dkv, dkvp, dfar, gacc, snd_p, got_p, s_p, t_p, snd_c, got_c, s_c, t_c,
    dsnd_p, dgot_p, ds_p, dt_p, dsnd_c, dgot_c, ds_c, dt_c, dup, duc, outp, outc, tgp, tgc, tmp,
    l0s, l0x, l0z, l0, l1s, l1x, l1z, l2s, l2x, l2z, t1, t2, xr, zs, zr,
    lsem, osem, dsem, ysem, psem, csem, dpsem, dcsem, nsem, q1, q2, f0, f1, f2, f3, *rsems,
):
    d, t = place()
    sc = [ids_p[0], ids_c[0], ids_c[1], group_map[d * CONT_DEV], group_map[d * CONT_DEV + 1]]
    lo = t % 2
    hi = n_dp // 2
    width = wq.shape[0]
    qw = wq.shape[1]
    kvw = wkv.shape[1] // 2
    quarter = n1q_h.shape[1]
    hpn, hcn = PLEN // 2, CLEN
    greet(d, t, n_dp)
    qlanes = pl.ds(pl.multiple_of(lo * quarter, quarter), quarter)
    every = PairReduce(None, None, None, gef, rsems[0:8], d, t, n_dp)
    pairs = [
        (ge_h, gef.at[every.part(d // 2)]), (dac_h, dac), (wo_h, wo), (o_h, o), (aoT_h, aoT), (bo_h, bo), (n2c_h, n2c),
        (uoc_h, uoc), (q_h, q), (kv_h, kv), (far_h, far), (pc_h, pc), (cos_h, cos), (sin_h, sin), (dap_h, dap),
        (pp_h, pp), (n2p_h, n2p), (uop_h, uop), (u_h, u), (wq_h, wq), (wkv_h, wkv), (bq_h, bq),
        (smp_h, smp), (hp_h, hp), (bd_h, bd), (smc_h, smc), (hc_h, hc),
        (aT_h, aT), (tok_h.at[pl.ds(pl.multiple_of(PLEN + lo * hcn, hcn), hcn)], xc),
        (tok_h.at[pl.ds(pl.multiple_of(lo * hpn, hpn), hpn)], xp),
    ]
    loads = {}

    def fetch(first, last):
        for n in range(first, last):
            src, dst = pairs[n]
            c = pltpu.make_async_copy(src, dst, lsem.at[n])
            c.start()
            loads[id(dst) if n else 0] = c

    fetch(0, 14)

    def need(*refs):
        for ref in refs:
            loads.pop(id(ref)).wait()

    stores = []

    def store(src, dst):
        c = pltpu.make_async_copy(src, dst, osem.at[len(stores)])
        c.start()
        stores.append(c)

    greeted(n_dp)
    mlp_p = remote(smp_h, tmp_p, ysem.at[0], ysem.at[1], (d, t ^ 2))
    mlp_p.start()
    mlp_c = remote(smc_h, tmp_c, ysem.at[2], ysem.at[3], (d, t ^ 2))
    mlp_c.start()
    loads.pop(0).wait()
    every.spread()

    at = np.cumsum([0, quarter, quarter, quarter, qw, qw, 2 * kvw]).tolist()
    bkv = dn(evens_first(2 * RK), bkv_ref[...].reshape(2 * RK, kvw)).astype(BF)

    def out_grads(da, n2, uo, sel, r0, first):
        half = da.shape[1]
        r = 2 * half
        dav = da[:, :, :width].reshape(r, width)
        duo = (dt(dav, bo[...]) * sel).astype(BF)
        do[r0 : r0 + r] = (dt(dav, wo[...]) + dn(duo, aoT[...])).astype(BF)
        gao = dr(duo, o[r0 : r0 + r])
        dum = da[:, :, width:].reshape(r, 2 * RK)
        gam = dr(dum, n2[...].reshape(r, quarter))
        gbo = dr(uo[:, :, :RK].reshape(r, RK), da[:, :, qlanes].reshape(r, quarter))
        parts = (gbo, gam[:RK], gam[RK:], gao)
        for n, part in enumerate(parts):
            lanes = slice(at[n], at[n + 1])
            gacc[:, lanes] = part if first else gacc[:, lanes] + part

    def unrotate(r0, r):
        here = slice(r0, r0 + r)
        for c in range(qw // LANE):
            lanes = slice(c * LANE, (c + 1) * LANE)
            dqp[here, lanes] = rot(dqp[here, lanes].astype(F32), cos[here], -sin[here]).astype(BF)
        dkvp[here, :kvw] = rot(dkv[here, :kvw].astype(BF).astype(F32), cos[here], -sin[here]).astype(BF)
        dkvp[here, kvw:] = dkv[here, kvw:].astype(BF)

    need(dac, wo, o, aoT, bo, n2c, uoc)
    sel_c = jnp.concatenate([jnp.broadcast_to(sel_row(sc[1]), (hcn, RK)), jnp.broadcast_to(sel_row(sc[2]), (hcn, RK))], axis=0)
    out_grads(dac, n2c, uoc, sel_c, PLEN, True)
    fetch(14, 22)
    need(q, kv, far, pc)

    def attend(j):
        r0 = pl.multiple_of(PLEN + j * CLEN, CLEN)
        own = pl.ds(r0, CLEN)
        for g in range(2):
            lanes = slice(g * HD, (g + 1) * HD)
            vlanes = slice(kvw + g * HD, kvw + (g + 1) * HD)
            qi = stack_heads(q, r0, g)
            doi = stack_heads(do, r0, g)
            p = pc[2 * j + g]
            dp = jnp.concatenate([dt(doi, far[j, :, vlanes]), dt(doi, kv[own, vlanes])], axis=1)
            ds = back_scores(p, dp)
            dqv = dn(ds[:, :PLEN], far[j, :, lanes]) + dn(ds[:, PLEN:], kv[own, lanes])
            put_dq((dqv * 0.125).astype(BF), dqp, r0, g)
            dk = dr(ds, qi)
            dv = dr(p, doi)
            dfar[j, :, lanes] = dk[:PLEN].astype(BF)
            dfar[j, :, vlanes] = dv[:PLEN].astype(BF)
            dkv[own, lanes] = dk[PLEN:]
            dkv[own, vlanes] = dv[PLEN:]
        fold.across(j).start()

    mate = (d ^ 1) * CONT_DEV
    others = [group_map[mate + j] for j in range(CONT_DEV)]
    fold = Fold(dfar, xr, zs, zr, (f0, f1, f2, f3), sc[3:], others, d, t, hi)
    loop(0, CONT_DEV, attend)
    fetch(22, len(pairs))
    need(cos, sin)
    unrotate(PLEN, 2 * hcn)

    def dn1(r0, snd, dsnd, dsum, first):
        half = snd.shape[1]
        r = 2 * half
        here = slice(r0, r0 + r)
        a, b = dqp[here], dkvp[here]
        du = jnp.concatenate(
            [dt(a, bq[...]), dt(b[:, :kvw], bkv[:RK]), dt(b[:, kvw:], bkv[RK:]), jnp.zeros((r, RK), F32)], axis=1
        ).astype(BF)
        dsnd[0] = du[:half]
        dsnd[1] = du[half:]
        dsum.begin()

        def columns(n):
            lanes = pl.ds(pl.multiple_of(n * 512, 512), 512)
            part = (dt(a, wq[lanes]) + dt(b, wkv[lanes])).astype(BF)
            snd[0, :, lanes] = part[:half]
            snd[1, :, lanes] = part[half:]

        loop(0, width // 512, columns)
        gbq = dr(u[here, :RK], a)
        gkv = dr(u[here, RK:], b)
        parts = (gbq, gkv[:RK, :kvw], gkv[RK:, kvw:])
        for part, start in zip(parts, (at[4], at[5], at[5] + kvw)):
            lanes = slice(start, start + part.shape[1])
            gacc[:, lanes] = part if first else gacc[:, lanes] + part

    need(wq, wkv, u, bq)
    dsum_c = TensorSum(dsnd_c, dgot_c, ds_c, dt_c, dcsem, d, t)
    dn1(PLEN, snd_c, dsnd_c, dsum_c, True)
    sum_c = TensorSum(snd_c, got_c, s_c, t_c, csem, d, t)
    sum_c.begin()
    fold.fold()

    need(dap, n2p, uop)
    out_grads(dap, n2p, uop, jnp.broadcast_to(sel_row(sc[0]), (PLEN, RK)), 0, False)
    load_dy = []
    for n in range(2):
        for ref, start, half in ((dap, n * hpn, hpn), (dac, PLEN + n * hcn, hcn)):
            here = pl.ds(start, half)
            for src, lanes in ((dy_h.at[here, qlanes], slice(0, quarter)), (n1q_h.at[here], slice(quarter, 2 * quarter))):
                c = pltpu.make_async_copy(src, ref.at[n, :, lanes], dsem.at[len(load_dy)])
                c.start()
                load_dy.append(c)
    dsum_c.middle()
    sum_c.middle()
    need(pp)
    for g in range(2):
        lanes = slice(g * HD, (g + 1) * HD)
        vlanes = slice(kvw + g * HD, kvw + (g + 1) * HD)
        kg = kv[:PLEN, lanes]
        vg = kv[:PLEN, vlanes]
        for i in reversed(range(PLEN // CLEN)):
            size = (i + 1) * CLEN
            qi = stack_heads(q, i * CLEN, g)
            doi = stack_heads(do, i * CLEN, g)
            p = pp[g, :, P_OFF[i] : P_OFF[i] + size]
            ds = back_scores(p, dt(doi, vg[:size]))
            put_dq((dn(ds, kg[:size]) * 0.125).astype(BF), dqp, i * CLEN, g)
            dk = dr(ds, qi)
            dv = dr(p, doi)
            if size == PLEN:
                dkv[:size, lanes] = dk
                dkv[:size, vlanes] = dv
            else:
                dkv[:size, lanes] += dk
                dkv[:size, vlanes] += dv
    every.cross()

    def finish_out(which, sm, theirs, copy, h, out, r0, adapter):
        half = h.shape[0]
        copy.wait_recv()
        sr = sel_row(adapter)
        ud = ((sm[:, width : width + RK].astype(F32) + theirs[:, width : width + RK].astype(F32)) * sr).astype(BF)
        tmp[:half] = dn(ud, bd[...])

        def one(r):
            here = pl.ds(r, 64)
            out[lo, here, :width] = (
                h[here] + (sm[here, :width].astype(F32) + theirs[here, :width].astype(F32)) + tmp[here]
            ).astype(BF)

        rows_loop(half, 64, one)
        out[lo, :, width:] = jnp.concatenate([ud, jnp.zeros((half, LANE - RK), BF)], axis=1)
        c = remote(out.at[lo], out.at[lo], nsem.at[which, 0], nsem.at[which, 1], (d, t ^ 1))
        c.start()
        return c

    def arrived(which, out):
        remote(out.at[1 - lo], out.at[1 - lo], nsem.at[which, 0], nsem.at[which, 1], (d, t ^ 1)).wait_recv()

    need(smp, hp, bd)
    out_copy_p = finish_out(0, smp, tmp_p, mlp_p, hp, outp, 0, sc[0])
    load_dhp = pltpu.make_async_copy(dhp_h, hp, lsem.at[32])
    load_dhp.start()

    adapter_c = jnp.where(lo == 0, sc[1], sc[2])
    per = quarter // LANE * (RK // 16)

    def fill(blocks, used):
        if blocks.shape[0] > used:
            blocks[used:] = jnp.zeros((blocks.shape[0] - used, *UNIT), BF)

    def share_du(which, total, du, adapter):
        total.end()
        sr = sel_row(adapter)
        raw = total.mine[:, : 3 * RK].astype(F32) + total.theirs[:, : 3 * RK].astype(F32)
        duq = (raw * jnp.concatenate([sr, sr, sr], axis=1)).astype(BF)
        du[lo] = jnp.concatenate([duq, jnp.zeros((duq.shape[0], RK), BF)], axis=1)
        c = remote(du.at[lo], du.at[lo], nsem.at[which, 0], nsem.at[which, 1], (d, t ^ 1))
        c.start()
        return c

    need(smc, hc, aT)
    out_copy_c = finish_out(1, smc, tmp_c, mlp_c, hc, outc, PLEN, adapter_c)
    load_dhc = pltpu.make_async_copy(dhc_h, hc, lsem.at[33])
    load_dhc.start()
    du_copy_c = share_du(4, dsum_c, duc, adapter_c)
    for c in load_dy:
        c.wait()
    arrived(0, outp)
    gbd = dr(outp[:, :, width : width + RK].reshape(PLEN, RK), dap[:, :, :quarter].reshape(PLEN, quarter))
    arrived(1, outc)
    gbd = gbd + dr(outc[:, :, width : width + RK].reshape(2 * hcn, RK), dac[:, :, :quarter].reshape(2 * hcn, quarter))

    put_units(l1s, 0, gacc[:, : at[3]].astype(BF))
    put_units(l1s, 3 * per, gbd.astype(BF))
    fill(l1s, 4 * per)
    red1 = PairReduce(l1s, l1x, l1z, t1.at[lo], rsems[8:16], d, t, n_dp)
    red1.start()
    trade1 = Trade(t1, q1, d, t)
    for n in range(2):
        store(outp.at[n, :, :width], out_h.at[pl.ds(n * hpn, hpn)])
        store(outc.at[n, :, :width], out_h.at[pl.ds(PLEN + n * hcn, hcn)])
    arrived(4, duc)
    ga_c = dr(duc[:, :, : 3 * RK].reshape(2 * hcn, 3 * RK), dac[:, :, quarter : 2 * quarter].reshape(2 * hcn, quarter))

    fold.finish(dkv.at[:PLEN])
    unrotate(0, PLEN)
    dsum_p = TensorSum(dsnd_p, dgot_p, ds_p, dt_p, dpsem, d, t)
    dn1(0, snd_p, dsnd_p, dsum_p, False)
    sum_p = TensorSum(snd_p, got_p, s_p, t_p, psem, d, t)
    dsum_p.middle()
    sum_p.begin()
    put_units(l0s, 0, gacc[:, at[3] :].astype(BF))
    fill(l0s, (at[6] - at[3]) // LANE * (RK // 16))
    red0 = PairReduce(l0s, l0x, l0z, l0, rsems[16:24], d, t, n_dp)
    red0.start()
    sum_p.middle()
    red1.middle()
    du_copy_p = share_du(5, dsum_p, dup, sc[0])
    arrived(5, dup)
    ga_p = dr(dup[:, :, : 3 * RK].reshape(PLEN, 3 * RK), dap[:, :, quarter : 2 * quarter].reshape(PLEN, quarter))
    ga = (ga_c + ga_p).astype(BF)
    for n in range(3):
        put_units(l2s, n * per, ga[n * RK : (n + 1) * RK])
    fill(l2s, 3 * per)
    red2 = PairReduce(l2s, l2x, l2z, t2.at[lo], rsems[24:32], d, t, n_dp)
    red2.start()
    trade2 = Trade(t2, q2, d, t)

    def last(which, total, du, x, dh, tg):
        half = x.shape[0]
        tmp[:half] = dn(du[lo, :, : 3 * RK], aT[...])
        gain = gain1[...].astype(F32).reshape(1, width)
        total.end()

        def one(r):
            here = pl.ds(r, 64)
            dn1v = total.mine[here].astype(F32) + total.theirs[here].astype(F32) + tmp[here]
            grad = dh[here] + norm_back(x[here].astype(F32), gain, dn1v)
            tg[lo, here] = grad.astype(BF)

        rows_loop(half, 64, one)
        c = remote(tg.at[lo], tg.at[lo], nsem.at[which, 0], nsem.at[which, 1], (d, t ^ 1))
        c.start()
        return c

    red1.add()
    red0.middle()
    need(xc)
    load_dhc.wait()
    tg_copy_c = last(2, sum_c, duc, xc, hc, tgc)
    red2.middle()
    red1.cross()
    red0.add()
    every.finish()
    store(gef, gef_h)
    red2.add()
    arrived(2, tgc)
    for n in range(2):
        store(tgc.at[n], tg_h.at[pl.ds(PLEN + n * hcn, hcn)])
    red0.cross()
    red1.finish()
    trade1.start()
    red2.cross()
    trade1.finish()
    store(t1, t1_h)
    need(xp)
    load_dhp.wait()
    tg_copy_p = last(3, sum_p, dup, xp, hp, tgp)
    red0.finish()
    store(l0, l0_h)
    red2.finish()
    trade2.start()
    arrived(3, tgp)
    for n in range(2):
        store(tgp.at[n], tg_h.at[pl.ds(n * hpn, hpn)])
    trade2.finish()
    store(t2, t2_h)
    for c in (out_copy_p, out_copy_c, tg_copy_c, tg_copy_p, du_copy_c, du_copy_p, mlp_p, mlp_c):
        c.wait_send()
    for total in (sum_p, sum_c, dsum_p, dsum_c):
        total.drain()
    fold.drain()
    every.spread_sent()
    for red in (red0, red1, red2):
        red.sent()
        red.spread_sent()
    trade1.sent()
    trade2.sent()
    for c in stores:
        c.wait()


def backward(n_dp, scalars, small, large):
    (dac, wo, o, aoT, bo, n2c, uoc, q, kv, far, pc, cos, sin, dap, pp, n2p, uop, u, wq, wkv, bq, smp, hp, bd, smc, hc, dy, n1q,
     dhc, aT, dhp, tok, ge) = large
    rows, width = tok.shape
    qw = wq.shape[1]
    kvw2 = wkv.shape[1]
    quarter = n1q.shape[1]
    wide = dap.shape[2]
    hpn, hcn = PLEN // 2, CLEN
    per = quarter // LANE * (RK // 16)
    up = lambda a: -(-a // n_dp) * n_dp
    ue = ge.shape[0] * n_dp
    u0 = up((2 * qw + kvw2) // LANE * (RK // 16))
    u1 = up(4 * per)
    u2 = up(3 * per)
    outs = [
        ((rows, width), BF), ((rows, width), BF), ((ue, *UNIT), BF), ((u0, *UNIT), BF), ((2, u1, *UNIT), BF),
        ((2, u2, *UNIT), BF),
    ]
    dma = pltpu.SemaphoreType.DMA
    hi = n_dp // 2
    same = lambda a: VM(a.shape, a.dtype)

    def sums(half, n):
        return [VM((2, half, n), BF), VM((half, n), BF), VM((half, n), BF), VM((half, n), BF)]

    scratch = [
        same(dac), same(wo), same(o), same(aoT), same(bo), VM((2, hcn, quarter), BF), VM((2, hcn, LANE), BF), same(q), same(kv),
        same(far), same(pc), same(cos), same(sin), same(dap), same(pp), VM((2, hpn, quarter), BF), VM((2, hpn, LANE), BF),
        same(u), same(wq), same(wkv), same(bq), same(smp), same(hp), same(bd), same(smc), same(hc),
        same(aT), VM((hcn, width), BF), VM((hpn, width), BF), VM((ue, *UNIT), BF),
        same(smp), same(smc),
        VM((rows, qw), BF), VM((rows, qw), BF), VM((rows, kvw2), F32), VM((rows, kvw2), BF),
        VM((CONT_DEV, PLEN, kvw2), BF), VM((RK, 2 * qw + 3 * quarter + kvw2), F32),
        *sums(hpn, width), *sums(hcn, width), *sums(hpn, 2 * LANE), *sums(hcn, 2 * LANE),
        VM((2, hpn, 2 * LANE), BF), VM((2, hcn, 2 * LANE), BF),
        VM((2, hpn, wide), BF), VM((2, hcn, wide), BF), VM((2, hpn, width), BF), VM((2, hcn, width), BF), VM((hpn, width), F32),
        VM((u0, *UNIT), BF), VM((u0 // 2, *UNIT), BF), VM((hi, u0 // n_dp, *UNIT), BF), VM((u0, *UNIT), BF),
        VM((u1, *UNIT), BF), VM((u1 // 2, *UNIT), BF), VM((hi, u1 // n_dp, *UNIT), BF),
        VM((u2, *UNIT), BF), VM((u2 // 2, *UNIT), BF), VM((hi, u2 // n_dp, *UNIT), BF),
        VM((2, u1, *UNIT), BF), VM((2, u2, *UNIT), BF),
        VM((CONT_DEV, PLEN, kvw2), BF), VM((hi, PLEN, kvw2), BF), VM((hi, PLEN, kvw2), BF),
        dma((34,)), dma((13,)), dma((8,)), dma((4,)), dma((4,)), dma((4,)), dma((4,)), dma((4,)), dma((6, 2)), dma((2,)), dma((2,)),
    ] + [dma((CONT_DEV,))] * 2 + [dma((hi,))] * 2 + [dma((n_dp,))] * 32
    vm = pl.BlockSpec(memory_space=VM)
    anyspace = pl.BlockSpec(memory_space=pl.ANY)
    return pl.pallas_call(
        functools.partial(back_kernel, n_dp),
        out_shape=[jax.ShapeDtypeStruct(s, dtype) for s, dtype in outs],
        in_specs=[pl.BlockSpec(memory_space=pltpu.SMEM)] * 3 + [vm] * len(small) + [anyspace] * len(large),
        out_specs=[anyspace] * len(outs),
        scratch_shapes=scratch,
        compiler_params=pltpu.CompilerParams(vmem_limit_bytes=63 << 20, collective_id=3, has_side_effects=True),
        cost_estimate=pl.CostEstimate(flops=6 * rows * width * (2 * qw + kvw2), bytes_accessed=40 << 20, transcendentals=0),
        name="back",
    )(*scalars, *small, *large)


def emit_kernel(
    qw, kvw, quarter, hidden, ge, l0, t1, t2, out_h, tg_h,
    gbm_o, gad_o, gao_o, gbq_o, gbkv_o, gbo_o, gam_o, gbd_o, ga_o, out_o, tg_o,
    gbm, gad, gao, gbq, gbkv, gbo, gam, gbd, ga, buf, sem, wsem,
):
    pairs = ((out_h, out_o), (tg_h, tg_o))
    copies = [pltpu.make_async_copy(src, buf.at[n], sem.at[n]) for n, (src, _) in enumerate(pairs)]
    for c in copies:
        c.start()
    high = RK // 16
    writes = []

    def write(src, dst):
        c = pltpu.make_async_copy(src, dst, wsem.at[len(writes)])
        c.start()
        writes.append(c)

    def take(blocks, first, count, put):
        for b in range(count // LANE):
            for r in range(high):
                put(slice(r * 16, (r + 1) * 16), slice(b * LANE, (b + 1) * LANE), blocks[first + b * high + r].astype(F32))

    def plain(dst, row=0, lane=0):
        def put(rows, lanes, value):
            dst[rows.start + row : rows.stop + row, lanes.start + lane : lanes.stop + lane] = value

        return put

    def paired(dst, n):
        def put(rows, lanes, value):
            dst[rows, n, lanes] = value

        return put

    seg = hidden // LANE * high
    take(ge, 2 * seg, hidden, plain(gad))
    write(gad, gad_o)
    take(ge, 0, hidden, paired(gbm, 0))
    take(ge, seg, hidden, paired(gbm, 1))
    write(gbm, gbm_o)
    for n, (c, (_, dst)) in enumerate(zip(copies, pairs)):
        c.wait()
        write(buf.at[n], dst)
    per = quarter // LANE * high
    for t in range(t1.shape[0]):
        take(t1.at[t], 0, quarter, plain(gbo, 0, t * quarter))
        take(t1.at[t], per, quarter, plain(gam, 0, t * quarter))
        take(t1.at[t], 2 * per, quarter, plain(gam, RK, t * quarter))
        take(t1.at[t], 3 * per, quarter, plain(gbd, 0, t * quarter))
        for n in range(3):
            take(t2.at[t], n * per, quarter, plain(ga, n * RK, t * quarter))
    write(gbo, gbo_o)
    write(gam, gam_o)
    write(gbd, gbd_o)
    write(ga, ga_o)
    take(l0, 0, qw, plain(gao))
    write(gao, gao_o)
    begin = qw // LANE * high
    take(l0, begin, qw, plain(gbq))
    write(gbq, gbq_o)
    take(l0, 2 * begin, kvw, paired(gbkv, 0))
    take(l0, 2 * begin + kvw // LANE * high, kvw, paired(gbkv, 1))
    write(gbkv, gbkv_o)
    for c in writes:
        c.wait()


def emit(qw, kvw, quarter, hidden, grads, results):
    width = 2 * quarter
    outs = [
        ((RK, 2, hidden), F32), ((RK, hidden), F32), ((RK, qw), F32), ((RK, qw), F32), ((RK, 2, kvw), F32), ((RK, width), F32),
        ((2 * RK, width), F32), ((RK, width), F32), ((3 * RK, width), F32),
    ]
    vm = pl.BlockSpec(memory_space=VM)
    anyspace = pl.BlockSpec(memory_space=pl.ANY)
    return pl.pallas_call(
        functools.partial(emit_kernel, qw, kvw, quarter, hidden),
        out_shape=[jax.ShapeDtypeStruct(s, dtype) for s, dtype in outs]
        + [jax.ShapeDtypeStruct(a.shape, a.dtype) for a in results],
        in_specs=[vm] * len(grads) + [anyspace] * len(results),
        out_specs=[anyspace] * (len(outs) + len(results)),
        scratch_shapes=[VM(s, dtype) for s, dtype in outs]
        + [VM((2, *results[0].shape), BF), pltpu.SemaphoreType.DMA((2,)), pltpu.SemaphoreType.DMA((11,))],
        compiler_params=pltpu.CompilerParams(vmem_limit_bytes=61 << 20),
        cost_estimate=pl.CostEstimate(flops=0, bytes_accessed=20 << 20, transcendentals=0),
        name="emit",
    )(*grads, *results)


def rope_tables():
    position = np.concatenate([np.arange(PLEN)] + [PLEN + np.arange(CLEN)] * CONT_DEV).astype(np.float32)
    exponent = np.arange(HD // 2, dtype=np.float32) * np.float32(2.0 / HD)
    frequency = np.exp(np.float32(-math.log(ROPE_BASE)) * exponent).astype(np.float32)
    angle = position[:, None] * frequency[None, :]
    cos, sin = np.cos(angle).astype(np.float32), np.sin(angle).astype(np.float32)
    return np.tile(cos, (1, 4)), np.concatenate([-sin, sin, -sin, sin], axis=1)


def shards(
    tokens, cotangent, gain_attn, gain_mlp, w_query, w_kv, w_out, w_gate_up, w_down, a_attn, b_query, b_kv,
    a_out, b_out, a_mlp, b_mlp, a_down, b_down, prompt_adapter, cont_adapter, group_map,
):
    rows, width = tokens.shape
    qw = w_query.shape[1]
    kvw = w_kv.shape[2]
    hidden = w_down.shape[0]
    n_dp = lax.axis_size("dp")
    quarter = width // 2
    cos_np, sin_np = rope_tables()
    cos, sin = jnp.asarray(cos_np), jnp.asarray(sin_np)
    gain1, gain2 = gain_attn, gain_mlp
    aT = a_attn.transpose(1, 2, 3, 0).reshape(3 * RK, width)
    aoT = a_out.transpose(1, 2, 0).reshape(RK, qw)
    amT = a_mlp.transpose(1, 2, 3, 0).reshape(2 * RK, width)
    adT = a_down.transpose(1, 2, 0).reshape(RK, hidden)
    bq = b_query.reshape(RK, qw)
    bkv = b_kv.reshape(RK, 2, kvw)
    bo = b_out.reshape(RK, width)
    bm = b_mlp.reshape(RK, 2, hidden)
    bd = b_down.reshape(RK, width)
    wkv = w_kv.reshape(width, 2 * kvw)
    (n1q, q, kv, u, pp, pc, o, far, h_p, h_c, n2p, n2c, uop, uoc, _, dh_p, dh_c, dap, dac, sm_p, sm_c, ge) = first(
        n_dp, [prompt_adapter, cont_adapter, group_map], [gain1, gain2, bkv, bm, amT, adT, bo],
        [tokens, aT, wkv, cos, sin, w_query, bq, aoT, w_out, cotangent, bd, w_down, w_gate_up],
    )
    results = backward(
        n_dp, [prompt_adapter, cont_adapter, group_map], [gain1, bkv],
        [dac, w_out, o, aoT, bo, n2c, uoc, q, kv, far, pc, cos, sin, dap, pp, n2p, uop, u, w_query, wkv, bq, sm_p, h_p, bd, sm_c,
         h_c, cotangent, n1q, dh_c, aT, dh_p, tokens, ge],
    )
    gbm, gad, gao, gbq, gbkv, gbo, gam, gbd, ga, output, tokens_grad = emit(qw, kvw, quarter, hidden, results[2:], results[:2])
    return (
        output,
        tokens_grad,
        ga.reshape(3, NA, R, width).transpose(3, 0, 1, 2),
        gbq.reshape(b_query.shape),
        gbkv.reshape(b_kv.shape),
        gao.reshape(NA, R, qw).transpose(2, 0, 1),
        gbo.reshape(b_out.shape),
        gam.reshape(2, NA, R, width).transpose(3, 0, 1, 2),
        gbm.reshape(b_mlp.shape),
        gad.reshape(NA, R, hidden).transpose(2, 0, 1),
        gbd.reshape(b_down.shape),
    )


def solution(mesh):
    in_specs = (
        P("dp", None), P("dp", None), P(), P(), P(None, "tensor"), P(None, None, "tensor"), P("tensor", None),
        P(None, None, "tensor"), P("tensor", None), P(), P(None, None, "tensor"), P(None, None, None, "tensor"),
        P("tensor", None, None), P(), P(), P(None, None, None, "tensor"), P("tensor", None, None), P(),
        P("dp"), P("dp"), P(),
    )
    out_specs = (
        P("dp", None), P("dp", None), P(), P(None, None, "tensor"), P(None, None, None, "tensor"),
        P("tensor", None, None), P(), P(), P(None, None, None, "tensor"), P("tensor", None, None), P(),
    )
    return jax.shard_map(shards, mesh=mesh, in_specs=in_specs, out_specs=out_specs, check_vma=False)
```

```python
import functools
import math

import jax
import jax.numpy as jnp
import numpy as np
from jax import lax
from jax.experimental import pallas as pl
from jax.experimental.pallas import tpu as pltpu
from jax.sharding import PartitionSpec as P

HD = 64
R = 16
NA = 4
RK = NA * R
PLEN = 384
CLEN = 128
CONT_DEV = 2
ROWS = PLEN + CONT_DEV * CLEN
EPSILON = 1e-05
ROPE_BASE = 500000.0
MASKED_SCORE = -1e30

BF = jnp.bfloat16
F32 = jnp.float32
VM = pltpu.VMEM
LANE = 128


def dn(a, b):
    return jnp.dot(a, b, preferred_element_type=F32)


def dt(a, b):
    return lax.dot_general(a, b, (((1,), (1,)), ((), ())), preferred_element_type=F32)


def dr(a, b):
    return lax.dot_general(a, b, (((0,), (0,)), ((), ())), preferred_element_type=F32)


def sel_row(adapter):
    lane = lax.broadcasted_iota(jnp.int32, (1, RK), 1)
    return (lax.shift_right_logical(lane, 4) == adapter).astype(F32)


def swap_halves(v):
    lane = lax.broadcasted_iota(jnp.int32, v.shape, 1)
    return jnp.where((lane & 63) < 32, pltpu.roll(v, LANE - 32, 1), pltpu.roll(v, 32, 1))


def rot(v, cos, sin):
    return v * cos + swap_halves(v) * sin


def stack_heads(ref, r0, g):
    return jnp.concatenate(
        [ref[pl.ds(r0, CLEN), (4 * g + h) * HD : (4 * g + h + 1) * HD] for h in range(4)], axis=0
    )


def softmax_low(s):
    top = jnp.max(s, axis=-1, keepdims=True)
    e = jnp.exp(s - top)
    return (e * (1.0 / jnp.sum(e, axis=-1, keepdims=True))).astype(BF)


def causal_tile():
    r = lax.broadcasted_iota(jnp.int32, (4 * CLEN, CLEN), 0) & (CLEN - 1)
    c = lax.broadcasted_iota(jnp.int32, (4 * CLEN, CLEN), 1)
    return c <= r


P_OFF = (0, 128, 384)


def norm_back(v, gain, upstream):
    inv = lax.rsqrt(jnp.mean(v * v, axis=-1, keepdims=True) + EPSILON)
    scaled = v * inv
    weighted = upstream * gain
    return inv * (weighted - scaled * jnp.mean(weighted * scaled, axis=-1, keepdims=True))


def put_dq(dq, dq_ref, r0, g):
    for h in range(4):
        dq_ref[pl.ds(r0, CLEN), (4 * g + h) * HD : (4 * g + h + 1) * HD] = dq[h * CLEN : (h + 1) * CLEN]


def back_scores(p, dp):
    pf = p.astype(F32)
    return (pf * (dp - jnp.sum(pf * dp, axis=-1, keepdims=True))).astype(BF)


MESH = pl.DeviceIdType.MESH


def rows_loop(total, step, body):
    def one(i, carry):
        body(pl.multiple_of(i * step, step))
        return carry

    lax.fori_loop(0, total // step, one, 0)


def loop(first, last, body):
    def one(i, carry):
        body(i)
        return carry

    lax.fori_loop(first, last, one, 0)


def place():
    d = lax.axis_index("dp")
    t = lax.axis_index("tensor")
    return d, t


def remote(src, dst, send, recv, device):
    return pltpu.make_async_remote_copy(
        src_ref=src, dst_ref=dst, send_sem=send, recv_sem=recv, device_id=device, device_id_type=MESH
    )


def greet(d, t, n_dp):
    barrier = pltpu.get_barrier_semaphore()
    for device in [(d, t ^ 1), (d, t ^ 2)] + [((d + k) % n_dp, t) for k in range(1, n_dp)]:
        pl.semaphore_signal(barrier, inc=1, device_id=device, device_id_type=MESH)


def greeted(n_dp):
    pl.semaphore_wait(pltpu.get_barrier_semaphore(), n_dp + 1)


class Spread:
    def __init__(self, every, sems, d, t, hi):
        self.every, self.sems, self.d, self.t, self.hi = every, sems, d, t, hi
        self.z, self.x = d // 2, d % 2

    def across(self, z):
        block = z * 2 + self.x
        up_s, up_r, down_s, down_r, x_s, x_r = self.sems
        return remote(self.every.at[block], self.every.at[block], x_s.at[z], x_r.at[z], (self.d ^ 1, self.t))

    def along(self, z, s, up):
        block = z * 2 + self.x
        up_s, up_r, down_s, down_r, x_s, x_r = self.sems
        send, recv, step = (up_s, up_r, 2) if up else (down_s, down_r, -2)
        return remote(self.every.at[block], self.every.at[block], send.at[s], recv.at[s], (self.d + step, self.t))

    def start(self):
        self.across(self.z).start()

        @pl.when(self.z < self.hi - 1)
        def _():
            self.along(self.z, 1, True).start()

        @pl.when(self.z > 0)
        def _():
            self.along(self.z, 1, False).start()

    def hop(self, s):
        if s > self.hi - 1:
            return
        for up in (True, False):
            origin = self.z - s if up else self.z + s
            held = origin >= 0 if up else origin < self.hi
            further = self.z < self.hi - 1 if up else self.z > 0

            @pl.when(held)
            def _(origin=origin, up=up, further=further):
                self.along(origin, s, up).wait_recv()
                self.across(origin).start()
                if s + 1 <= self.hi - 1:

                    @pl.when(further)
                    def _():
                        self.along(origin, s + 1, up).start()

    def finish(self):
        for z in range(self.hi):
            across = self.across(z)
            across.wait_send()
            block = z * 2 + 1 - self.x
            up_s, up_r, down_s, down_r, x_s, x_r = self.sems
            remote(self.every.at[block], self.every.at[block], x_s.at[z], x_r.at[z], (self.d ^ 1, self.t)).wait_recv()
        for s in range(1, self.hi):
            for up in (True, False):
                origin = self.z - s + 1 if up else self.z + s - 1
                held = origin >= 0 if up else origin < self.hi
                further = self.z < self.hi - 1 if up else self.z > 0

                @pl.when(held & further)
                def _(origin=origin, up=up, s=s):
                    self.along(origin, s, up).wait_send()


class TensorSum:
    def __init__(self, snd, got, mine, theirs, sems, d, t):
        self.snd, self.got, self.mine, self.theirs, self.sems, self.t = snd, got, mine, theirs, sems, t
        self.lo = t % 2
        self.core = remote(snd.at[1 - self.lo], got, sems.at[0], sems.at[1], (d, t ^ 1))
        self.chip = remote(mine, theirs, sems.at[2], sems.at[3], (d, t ^ 2))

    def begin(self):
        self.core.start()

    def middle(self):
        self.core.wait_recv()

        def add(r):
            rows = pl.ds(r, 64)
            self.mine[rows] = (self.snd[self.lo, rows].astype(F32) + self.got[rows].astype(F32)).astype(BF)

        rows_loop(self.mine.shape[0], 64, add)
        self.chip.start()

    def end(self):
        self.chip.wait_recv()

    def drain(self):
        self.core.wait_send()
        self.chip.wait_send()


UNIT = (16, LANE)


def put_units(blocks, first, value):
    for b in range(value.shape[1] // LANE):
        for r in range(RK // 16):
            blocks[first + b * (RK // 16) + r] = value[r * 16 : (r + 1) * 16, b * LANE : (b + 1) * LANE]


class DirectReduce:
    def __init__(self, src, got, out, sems, d, t, n_dp):
        self.src, self.got, self.out, self.sems, self.d, self.t, self.n = src, got, out, sems, d, t, n_dp
        self.share = src.shape[0] // n_dp if src is not None else out.shape[0] // n_dp

    def part(self, d):
        return pl.ds(((d % 2) * (self.n // 2) + d // 2) * self.share, self.share)

    def to(self, k):
        peer = (self.d + k) % self.n
        return remote(self.src.at[self.part(peer)], self.got.at[k], self.sems[0].at[k], self.sems[1].at[k], (peer, self.t))

    def back(self, k):
        peer = (self.d + k) % self.n
        here = self.part(self.d)
        return remote(self.out.at[here], self.out.at[here], self.sems[2].at[k], self.sems[3].at[k], (peer, self.t))

    def from_back(self, k):
        peer = (self.d + self.n - k) % self.n
        there = self.part(peer)
        return remote(self.out.at[there], self.out.at[there], self.sems[2].at[k], self.sems[3].at[k], (peer, self.t))

    def start(self):
        for k in range(1, self.n):
            self.to(k).start()

    def add(self):
        for k in range(1, self.n):
            self.to(k).wait_recv()
        here = self.part(self.d)
        total = self.src[here].astype(F32)
        for k in range(1, self.n):
            total = total + self.got[k].astype(F32)
        self.out[here] = total.astype(BF)

    def sent(self):
        for k in range(1, self.n):
            self.to(k).wait_send()

    def spread(self):
        for k in range(1, self.n):
            self.back(k).start()

    def finish(self):
        for k in range(1, self.n):
            self.from_back(k).wait_recv()

    def spread_sent(self):
        for k in range(1, self.n):
            self.back(k).wait_send()


class PairReduce:
    def __init__(self, src, gx, gz, out, sems, d, t, n_dp):
        self.src, self.gx, self.gz, self.out, self.sems, self.t = src, gx, gz, out, sems, t
        self.hi, self.z, self.x = n_dp // 2, d // 2, d % 2
        self.share = out.shape[0] // n_dp
        self.mate = (d ^ 1, t)

    def part(self, z):
        return pl.ds((self.x * self.hi + z) * self.share, self.share)

    def half(self, x):
        return pl.ds(x * self.hi * self.share, self.hi * self.share)

    def on_line(self, k):
        z = (self.z + k) % self.hi
        return z, (z * 2 + self.x, self.t)

    def over(self):
        return remote(self.src.at[self.half(1 - self.x)], self.gx, self.sems[0].at[0], self.sems[1].at[0], self.mate)

    def to(self, k):
        z, device = self.on_line(k)
        return remote(self.src.at[self.part(z)], self.gz.at[k], self.sems[2].at[k], self.sems[3].at[k], device)

    def back(self, k, come=False):
        z, device = self.on_line(self.hi - k if come else k)
        here = self.part(z if come else self.z)
        return remote(self.out.at[here], self.out.at[here], self.sems[4].at[k], self.sems[5].at[k], device)

    def over_back(self, x):
        here = self.half(x)
        return remote(self.out.at[here], self.out.at[here], self.sems[6].at[0], self.sems[7].at[0], self.mate)

    def start(self):
        self.over().start()

    def middle(self):
        self.over().wait_recv()
        here = self.half(self.x)
        self.src[here] = (self.src[here].astype(F32) + self.gx[...].astype(F32)).astype(BF)
        for k in range(1, self.hi):
            self.to(k).start()

    def add(self):
        here = self.part(self.z)
        total = self.src[here].astype(F32)
        for k in range(1, self.hi):
            self.to(k).wait_recv()
            total = total + self.gz[k].astype(F32)
        self.out[here] = total.astype(BF)
        self.spread()

    def spread(self):
        for k in range(1, self.hi):
            self.back(k).start()

    def cross(self):
        for k in range(1, self.hi):
            self.back(k, True).wait_recv()
        self.over_back(self.x).start()

    def finish(self):
        self.over_back(1 - self.x).wait_recv()

    def spread_sent(self):
        for k in range(1, self.hi):
            self.back(k).wait_send()
        self.over_back(self.x).wait_send()

    def sent(self):
        self.over().wait_send()
        for k in range(1, self.hi):
            self.to(k).wait_send()


class Trade:
    def __init__(self, halves, sems, d, t):
        self.halves, self.sems, self.d, self.t = halves, sems, d, t

    def slot(self, n):
        return remote(self.halves.at[n], self.halves.at[n], self.sems.at[0], self.sems.at[1], (self.d, self.t ^ 1))

    def start(self):
        self.slot(self.t % 2).start()

    def finish(self):
        self.slot(1 - self.t % 2).wait_recv()

    def sent(self):
        self.slot(self.t % 2).wait_send()


def evens_first(n):
    r = lax.broadcasted_iota(jnp.int32, (n, n), 0)
    c = lax.broadcasted_iota(jnp.int32, (n, n), 1)
    return (c == jnp.where(r < n // 2, 2 * r, 2 * (r - n // 2) + 1)).astype(BF)


def all_sel(sc):
    return jnp.concatenate(
        [
            jnp.broadcast_to(sel_row(sc[0]), (PLEN, RK)),
            jnp.broadcast_to(sel_row(sc[1]), (CLEN, RK)),
            jnp.broadcast_to(sel_row(sc[2]), (CLEN, RK)),
        ],
        axis=0,
    )


def first_kernel(
    n_dp, ids_p, ids_c, group_map, gain1, gain2, bkv_ref, bm_h, amT_h, adT_h, bo_h,
    tok_h, aT_h, wkv_h, cos_h, sin_h, wq_h, bq_h, aoT_h, wo_h, dy_h, bd_h, wd_h, raw_h,
    n1q_h, q_h, kv_h, u_h, pp_h, pc_h, o_h, far_h, hp_h, hc_h, n2p_h, n2c_h, uop_h, uoc_h, wgu_h,
    dhp_h, dhc_h, dap_h, dac_h, smp_h, smc_h, ge_h,
    every, snd_p, s_p, snd_c, s_c, got0_p, t0_p, got0_c, t0_c, got1_p, t1_p, got1_c, t1_c,
    n2p, n2c, uop, uoc, hp, hc, xp, xc, dyp, dyc, dact, dud, tmp, ge, gots, bm, amT, adT, bo,
    lsem, osem, wsem, rsem, fsem, vsem, psem, csem, psem2, csem2, msem, nsem, up_s, up_r, down_s, down_r, x_s, x_r, g0, g1,
):
    d, t = place()
    sc = [ids_p[0], ids_c[0], ids_c[1], group_map[d * CONT_DEV], group_map[d * CONT_DEV + 1]]
    lo = t % 2
    hi = n_dp // 2
    rows, width = tok_h.shape
    wide = n2p.shape[2]
    qw = wq_h.shape[1]
    kvw = wkv_h.shape[1] // 2
    hidden = wd_h.shape[0]
    ht = 512
    steps = hidden // ht
    hpn, hcn = PLEN // 2, CLEN
    part = n1q_h.shape[1]
    qlanes = pl.ds(pl.multiple_of(lo * part, part), part)
    adapter_c = jnp.where(lo == 0, sc[1], sc[2])
    greet(d, t, n_dp)
    counts = [0, 0]

    def load(src, dst):
        c = pltpu.make_async_copy(src, dst, lsem.at[counts[0]])
        counts[0] += 1
        c.start()
        return c

    def store(src, dst):
        c = pltpu.make_async_copy(src, dst, osem.at[counts[1]])
        counts[1] += 1
        c.start()
        return c

    spread = Spread(every, (up_s, up_r, down_s, down_r, x_s, x_r), d, t, hi)
    sum_p = TensorSum(snd_p, got0_p, s_p, t0_p, psem, d, t)
    sum_c = TensorSum(snd_c, got0_c, s_c, t0_c, csem, d, t)
    sel = all_sel(sc)
    b2 = 2 * RK

    def attention(tok, n1, aT, wkv, cos, sin, wq, bq, aoT, wo, bd, wdc, raw, flat, bflat, kv, q, u, far, pp, pc, o):
        kt = raw.shape[1]
        raw_steps = width // kt

        def raw_copy(i, slot):
            return pltpu.make_async_copy(raw_h.at[pl.ds(i * kt, kt)], raw.at[slot], rsem.at[slot])

        def flat_copies(i, slot):
            here = pl.ds(i * kt, kt)
            return (
                pltpu.make_async_copy(flat.at[slot, 0], wgu_h.at[here, :hidden], fsem.at[slot, 0]),
                pltpu.make_async_copy(flat.at[slot, 1], wgu_h.at[here, hidden:], fsem.at[slot, 1]),
            )

        def wd_copy(i, slot):
            return pltpu.make_async_copy(wd_h.at[pl.ds(i * ht, ht)], wdc.at[slot, :, :width], wsem.at[slot, 0])

        load_tok = load(tok_h, tok.at[:, :width])
        load_kv = [load(a, b) for a, b in ((aT_h, aT), (wkv_h, wkv), (cos_h, cos), (sin_h, sin))]
        load_q = [load(a, b) for a, b in ((wq_h, wq), (bq_h, bq))]
        stores = []

        bkv = dn(evens_first(b2), bkv_ref[...].reshape(b2, kvw)).astype(BF)
        gain_row = gain1[...].astype(F32).reshape(1, width)
        load_tok.wait()

        def norm1(r):
            x = tok[pl.ds(r, 128), :width].astype(F32)
            inv = lax.rsqrt(jnp.mean(x * x, axis=-1, keepdims=True) + EPSILON)
            n1[pl.ds(r, 128)] = (x * inv * gain_row).astype(BF)

        rows_loop(rows, 128, norm1)
        load_o = [load(a, b) for a, b in ((aoT_h, aoT), (wo_h, wo))]
        load_dy = [load(a, b) for a, b in ((dy_h, tok.at[:, :width]), (bd_h, bd), (adT_h, adT))]
        for i in range(2):
            wd_copy(i, i).start()
        for i in range(raw.shape[0]):
            raw_copy(i, i).start()
        load_bm = load(bm_h, bm)
        load_x = [
            load(tok_h.at[pl.ds(pl.multiple_of(lo * hpn, hpn), hpn)], xp),
            load(tok_h.at[pl.ds(pl.multiple_of(PLEN + lo * hcn, hcn), hcn)], xc),
            load(amT_h, amT),
            load(bo_h, bo),
        ]
        for c in load_kv:
            c.wait()
        uf = dt(n1[...], aT[...])
        for part in range(3):
            u[:, part * RK : (part + 1) * RK] = (uf[:, part * RK : (part + 1) * RK] * sel).astype(BF)
        kvf = dn(n1[...], wkv[...])
        kv[:, :kvw] = rot(kvf[:, :kvw] + dn(u[:, RK : 2 * RK], bkv[:RK]), cos[...], sin[...]).astype(BF)
        kv[:, kvw:] = (kvf[:, kvw:] + dn(u[:, 2 * RK :], bkv[RK:])).astype(BF)
        every[d] = kv[:PLEN]
        greeted(n_dp)
        spread.start()

        for c in load_q:
            c.wait()
        qf = dn(n1[...], wq[...]) + dn(u[:, :RK], bq[...])
        for c in range(qw // LANE):
            lanes = slice(c * LANE, (c + 1) * LANE)
            q[:, lanes] = rot(qf[:, lanes], cos[...], sin[...]).astype(BF) * BF(0.125)
        stores.append(store(n1.at[:, qlanes], n1q_h))
        stores.append(store(q, q_h))
        stores.append(store(kv, kv_h))
        stores.append(store(u, u_h))

        def keep_o(of, r0, g):
            for h in range(4):
                o[pl.ds(r0, CLEN), (4 * g + h) * HD : (4 * g + h + 1) * HD] = of[h * CLEN : (h + 1) * CLEN]

        mask = causal_tile()
        for g in range(2):
            kg = kv[:PLEN, g * HD : (g + 1) * HD]
            vg = kv[:PLEN, kvw + g * HD : kvw + (g + 1) * HD]
            for i in range(PLEN // CLEN):
                size = (i + 1) * CLEN
                s = dt(stack_heads(q, i * CLEN, g), kg[:size])
                tail = jnp.where(mask, s[:, size - CLEN :], MASKED_SCORE)
                s = tail if i == 0 else jnp.concatenate([s[:, : size - CLEN], tail], axis=1)
                p = softmax_low(s)
                pp[g, :, P_OFF[i] : P_OFF[i] + size] = p
                keep_o(dn(p, vg[:size]).astype(BF), i * CLEN, g)
        stores.append(store(pp, pp_h))
        spread.hop(1)

        def project(r0, half, snd):
            ov = o[r0 : r0 + 2 * half]

            def columns(n):
                lanes = pl.ds(pl.multiple_of(n * 512, 512), 512)
                part = dn(ov, wo[:, lanes]).astype(BF)
                snd[0, :, lanes] = part[:half]
                snd[1, :, lanes] = part[half:]

            loop(0, width // 512, columns)
            uo = dt(ov, aoT[...]).astype(BF)
            pad = jnp.zeros((half, LANE - RK), BF)
            snd[0, :, width:] = jnp.concatenate([uo[:half], pad], axis=1)
            snd[1, :, width:] = jnp.concatenate([uo[half:], pad], axis=1)

        for c in load_o:
            c.wait()
        project(0, hpn, snd_p)
        sum_p.begin()

        for c in load_dy:
            c.wait()
        dudv = (dt(tok[:, :width], bd[...]) * sel).astype(BF)
        dud[...] = jnp.concatenate([dudv, jnp.zeros((rows, LANE - RK), BF)], axis=1)
        tok[:, width:] = dud[...]
        eye = (lax.broadcasted_iota(jnp.int32, (RK, RK), 0) == lax.broadcasted_iota(jnp.int32, (RK, RK), 1)).astype(BF)
        split = evens_first(256)

        slots, flats = raw.shape[0], flat.shape[0]

        def part_weights(i):
            slot = i % slots
            raw_copy(i, slot).wait()

            put = i % flats

            @pl.when(i >= flats)
            def _():
                for c in flat_copies(i - flats, put):
                    c.wait()

            apart = dn(split, raw[slot].reshape(2 * kt, hidden)).astype(BF)
            flat[put, 0] = apart[:kt]
            flat[put, 1] = apart[kt:]
            for c in flat_copies(i, put):
                c.start()

            @pl.when(i + slots < raw_steps)
            def _():
                raw_copy(i + slots, slot).start()

        def act_grad(i):
            slot = i % 2
            wd_copy(i, slot).wait()
            lanes = pl.ds(pl.multiple_of(i * ht, ht), ht)
            ad = dr(adT[:, lanes], eye).astype(BF)
            wdc[slot, :, width:] = jnp.concatenate([ad, jnp.zeros((ht, LANE - RK), BF)], axis=1)
            dact[:, lanes] = dt(tok[...], wdc[slot]).astype(BF)

            @pl.when(i + 2 < steps)
            def _():
                wd_copy(i + 2, slot).start()

        def both(i):
            act_grad(i)

            @pl.when(i == 0)
            def _():
                spread.hop(2)

            @pl.when(i == 1)
            def _():
                spread.hop(3)

            per = raw_steps // steps
            loop(i * per, (i + 1) * per, part_weights)

        def continuations():
            far[0] = every[sc[3]]
            far[1] = every[sc[4]]
            stores.append(store(far, far_h))

            def attend(j):
                r0 = pl.multiple_of(PLEN + j * CLEN, CLEN)
                own = pl.ds(r0, CLEN)
                for g in range(2):
                    lanes = slice(g * HD, (g + 1) * HD)
                    vlanes = slice(kvw + g * HD, kvw + (g + 1) * HD)
                    qs = stack_heads(q, r0, g)
                    sf = dt(qs, far[j, :, lanes])
                    so = jnp.where(mask, dt(qs, kv[own, lanes]), MASKED_SCORE)
                    p = softmax_low(jnp.concatenate([sf, so], axis=1))
                    pc[2 * j + g] = p
                    keep_o((dn(p[:, :PLEN], far[j, :, vlanes]) + dn(p[:, PLEN:], kv[own, vlanes])).astype(BF), r0, g)

            loop(0, CONT_DEV, attend)
            stores.append(store(pc, pc_h))
            stores.append(store(o, o_h))
            project(PLEN, hcn, snd_c)
            sum_c.begin()

        sum_p.middle()
        loop(0, steps - 1, both)
        for s in range(4, hi):
            spread.hop(s)
        spread.finish()
        continuations()
        act_grad(steps - 1)
        sum_c.middle()
        loop((steps - 1) * (raw_steps // steps), raw_steps, part_weights)
        load_bm.wait()
        bsplit = dn(evens_first(b2), bm[...].reshape(b2, hidden)).astype(BF)
        zero = jnp.zeros((RK, hidden), BF)
        bflat[:RK, :hidden] = bsplit[:RK]
        bflat[:RK, hidden:] = zero
        bflat[RK:, :hidden] = zero
        bflat[RK:, hidden:] = bsplit[RK:]
        stores.append(store(bflat, wgu_h.at[pl.ds(width, b2)]))
        for c in load_x:
            c.wait()
        for i in range(raw_steps - flats, raw_steps):
            for c in flat_copies(i, i % flats):
                c.wait()
        for c in stores:
            c.wait()

    pl.run_scoped(
        attention,
        VM((rows, wide), BF), VM((rows, width), BF), VM(aT_h.shape, BF), VM(wkv_h.shape, BF), VM(cos_h.shape, F32),
        VM(sin_h.shape, F32), VM(wq_h.shape, BF), VM(bq_h.shape, BF), VM(aoT_h.shape, BF), VM(wo_h.shape, BF), VM(bd_h.shape, BF),
        VM((2, ht, wide), BF), VM((4, 128, 2, hidden), BF), VM((3, 2, 128, hidden), BF), VM((b2, 2 * hidden), BF),
        VM((rows, 2 * kvw), BF), VM((rows, qw), BF), VM((rows, 3 * RK), BF), VM((CONT_DEV, PLEN, 2 * kvw), BF),
        VM((2, 4 * CLEN, 768), BF), VM((4, 4 * CLEN, 4 * CLEN), BF), VM((rows, qw), BF),
    )

    def feed_forward(wcat, wdn, acc, gu, dga, act, gg):
        nt = wdn.shape[2]

        def weights(k, slot):
            i = k % steps
            here = pl.ds(pl.multiple_of(i * ht, ht), ht)
            there = pl.ds(pl.multiple_of(hidden + i * ht, ht), ht)
            return [
                pltpu.make_async_copy(src, dst, wsem.at[slot, n])
                for n, (src, dst) in enumerate(
                    [(wgu_h.at[:, here], wcat.at[slot, :, :ht]), (wgu_h.at[:, there], wcat.at[slot, :, ht:])]
                )
            ]

        def down(n, slot):
            return pltpu.make_async_copy(wd_h.at[:, pl.ds(n * nt, nt)], wdn.at[slot], vsem.at[slot])

        for c in weights(0, 0):
            c.start()
        load_dy = [
            load(dy_h.at[pl.ds(pl.multiple_of(lo * hpn, hpn), hpn)], dyp),
            load(dy_h.at[pl.ds(pl.multiple_of(PLEN + lo * hcn, hcn), hcn)], dyc),
        ]
        for n in range(2):
            down(n, n).start()

        def norm2(which, total, x, h, n2, adapter):
            half = h.shape[0]
            total.end()
            sr = sel_row(adapter)
            uo = (total.mine[:, width : width + RK].astype(F32) + total.theirs[:, width : width + RK].astype(F32)) * sr
            uo = uo.astype(BF)
            tmp[:half] = dn(uo, bo[...])
            gain_two = gain2[...].astype(F32).reshape(1, width)

            def one(r):
                here = pl.ds(r, 64)
                hv = (
                    x[here].astype(F32)
                    + (total.mine[here, :width].astype(F32) + total.theirs[here, :width].astype(F32))
                    + tmp[here]
                )
                h[here] = hv
                inv = lax.rsqrt(jnp.mean(hv * hv, axis=-1, keepdims=True) + EPSILON)
                n2[lo, here, :width] = (hv * inv * gain_two).astype(BF)

            rows_loop(half, 64, one)
            n2[lo, :, width:] = jnp.concatenate([uo, jnp.zeros((half, LANE - RK), BF)], axis=1)
            c = remote(n2.at[lo], n2.at[lo], nsem.at[which, 0], nsem.at[which, 1], (d, t ^ 1))
            c.start()
            return c

        def arrived(which, n2):
            remote(n2.at[1 - lo], n2.at[1 - lo], nsem.at[which, 0], nsem.at[which, 1], (d, t ^ 1)).wait_recv()

        def begin(n2, uo, chosen):
            half = n2.shape[1]
            r = 2 * half
            um = dt(n2[:, :, :width].reshape(r, width), amT[...])
            um = jnp.concatenate([(um[:, :RK] * chosen).astype(BF), (um[:, RK:] * chosen).astype(BF)], axis=1)
            uo[...] = n2[:, :, width:]
            n2[:, :, width:] = um.reshape(2, half, 2 * RK)
            acc[:r] = jnp.zeros((r, wide), F32)

        def tile(k, n2, base, add):
            r = 2 * n2.shape[1]
            slot = k % 2
            i = k % steps
            for c in weights(k, slot):
                c.wait()

            @pl.when(k + 1 < 2 * steps)
            def _():
                for c in weights(k + 1, 1 - slot):
                    c.start()

            gu[:r] = dn(n2[...].reshape(r, wide), wcat[slot])
            lanes = pl.ds(pl.multiple_of(i * ht, ht), ht)

            def swiglu(r0):
                here = pl.ds(r0, 64)
                gate = gu[here, :ht]
                upper = gu[here, ht:]
                sigma = 1.0 / (1.0 + jnp.exp(-gate))
                silu = gate * sigma
                there = pl.ds(base + r0, 64)
                da = dact[there, lanes].astype(F32)
                dga[here, :ht] = (da * upper * (sigma * (1.0 + gate * (1.0 - sigma)))).astype(BF)
                dga[here, ht : 2 * ht] = (da * silu).astype(BF)
                av = (silu * upper).astype(BF)
                dga[here, 2 * ht :] = av
                act[there, lanes] = av

            for r0 in range(0, r, 64):
                swiglu(r0)
            acc[:r] += dt(dga[:r, : 2 * ht], wcat[slot])
            small = jnp.concatenate([n2[:, :, width:].reshape(r, 2 * RK), dud[base : base + r, :RK]], axis=1)
            g = dr(small, dga[:r])
            for n in range(3):
                part = g[n * RK : (n + 1) * RK, n * ht : (n + 1) * ht]
                if add:
                    total = (gg[n, :, lanes] + part).astype(BF)
                    units = ht // LANE * (RK // 16)
                    put_units(ge, n * (hidden // LANE * (RK // 16)) + i * units, total)
                else:
                    gg[n, :, lanes] = part

        def halves(a, snd):
            half = snd.shape[1]

            def one(r0):
                for n in range(2):
                    snd[n, pl.ds(r0, 64)] = a[pl.ds(pl.multiple_of(n * half + r0, 64), 64)].astype(BF)

            rows_loop(half, 64, one)

        n2_copy_p = norm2(0, sum_p, xp, hp, n2p, sc[0])
        store_hp = store(hp, hp_h)
        arrived(0, n2p)
        n2_copy_p.wait_send()
        store_n2p = store(n2p.at[:, :, qlanes], n2p_h)
        begin(n2p, uop, sel_row(sc[0]))
        tail_stores = [store(uop, uop_h)]

        loop(0, steps, lambda k: tile(k, n2p, 0, False))
        sum_p.drain()
        halves(acc, snd_p)
        store_n2p.wait()
        sum2_p = TensorSum(snd_p, got1_p, s_p, t1_p, psem2, d, t)
        sum2_p.begin()

        n2_copy_c = norm2(1, sum_c, xc, hc, n2c, adapter_c)
        store_hc = store(hc, hc_h)
        sum2_p.middle()
        arrived(1, n2c)
        n2_copy_c.wait_send()
        store_n2c = store(n2c.at[:, :, qlanes], n2c_h)
        begin(
            n2c, uoc,
            jnp.concatenate([jnp.broadcast_to(sel_row(sc[1]), (hcn, RK)), jnp.broadcast_to(sel_row(sc[2]), (hcn, RK))], axis=0),
        )
        tail_stores.append(store(uoc, uoc_h))

        loop(steps, 2 * steps, lambda k: tile(k, n2c, PLEN, True))
        sum_c.drain()
        halves(acc, snd_c)
        store_n2c.wait()
        sum2_c = TensorSum(snd_c, got1_c, s_c, t1_c, csem2, d, t)
        sum2_c.begin()
        reduce = DirectReduce(ge, gots, ge, (g0, g1, None, None), d, t, n_dp)
        reduce.start()

        ud = dt(act[...], adT[...]).astype(BF)
        sum2_c.middle()
        sum2_p.core.wait_send()
        sum2_c.core.wait_send()
        pad = jnp.zeros((hpn, LANE - RK), BF)
        for n in range(2):
            snd_p[n, :, width:] = jnp.concatenate([ud[n * hpn : (n + 1) * hpn], pad], axis=1)
            snd_c[n, :, width:] = jnp.concatenate([ud[PLEN + n * hcn : PLEN + (n + 1) * hcn], pad[:hcn]], axis=1)

        def project_down(n):
            slot = n % 2
            down(n, slot).wait()
            part = dn(act[...], wdn[slot]).astype(BF)
            lanes = pl.ds(pl.multiple_of(n * nt, nt), nt)
            for i in range(2):
                snd_p[i, :, lanes] = part[i * hpn : (i + 1) * hpn]
                snd_c[i, :, lanes] = part[PLEN + i * hcn : PLEN + (i + 1) * hcn]

            @pl.when(n + 2 < width // nt)
            def _():
                down(n + 2, slot).start()

        loop(0, width // nt, project_down)
        mcore_p = remote(snd_p.at[1 - lo], got0_p, msem.at[0], msem.at[1], (d, t ^ 1))
        mcore_p.start()
        mcore_c = remote(snd_c.at[1 - lo], got0_c, msem.at[2], msem.at[3], (d, t ^ 1))
        mcore_c.start()

        def mlp_sum(core, snd, got, out):
            core.wait_recv()

            def add(r0):
                here = pl.ds(r0, 64)
                got[here] = (snd[lo, here].astype(F32) + got[here].astype(F32)).astype(BF)

            rows_loop(got.shape[0], 64, add)
            tail_stores.append(store(got, out))

        def back(which, total, h, dy, da, adapter):
            half = h.shape[0]
            total.end()
            sr = sel_row(adapter)
            du = total.mine[:, width:].astype(F32) + total.theirs[:, width:].astype(F32)
            dum = (du * jnp.concatenate([sr, sr], axis=1)).astype(BF)
            tmp[:half] = dn(dum, amT[...])
            gain = gain2[...].astype(F32).reshape(1, width)

            def one(r0):
                here = pl.ds(r0, 64)
                dn2 = total.mine[here, :width].astype(F32) + total.theirs[here, :width].astype(F32) + tmp[here]
                dh = dy[here].astype(F32) + norm_back(h[here], gain, dn2)
                h[here] = dh
                da[lo, here, :width] = dh.astype(BF)

            rows_loop(half, 64, one)
            da[lo, :, width:] = dum
            c = remote(da.at[lo], da.at[lo], nsem.at[which, 0], nsem.at[which, 1], (d, t ^ 1))
            c.start()
            return c

        for c in load_dy:
            c.wait()
        store_hp.wait()
        store_hc.wait()
        copy_p = back(2, sum2_p, hp, dyp, n2p, sc[0])
        tail_stores.append(store(hp, dhp_h))
        mlp_sum(mcore_p, snd_p, got0_p, smp_h)
        mlp_sum(mcore_c, snd_c, got0_c, smc_h)
        arrived(2, n2p)
        tail_stores.append(store(n2p, dap_h))
        reduce.add()
        tail_stores.append(store(ge.at[reduce.part(d)], ge_h))
        copy_c = back(3, sum2_c, hc, dyc, n2c, adapter_c)
        tail_stores.append(store(hc, dhc_h))
        arrived(3, n2c)
        tail_stores.append(store(n2c, dac_h))
        copy_p.wait_send()
        copy_c.wait_send()
        sum2_p.chip.wait_send()
        sum2_c.chip.wait_send()
        mcore_p.wait_send()
        mcore_c.wait_send()
        reduce.sent()
        for c in tail_stores:
            c.wait()

    pl.run_scoped(
        feed_forward,
        VM((2, wide, 2 * ht), BF), VM((2, hidden, 512), BF), VM((PLEN, wide), F32), VM((PLEN, 2 * ht), F32), VM((PLEN, 3 * ht), BF),
        VM((rows, hidden), BF), VM((3, RK, hidden), F32),
    )


def first(n_dp, scalars, small, large):
    tok, aT, wkv, cos, sin, wq, bq, aoT, wo, dy, bd, wd, raw = large
    rows, width = tok.shape
    qw = wq.shape[1]
    kvw2 = wkv.shape[1]
    hidden = wd.shape[0]
    quarter = width // 2
    wide = width + LANE
    hpn, hcn = PLEN // 2, CLEN
    units = 3 * hidden // LANE * (RK // 16)
    share = units // n_dp
    outs = [
        ((rows, quarter), BF), ((rows, qw), BF), ((rows, kvw2), BF), ((rows, 3 * RK), BF), ((2, 4 * CLEN, 768), BF),
        ((4, 4 * CLEN, 4 * CLEN), BF), ((rows, qw), BF), ((CONT_DEV, PLEN, kvw2), BF), ((hpn, width), F32),
        ((hcn, width), F32), ((2, hpn, quarter), BF), ((2, hcn, quarter), BF), ((2, hpn, LANE), BF), ((2, hcn, LANE), BF),
        ((width + 2 * RK, 2 * hidden), BF),
        ((hpn, width), F32), ((hcn, width), F32), ((2, hpn, wide), BF), ((2, hcn, wide), BF), ((hpn, wide), BF),
        ((hcn, wide), BF), ((share, *UNIT), BF),
    ]
    dma = pltpu.SemaphoreType.DMA
    scratch = [
        VM((n_dp, PLEN, kvw2), BF), VM((2, hpn, wide), BF), VM((hpn, wide), BF), VM((2, hcn, wide), BF), VM((hcn, wide), BF),
    ] + [VM((hpn, wide), BF), VM((hpn, wide), BF), VM((hcn, wide), BF), VM((hcn, wide), BF)] * 2 + [
        VM((2, hpn, wide), BF), VM((2, hcn, wide), BF), VM((2, hpn, LANE), BF), VM((2, hcn, LANE), BF),
        VM((hpn, width), F32), VM((hcn, width), F32), VM((hpn, width), BF), VM((hcn, width), BF), VM((hpn, width), BF),
        VM((hcn, width), BF), VM((rows, hidden), BF), VM((rows, LANE), BF), VM((hpn, width), F32),
        VM((units, *UNIT), BF), VM((n_dp, share, *UNIT), BF),
        VM((RK, 2, hidden), BF), VM((2 * RK, width), BF), VM((RK, hidden), BF), VM((RK, width), BF),
        dma((20,)), dma((22,)), dma((2, 2)), dma((4,)), dma((4, 2)), dma((2,)), dma((4,)), dma((4,)), dma((4,)), dma((4,)),
        dma((4,)), dma((4, 2)),
    ] + [dma((n_dp // 2 + 1,))] * 6 + [dma((n_dp,))] * 2
    vm = pl.BlockSpec(memory_space=VM)
    anyspace = pl.BlockSpec(memory_space=pl.ANY)
    return pl.pallas_call(
        functools.partial(first_kernel, n_dp),
        out_shape=[jax.ShapeDtypeStruct(s, dtype) for s, dtype in outs],
        in_specs=[pl.BlockSpec(memory_space=pltpu.SMEM)] * 3 + [vm] * 3 + [anyspace] * (len(small) - 3 + len(large)),
        out_specs=[anyspace] * len(outs),
        scratch_shapes=scratch,
        compiler_params=pltpu.CompilerParams(vmem_limit_bytes=127 << 19, collective_id=1, has_side_effects=True),
        cost_estimate=pl.CostEstimate(flops=12 * rows * width * hidden, bytes_accessed=120 << 20, transcendentals=0),
        name="first",
    )(*scalars, *small, *large)


class Fold:
    def __init__(self, dfar, xr, zs, zr, sems, owners, others, d, t, hi):
        self.dfar, self.xr, self.zs, self.zr, self.sems = dfar, xr, zs, zr, sems
        self.owners, self.others, self.d, self.t, self.hi = owners, others, d, t, hi
        self.z, self.x = d // 2, d % 2

    def across(self, j):
        return remote(self.dfar.at[j], self.xr.at[j], self.sems[0].at[j], self.sems[1].at[j], (self.d ^ 1, self.t))

    def along(self, z, come=False):
        slot = z if come else self.z
        return remote(
            self.zr.at[slot] if come else self.zs.at[z], self.zr.at[slot], self.sems[2].at[z], self.sems[3].at[slot],
            (z * 2 + self.x, self.t),
        )

    def held(self, z, rows):
        dest = z * 2 + self.x
        total = None
        for parts, owners in ((self.dfar, self.owners), (self.xr, self.others)):
            for j in range(CONT_DEV):
                term = parts[j, rows].astype(F32) * (owners[j] == dest).astype(F32)
                total = term if total is None else total + term
        return total

    def fold(self):
        for j in range(CONT_DEV):
            self.across(j).wait_recv()
        order = sorted(range(self.hi), key=lambda z: min(z, self.hi - 1 - z))
        for z in order:

            @pl.when(self.z != z)
            def _(z=z):
                def put(r):
                    rows = pl.ds(r, 64)
                    self.zs[z, rows] = self.held(z, rows).astype(BF)

                rows_loop(PLEN, 64, put)
                self.along(z).start()

    def finish(self, total):
        def own(r):
            rows = pl.ds(r, 64)
            total[rows] += self.held(self.z, rows)

        rows_loop(PLEN, 64, own)
        for z in range(self.hi):

            @pl.when(self.z != z)
            def _(z=z):
                self.along(z, True).wait_recv()
                total[...] += self.zr[z].astype(F32)

    def drain(self):
        for j in range(CONT_DEV):
            self.across(j).wait_send()
        for z in range(self.hi):

            @pl.when(self.z != z)
            def _(z=z):
                self.along(z).wait_send()


def back_kernel(
    n_dp, ids_p, ids_c, group_map, gain1, bkv_ref,
    dac_h, wo_h, o_h, aoT_h, bo_h, n2c_h, uoc_h, q_h, kv_h, far_h, pc_h, cos_h, sin_h, dap_h, pp_h, n2p_h, uop_h, u_h, wq_h, wkv_h, bq_h,
    smp_h, hp_h, bd_h, smc_h, hc_h, dy_h, n1q_h, dhc_h, aT_h, dhp_h, tok_h, ge_h,
    out_h, tg_h, gef_h, l0_h, t1_h, t2_h,
    dac, wo, o, aoT, bo, n2c, uoc, q, kv, far, pc, cos, sin, dap, pp, n2p, uop, u, wq, wkv, bq,
    smp, hp, bd, smc, hc, aT, xc, xp, gef, tmp_p, tmp_c,
    do, dqp, dkv, dkvp, dfar, gacc, snd_p, got_p, s_p, t_p, snd_c, got_c, s_c, t_c,
    dsnd_p, dgot_p, ds_p, dt_p, dsnd_c, dgot_c, ds_c, dt_c, dup, duc, outp, outc, tgp, tgc, tmp,
    l0s, l0x, l0z, l0, l1s, l1x, l1z, l2s, l2x, l2z, t1, t2, xr, zs, zr,
    lsem, osem, dsem, ysem, psem, csem, dpsem, dcsem, nsem, q1, q2, f0, f1, f2, f3, *rsems,
):
    d, t = place()
    sc = [ids_p[0], ids_c[0], ids_c[1], group_map[d * CONT_DEV], group_map[d * CONT_DEV + 1]]
    lo = t % 2
    hi = n_dp // 2
    width = wq.shape[0]
    qw = wq.shape[1]
    kvw = wkv.shape[1] // 2
    quarter = n1q_h.shape[1]
    hpn, hcn = PLEN // 2, CLEN
    greet(d, t, n_dp)
    qlanes = pl.ds(pl.multiple_of(lo * quarter, quarter), quarter)
    every = PairReduce(None, None, None, gef, rsems[0:8], d, t, n_dp)
    pairs = [
        (ge_h, gef.at[every.part(d // 2)]), (dac_h, dac), (wo_h, wo), (o_h, o), (aoT_h, aoT), (bo_h, bo), (n2c_h, n2c),
        (uoc_h, uoc), (q_h, q), (kv_h, kv), (far_h, far), (pc_h, pc), (cos_h, cos), (sin_h, sin), (dap_h, dap),
        (pp_h, pp), (n2p_h, n2p), (uop_h, uop), (u_h, u), (wq_h, wq), (wkv_h, wkv), (bq_h, bq),
        (smp_h, smp), (hp_h, hp), (bd_h, bd), (smc_h, smc), (hc_h, hc),
        (aT_h, aT), (tok_h.at[pl.ds(pl.multiple_of(PLEN + lo * hcn, hcn), hcn)], xc),
        (tok_h.at[pl.ds(pl.multiple_of(lo * hpn, hpn), hpn)], xp),
    ]
    loads = {}

    def fetch(first, last):
        for n in range(first, last):
            src, dst = pairs[n]
            c = pltpu.make_async_copy(src, dst, lsem.at[n])
            c.start()
            loads[id(dst) if n else 0] = c

    fetch(0, 14)

    def need(*refs):
        for ref in refs:
            loads.pop(id(ref)).wait()

    stores = []

    def store(src, dst):
        c = pltpu.make_async_copy(src, dst, osem.at[len(stores)])
        c.start()
        stores.append(c)

    greeted(n_dp)
    mlp_p = remote(smp_h, tmp_p, ysem.at[0], ysem.at[1], (d, t ^ 2))
    mlp_p.start()
    mlp_c = remote(smc_h, tmp_c, ysem.at[2], ysem.at[3], (d, t ^ 2))
    mlp_c.start()
    loads.pop(0).wait()
    every.spread()

    at = np.cumsum([0, quarter, quarter, quarter, qw, qw, 2 * kvw]).tolist()
    bkv = dn(evens_first(2 * RK), bkv_ref[...].reshape(2 * RK, kvw)).astype(BF)

    def out_grads(da, n2, uo, sel, r0, first):
        half = da.shape[1]
        r = 2 * half
        dav = da[:, :, :width].reshape(r, width)
        duo = (dt(dav, bo[...]) * sel).astype(BF)
        do[r0 : r0 + r] = (dt(dav, wo[...]) + dn(duo, aoT[...])).astype(BF)
        gao = dr(duo, o[r0 : r0 + r])
        dum = da[:, :, width:].reshape(r, 2 * RK)
        gam = dr(dum, n2[...].reshape(r, quarter))
        gbo = dr(uo[:, :, :RK].reshape(r, RK), da[:, :, qlanes].reshape(r, quarter))
        parts = (gbo, gam[:RK], gam[RK:], gao)
        for n, part in enumerate(parts):
            lanes = slice(at[n], at[n + 1])
            gacc[:, lanes] = part if first else gacc[:, lanes] + part

    def unrotate(r0, r):
        here = slice(r0, r0 + r)
        for c in range(qw // LANE):
            lanes = slice(c * LANE, (c + 1) * LANE)
            dqp[here, lanes] = rot(dqp[here, lanes].astype(F32), cos[here], -sin[here]).astype(BF)
        dkvp[here, :kvw] = rot(dkv[here, :kvw].astype(BF).astype(F32), cos[here], -sin[here]).astype(BF)
        dkvp[here, kvw:] = dkv[here, kvw:].astype(BF)

    need(dac, wo, o, aoT, bo, n2c, uoc)
    sel_c = jnp.concatenate([jnp.broadcast_to(sel_row(sc[1]), (hcn, RK)), jnp.broadcast_to(sel_row(sc[2]), (hcn, RK))], axis=0)
    out_grads(dac, n2c, uoc, sel_c, PLEN, True)
    fetch(14, 22)
    need(q, kv, far, pc)

    def attend(j):
        r0 = pl.multiple_of(PLEN + j * CLEN, CLEN)
        own = pl.ds(r0, CLEN)
        for g in range(2):
            lanes = slice(g * HD, (g + 1) * HD)
            vlanes = slice(kvw + g * HD, kvw + (g + 1) * HD)
            qi = stack_heads(q, r0, g)
            doi = stack_heads(do, r0, g)
            p = pc[2 * j + g]
            dp = jnp.concatenate([dt(doi, far[j, :, vlanes]), dt(doi, kv[own, vlanes])], axis=1)
            ds = back_scores(p, dp)
            dqv = dn(ds[:, :PLEN], far[j, :, lanes]) + dn(ds[:, PLEN:], kv[own, lanes])
            put_dq((dqv * 0.125).astype(BF), dqp, r0, g)
            dk = dr(ds, qi)
            dv = dr(p, doi)
            dfar[j, :, lanes] = dk[:PLEN].astype(BF)
            dfar[j, :, vlanes] = dv[:PLEN].astype(BF)
            dkv[own, lanes] = dk[PLEN:]
            dkv[own, vlanes] = dv[PLEN:]
        fold.across(j).start()

    mate = (d ^ 1) * CONT_DEV
    others = [group_map[mate + j] for j in range(CONT_DEV)]
    fold = Fold(dfar, xr, zs, zr, (f0, f1, f2, f3), sc[3:], others, d, t, hi)
    loop(0, CONT_DEV, attend)
    fetch(22, len(pairs))
    need(cos, sin)
    unrotate(PLEN, 2 * hcn)

    def dn1(r0, snd, dsnd, dsum, first):
        half = snd.shape[1]
        r = 2 * half
        here = slice(r0, r0 + r)
        a, b = dqp[here], dkvp[here]
        du = jnp.concatenate(
            [dt(a, bq[...]), dt(b[:, :kvw], bkv[:RK]), dt(b[:, kvw:], bkv[RK:]), jnp.zeros((r, RK), F32)], axis=1
        ).astype(BF)
        dsnd[0] = du[:half]
        dsnd[1] = du[half:]
        dsum.begin()

        def columns(n):
            lanes = pl.ds(pl.multiple_of(n * 512, 512), 512)
            part = (dt(a, wq[lanes]) + dt(b, wkv[lanes])).astype(BF)
            snd[0, :, lanes] = part[:half]
            snd[1, :, lanes] = part[half:]

        loop(0, width // 512, columns)
        gbq = dr(u[here, :RK], a)
        gkv = dr(u[here, RK:], b)
        parts = (gbq, gkv[:RK, :kvw], gkv[RK:, kvw:])
        for part, start in zip(parts, (at[4], at[5], at[5] + kvw)):
            lanes = slice(start, start + part.shape[1])
            gacc[:, lanes] = part if first else gacc[:, lanes] + part

    need(wq, wkv, u, bq)
    dsum_c = TensorSum(dsnd_c, dgot_c, ds_c, dt_c, dcsem, d, t)
    dn1(PLEN, snd_c, dsnd_c, dsum_c, True)
    sum_c = TensorSum(snd_c, got_c, s_c, t_c, csem, d, t)
    sum_c.begin()
    fold.fold()

    need(dap, n2p, uop)
    out_grads(dap, n2p, uop, jnp.broadcast_to(sel_row(sc[0]), (PLEN, RK)), 0, False)
    load_dy = []
    for n in range(2):
        for ref, start, half in ((dap, n * hpn, hpn), (dac, PLEN + n * hcn, hcn)):
            here = pl.ds(start, half)
            for src, lanes in ((dy_h.at[here, qlanes], slice(0, quarter)), (n1q_h.at[here], slice(quarter, 2 * quarter))):
                c = pltpu.make_async_copy(src, ref.at[n, :, lanes], dsem.at[len(load_dy)])
                c.start()
                load_dy.append(c)
    dsum_c.middle()
    sum_c.middle()
    need(pp)
    for g in range(2):
        lanes = slice(g * HD, (g + 1) * HD)
        vlanes = slice(kvw + g * HD, kvw + (g + 1) * HD)
        kg = kv[:PLEN, lanes]
        vg = kv[:PLEN, vlanes]
        for i in reversed(range(PLEN // CLEN)):
            size = (i + 1) * CLEN
            qi = stack_heads(q, i * CLEN, g)
            doi = stack_heads(do, i * CLEN, g)
            p = pp[g, :, P_OFF[i] : P_OFF[i] + size]
            ds = back_scores(p, dt(doi, vg[:size]))
            put_dq((dn(ds, kg[:size]) * 0.125).astype(BF), dqp, i * CLEN, g)
            dk = dr(ds, qi)
            dv = dr(p, doi)
            if size == PLEN:
                dkv[:size, lanes] = dk
                dkv[:size, vlanes] = dv
            else:
                dkv[:size, lanes] += dk
                dkv[:size, vlanes] += dv
    every.cross()

    def finish_out(which, sm, theirs, copy, h, out, r0, adapter):
        half = h.shape[0]
        copy.wait_recv()
        sr = sel_row(adapter)
        ud = ((sm[:, width : width + RK].astype(F32) + theirs[:, width : width + RK].astype(F32)) * sr).astype(BF)
        tmp[:half] = dn(ud, bd[...])

        def one(r):
            here = pl.ds(r, 64)
            out[lo, here, :width] = (
                h[here] + (sm[here, :width].astype(F32) + theirs[here, :width].astype(F32)) + tmp[here]
            ).astype(BF)

        rows_loop(half, 64, one)
        out[lo, :, width:] = jnp.concatenate([ud, jnp.zeros((half, LANE - RK), BF)], axis=1)
        c = remote(out.at[lo], out.at[lo], nsem.at[which, 0], nsem.at[which, 1], (d, t ^ 1))
        c.start()
        return c

    def arrived(which, out):
        remote(out.at[1 - lo], out.at[1 - lo], nsem.at[which, 0], nsem.at[which, 1], (d, t ^ 1)).wait_recv()

    need(smp, hp, bd)
    out_copy_p = finish_out(0, smp, tmp_p, mlp_p, hp, outp, 0, sc[0])
    load_dhp = pltpu.make_async_copy(dhp_h, hp, lsem.at[32])
    load_dhp.start()

    adapter_c = jnp.where(lo == 0, sc[1], sc[2])
    per = quarter // LANE * (RK // 16)

    def fill(blocks, used):
        if blocks.shape[0] > used:
            blocks[used:] = jnp.zeros((blocks.shape[0] - used, *UNIT), BF)

    def share_du(which, total, du, adapter):
        total.end()
        sr = sel_row(adapter)
        raw = total.mine[:, : 3 * RK].astype(F32) + total.theirs[:, : 3 * RK].astype(F32)
        duq = (raw * jnp.concatenate([sr, sr, sr], axis=1)).astype(BF)
        du[lo] = jnp.concatenate([duq, jnp.zeros((duq.shape[0], RK), BF)], axis=1)
        c = remote(du.at[lo], du.at[lo], nsem.at[which, 0], nsem.at[which, 1], (d, t ^ 1))
        c.start()
        return c

    need(smc, hc, aT)
    out_copy_c = finish_out(1, smc, tmp_c, mlp_c, hc, outc, PLEN, adapter_c)
    load_dhc = pltpu.make_async_copy(dhc_h, hc, lsem.at[33])
    load_dhc.start()
    du_copy_c = share_du(4, dsum_c, duc, adapter_c)
    for c in load_dy:
        c.wait()
    arrived(0, outp)
    gbd = dr(outp[:, :, width : width + RK].reshape(PLEN, RK), dap[:, :, :quarter].reshape(PLEN, quarter))
    arrived(1, outc)
    gbd = gbd + dr(outc[:, :, width : width + RK].reshape(2 * hcn, RK), dac[:, :, :quarter].reshape(2 * hcn, quarter))

    put_units(l1s, 0, gacc[:, : at[3]].astype(BF))
    put_units(l1s, 3 * per, gbd.astype(BF))
    fill(l1s, 4 * per)
    red1 = PairReduce(l1s, l1x, l1z, t1.at[lo], rsems[8:16], d, t, n_dp)
    red1.start()
    trade1 = Trade(t1, q1, d, t)
    for n in range(2):
        store(outp.at[n, :, :width], out_h.at[pl.ds(n * hpn, hpn)])
        store(outc.at[n, :, :width], out_h.at[pl.ds(PLEN + n * hcn, hcn)])
    arrived(4, duc)
    ga_c = dr(duc[:, :, : 3 * RK].reshape(2 * hcn, 3 * RK), dac[:, :, quarter : 2 * quarter].reshape(2 * hcn, quarter))

    fold.finish(dkv.at[:PLEN])
    unrotate(0, PLEN)
    dsum_p = TensorSum(dsnd_p, dgot_p, ds_p, dt_p, dpsem, d, t)
    dn1(0, snd_p, dsnd_p, dsum_p, False)
    sum_p = TensorSum(snd_p, got_p, s_p, t_p, psem, d, t)
    dsum_p.middle()
    sum_p.begin()
    put_units(l0s, 0, gacc[:, at[3] :].astype(BF))
    fill(l0s, (at[6] - at[3]) // LANE * (RK // 16))
    red0 = PairReduce(l0s, l0x, l0z, l0, rsems[16:24], d, t, n_dp)
    red0.start()
    sum_p.middle()
    red1.middle()
    du_copy_p = share_du(5, dsum_p, dup, sc[0])
    arrived(5, dup)
    ga_p = dr(dup[:, :, : 3 * RK].reshape(PLEN, 3 * RK), dap[:, :, quarter : 2 * quarter].reshape(PLEN, quarter))
    ga = (ga_c + ga_p).astype(BF)
    for n in range(3):
        put_units(l2s, n * per, ga[n * RK : (n + 1) * RK])
    fill(l2s, 3 * per)
    red2 = PairReduce(l2s, l2x, l2z, t2.at[lo], rsems[24:32], d, t, n_dp)
    red2.start()
    trade2 = Trade(t2, q2, d, t)

    def last(which, total, du, x, dh, tg):
        half = x.shape[0]
        tmp[:half] = dn(du[lo, :, : 3 * RK], aT[...])
        gain = gain1[...].astype(F32).reshape(1, width)
        total.end()

        def one(r):
            here = pl.ds(r, 64)
            dn1v = total.mine[here].astype(F32) + total.theirs[here].astype(F32) + tmp[here]
            grad = dh[here] + norm_back(x[here].astype(F32), gain, dn1v)
            tg[lo, here] = grad.astype(BF)

        rows_loop(half, 64, one)
        c = remote(tg.at[lo], tg.at[lo], nsem.at[which, 0], nsem.at[which, 1], (d, t ^ 1))
        c.start()
        return c

    red1.add()
    red0.middle()
    need(xc)
    load_dhc.wait()
    tg_copy_c = last(2, sum_c, duc, xc, hc, tgc)
    red2.middle()
    red1.cross()
    red0.add()
    every.finish()
    store(gef, gef_h)
    red2.add()
    arrived(2, tgc)
    for n in range(2):
        store(tgc.at[n], tg_h.at[pl.ds(PLEN + n * hcn, hcn)])
    red0.cross()
    red1.finish()
    trade1.start()
    red2.cross()
    trade1.finish()
    store(t1, t1_h)
    need(xp)
    load_dhp.wait()
    tg_copy_p = last(3, sum_p, dup, xp, hp, tgp)
    red0.finish()
    store(l0, l0_h)
    red2.finish()
    trade2.start()
    arrived(3, tgp)
    for n in range(2):
        store(tgp.at[n], tg_h.at[pl.ds(n * hpn, hpn)])
    trade2.finish()
    store(t2, t2_h)
    for c in (out_copy_p, out_copy_c, tg_copy_c, tg_copy_p, du_copy_c, du_copy_p, mlp_p, mlp_c):
        c.wait_send()
    for total in (sum_p, sum_c, dsum_p, dsum_c):
        total.drain()
    fold.drain()
    every.spread_sent()
    for red in (red0, red1, red2):
        red.sent()
        red.spread_sent()
    trade1.sent()
    trade2.sent()
    for c in stores:
        c.wait()


def backward(n_dp, scalars, small, large):
    (dac, wo, o, aoT, bo, n2c, uoc, q, kv, far, pc, cos, sin, dap, pp, n2p, uop, u, wq, wkv, bq, smp, hp, bd, smc, hc, dy, n1q,
     dhc, aT, dhp, tok, ge) = large
    rows, width = tok.shape
    qw = wq.shape[1]
    kvw2 = wkv.shape[1]
    quarter = n1q.shape[1]
    wide = dap.shape[2]
    hpn, hcn = PLEN // 2, CLEN
    per = quarter // LANE * (RK // 16)
    up = lambda a: -(-a // n_dp) * n_dp
    ue = ge.shape[0] * n_dp
    u0 = up((2 * qw + kvw2) // LANE * (RK // 16))
    u1 = up(4 * per)
    u2 = up(3 * per)
    outs = [
        ((rows, width), BF), ((rows, width), BF), ((ue, *UNIT), BF), ((u0, *UNIT), BF), ((2, u1, *UNIT), BF),
        ((2, u2, *UNIT), BF),
    ]
    dma = pltpu.SemaphoreType.DMA
    hi = n_dp // 2
    same = lambda a: VM(a.shape, a.dtype)

    def sums(half, n):
        return [VM((2, half, n), BF), VM((half, n), BF), VM((half, n), BF), VM((half, n), BF)]

    scratch = [
        same(dac), same(wo), same(o), same(aoT), same(bo), VM((2, hcn, quarter), BF), VM((2, hcn, LANE), BF), same(q), same(kv),
        same(far), same(pc), same(cos), same(sin), same(dap), same(pp), VM((2, hpn, quarter), BF), VM((2, hpn, LANE), BF),
        same(u), same(wq), same(wkv), same(bq), same(smp), same(hp), same(bd), same(smc), same(hc),
        same(aT), VM((hcn, width), BF), VM((hpn, width), BF), VM((ue, *UNIT), BF),
        same(smp), same(smc),
        VM((rows, qw), BF), VM((rows, qw), BF), VM((rows, kvw2), F32), VM((rows, kvw2), BF),
        VM((CONT_DEV, PLEN, kvw2), BF), VM((RK, 2 * qw + 3 * quarter + kvw2), F32),
        *sums(hpn, width), *sums(hcn, width), *sums(hpn, 2 * LANE), *sums(hcn, 2 * LANE),
        VM((2, hpn, 2 * LANE), BF), VM((2, hcn, 2 * LANE), BF),
        VM((2, hpn, wide), BF), VM((2, hcn, wide), BF), VM((2, hpn, width), BF), VM((2, hcn, width), BF), VM((hpn, width), F32),
        VM((u0, *UNIT), BF), VM((u0 // 2, *UNIT), BF), VM((hi, u0 // n_dp, *UNIT), BF), VM((u0, *UNIT), BF),
        VM((u1, *UNIT), BF), VM((u1 // 2, *UNIT), BF), VM((hi, u1 // n_dp, *UNIT), BF),
        VM((u2, *UNIT), BF), VM((u2 // 2, *UNIT), BF), VM((hi, u2 // n_dp, *UNIT), BF),
        VM((2, u1, *UNIT), BF), VM((2, u2, *UNIT), BF),
        VM((CONT_DEV, PLEN, kvw2), BF), VM((hi, PLEN, kvw2), BF), VM((hi, PLEN, kvw2), BF),
        dma((34,)), dma((13,)), dma((8,)), dma((4,)), dma((4,)), dma((4,)), dma((4,)), dma((4,)), dma((6, 2)), dma((2,)), dma((2,)),
    ] + [dma((CONT_DEV,))] * 2 + [dma((hi,))] * 2 + [dma((n_dp,))] * 32
    vm = pl.BlockSpec(memory_space=VM)
    anyspace = pl.BlockSpec(memory_space=pl.ANY)
    return pl.pallas_call(
        functools.partial(back_kernel, n_dp),
        out_shape=[jax.ShapeDtypeStruct(s, dtype) for s, dtype in outs],
        in_specs=[pl.BlockSpec(memory_space=pltpu.SMEM)] * 3 + [vm] * len(small) + [anyspace] * len(large),
        out_specs=[anyspace] * len(outs),
        scratch_shapes=scratch,
        compiler_params=pltpu.CompilerParams(vmem_limit_bytes=63 << 20, collective_id=3, has_side_effects=True),
        cost_estimate=pl.CostEstimate(flops=6 * rows * width * (2 * qw + kvw2), bytes_accessed=40 << 20, transcendentals=0),
        name="back",
    )(*scalars, *small, *large)


def emit_kernel(
    qw, kvw, quarter, hidden, ge, l0, t1, t2, out_h, tg_h,
    gbm, gad, gao, gbq, gbkv, gbo, gam, gbd, ga, out_o, tg_o, buf, sem,
):
    pairs = ((out_h, out_o), (tg_h, tg_o))
    copies = [pltpu.make_async_copy(src, buf.at[n], sem.at[n]) for n, (src, _) in enumerate(pairs)]
    for c in copies:
        c.start()
    high = RK // 16

    def take(blocks, first, count, put):
        for b in range(count // LANE):
            for r in range(high):
                put(slice(r * 16, (r + 1) * 16), slice(b * LANE, (b + 1) * LANE), blocks[first + b * high + r].astype(F32))

    def plain(dst, row=0, lane=0):
        def put(rows, lanes, value):
            dst[rows.start + row : rows.stop + row, lanes.start + lane : lanes.stop + lane] = value

        return put

    def paired(dst, n):
        def put(rows, lanes, value):
            dst[rows, n, lanes] = value

        return put

    seg = hidden // LANE * high
    take(ge, 0, hidden, paired(gbm, 0))
    take(ge, seg, hidden, paired(gbm, 1))
    take(ge, 2 * seg, hidden, plain(gad))
    take(l0, 0, qw, plain(gao))
    begin = qw // LANE * high
    half = kvw // LANE * high
    take(l0, begin, qw, plain(gbq))
    take(l0, 2 * begin, kvw, paired(gbkv, 0))
    take(l0, 2 * begin + half, kvw, paired(gbkv, 1))
    per = quarter // LANE * high
    for c in copies:
        c.wait()
    copies = [pltpu.make_async_copy(buf.at[n], dst, sem.at[2 + n]) for n, (_, dst) in enumerate(pairs)]
    for c in copies:
        c.start()
    for t in range(t1.shape[0]):
        take(t1.at[t], 0, quarter, plain(gbo, 0, t * quarter))
        take(t1.at[t], per, quarter, plain(gam, 0, t * quarter))
        take(t1.at[t], 2 * per, quarter, plain(gam, RK, t * quarter))
        take(t1.at[t], 3 * per, quarter, plain(gbd, 0, t * quarter))
        for n in range(3):
            take(t2.at[t], n * per, quarter, plain(ga, n * RK, t * quarter))
    for c in copies:
        c.wait()


def emit(qw, kvw, quarter, hidden, grads, results):
    width = 2 * quarter
    outs = [
        ((RK, 2, hidden), F32), ((RK, hidden), F32), ((RK, qw), F32), ((RK, qw), F32), ((RK, 2, kvw), F32), ((RK, width), F32),
        ((2 * RK, width), F32), ((RK, width), F32), ((3 * RK, width), F32),
    ] + [(a.shape, a.dtype) for a in results]
    vm = pl.BlockSpec(memory_space=VM)
    anyspace = pl.BlockSpec(memory_space=pl.ANY)
    return pl.pallas_call(
        functools.partial(emit_kernel, qw, kvw, quarter, hidden),
        out_shape=[jax.ShapeDtypeStruct(s, dtype) for s, dtype in outs],
        in_specs=[vm] * len(grads) + [anyspace] * len(results),
        out_specs=[vm] * 9 + [anyspace] * 2,
        scratch_shapes=[VM((2, *results[0].shape), BF), pltpu.SemaphoreType.DMA((4,))],
        compiler_params=pltpu.CompilerParams(vmem_limit_bytes=61 << 20),
        cost_estimate=pl.CostEstimate(flops=0, bytes_accessed=20 << 20, transcendentals=0),
        name="emit",
    )(*grads, *results)


def rope_tables():
    position = np.concatenate([np.arange(PLEN)] + [PLEN + np.arange(CLEN)] * CONT_DEV).astype(np.float32)
    exponent = np.arange(HD // 2, dtype=np.float32) * np.float32(2.0 / HD)
    frequency = np.exp(np.float32(-math.log(ROPE_BASE)) * exponent).astype(np.float32)
    angle = position[:, None] * frequency[None, :]
    cos, sin = np.cos(angle).astype(np.float32), np.sin(angle).astype(np.float32)
    return np.tile(cos, (1, 4)), np.concatenate([-sin, sin, -sin, sin], axis=1)


def shards(
    tokens, cotangent, gain_attn, gain_mlp, w_query, w_kv, w_out, w_gate_up, w_down, a_attn, b_query, b_kv,
    a_out, b_out, a_mlp, b_mlp, a_down, b_down, prompt_adapter, cont_adapter, group_map,
):
    rows, width = tokens.shape
    qw = w_query.shape[1]
    kvw = w_kv.shape[2]
    hidden = w_down.shape[0]
    n_dp = lax.axis_size("dp")
    quarter = width // 2
    cos_np, sin_np = rope_tables()
    cos, sin = jnp.asarray(cos_np), jnp.asarray(sin_np)
    gain1, gain2 = gain_attn, gain_mlp
    aT = a_attn.transpose(1, 2, 3, 0).reshape(3 * RK, width)
    aoT = a_out.transpose(1, 2, 0).reshape(RK, qw)
    amT = a_mlp.transpose(1, 2, 3, 0).reshape(2 * RK, width)
    adT = a_down.transpose(1, 2, 0).reshape(RK, hidden)
    bq = b_query.reshape(RK, qw)
    bkv = b_kv.reshape(RK, 2, kvw)
    bo = b_out.reshape(RK, width)
    bm = b_mlp.reshape(RK, 2, hidden)
    bd = b_down.reshape(RK, width)
    wkv = w_kv.reshape(width, 2 * kvw)
    (n1q, q, kv, u, pp, pc, o, far, h_p, h_c, n2p, n2c, uop, uoc, _, dh_p, dh_c, dap, dac, sm_p, sm_c, ge) = first(
        n_dp, [prompt_adapter, cont_adapter, group_map], [gain1, gain2, bkv, bm, amT, adT, bo],
        [tokens, aT, wkv, cos, sin, w_query, bq, aoT, w_out, cotangent, bd, w_down, w_gate_up],
    )
    results = backward(
        n_dp, [prompt_adapter, cont_adapter, group_map], [gain1, bkv],
        [dac, w_out, o, aoT, bo, n2c, uoc, q, kv, far, pc, cos, sin, dap, pp, n2p, uop, u, w_query, wkv, bq, sm_p, h_p, bd, sm_c,
         h_c, cotangent, n1q, dh_c, aT, dh_p, tokens, ge],
    )
    gbm, gad, gao, gbq, gbkv, gbo, gam, gbd, ga, output, tokens_grad = emit(qw, kvw, quarter, hidden, results[2:], results[:2])
    return (
        output,
        tokens_grad,
        ga.reshape(3, NA, R, width).transpose(3, 0, 1, 2),
        gbq.reshape(b_query.shape),
        gbkv.reshape(b_kv.shape),
        gao.reshape(NA, R, qw).transpose(2, 0, 1),
        gbo.reshape(b_out.shape),
        gam.reshape(2, NA, R, width).transpose(3, 0, 1, 2),
        gbm.reshape(b_mlp.shape),
        gad.reshape(NA, R, hidden).transpose(2, 0, 1),
        gbd.reshape(b_down.shape),
    )


def solution(mesh):
    in_specs = (
        P("dp", None), P("dp", None), P(), P(), P(None, "tensor"), P(None, None, "tensor"), P("tensor", None),
        P(None, None, "tensor"), P("tensor", None), P(), P(None, None, "tensor"), P(None, None, None, "tensor"),
        P("tensor", None, None), P(), P(), P(None, None, None, "tensor"), P("tensor", None, None), P(),
        P("dp"), P("dp"), P(),
    )
    out_specs = (
        P("dp", None), P("dp", None), P(), P(None, None, "tensor"), P(None, None, None, "tensor"),
        P("tensor", None, None), P(), P(), P(None, None, None, "tensor"), P("tensor", None, None), P(),
    )
    return jax.shard_map(shards, mesh=mesh, in_specs=in_specs, out_specs=out_specs, check_vma=False)
```

```python
import functools
import math

import jax
import jax.numpy as jnp
import numpy as np
from jax import lax
from jax.experimental import pallas as pl
from jax.experimental.pallas import tpu as pltpu
from jax.sharding import PartitionSpec as P

HD = 64
R = 16
NA = 4
RK = NA * R
PLEN = 384
CLEN = 128
CONT_DEV = 2
ROWS = PLEN + CONT_DEV * CLEN
EPSILON = 1e-05
ROPE_BASE = 500000.0
MASKED_SCORE = -1e30

BF = jnp.bfloat16
F32 = jnp.float32
VM = pltpu.VMEM
LANE = 128


def dn(a, b):
    return jnp.dot(a, b, preferred_element_type=F32)


def dt(a, b):
    return lax.dot_general(a, b, (((1,), (1,)), ((), ())), preferred_element_type=F32)


def dr(a, b):
    return lax.dot_general(a, b, (((0,), (0,)), ((), ())), preferred_element_type=F32)


def sel_row(adapter):
    lane = lax.broadcasted_iota(jnp.int32, (1, RK), 1)
    return (lax.shift_right_logical(lane, 4) == adapter).astype(F32)


def swap_halves(v):
    lane = lax.broadcasted_iota(jnp.int32, v.shape, 1)
    return jnp.where((lane & 63) < 32, pltpu.roll(v, LANE - 32, 1), pltpu.roll(v, 32, 1))


def rot(v, cos, sin):
    return v * cos + swap_halves(v) * sin


def stack_heads(ref, r0, g):
    return jnp.concatenate(
        [ref[pl.ds(r0, CLEN), (4 * g + h) * HD : (4 * g + h + 1) * HD] for h in range(4)], axis=0
    )


def softmax_low(s):
    top = jnp.max(s, axis=-1, keepdims=True)
    e = jnp.exp(s - top)
    return (e * (1.0 / jnp.sum(e, axis=-1, keepdims=True))).astype(BF)


def causal_tile():
    r = lax.broadcasted_iota(jnp.int32, (4 * CLEN, CLEN), 0) & (CLEN - 1)
    c = lax.broadcasted_iota(jnp.int32, (4 * CLEN, CLEN), 1)
    return c <= r


P_OFF = (0, 128, 384)


def norm_back(v, gain, upstream):
    inv = lax.rsqrt(jnp.mean(v * v, axis=-1, keepdims=True) + EPSILON)
    scaled = v * inv
    weighted = upstream * gain
    return inv * (weighted - scaled * jnp.mean(weighted * scaled, axis=-1, keepdims=True))


def put_dq(dq, dq_ref, r0, g):
    for h in range(4):
        dq_ref[pl.ds(r0, CLEN), (4 * g + h) * HD : (4 * g + h + 1) * HD] = dq[h * CLEN : (h + 1) * CLEN]


def back_scores(p, dp):
    pf = p.astype(F32)
    return (pf * (dp - jnp.sum(pf * dp, axis=-1, keepdims=True))).astype(BF)


MESH = pl.DeviceIdType.MESH


def rows_loop(total, step, body):
    def one(i, carry):
        body(pl.multiple_of(i * step, step))
        return carry

    lax.fori_loop(0, total // step, one, 0)


def loop(first, last, body):
    def one(i, carry):
        body(i)
        return carry

    lax.fori_loop(first, last, one, 0)


def place():
    d = lax.axis_index("dp")
    t = lax.axis_index("tensor")
    return d, t


def remote(src, dst, send, recv, device):
    return pltpu.make_async_remote_copy(
        src_ref=src, dst_ref=dst, send_sem=send, recv_sem=recv, device_id=device, device_id_type=MESH
    )


def greet(d, t, n_dp):
    barrier = pltpu.get_barrier_semaphore()
    for device in [(d, t ^ 1), (d, t ^ 2)] + [((d + k) % n_dp, t) for k in range(1, n_dp)]:
        pl.semaphore_signal(barrier, inc=1, device_id=device, device_id_type=MESH)


def greeted(n_dp):
    pl.semaphore_wait(pltpu.get_barrier_semaphore(), n_dp + 1)


class Spread:
    def __init__(self, every, sems, d, t, hi):
        self.every, self.sems, self.d, self.t, self.hi = every, sems, d, t, hi
        self.z, self.x = d // 2, d % 2

    def across(self, z):
        block = z * 2 + self.x
        up_s, up_r, down_s, down_r, x_s, x_r = self.sems
        return remote(self.every.at[block], self.every.at[block], x_s.at[z], x_r.at[z], (self.d ^ 1, self.t))

    def along(self, z, s, up):
        block = z * 2 + self.x
        up_s, up_r, down_s, down_r, x_s, x_r = self.sems
        send, recv, step = (up_s, up_r, 2) if up else (down_s, down_r, -2)
        return remote(self.every.at[block], self.every.at[block], send.at[s], recv.at[s], (self.d + step, self.t))

    def start(self):
        self.across(self.z).start()

        @pl.when(self.z < self.hi - 1)
        def _():
            self.along(self.z, 1, True).start()

        @pl.when(self.z > 0)
        def _():
            self.along(self.z, 1, False).start()

    def hop(self, s):
        if s > self.hi - 1:
            return
        for up in (True, False):
            origin = self.z - s if up else self.z + s
            held = origin >= 0 if up else origin < self.hi
            further = self.z < self.hi - 1 if up else self.z > 0

            @pl.when(held)
            def _(origin=origin, up=up, further=further):
                self.along(origin, s, up).wait_recv()
                self.across(origin).start()
                if s + 1 <= self.hi - 1:

                    @pl.when(further)
                    def _():
                        self.along(origin, s + 1, up).start()

    def finish(self):
        for z in range(self.hi):
            across = self.across(z)
            across.wait_send()
            block = z * 2 + 1 - self.x
            up_s, up_r, down_s, down_r, x_s, x_r = self.sems
            remote(self.every.at[block], self.every.at[block], x_s.at[z], x_r.at[z], (self.d ^ 1, self.t)).wait_recv()
        for s in range(1, self.hi):
            for up in (True, False):
                origin = self.z - s + 1 if up else self.z + s - 1
                held = origin >= 0 if up else origin < self.hi
                further = self.z < self.hi - 1 if up else self.z > 0

                @pl.when(held & further)
                def _(origin=origin, up=up, s=s):
                    self.along(origin, s, up).wait_send()


class TensorSum:
    def __init__(self, snd, got, mine, theirs, sems, d, t):
        self.snd, self.got, self.mine, self.theirs, self.sems, self.t = snd, got, mine, theirs, sems, t
        self.lo = t % 2
        self.core = remote(snd.at[1 - self.lo], got, sems.at[0], sems.at[1], (d, t ^ 1))
        self.chip = remote(mine, theirs, sems.at[2], sems.at[3], (d, t ^ 2))

    def begin(self):
        self.core.start()

    def middle(self):
        self.core.wait_recv()

        def add(r):
            rows = pl.ds(r, 64)
            self.mine[rows] = (self.snd[self.lo, rows].astype(F32) + self.got[rows].astype(F32)).astype(BF)

        rows_loop(self.mine.shape[0], 64, add)
        self.chip.start()

    def end(self):
        self.chip.wait_recv()

    def drain(self):
        self.core.wait_send()
        self.chip.wait_send()


UNIT = (16, LANE)


def put_units(blocks, first, value):
    for b in range(value.shape[1] // LANE):
        for r in range(RK // 16):
            blocks[first + b * (RK // 16) + r] = value[r * 16 : (r + 1) * 16, b * LANE : (b + 1) * LANE]


class DirectReduce:
    def __init__(self, src, got, out, sems, d, t, n_dp):
        self.src, self.got, self.out, self.sems, self.d, self.t, self.n = src, got, out, sems, d, t, n_dp
        self.share = src.shape[0] // n_dp if src is not None else out.shape[0] // n_dp

    def part(self, d):
        return pl.ds(((d % 2) * (self.n // 2) + d // 2) * self.share, self.share)

    def to(self, k):
        peer = (self.d + k) % self.n
        return remote(self.src.at[self.part(peer)], self.got.at[k], self.sems[0].at[k], self.sems[1].at[k], (peer, self.t))

    def back(self, k):
        peer = (self.d + k) % self.n
        here = self.part(self.d)
        return remote(self.out.at[here], self.out.at[here], self.sems[2].at[k], self.sems[3].at[k], (peer, self.t))

    def from_back(self, k):
        peer = (self.d + self.n - k) % self.n
        there = self.part(peer)
        return remote(self.out.at[there], self.out.at[there], self.sems[2].at[k], self.sems[3].at[k], (peer, self.t))

    def start(self):
        for k in range(1, self.n):
            self.to(k).start()

    def add(self):
        for k in range(1, self.n):
            self.to(k).wait_recv()
        here = self.part(self.d)
        total = self.src[here].astype(F32)
        for k in range(1, self.n):
            total = total + self.got[k].astype(F32)
        self.out[here] = total.astype(BF)

    def sent(self):
        for k in range(1, self.n):
            self.to(k).wait_send()

    def spread(self):
        for k in range(1, self.n):
            self.back(k).start()

    def finish(self):
        for k in range(1, self.n):
            self.from_back(k).wait_recv()

    def spread_sent(self):
        for k in range(1, self.n):
            self.back(k).wait_send()


class PairReduce:
    def __init__(self, src, gx, gz, out, sems, d, t, n_dp):
        self.src, self.gx, self.gz, self.out, self.sems, self.t = src, gx, gz, out, sems, t
        self.hi, self.z, self.x = n_dp // 2, d // 2, d % 2
        self.share = out.shape[0] // n_dp
        self.mate = (d ^ 1, t)

    def part(self, z):
        return pl.ds((self.x * self.hi + z) * self.share, self.share)

    def half(self, x):
        return pl.ds(x * self.hi * self.share, self.hi * self.share)

    def on_line(self, k):
        z = (self.z + k) % self.hi
        return z, (z * 2 + self.x, self.t)

    def over(self):
        return remote(self.src.at[self.half(1 - self.x)], self.gx, self.sems[0].at[0], self.sems[1].at[0], self.mate)

    def to(self, k):
        z, device = self.on_line(k)
        return remote(self.src.at[self.part(z)], self.gz.at[k], self.sems[2].at[k], self.sems[3].at[k], device)

    def back(self, k, come=False):
        z, device = self.on_line(self.hi - k if come else k)
        here = self.part(z if come else self.z)
        return remote(self.out.at[here], self.out.at[here], self.sems[4].at[k], self.sems[5].at[k], device)

    def over_back(self, x):
        here = self.half(x)
        return remote(self.out.at[here], self.out.at[here], self.sems[6].at[0], self.sems[7].at[0], self.mate)

    def start(self):
        self.over().start()

    def middle(self):
        self.over().wait_recv()
        here = self.half(self.x)
        self.src[here] = (self.src[here].astype(F32) + self.gx[...].astype(F32)).astype(BF)
        for k in range(1, self.hi):
            self.to(k).start()

    def add(self):
        here = self.part(self.z)
        total = self.src[here].astype(F32)
        for k in range(1, self.hi):
            self.to(k).wait_recv()
            total = total + self.gz[k].astype(F32)
        self.out[here] = total.astype(BF)
        self.spread()

    def spread(self):
        for k in range(1, self.hi):
            self.back(k).start()

    def cross(self):
        for k in range(1, self.hi):
            self.back(k, True).wait_recv()
        self.over_back(self.x).start()

    def finish(self):
        self.over_back(1 - self.x).wait_recv()

    def spread_sent(self):
        for k in range(1, self.hi):
            self.back(k).wait_send()
        self.over_back(self.x).wait_send()

    def sent(self):
        self.over().wait_send()
        for k in range(1, self.hi):
            self.to(k).wait_send()


class Trade:
    def __init__(self, halves, sems, d, t):
        self.halves, self.sems, self.d, self.t = halves, sems, d, t

    def slot(self, n):
        return remote(self.halves.at[n], self.halves.at[n], self.sems.at[0], self.sems.at[1], (self.d, self.t ^ 1))

    def start(self):
        self.slot(self.t % 2).start()

    def finish(self):
        self.slot(1 - self.t % 2).wait_recv()

    def sent(self):
        self.slot(self.t % 2).wait_send()


def evens_first(n):
    r = lax.broadcasted_iota(jnp.int32, (n, n), 0)
    c = lax.broadcasted_iota(jnp.int32, (n, n), 1)
    return (c == jnp.where(r < n // 2, 2 * r, 2 * (r - n // 2) + 1)).astype(BF)


def all_sel(sc):
    return jnp.concatenate(
        [
            jnp.broadcast_to(sel_row(sc[0]), (PLEN, RK)),
            jnp.broadcast_to(sel_row(sc[1]), (CLEN, RK)),
            jnp.broadcast_to(sel_row(sc[2]), (CLEN, RK)),
        ],
        axis=0,
    )


def first_kernel(
    n_dp, ids_p, ids_c, group_map, gain1, gain2, bkv_ref, bm_h, amT_h, adT_h, bo_h,
    tok_h, aT_h, wkv_h, cos_h, sin_h, wq_h, bq_h, aoT_h, wo_h, dy_h, bd_h, wd_h, raw_h,
    n1q_h, q_h, kv_h, u_h, pp_h, pc_h, o_h, far_h, hp_h, hc_h, n2p_h, n2c_h, uop_h, uoc_h, wgu_h,
    dhp_h, dhc_h, dap_h, dac_h, smp_h, smc_h, ge_h,
    every, snd_p, s_p, snd_c, s_c, got0_p, t0_p, got0_c, t0_c, got1_p, t1_p, got1_c, t1_c,
    n2p, n2c, uop, uoc, hp, hc, xp, xc, dyp, dyc, dact, dud, tmp, ge, gots, bm, amT, adT, bo,
    lsem, osem, wsem, rsem, fsem, vsem, psem, csem, psem2, csem2, msem, nsem, up_s, up_r, down_s, down_r, x_s, x_r, g0, g1,
):
    d, t = place()
    sc = [ids_p[0], ids_c[0], ids_c[1], group_map[d * CONT_DEV], group_map[d * CONT_DEV + 1]]
    lo = t % 2
    hi = n_dp // 2
    rows, width = tok_h.shape
    wide = n2p.shape[2]
    qw = wq_h.shape[1]
    kvw = wkv_h.shape[1] // 2
    hidden = wd_h.shape[0]
    ht = 512
    steps = hidden // ht
    hpn, hcn = PLEN // 2, CLEN
    part = n1q_h.shape[1]
    qlanes = pl.ds(pl.multiple_of(lo * part, part), part)
    adapter_c = jnp.where(lo == 0, sc[1], sc[2])
    greet(d, t, n_dp)
    counts = [0, 0]

    def load(src, dst):
        c = pltpu.make_async_copy(src, dst, lsem.at[counts[0]])
        counts[0] += 1
        c.start()
        return c

    def store(src, dst):
        c = pltpu.make_async_copy(src, dst, osem.at[counts[1]])
        counts[1] += 1
        c.start()
        return c

    spread = Spread(every, (up_s, up_r, down_s, down_r, x_s, x_r), d, t, hi)
    sum_p = TensorSum(snd_p, got0_p, s_p, t0_p, psem, d, t)
    sum_c = TensorSum(snd_c, got0_c, s_c, t0_c, csem, d, t)
    sel = all_sel(sc)
    b2 = 2 * RK

    def attention(tok, n1, aT, wkv, cos, sin, wq, bq, aoT, wo, bd, wdc, raw, flat, bflat, kv, q, u, far, pp, pc, o):
        kt = raw.shape[1]
        raw_steps = width // kt

        def raw_copy(i, slot):
            return pltpu.make_async_copy(raw_h.at[pl.ds(i * kt, kt)], raw.at[slot], rsem.at[slot])

        def flat_copies(i, slot):
            here = pl.ds(i * kt, kt)
            return (
                pltpu.make_async_copy(flat.at[slot, 0], wgu_h.at[here, :hidden], fsem.at[slot, 0]),
                pltpu.make_async_copy(flat.at[slot, 1], wgu_h.at[here, hidden:], fsem.at[slot, 1]),
            )

        def wd_copy(i, slot):
            return pltpu.make_async_copy(wd_h.at[pl.ds(i * ht, ht)], wdc.at[slot, :, :width], wsem.at[slot, 0])

        load_tok = load(tok_h, tok.at[:, :width])
        load_kv = [load(a, b) for a, b in ((aT_h, aT), (wkv_h, wkv), (cos_h, cos), (sin_h, sin))]
        load_q = [load(a, b) for a, b in ((wq_h, wq), (bq_h, bq))]
        stores = []

        bkv = dn(evens_first(b2), bkv_ref[...].reshape(b2, kvw)).astype(BF)
        gain_row = gain1[...].astype(F32).reshape(1, width)
        load_tok.wait()

        def norm1(r):
            x = tok[pl.ds(r, 128), :width].astype(F32)
            inv = lax.rsqrt(jnp.mean(x * x, axis=-1, keepdims=True) + EPSILON)
            n1[pl.ds(r, 128)] = (x * inv * gain_row).astype(BF)

        rows_loop(rows, 128, norm1)
        load_o = [load(a, b) for a, b in ((aoT_h, aoT), (wo_h, wo))]
        load_dy = [load(a, b) for a, b in ((dy_h, tok.at[:, :width]), (bd_h, bd), (adT_h, adT))]
        for i in range(2):
            wd_copy(i, i).start()
        for i in range(raw.shape[0]):
            raw_copy(i, i).start()
        load_bm = load(bm_h, bm)
        load_x = [
            load(tok_h.at[pl.ds(pl.multiple_of(lo * hpn, hpn), hpn)], xp),
            load(tok_h.at[pl.ds(pl.multiple_of(PLEN + lo * hcn, hcn), hcn)], xc),
            load(amT_h, amT),
            load(bo_h, bo),
        ]
        for c in load_kv:
            c.wait()
        uf = dt(n1[...], aT[...])
        for part in range(3):
            u[:, part * RK : (part + 1) * RK] = (uf[:, part * RK : (part + 1) * RK] * sel).astype(BF)
        kvf = dn(n1[...], wkv[...])
        kv[:, :kvw] = rot(kvf[:, :kvw] + dn(u[:, RK : 2 * RK], bkv[:RK]), cos[...], sin[...]).astype(BF)
        kv[:, kvw:] = (kvf[:, kvw:] + dn(u[:, 2 * RK :], bkv[RK:])).astype(BF)
        every[d] = kv[:PLEN]
        greeted(n_dp)
        spread.start()

        for c in load_q:
            c.wait()
        qf = dn(n1[...], wq[...]) + dn(u[:, :RK], bq[...])
        for c in range(qw // LANE):
            lanes = slice(c * LANE, (c + 1) * LANE)
            q[:, lanes] = rot(qf[:, lanes], cos[...], sin[...]).astype(BF) * BF(0.125)
        stores.append(store(n1.at[:, qlanes], n1q_h))
        stores.append(store(q, q_h))
        stores.append(store(kv, kv_h))
        stores.append(store(u, u_h))

        def keep_o(of, r0, g):
            for h in range(4):
                o[pl.ds(r0, CLEN), (4 * g + h) * HD : (4 * g + h + 1) * HD] = of[h * CLEN : (h + 1) * CLEN]

        mask = causal_tile()
        for g in range(2):
            kg = kv[:PLEN, g * HD : (g + 1) * HD]
            vg = kv[:PLEN, kvw + g * HD : kvw + (g + 1) * HD]
            for i in range(PLEN // CLEN):
                size = (i + 1) * CLEN
                s = dt(stack_heads(q, i * CLEN, g), kg[:size])
                tail = jnp.where(mask, s[:, size - CLEN :], MASKED_SCORE)
                s = tail if i == 0 else jnp.concatenate([s[:, : size - CLEN], tail], axis=1)
                p = softmax_low(s)
                pp[g, :, P_OFF[i] : P_OFF[i] + size] = p
                keep_o(dn(p, vg[:size]).astype(BF), i * CLEN, g)
        stores.append(store(pp, pp_h))
        spread.hop(1)

        def project(r0, half, snd):
            ov = o[r0 : r0 + 2 * half]

            def columns(n):
                lanes = pl.ds(pl.multiple_of(n * 512, 512), 512)
                part = dn(ov, wo[:, lanes]).astype(BF)
                snd[0, :, lanes] = part[:half]
                snd[1, :, lanes] = part[half:]

            loop(0, width // 512, columns)
            uo = dt(ov, aoT[...]).astype(BF)
            pad = jnp.zeros((half, LANE - RK), BF)
            snd[0, :, width:] = jnp.concatenate([uo[:half], pad], axis=1)
            snd[1, :, width:] = jnp.concatenate([uo[half:], pad], axis=1)

        for c in load_o:
            c.wait()
        project(0, hpn, snd_p)
        sum_p.begin()

        for c in load_dy:
            c.wait()
        dudv = (dt(tok[:, :width], bd[...]) * sel).astype(BF)
        dud[...] = jnp.concatenate([dudv, jnp.zeros((rows, LANE - RK), BF)], axis=1)
        tok[:, width:] = dud[...]
        eye = (lax.broadcasted_iota(jnp.int32, (RK, RK), 0) == lax.broadcasted_iota(jnp.int32, (RK, RK), 1)).astype(BF)
        split = evens_first(256)

        slots, flats = raw.shape[0], flat.shape[0]

        def part_weights(i):
            slot = i % slots
            raw_copy(i, slot).wait()

            put = i % flats

            @pl.when(i >= flats)
            def _():
                for c in flat_copies(i - flats, put):
                    c.wait()

            apart = dn(split, raw[slot].reshape(2 * kt, hidden)).astype(BF)
            flat[put, 0] = apart[:kt]
            flat[put, 1] = apart[kt:]
            for c in flat_copies(i, put):
                c.start()

            @pl.when(i + slots < raw_steps)
            def _():
                raw_copy(i + slots, slot).start()

        def act_grad(i):
            slot = i % 2
            wd_copy(i, slot).wait()
            lanes = pl.ds(pl.multiple_of(i * ht, ht), ht)
            ad = dr(adT[:, lanes], eye).astype(BF)
            wdc[slot, :, width:] = jnp.concatenate([ad, jnp.zeros((ht, LANE - RK), BF)], axis=1)
            dact[:, lanes] = dt(tok[...], wdc[slot]).astype(BF)

            @pl.when(i + 2 < steps)
            def _():
                wd_copy(i + 2, slot).start()

        def both(i):
            act_grad(i)

            @pl.when(i == 0)
            def _():
                spread.hop(2)

            @pl.when(i == 1)
            def _():
                spread.hop(3)

            per = raw_steps // steps
            loop(i * per, (i + 1) * per, part_weights)

        def continuations():
            far[0] = every[sc[3]]
            far[1] = every[sc[4]]
            stores.append(store(far, far_h))

            def attend(j):
                r0 = pl.multiple_of(PLEN + j * CLEN, CLEN)
                own = pl.ds(r0, CLEN)
                for g in range(2):
                    lanes = slice(g * HD, (g + 1) * HD)
                    vlanes = slice(kvw + g * HD, kvw + (g + 1) * HD)
                    qs = stack_heads(q, r0, g)
                    sf = dt(qs, far[j, :, lanes])
                    so = jnp.where(mask, dt(qs, kv[own, lanes]), MASKED_SCORE)
                    p = softmax_low(jnp.concatenate([sf, so], axis=1))
                    pc[2 * j + g] = p
                    keep_o((dn(p[:, :PLEN], far[j, :, vlanes]) + dn(p[:, PLEN:], kv[own, vlanes])).astype(BF), r0, g)

            loop(0, CONT_DEV, attend)
            stores.append(store(pc, pc_h))
            stores.append(store(o, o_h))
            project(PLEN, hcn, snd_c)
            sum_c.begin()

        sum_p.middle()
        loop(0, steps - 1, both)
        for s in range(4, hi):
            spread.hop(s)
        spread.finish()
        continuations()
        act_grad(steps - 1)
        sum_c.middle()
        loop((steps - 1) * (raw_steps // steps), raw_steps, part_weights)
        load_bm.wait()
        bsplit = dn(evens_first(b2), bm[...].reshape(b2, hidden)).astype(BF)
        zero = jnp.zeros((RK, hidden), BF)
        bflat[:RK, :hidden] = bsplit[:RK]
        bflat[:RK, hidden:] = zero
        bflat[RK:, :hidden] = zero
        bflat[RK:, hidden:] = bsplit[RK:]
        stores.append(store(bflat, wgu_h.at[pl.ds(width, b2)]))
        for c in load_x:
            c.wait()
        for i in range(raw_steps - flats, raw_steps):
            for c in flat_copies(i, i % flats):
                c.wait()
        for c in stores:
            c.wait()

    pl.run_scoped(
        attention,
        VM((rows, wide), BF), VM((rows, width), BF), VM(aT_h.shape, BF), VM(wkv_h.shape, BF), VM(cos_h.shape, F32),
        VM(sin_h.shape, F32), VM(wq_h.shape, BF), VM(bq_h.shape, BF), VM(aoT_h.shape, BF), VM(wo_h.shape, BF), VM(bd_h.shape, BF),
        VM((2, ht, wide), BF), VM((3, 128, 2, hidden), BF), VM((3, 2, 128, hidden), BF), VM((b2, 2 * hidden), BF),
        VM((rows, 2 * kvw), BF), VM((rows, qw), BF), VM((rows, 3 * RK), BF), VM((CONT_DEV, PLEN, 2 * kvw), BF),
        VM((2, 4 * CLEN, 768), BF), VM((4, 4 * CLEN, 4 * CLEN), BF), VM((rows, qw), BF),
    )

    def feed_forward(wcat, wdn, acc, gu, dga, act, gg):
        nt = wdn.shape[2]

        def weights(k, slot):
            i = k % steps
            here = pl.ds(pl.multiple_of(i * ht, ht), ht)
            there = pl.ds(pl.multiple_of(hidden + i * ht, ht), ht)
            return [
                pltpu.make_async_copy(src, dst, wsem.at[slot, n])
                for n, (src, dst) in enumerate(
                    [(wgu_h.at[:, here], wcat.at[slot, :, :ht]), (wgu_h.at[:, there], wcat.at[slot, :, ht:])]
                )
            ]

        def down(n, slot):
            return pltpu.make_async_copy(wd_h.at[:, pl.ds(n * nt, nt)], wdn.at[slot], vsem.at[slot])

        for c in weights(0, 0):
            c.start()
        load_dy = [
            load(dy_h.at[pl.ds(pl.multiple_of(lo * hpn, hpn), hpn)], dyp),
            load(dy_h.at[pl.ds(pl.multiple_of(PLEN + lo * hcn, hcn), hcn)], dyc),
        ]
        for n in range(2):
            down(n, n).start()

        def norm2(which, total, x, h, n2, adapter):
            half = h.shape[0]
            total.end()
            sr = sel_row(adapter)
            uo = (total.mine[:, width : width + RK].astype(F32) + total.theirs[:, width : width + RK].astype(F32)) * sr
            uo = uo.astype(BF)
            tmp[:half] = dn(uo, bo[...])
            gain_two = gain2[...].astype(F32).reshape(1, width)

            def one(r):
                here = pl.ds(r, 64)
                hv = (
                    x[here].astype(F32)
                    + (total.mine[here, :width].astype(F32) + total.theirs[here, :width].astype(F32))
                    + tmp[here]
                )
                h[here] = hv
                inv = lax.rsqrt(jnp.mean(hv * hv, axis=-1, keepdims=True) + EPSILON)
                n2[lo, here, :width] = (hv * inv * gain_two).astype(BF)

            rows_loop(half, 64, one)
            n2[lo, :, width:] = jnp.concatenate([uo, jnp.zeros((half, LANE - RK), BF)], axis=1)
            c = remote(n2.at[lo], n2.at[lo], nsem.at[which, 0], nsem.at[which, 1], (d, t ^ 1))
            c.start()
            return c

        def arrived(which, n2):
            remote(n2.at[1 - lo], n2.at[1 - lo], nsem.at[which, 0], nsem.at[which, 1], (d, t ^ 1)).wait_recv()

        def begin(n2, uo, chosen):
            half = n2.shape[1]
            r = 2 * half
            um = dt(n2[:, :, :width].reshape(r, width), amT[...])
            um = jnp.concatenate([(um[:, :RK] * chosen).astype(BF), (um[:, RK:] * chosen).astype(BF)], axis=1)
            uo[...] = n2[:, :, width:]
            n2[:, :, width:] = um.reshape(2, half, 2 * RK)
            acc[:r] = jnp.zeros((r, wide), F32)

        def tile(k, n2, base, add):
            r = 2 * n2.shape[1]
            slot = k % 2
            i = k % steps
            for c in weights(k, slot):
                c.wait()

            @pl.when(k + 1 < 2 * steps)
            def _():
                for c in weights(k + 1, 1 - slot):
                    c.start()

            gu[:r] = dn(n2[...].reshape(r, wide), wcat[slot])
            lanes = pl.ds(pl.multiple_of(i * ht, ht), ht)

            def swiglu(r0):
                here = pl.ds(r0, 64)
                gate = gu[here, :ht]
                upper = gu[here, ht:]
                sigma = 1.0 / (1.0 + jnp.exp(-gate))
                silu = gate * sigma
                there = pl.ds(base + r0, 64)
                da = dact[there, lanes].astype(F32)
                dga[here, :ht] = (da * upper * (sigma * (1.0 + gate * (1.0 - sigma)))).astype(BF)
                dga[here, ht : 2 * ht] = (da * silu).astype(BF)
                av = (silu * upper).astype(BF)
                dga[here, 2 * ht :] = av
                act[there, lanes] = av

            for r0 in range(0, r, 64):
                swiglu(r0)
            acc[:r] += dt(dga[:r, : 2 * ht], wcat[slot])
            small = jnp.concatenate([n2[:, :, width:].reshape(r, 2 * RK), dud[base : base + r, :RK]], axis=1)
            g = dr(small, dga[:r])
            for n in range(3):
                part = g[n * RK : (n + 1) * RK, n * ht : (n + 1) * ht]
                if add:
                    total = (gg[n, :, lanes] + part).astype(BF)
                    units = ht // LANE * (RK // 16)
                    put_units(ge, n * (hidden // LANE * (RK // 16)) + i * units, total)
                else:
                    gg[n, :, lanes] = part

        def halves(a, snd):
            half = snd.shape[1]

            def one(r0):
                for n in range(2):
                    snd[n, pl.ds(r0, 64)] = a[pl.ds(pl.multiple_of(n * half + r0, 64), 64)].astype(BF)

            rows_loop(half, 64, one)

        n2_copy_p = norm2(0, sum_p, xp, hp, n2p, sc[0])
        store_hp = store(hp, hp_h)
        arrived(0, n2p)
        n2_copy_p.wait_send()
        store_n2p = store(n2p.at[:, :, qlanes], n2p_h)
        begin(n2p, uop, sel_row(sc[0]))
        tail_stores = [store(uop, uop_h)]

        loop(0, steps, lambda k: tile(k, n2p, 0, False))
        sum_p.drain()
        halves(acc, snd_p)
        store_n2p.wait()
        sum2_p = TensorSum(snd_p, got1_p, s_p, t1_p, psem2, d, t)
        sum2_p.begin()

        n2_copy_c = norm2(1, sum_c, xc, hc, n2c, adapter_c)
        store_hc = store(hc, hc_h)
        sum2_p.middle()
        arrived(1, n2c)
        n2_copy_c.wait_send()
        store_n2c = store(n2c.at[:, :, qlanes], n2c_h)
        begin(
            n2c, uoc,
            jnp.concatenate([jnp.broadcast_to(sel_row(sc[1]), (hcn, RK)), jnp.broadcast_to(sel_row(sc[2]), (hcn, RK))], axis=0),
        )
        tail_stores.append(store(uoc, uoc_h))

        loop(steps, 2 * steps, lambda k: tile(k, n2c, PLEN, True))
        sum_c.drain()
        halves(acc, snd_c)
        store_n2c.wait()
        sum2_c = TensorSum(snd_c, got1_c, s_c, t1_c, csem2, d, t)
        sum2_c.begin()
        reduce = DirectReduce(ge, gots, ge, (g0, g1, None, None), d, t, n_dp)
        reduce.start()

        ud = dt(act[...], adT[...]).astype(BF)
        sum2_c.middle()
        sum2_p.core.wait_send()
        sum2_c.core.wait_send()
        pad = jnp.zeros((hpn, LANE - RK), BF)
        for n in range(2):
            snd_p[n, :, width:] = jnp.concatenate([ud[n * hpn : (n + 1) * hpn], pad], axis=1)
            snd_c[n, :, width:] = jnp.concatenate([ud[PLEN + n * hcn : PLEN + (n + 1) * hcn], pad[:hcn]], axis=1)

        def project_down(n):
            slot = n % 2
            down(n, slot).wait()
            part = dn(act[...], wdn[slot]).astype(BF)
            lanes = pl.ds(pl.multiple_of(n * nt, nt), nt)
            for i in range(2):
                snd_p[i, :, lanes] = part[i * hpn : (i + 1) * hpn]
                snd_c[i, :, lanes] = part[PLEN + i * hcn : PLEN + (i + 1) * hcn]

            @pl.when(n + 2 < width // nt)
            def _():
                down(n + 2, slot).start()

        loop(0, width // nt, project_down)
        mcore_p = remote(snd_p.at[1 - lo], got0_p, msem.at[0], msem.at[1], (d, t ^ 1))
        mcore_p.start()
        mcore_c = remote(snd_c.at[1 - lo], got0_c, msem.at[2], msem.at[3], (d, t ^ 1))
        mcore_c.start()

        def mlp_sum(core, snd, got, out):
            core.wait_recv()

            def add(r0):
                here = pl.ds(r0, 64)
                got[here] = (snd[lo, here].astype(F32) + got[here].astype(F32)).astype(BF)

            rows_loop(got.shape[0], 64, add)
            tail_stores.append(store(got, out))

        def back(which, total, h, dy, da, adapter):
            half = h.shape[0]
            total.end()
            sr = sel_row(adapter)
            du = total.mine[:, width:].astype(F32) + total.theirs[:, width:].astype(F32)
            dum = (du * jnp.concatenate([sr, sr], axis=1)).astype(BF)
            tmp[:half] = dn(dum, amT[...])
            gain = gain2[...].astype(F32).reshape(1, width)

            def one(r0):
                here = pl.ds(r0, 64)
                dn2 = total.mine[here, :width].astype(F32) + total.theirs[here, :width].astype(F32) + tmp[here]
                dh = dy[here].astype(F32) + norm_back(h[here], gain, dn2)
                h[here] = dh
                da[lo, here, :width] = dh.astype(BF)

            rows_loop(half, 64, one)
            da[lo, :, width:] = dum
            c = remote(da.at[lo], da.at[lo], nsem.at[which, 0], nsem.at[which, 1], (d, t ^ 1))
            c.start()
            return c

        for c in load_dy:
            c.wait()
        store_hp.wait()
        store_hc.wait()
        copy_p = back(2, sum2_p, hp, dyp, n2p, sc[0])
        tail_stores.append(store(hp, dhp_h))
        mlp_sum(mcore_p, snd_p, got0_p, smp_h)
        mlp_sum(mcore_c, snd_c, got0_c, smc_h)
        arrived(2, n2p)
        tail_stores.append(store(n2p, dap_h))
        reduce.add()
        tail_stores.append(store(ge.at[reduce.part(d)], ge_h))
        copy_c = back(3, sum2_c, hc, dyc, n2c, adapter_c)
        tail_stores.append(store(hc, dhc_h))
        arrived(3, n2c)
        tail_stores.append(store(n2c, dac_h))
        copy_p.wait_send()
        copy_c.wait_send()
        sum2_p.chip.wait_send()
        sum2_c.chip.wait_send()
        mcore_p.wait_send()
        mcore_c.wait_send()
        reduce.sent()
        for c in tail_stores:
            c.wait()

    pl.run_scoped(
        feed_forward,
        VM((2, wide, 2 * ht), BF), VM((2, hidden, 512), BF), VM((PLEN, wide), F32), VM((PLEN, 2 * ht), F32), VM((PLEN, 3 * ht), BF),
        VM((rows, hidden), BF), VM((3, RK, hidden), F32),
    )


def first(n_dp, scalars, small, large):
    tok, aT, wkv, cos, sin, wq, bq, aoT, wo, dy, bd, wd, raw = large
    rows, width = tok.shape
    qw = wq.shape[1]
    kvw2 = wkv.shape[1]
    hidden = wd.shape[0]
    quarter = width // 2
    wide = width + LANE
    hpn, hcn = PLEN // 2, CLEN
    units = 3 * hidden // LANE * (RK // 16)
    share = units // n_dp
    outs = [
        ((rows, quarter), BF), ((rows, qw), BF), ((rows, kvw2), BF), ((rows, 3 * RK), BF), ((2, 4 * CLEN, 768), BF),
        ((4, 4 * CLEN, 4 * CLEN), BF), ((rows, qw), BF), ((CONT_DEV, PLEN, kvw2), BF), ((hpn, width), F32),
        ((hcn, width), F32), ((2, hpn, quarter), BF), ((2, hcn, quarter), BF), ((2, hpn, LANE), BF), ((2, hcn, LANE), BF),
        ((width + 2 * RK, 2 * hidden), BF),
        ((hpn, width), F32), ((hcn, width), F32), ((2, hpn, wide), BF), ((2, hcn, wide), BF), ((hpn, wide), BF),
        ((hcn, wide), BF), ((share, *UNIT), BF),
    ]
    dma = pltpu.SemaphoreType.DMA
    scratch = [
        VM((n_dp, PLEN, kvw2), BF), VM((2, hpn, wide), BF), VM((hpn, wide), BF), VM((2, hcn, wide), BF), VM((hcn, wide), BF),
    ] + [VM((hpn, wide), BF), VM((hpn, wide), BF), VM((hcn, wide), BF), VM((hcn, wide), BF)] * 2 + [
        VM((2, hpn, wide), BF), VM((2, hcn, wide), BF), VM((2, hpn, LANE), BF), VM((2, hcn, LANE), BF),
        VM((hpn, width), F32), VM((hcn, width), F32), VM((hpn, width), BF), VM((hcn, width), BF), VM((hpn, width), BF),
        VM((hcn, width), BF), VM((rows, hidden), BF), VM((rows, LANE), BF), VM((hpn, width), F32),
        VM((units, *UNIT), BF), VM((n_dp, share, *UNIT), BF),
        VM((RK, 2, hidden), BF), VM((2 * RK, width), BF), VM((RK, hidden), BF), VM((RK, width), BF),
        dma((20,)), dma((22,)), dma((2, 2)), dma((4,)), dma((4, 2)), dma((2,)), dma((4,)), dma((4,)), dma((4,)), dma((4,)),
        dma((4,)), dma((4, 2)),
    ] + [dma((n_dp // 2 + 1,))] * 6 + [dma((n_dp,))] * 2
    vm = pl.BlockSpec(memory_space=VM)
    anyspace = pl.BlockSpec(memory_space=pl.ANY)
    return pl.pallas_call(
        functools.partial(first_kernel, n_dp),
        out_shape=[jax.ShapeDtypeStruct(s, dtype) for s, dtype in outs],
        in_specs=[pl.BlockSpec(memory_space=pltpu.SMEM)] * 3 + [vm] * 3 + [anyspace] * (len(small) - 3 + len(large)),
        out_specs=[anyspace] * len(outs),
        scratch_shapes=scratch,
        compiler_params=pltpu.CompilerParams(vmem_limit_bytes=63 << 20, collective_id=1, has_side_effects=True),
        cost_estimate=pl.CostEstimate(flops=12 * rows * width * hidden, bytes_accessed=120 << 20, transcendentals=0),
        name="first",
    )(*scalars, *small, *large)


class Fold:
    def __init__(self, dfar, xr, zs, zr, sems, owners, others, d, t, hi):
        self.dfar, self.xr, self.zs, self.zr, self.sems = dfar, xr, zs, zr, sems
        self.owners, self.others, self.d, self.t, self.hi = owners, others, d, t, hi
        self.z, self.x = d // 2, d % 2

    def across(self, j):
        return remote(self.dfar.at[j], self.xr.at[j], self.sems[0].at[j], self.sems[1].at[j], (self.d ^ 1, self.t))

    def along(self, z, come=False):
        slot = z if come else self.z
        return remote(
            self.zr.at[slot] if come else self.zs.at[z], self.zr.at[slot], self.sems[2].at[z], self.sems[3].at[slot],
            (z * 2 + self.x, self.t),
        )

    def held(self, z, rows):
        dest = z * 2 + self.x
        total = None
        for parts, owners in ((self.dfar, self.owners), (self.xr, self.others)):
            for j in range(CONT_DEV):
                term = parts[j, rows].astype(F32) * (owners[j] == dest).astype(F32)
                total = term if total is None else total + term
        return total

    def fold(self):
        for j in range(CONT_DEV):
            self.across(j).wait_recv()
        order = sorted(range(self.hi), key=lambda z: min(z, self.hi - 1 - z))
        for z in order:

            @pl.when(self.z != z)
            def _(z=z):
                def put(r):
                    rows = pl.ds(r, 64)
                    self.zs[z, rows] = self.held(z, rows).astype(BF)

                rows_loop(PLEN, 64, put)
                self.along(z).start()

    def finish(self, total):
        def own(r):
            rows = pl.ds(r, 64)
            total[rows] += self.held(self.z, rows)

        rows_loop(PLEN, 64, own)
        for z in range(self.hi):

            @pl.when(self.z != z)
            def _(z=z):
                self.along(z, True).wait_recv()
                total[...] += self.zr[z].astype(F32)

    def drain(self):
        for j in range(CONT_DEV):
            self.across(j).wait_send()
        for z in range(self.hi):

            @pl.when(self.z != z)
            def _(z=z):
                self.along(z).wait_send()


def back_kernel(
    n_dp, ids_p, ids_c, group_map, gain1, bkv_ref,
    dac_h, wo_h, o_h, aoT_h, bo_h, n2c_h, uoc_h, q_h, kv_h, far_h, pc_h, cos_h, sin_h, dap_h, pp_h, n2p_h, uop_h, u_h, wq_h, wkv_h, bq_h,
    smp_h, hp_h, bd_h, smc_h, hc_h, dy_h, n1q_h, dhc_h, aT_h, dhp_h, tok_h, ge_h,
    out_h, tg_h, gef_h, l0_h, t1_h, t2_h,
    dac, wo, o, aoT, bo, n2c, uoc, q, kv, far, pc, cos, sin, dap, pp, n2p, uop, u, wq, wkv, bq,
    smp, hp, bd, smc, hc, aT, xc, xp, gef, tmp_p, tmp_c,
    do, dqp, dkv, dkvp, dfar, gacc, snd_p, got_p, s_p, t_p, snd_c, got_c, s_c, t_c,
    dsnd_p, dgot_p, ds_p, dt_p, dsnd_c, dgot_c, ds_c, dt_c, dup, duc, outp, outc, tgp, tgc, tmp,
    l0s, l0x, l0z, l0, l1s, l1x, l1z, l2s, l2x, l2z, t1, t2, xr, zs, zr,
    lsem, osem, dsem, ysem, psem, csem, dpsem, dcsem, nsem, q1, q2, f0, f1, f2, f3, *rsems,
):
    d, t = place()
    sc = [ids_p[0], ids_c[0], ids_c[1], group_map[d * CONT_DEV], group_map[d * CONT_DEV + 1]]
    lo = t % 2
    hi = n_dp // 2
    width = wq.shape[0]
    qw = wq.shape[1]
    kvw = wkv.shape[1] // 2
    quarter = n1q_h.shape[1]
    hpn, hcn = PLEN // 2, CLEN
    greet(d, t, n_dp)
    qlanes = pl.ds(pl.multiple_of(lo * quarter, quarter), quarter)
    every = PairReduce(None, None, None, gef, rsems[0:8], d, t, n_dp)
    pairs = [
        (ge_h, gef.at[every.part(d // 2)]), (dac_h, dac), (wo_h, wo), (o_h, o), (aoT_h, aoT), (bo_h, bo), (n2c_h, n2c),
        (uoc_h, uoc), (q_h, q), (kv_h, kv), (far_h, far), (pc_h, pc), (cos_h, cos), (sin_h, sin), (dap_h, dap),
        (pp_h, pp), (n2p_h, n2p), (uop_h, uop), (u_h, u), (wq_h, wq), (wkv_h, wkv), (bq_h, bq),
        (smp_h, smp), (hp_h, hp), (bd_h, bd), (smc_h, smc), (hc_h, hc),
        (aT_h, aT), (tok_h.at[pl.ds(pl.multiple_of(PLEN + lo * hcn, hcn), hcn)], xc),
        (tok_h.at[pl.ds(pl.multiple_of(lo * hpn, hpn), hpn)], xp),
    ]
    loads = {}

    def fetch(first, last):
        for n in range(first, last):
            src, dst = pairs[n]
            c = pltpu.make_async_copy(src, dst, lsem.at[n])
            c.start()
            loads[id(dst) if n else 0] = c

    fetch(0, 14)

    def need(*refs):
        for ref in refs:
            loads.pop(id(ref)).wait()

    stores = []

    def store(src, dst):
        c = pltpu.make_async_copy(src, dst, osem.at[len(stores)])
        c.start()
        stores.append(c)

    greeted(n_dp)
    mlp_p = remote(smp_h, tmp_p, ysem.at[0], ysem.at[1], (d, t ^ 2))
    mlp_p.start()
    mlp_c = remote(smc_h, tmp_c, ysem.at[2], ysem.at[3], (d, t ^ 2))
    mlp_c.start()
    loads.pop(0).wait()
    every.spread()

    at = np.cumsum([0, quarter, quarter, quarter, qw, qw, 2 * kvw]).tolist()
    bkv = dn(evens_first(2 * RK), bkv_ref[...].reshape(2 * RK, kvw)).astype(BF)

    def out_grads(da, n2, uo, sel, r0, first):
        half = da.shape[1]
        r = 2 * half
        dav = da[:, :, :width].reshape(r, width)
        duo = (dt(dav, bo[...]) * sel).astype(BF)
        do[r0 : r0 + r] = (dt(dav, wo[...]) + dn(duo, aoT[...])).astype(BF)
        gao = dr(duo, o[r0 : r0 + r])
        dum = da[:, :, width:].reshape(r, 2 * RK)
        gam = dr(dum, n2[...].reshape(r, quarter))
        gbo = dr(uo[:, :, :RK].reshape(r, RK), da[:, :, qlanes].reshape(r, quarter))
        parts = (gbo, gam[:RK], gam[RK:], gao)
        for n, part in enumerate(parts):
            lanes = slice(at[n], at[n + 1])
            gacc[:, lanes] = part if first else gacc[:, lanes] + part

    def unrotate(r0, r):
        here = slice(r0, r0 + r)
        for c in range(qw // LANE):
            lanes = slice(c * LANE, (c + 1) * LANE)
            dqp[here, lanes] = rot(dqp[here, lanes].astype(F32), cos[here], -sin[here]).astype(BF)
        dkvp[here, :kvw] = rot(dkv[here, :kvw].astype(BF).astype(F32), cos[here], -sin[here]).astype(BF)
        dkvp[here, kvw:] = dkv[here, kvw:].astype(BF)

    need(dac, wo, o, aoT, bo, n2c, uoc)
    sel_c = jnp.concatenate([jnp.broadcast_to(sel_row(sc[1]), (hcn, RK)), jnp.broadcast_to(sel_row(sc[2]), (hcn, RK))], axis=0)
    out_grads(dac, n2c, uoc, sel_c, PLEN, True)
    fetch(14, 22)
    need(q, kv, far, pc)

    def attend(j):
        r0 = pl.multiple_of(PLEN + j * CLEN, CLEN)
        own = pl.ds(r0, CLEN)
        for g in range(2):
            lanes = slice(g * HD, (g + 1) * HD)
            vlanes = slice(kvw + g * HD, kvw + (g + 1) * HD)
            qi = stack_heads(q, r0, g)
            doi = stack_heads(do, r0, g)
            p = pc[2 * j + g]
            dp = jnp.concatenate([dt(doi, far[j, :, vlanes]), dt(doi, kv[own, vlanes])], axis=1)
            ds = back_scores(p, dp)
            dqv = dn(ds[:, :PLEN], far[j, :, lanes]) + dn(ds[:, PLEN:], kv[own, lanes])
            put_dq((dqv * 0.125).astype(BF), dqp, r0, g)
            dk = dr(ds, qi)
            dv = dr(p, doi)
            dfar[j, :, lanes] = dk[:PLEN].astype(BF)
            dfar[j, :, vlanes] = dv[:PLEN].astype(BF)
            dkv[own, lanes] = dk[PLEN:]
            dkv[own, vlanes] = dv[PLEN:]
        fold.across(j).start()

    mate = (d ^ 1) * CONT_DEV
    others = [group_map[mate + j] for j in range(CONT_DEV)]
    fold = Fold(dfar, xr, zs, zr, (f0, f1, f2, f3), sc[3:], others, d, t, hi)
    loop(0, CONT_DEV, attend)
    fetch(22, len(pairs))
    need(cos, sin)
    unrotate(PLEN, 2 * hcn)

    def dn1(r0, snd, dsnd, dsum, first):
        half = snd.shape[1]
        r = 2 * half
        here = slice(r0, r0 + r)
        a, b = dqp[here], dkvp[here]
        du = jnp.concatenate(
            [dt(a, bq[...]), dt(b[:, :kvw], bkv[:RK]), dt(b[:, kvw:], bkv[RK:]), jnp.zeros((r, RK), F32)], axis=1
        ).astype(BF)
        dsnd[0] = du[:half]
        dsnd[1] = du[half:]
        dsum.begin()

        def columns(n):
            lanes = pl.ds(pl.multiple_of(n * 512, 512), 512)
            part = (dt(a, wq[lanes]) + dt(b, wkv[lanes])).astype(BF)
            snd[0, :, lanes] = part[:half]
            snd[1, :, lanes] = part[half:]

        loop(0, width // 512, columns)
        gbq = dr(u[here, :RK], a)
        gkv = dr(u[here, RK:], b)
        parts = (gbq, gkv[:RK, :kvw], gkv[RK:, kvw:])
        for part, start in zip(parts, (at[4], at[5], at[5] + kvw)):
            lanes = slice(start, start + part.shape[1])
            gacc[:, lanes] = part if first else gacc[:, lanes] + part

    need(wq, wkv, u, bq)
    dsum_c = TensorSum(dsnd_c, dgot_c, ds_c, dt_c, dcsem, d, t)
    dn1(PLEN, snd_c, dsnd_c, dsum_c, True)
    sum_c = TensorSum(snd_c, got_c, s_c, t_c, csem, d, t)
    sum_c.begin()
    fold.fold()

    need(dap, n2p, uop)
    out_grads(dap, n2p, uop, jnp.broadcast_to(sel_row(sc[0]), (PLEN, RK)), 0, False)
    load_dy = []
    for n in range(2):
        for ref, start, half in ((dap, n * hpn, hpn), (dac, PLEN + n * hcn, hcn)):
            here = pl.ds(start, half)
            for src, lanes in ((dy_h.at[here, qlanes], slice(0, quarter)), (n1q_h.at[here], slice(quarter, 2 * quarter))):
                c = pltpu.make_async_copy(src, ref.at[n, :, lanes], dsem.at[len(load_dy)])
                c.start()
                load_dy.append(c)
    dsum_c.middle()
    sum_c.middle()
    need(pp)
    for g in range(2):
        lanes = slice(g * HD, (g + 1) * HD)
        vlanes = slice(kvw + g * HD, kvw + (g + 1) * HD)
        kg = kv[:PLEN, lanes]
        vg = kv[:PLEN, vlanes]
        for i in reversed(range(PLEN // CLEN)):
            size = (i + 1) * CLEN
            qi = stack_heads(q, i * CLEN, g)
            doi = stack_heads(do, i * CLEN, g)
            p = pp[g, :, P_OFF[i] : P_OFF[i] + size]
            ds = back_scores(p, dt(doi, vg[:size]))
            put_dq((dn(ds, kg[:size]) * 0.125).astype(BF), dqp, i * CLEN, g)
            dk = dr(ds, qi)
            dv = dr(p, doi)
            if size == PLEN:
                dkv[:size, lanes] = dk
                dkv[:size, vlanes] = dv
            else:
                dkv[:size, lanes] += dk
                dkv[:size, vlanes] += dv
    every.cross()

    def finish_out(which, sm, theirs, copy, h, out, r0, adapter):
        half = h.shape[0]
        copy.wait_recv()
        sr = sel_row(adapter)
        ud = ((sm[:, width : width + RK].astype(F32) + theirs[:, width : width + RK].astype(F32)) * sr).astype(BF)
        tmp[:half] = dn(ud, bd[...])

        def one(r):
            here = pl.ds(r, 64)
            out[lo, here, :width] = (
                h[here] + (sm[here, :width].astype(F32) + theirs[here, :width].astype(F32)) + tmp[here]
            ).astype(BF)

        rows_loop(half, 64, one)
        out[lo, :, width:] = jnp.concatenate([ud, jnp.zeros((half, LANE - RK), BF)], axis=1)
        c = remote(out.at[lo], out.at[lo], nsem.at[which, 0], nsem.at[which, 1], (d, t ^ 1))
        c.start()
        return c

    def arrived(which, out):
        remote(out.at[1 - lo], out.at[1 - lo], nsem.at[which, 0], nsem.at[which, 1], (d, t ^ 1)).wait_recv()

    need(smp, hp, bd)
    out_copy_p = finish_out(0, smp, tmp_p, mlp_p, hp, outp, 0, sc[0])
    load_dhp = pltpu.make_async_copy(dhp_h, hp, lsem.at[32])
    load_dhp.start()

    adapter_c = jnp.where(lo == 0, sc[1], sc[2])
    per = quarter // LANE * (RK // 16)

    def fill(blocks, used):
        if blocks.shape[0] > used:
            blocks[used:] = jnp.zeros((blocks.shape[0] - used, *UNIT), BF)

    def share_du(which, total, du, adapter):
        total.end()
        sr = sel_row(adapter)
        raw = total.mine[:, : 3 * RK].astype(F32) + total.theirs[:, : 3 * RK].astype(F32)
        duq = (raw * jnp.concatenate([sr, sr, sr], axis=1)).astype(BF)
        du[lo] = jnp.concatenate([duq, jnp.zeros((duq.shape[0], RK), BF)], axis=1)
        c = remote(du.at[lo], du.at[lo], nsem.at[which, 0], nsem.at[which, 1], (d, t ^ 1))
        c.start()
        return c

    need(smc, hc, aT)
    out_copy_c = finish_out(1, smc, tmp_c, mlp_c, hc, outc, PLEN, adapter_c)
    load_dhc = pltpu.make_async_copy(dhc_h, hc, lsem.at[33])
    load_dhc.start()
    du_copy_c = share_du(4, dsum_c, duc, adapter_c)
    for c in load_dy:
        c.wait()
    arrived(0, outp)
    gbd = dr(outp[:, :, width : width + RK].reshape(PLEN, RK), dap[:, :, :quarter].reshape(PLEN, quarter))
    arrived(1, outc)
    gbd = gbd + dr(outc[:, :, width : width + RK].reshape(2 * hcn, RK), dac[:, :, :quarter].reshape(2 * hcn, quarter))

    put_units(l1s, 0, gacc[:, : at[3]].astype(BF))
    put_units(l1s, 3 * per, gbd.astype(BF))
    fill(l1s, 4 * per)
    red1 = PairReduce(l1s, l1x, l1z, t1.at[lo], rsems[8:16], d, t, n_dp)
    red1.start()
    trade1 = Trade(t1, q1, d, t)
    for n in range(2):
        store(outp.at[n, :, :width], out_h.at[pl.ds(n * hpn, hpn)])
        store(outc.at[n, :, :width], out_h.at[pl.ds(PLEN + n * hcn, hcn)])
    arrived(4, duc)
    ga_c = dr(duc[:, :, : 3 * RK].reshape(2 * hcn, 3 * RK), dac[:, :, quarter : 2 * quarter].reshape(2 * hcn, quarter))

    fold.finish(dkv.at[:PLEN])
    unrotate(0, PLEN)
    dsum_p = TensorSum(dsnd_p, dgot_p, ds_p, dt_p, dpsem, d, t)
    dn1(0, snd_p, dsnd_p, dsum_p, False)
    sum_p = TensorSum(snd_p, got_p, s_p, t_p, psem, d, t)
    dsum_p.middle()
    sum_p.begin()
    put_units(l0s, 0, gacc[:, at[3] :].astype(BF))
    fill(l0s, (at[6] - at[3]) // LANE * (RK // 16))
    red0 = PairReduce(l0s, l0x, l0z, l0, rsems[16:24], d, t, n_dp)
    red0.start()
    sum_p.middle()
    red1.middle()
    du_copy_p = share_du(5, dsum_p, dup, sc[0])
    arrived(5, dup)
    ga_p = dr(dup[:, :, : 3 * RK].reshape(PLEN, 3 * RK), dap[:, :, quarter : 2 * quarter].reshape(PLEN, quarter))
    ga = (ga_c + ga_p).astype(BF)
    for n in range(3):
        put_units(l2s, n * per, ga[n * RK : (n + 1) * RK])
    fill(l2s, 3 * per)
    red2 = PairReduce(l2s, l2x, l2z, t2.at[lo], rsems[24:32], d, t, n_dp)
    red2.start()
    trade2 = Trade(t2, q2, d, t)

    def last(which, total, du, x, dh, tg):
        half = x.shape[0]
        tmp[:half] = dn(du[lo, :, : 3 * RK], aT[...])
        gain = gain1[...].astype(F32).reshape(1, width)
        total.end()

        def one(r):
            here = pl.ds(r, 64)
            dn1v = total.mine[here].astype(F32) + total.theirs[here].astype(F32) + tmp[here]
            grad = dh[here] + norm_back(x[here].astype(F32), gain, dn1v)
            tg[lo, here] = grad.astype(BF)

        rows_loop(half, 64, one)
        c = remote(tg.at[lo], tg.at[lo], nsem.at[which, 0], nsem.at[which, 1], (d, t ^ 1))
        c.start()
        return c

    red1.add()
    red0.middle()
    need(xc)
    load_dhc.wait()
    tg_copy_c = last(2, sum_c, duc, xc, hc, tgc)
    red2.middle()
    red1.cross()
    red0.add()
    every.finish()
    store(gef, gef_h)
    red2.add()
    arrived(2, tgc)
    for n in range(2):
        store(tgc.at[n], tg_h.at[pl.ds(PLEN + n * hcn, hcn)])
    red0.cross()
    red1.finish()
    trade1.start()
    red2.cross()
    trade1.finish()
    store(t1, t1_h)
    need(xp)
    load_dhp.wait()
    tg_copy_p = last(3, sum_p, dup, xp, hp, tgp)
    red0.finish()
    store(l0, l0_h)
    red2.finish()
    trade2.start()
    arrived(3, tgp)
    for n in range(2):
        store(tgp.at[n], tg_h.at[pl.ds(n * hpn, hpn)])
    trade2.finish()
    store(t2, t2_h)
    for c in (out_copy_p, out_copy_c, tg_copy_c, tg_copy_p, du_copy_c, du_copy_p, mlp_p, mlp_c):
        c.wait_send()
    for total in (sum_p, sum_c, dsum_p, dsum_c):
        total.drain()
    fold.drain()
    every.spread_sent()
    for red in (red0, red1, red2):
        red.sent()
        red.spread_sent()
    trade1.sent()
    trade2.sent()
    for c in stores:
        c.wait()


def backward(n_dp, scalars, small, large):
    (dac, wo, o, aoT, bo, n2c, uoc, q, kv, far, pc, cos, sin, dap, pp, n2p, uop, u, wq, wkv, bq, smp, hp, bd, smc, hc, dy, n1q,
     dhc, aT, dhp, tok, ge) = large
    rows, width = tok.shape
    qw = wq.shape[1]
    kvw2 = wkv.shape[1]
    quarter = n1q.shape[1]
    wide = dap.shape[2]
    hpn, hcn = PLEN // 2, CLEN
    per = quarter // LANE * (RK // 16)
    up = lambda a: -(-a // n_dp) * n_dp
    ue = ge.shape[0] * n_dp
    u0 = up((2 * qw + kvw2) // LANE * (RK // 16))
    u1 = up(4 * per)
    u2 = up(3 * per)
    outs = [
        ((rows, width), BF), ((rows, width), BF), ((ue, *UNIT), BF), ((u0, *UNIT), BF), ((2, u1, *UNIT), BF),
        ((2, u2, *UNIT), BF),
    ]
    dma = pltpu.SemaphoreType.DMA
    hi = n_dp // 2
    same = lambda a: VM(a.shape, a.dtype)

    def sums(half, n):
        return [VM((2, half, n), BF), VM((half, n), BF), VM((half, n), BF), VM((half, n), BF)]

    scratch = [
        same(dac), same(wo), same(o), same(aoT), same(bo), VM((2, hcn, quarter), BF), VM((2, hcn, LANE), BF), same(q), same(kv),
        same(far), same(pc), same(cos), same(sin), same(dap), same(pp), VM((2, hpn, quarter), BF), VM((2, hpn, LANE), BF),
        same(u), same(wq), same(wkv), same(bq), same(smp), same(hp), same(bd), same(smc), same(hc),
        same(aT), VM((hcn, width), BF), VM((hpn, width), BF), VM((ue, *UNIT), BF),
        same(smp), same(smc),
        VM((rows, qw), BF), VM((rows, qw), BF), VM((rows, kvw2), F32), VM((rows, kvw2), BF),
        VM((CONT_DEV, PLEN, kvw2), BF), VM((RK, 2 * qw + 3 * quarter + kvw2), F32),
        *sums(hpn, width), *sums(hcn, width), *sums(hpn, 2 * LANE), *sums(hcn, 2 * LANE),
        VM((2, hpn, 2 * LANE), BF), VM((2, hcn, 2 * LANE), BF),
        VM((2, hpn, wide), BF), VM((2, hcn, wide), BF), VM((2, hpn, width), BF), VM((2, hcn, width), BF), VM((hpn, width), F32),
        VM((u0, *UNIT), BF), VM((u0 // 2, *UNIT), BF), VM((hi, u0 // n_dp, *UNIT), BF), VM((u0, *UNIT), BF),
        VM((u1, *UNIT), BF), VM((u1 // 2, *UNIT), BF), VM((hi, u1 // n_dp, *UNIT), BF),
        VM((u2, *UNIT), BF), VM((u2 // 2, *UNIT), BF), VM((hi, u2 // n_dp, *UNIT), BF),
        VM((2, u1, *UNIT), BF), VM((2, u2, *UNIT), BF),
        VM((CONT_DEV, PLEN, kvw2), BF), VM((hi, PLEN, kvw2), BF), VM((hi, PLEN, kvw2), BF),
        dma((34,)), dma((13,)), dma((8,)), dma((4,)), dma((4,)), dma((4,)), dma((4,)), dma((4,)), dma((6, 2)), dma((2,)), dma((2,)),
    ] + [dma((CONT_DEV,))] * 2 + [dma((hi,))] * 2 + [dma((n_dp,))] * 32
    vm = pl.BlockSpec(memory_space=VM)
    anyspace = pl.BlockSpec(memory_space=pl.ANY)
    return pl.pallas_call(
        functools.partial(back_kernel, n_dp),
        out_shape=[jax.ShapeDtypeStruct(s, dtype) for s, dtype in outs],
        in_specs=[pl.BlockSpec(memory_space=pltpu.SMEM)] * 3 + [vm] * len(small) + [anyspace] * len(large),
        out_specs=[anyspace] * len(outs),
        scratch_shapes=scratch,
        compiler_params=pltpu.CompilerParams(vmem_limit_bytes=63 << 20, collective_id=3, has_side_effects=True),
        cost_estimate=pl.CostEstimate(flops=6 * rows * width * (2 * qw + kvw2), bytes_accessed=40 << 20, transcendentals=0),
        name="back",
    )(*scalars, *small, *large)


def emit_kernel(
    qw, kvw, quarter, hidden, ge, l0, t1, t2, out_h, tg_h,
    gbm_o, gad_o, gao_o, gbq_o, gbkv_o, gbo_o, gam_o, gbd_o, ga_o, out_o, tg_o,
    gbm, gad, gao, gbq, gbkv, gbo, gam, gbd, ga, buf, sem, wsem,
):
    pairs = ((out_h, out_o), (tg_h, tg_o))
    copies = [pltpu.make_async_copy(src, buf.at[n], sem.at[n]) for n, (src, _) in enumerate(pairs)]
    for c in copies:
        c.start()
    high = RK // 16
    writes = []

    def write(src, dst):
        c = pltpu.make_async_copy(src, dst, wsem.at[len(writes)])
        c.start()
        writes.append(c)

    def take(blocks, first, count, put):
        for b in range(count // LANE):
            for r in range(high):
                put(slice(r * 16, (r + 1) * 16), slice(b * LANE, (b + 1) * LANE), blocks[first + b * high + r].astype(F32))

    def plain(dst, row=0, lane=0):
        def put(rows, lanes, value):
            dst[rows.start + row : rows.stop + row, lanes.start + lane : lanes.stop + lane] = value

        return put

    def paired(dst, n):
        def put(rows, lanes, value):
            dst[rows, n, lanes] = value

        return put

    seg = hidden // LANE * high
    take(ge, 2 * seg, hidden, plain(gad))
    write(gad, gad_o)
    take(ge, 0, hidden, paired(gbm, 0))
    take(ge, seg, hidden, paired(gbm, 1))
    write(gbm, gbm_o)
    for n, (c, (_, dst)) in enumerate(zip(copies, pairs)):
        c.wait()
        write(buf.at[n], dst)
    per = quarter // LANE * high
    for t in range(t1.shape[0]):
        take(t1.at[t], 0, quarter, plain(gbo, 0, t * quarter))
        take(t1.at[t], per, quarter, plain(gam, 0, t * quarter))
        take(t1.at[t], 2 * per, quarter, plain(gam, RK, t * quarter))
        take(t1.at[t], 3 * per, quarter, plain(gbd, 0, t * quarter))
        for n in range(3):
            take(t2.at[t], n * per, quarter, plain(ga, n * RK, t * quarter))
    write(gbo, gbo_o)
    write(gam, gam_o)
    write(gbd, gbd_o)
    write(ga, ga_o)
    take(l0, 0, qw, plain(gao))
    write(gao, gao_o)
    begin = qw // LANE * high
    take(l0, begin, qw, plain(gbq))
    write(gbq, gbq_o)
    take(l0, 2 * begin, kvw, paired(gbkv, 0))
    take(l0, 2 * begin + kvw // LANE * high, kvw, paired(gbkv, 1))
    write(gbkv, gbkv_o)
    for c in writes:
        c.wait()


def emit(qw, kvw, quarter, hidden, grads, results):
    width = 2 * quarter
    outs = [
        ((RK, 2, hidden), F32), ((RK, hidden), F32), ((RK, qw), F32), ((RK, qw), F32), ((RK, 2, kvw), F32), ((RK, width), F32),
        ((2 * RK, width), F32), ((RK, width), F32), ((3 * RK, width), F32),
    ]
    vm = pl.BlockSpec(memory_space=VM)
    anyspace = pl.BlockSpec(memory_space=pl.ANY)
    return pl.pallas_call(
        functools.partial(emit_kernel, qw, kvw, quarter, hidden),
        out_shape=[jax.ShapeDtypeStruct(s, dtype) for s, dtype in outs]
        + [jax.ShapeDtypeStruct(a.shape, a.dtype) for a in results],
        in_specs=[vm] * len(grads) + [anyspace] * len(results),
        out_specs=[anyspace] * (len(outs) + len(results)),
        scratch_shapes=[VM(s, dtype) for s, dtype in outs]
        + [VM((2, *results[0].shape), BF), pltpu.SemaphoreType.DMA((2,)), pltpu.SemaphoreType.DMA((11,))],
        compiler_params=pltpu.CompilerParams(vmem_limit_bytes=61 << 20),
        cost_estimate=pl.CostEstimate(flops=0, bytes_accessed=20 << 20, transcendentals=0),
        name="emit",
    )(*grads, *results)


def rope_tables():
    position = np.concatenate([np.arange(PLEN)] + [PLEN + np.arange(CLEN)] * CONT_DEV).astype(np.float32)
    exponent = np.arange(HD // 2, dtype=np.float32) * np.float32(2.0 / HD)
    frequency = np.exp(np.float32(-math.log(ROPE_BASE)) * exponent).astype(np.float32)
    angle = position[:, None] * frequency[None, :]
    cos, sin = np.cos(angle).astype(np.float32), np.sin(angle).astype(np.float32)
    return np.tile(cos, (1, 4)), np.concatenate([-sin, sin, -sin, sin], axis=1)


def shards(
    tokens, cotangent, gain_attn, gain_mlp, w_query, w_kv, w_out, w_gate_up, w_down, a_attn, b_query, b_kv,
    a_out, b_out, a_mlp, b_mlp, a_down, b_down, prompt_adapter, cont_adapter, group_map,
):
    rows, width = tokens.shape
    qw = w_query.shape[1]
    kvw = w_kv.shape[2]
    hidden = w_down.shape[0]
    n_dp = lax.axis_size("dp")
    quarter = width // 2
    cos_np, sin_np = rope_tables()
    cos, sin = jnp.asarray(cos_np), jnp.asarray(sin_np)
    gain1, gain2 = gain_attn, gain_mlp
    aT = a_attn.transpose(1, 2, 3, 0).reshape(3 * RK, width)
    aoT = a_out.transpose(1, 2, 0).reshape(RK, qw)
    amT = a_mlp.transpose(1, 2, 3, 0).reshape(2 * RK, width)
    adT = a_down.transpose(1, 2, 0).reshape(RK, hidden)
    bq = b_query.reshape(RK, qw)
    bkv = b_kv.reshape(RK, 2, kvw)
    bo = b_out.reshape(RK, width)
    bm = b_mlp.reshape(RK, 2, hidden)
    bd = b_down.reshape(RK, width)
    wkv = w_kv.reshape(width, 2 * kvw)
    (n1q, q, kv, u, pp, pc, o, far, h_p, h_c, n2p, n2c, uop, uoc, _, dh_p, dh_c, dap, dac, sm_p, sm_c, ge) = first(
        n_dp, [prompt_adapter, cont_adapter, group_map], [gain1, gain2, bkv, bm, amT, adT, bo],
        [tokens, aT, wkv, cos, sin, w_query, bq, aoT, w_out, cotangent, bd, w_down, w_gate_up],
    )
    results = backward(
        n_dp, [prompt_adapter, cont_adapter, group_map], [gain1, bkv],
        [dac, w_out, o, aoT, bo, n2c, uoc, q, kv, far, pc, cos, sin, dap, pp, n2p, uop, u, w_query, wkv, bq, sm_p, h_p, bd, sm_c,
         h_c, cotangent, n1q, dh_c, aT, dh_p, tokens, ge],
    )
    gbm, gad, gao, gbq, gbkv, gbo, gam, gbd, ga, output, tokens_grad = emit(qw, kvw, quarter, hidden, results[2:], results[:2])
    return (
        output,
        tokens_grad,
        ga.reshape(3, NA, R, width).transpose(3, 0, 1, 2),
        gbq.reshape(b_query.shape),
        gbkv.reshape(b_kv.shape),
        gao.reshape(NA, R, qw).transpose(2, 0, 1),
        gbo.reshape(b_out.shape),
        gam.reshape(2, NA, R, width).transpose(3, 0, 1, 2),
        gbm.reshape(b_mlp.shape),
        gad.reshape(NA, R, hidden).transpose(2, 0, 1),
        gbd.reshape(b_down.shape),
    )


def solution(mesh):
    in_specs = (
        P("dp", None), P("dp", None), P(), P(), P(None, "tensor"), P(None, None, "tensor"), P("tensor", None),
        P(None, None, "tensor"), P("tensor", None), P(), P(None, None, "tensor"), P(None, None, None, "tensor"),
        P("tensor", None, None), P(), P(), P(None, None, None, "tensor"), P("tensor", None, None), P(),
        P("dp"), P("dp"), P(),
    )
    out_specs = (
        P("dp", None), P("dp", None), P(), P(None, None, "tensor"), P(None, None, None, "tensor"),
        P("tensor", None, None), P(), P(), P(None, None, None, "tensor"), P("tensor", None, None), P(),
    )
    return jax.shard_map(shards, mesh=mesh, in_specs=in_specs, out_specs=out_specs, check_vma=False)
```
